128 devices in a mesh: section: 2 (over core), dp: 16 (over y, z), tensor: 4 (over x).
Axes of the slice: x: 4, y: 4, z: 4, core: 2. Of those that a mesh axis runs over, the one named last changes fastest.
Arguments:
- tokens: bfloat16 [2, 4096, 1024], P(None, ('dp', 'tensor')), may hold values from -6 to 6
- segment_ids: int32 [2, 4096], P(None, ('dp', 'tensor')), may hold values from 0 to 2, as said below
- w_qkv: bfloat16 [2, 3, 1024, 1024], P('section', None, 'dp', 'tensor'), may hold values from -0.1875 to 0.1875
- w_out: bfloat16 [2, 1024, 1024], P('section', 'dp', 'tensor'), may hold values from -3 to 3
- w_up: bfloat16 [2, 1024, 4096], P('section', 'dp', 'tensor'), may hold values from -0.1875 to 0.1875
- w_down: bfloat16 [2, 1024, 4096], P('section', 'dp', 'tensor'), may hold values from -0.09375 to 0.09375
- vectors: bfloat16 [2, 13, 1024], P('section', None, 'dp'), may hold values from -1.6 to 1.6
- out_bias: bfloat16 [2, 1024], P('section', 'dp'), may hold values from -1.5 to 1.5
- cotangent: bfloat16 [2, 4096, 1024], P(None, ('dp', 'tensor')), may hold values from -6 to 6
Outputs:
- section_out: bfloat16 [2, 2, 4096, 1024], P('section', None, ('dp', 'tensor'))
- input_grad: float32 [2, 2, 4096, 1024], P('section', None, ('dp', 'tensor'))
- grad_qkv: float32 [2, 3, 1024, 1024], P('section', None, 'dp', 'tensor')
- grad_out: float32 [2, 1024, 1024], P('section', 'dp', 'tensor')
- grad_up: float32 [2, 1024, 4096], P('section', 'dp', 'tensor')
- grad_down: float32 [2, 1024, 4096], P('section', 'dp', 'tensor')
- grad_vectors: float32 [2, 13, 1024], P('section', None, 'dp')
- grad_out_bias: float32 [2, 1024], P('section', 'dp')
The draws below stay inside these ranges and needn't reach their ends.
Inputs may be any that keep to these rules, and one draw needn't show every extreme that they name: `segment_ids`: each micro-batch packs three images; within every aligned block of 256 tokens of a micro-batch the ids never fall and each of 0, 1 and 2 occurs.
All inputs are finite; a program needn't handle non-finite values.
Results may differ from the reference program's by a relative error of at most 0.02.
Values may be sent and summed in bfloat16 or wider, within the bound.
A program may use at most 192 MiB of HBM per device.

```python
from functools import partial
import jax
import jax.numpy as jnp
from jax import lax

D = 1024
HEADS = 16
HEAD_DIM = 64
FF = 4096
MICRO = 2
ROWS = 256
SEQ = 4096
VROWS = 13


def draw_segment_ids(key, part):
    key = jax.random.fold_in(key, 11)
    first_key, second_key = jax.random.split(key)
    blocks = SEQ // ROWS
    third = ROWS // 3
    jitter = max(ROWS // 8, 1)
    first_cut = jax.random.randint(first_key, (MICRO, blocks, 1), third - jitter, third + jitter + 1)
    second_run = jax.random.randint(second_key, (MICRO, blocks, 1), third - jitter, third + jitter + 1)
    second_cut = first_cut + second_run
    position = jnp.arange(ROWS)[None, None, :]
    labels = (position >= first_cut).astype(jnp.int32) + (position >= second_cut).astype(jnp.int32)
    return labels.reshape(MICRO, SEQ)


def draw_vectors(key, part):
    key = jax.random.fold_in(key, 12)
    normal_key, flat_key = jax.random.split(key)
    row_index = jnp.arange(VROWS)[None, :, None]
    is_gain = (row_index == 0) | (row_index == 5)
    is_scale = (row_index == 4) | (row_index == 8)
    noise_draw = jnp.clip(jax.random.normal(normal_key, (2, VROWS, D), jnp.float32), -5.0, 5.0)
    flat_draw = jax.random.uniform(flat_key, (2, VROWS, D), jnp.float32, 0.0, 1.0)
    gain_rows = 0.5 + flat_draw
    scales = 0.4 + 0.8 * flat_draw
    biases = 0.3 * noise_draw
    return jnp.where(is_gain, gain_rows, jnp.where(is_scale, scales, biases)).astype(jnp.bfloat16)


def steps_of(key, extent, cuts, low, largest):
    level, own = 1.0, jax.random.fold_in(key, 6)
    for dim, blocks in cuts:
        steps = jnp.exp(jax.random.uniform(jax.random.fold_in(own, dim), (blocks,), jnp.float32, low / len(cuts), largest / len(cuts)))
        level = level * jnp.repeat(steps, extent[dim] // blocks).reshape([-1 if axis == dim else 1 for axis in range(len(extent))])
    return level


def normal_values(own_key, shape, deviation, limit, pieces=(), held_as=jnp.bfloat16):
    values = jax.random.normal(own_key, shape, jnp.float32) * deviation
    if len(pieces) > 0:
        values = steps_of(own_key, shape, pieces, -0.22, 0.18) * values
    return jnp.clip(values, min=-limit, max=limit).astype(held_as)


def setup_inputs(seed: int = 0) -> dict:
    splits = jax.random.split(jax.random.key(seed), 10)
    return {
        "tokens": normal_values(splits[0], (MICRO, SEQ, D), 1.0, 6.0, ((1, 64),)),
        "segment_ids": draw_segment_ids(jax.random.fold_in(splits[9], 71), 0),
        "w_qkv": normal_values(splits[2], (2, 3, D, D), D ** -0.5, 0.1875, ((0, 2), (2, 16), (3, 4))),
        "w_out": normal_values(splits[3], (2, D, D), (max(D // 256, 1)) ** -0.5, 3.0, ((0, 2), (1, 16), (2, 4))),
        "w_up": normal_values(splits[4], (2, D, FF), D ** -0.5, 0.1875, ((0, 2), (1, 16), (2, 4))),
        "w_down": normal_values(splits[5], (2, D, FF), FF ** -0.5, 0.09375, ((0, 2), (1, 16), (2, 4))),
        "vectors": draw_vectors(jax.random.fold_in(splits[9], 71), 0),
        "out_bias": normal_values(splits[7], (2, D), 0.3, 1.5, ((0, 2), (1, 16))),
        "cotangent": normal_values(splits[8], (MICRO, SEQ, D), 1.0, 6.0, ((1, 64),)),
    }


@jax.custom_vjp
def low(v):
    return lax.optimization_barrier(v.astype(jnp.bfloat16)).astype(jnp.float32)

@jax.custom_vjp
def low_back(v):
    return v

def low_keep(v):
    return (low(v), None)

def low_pass(kept, grad):
    return (grad,)

def back_keep(v):
    return (v, None)

def back_low(kept, grad):
    return (low(grad),)
low.defvjp(low_keep, low_pass)
low_back.defvjp(back_keep, back_low)
EPSILON = 1e-06
MASKED_SCORE = -1e+30

def layer_norm(values, gain_row, shift_row):
    centre = values - lax.optimization_barrier(jnp.mean(values, axis=-1, keepdims=True))
    spread = lax.optimization_barrier(jnp.mean(centre * centre, axis=-1, keepdims=True))
    return centre * lax.rsqrt(spread + EPSILON) * gain_row + shift_row

def matmul(former, latter):
    return jnp.dot(former, latter, precision=lax.Precision.HIGHEST)

def attend_head(allowed, operands):
    query_rows, key_rows, value_rows = operands
    scores = low_back(matmul(query_rows, key_rows.T)) * HEAD_DIM ** (-0.5)
    scores = jnp.where(allowed, scores, MASKED_SCORE)
    weights = jax.nn.softmax(scores, axis=-1)
    return matmul(low(weights), value_rows)

def heads_first(matrix):
    return matrix.reshape(SEQ, HEADS, HEAD_DIM).transpose(1, 0, 2)

def one_layer(inputs, params, allowed):
    w_qkv, w_out, w_up, w_down, vectors, out_bias = params
    gain_one, shift_one, query_bias, value_bias = (vectors[0], vectors[1], vectors[2], vectors[3])
    scale_one, gain_two, shift_two, down_bias, scale_two = (vectors[4], vectors[5], vectors[6], vectors[7], vectors[8])
    up_bias = vectors[9:].reshape(FF)
    normed = low(layer_norm(inputs, gain_one, shift_one))
    query_rows = low(low_back(matmul(normed, w_qkv[0])) + query_bias)
    key_rows = low(low_back(matmul(normed, w_qkv[1])))
    value_rows = low(low_back(matmul(normed, w_qkv[2])) + value_bias)
    mixed_heads = lax.map(jax.checkpoint(partial(attend_head, allowed)), (heads_first(query_rows), heads_first(key_rows), heads_first(value_rows)))
    mixed_heads = low(low_back(mixed_heads.transpose(1, 0, 2).reshape(SEQ, D)))
    attn_out = low_back(matmul(mixed_heads, w_out.T)) + out_bias
    hidden = inputs + scale_one * attn_out
    normed_two = low(layer_norm(hidden, gain_two, shift_two))
    pre_act = low_back(matmul(normed_two, w_up)) + up_bias
    activated = low(jax.nn.gelu(pre_act, approximate=False))
    mlp_out = low_back(matmul(activated, w_down.T)) + down_bias
    return hidden + scale_two * mlp_out

def reference(tokens, segment_ids, w_qkv, w_out, w_up, w_down, vectors, out_bias, cotangent):
    params = tuple((weight.astype(jnp.float32) for weight in (w_qkv, w_out, w_up, w_down, vectors, out_bias)))
    inputs = tokens.astype(jnp.float32)
    between = jnp.zeros_like(inputs)

    def forward(params, inputs, between):
        first_list = []
        last_list = []
        first_params = tuple((weight[0] for weight in params))
        second_params = tuple((weight[1] for weight in params))
        for micro_index in range(MICRO):
            segment = segment_ids[micro_index]
            allowed = segment[:, None] == segment[None, :]
            first_out = low(low_back(one_layer(inputs[micro_index], first_params, allowed))) + between[micro_index]
            last_out = one_layer(first_out, second_params, allowed)
            first_list.append(first_out)
            last_list.append(last_out)
        return (jnp.stack(first_list), jnp.stack(last_list))
    (first_all, last_all), pullback = jax.vjp(forward, params, inputs, between)
    param_grads, input_grads, between_grads = pullback((jnp.zeros_like(first_all), cotangent.astype(jnp.float32)))
    section_out = jnp.stack([first_all, last_all]).astype(jnp.bfloat16)
    input_grad = jnp.stack([input_grads, between_grads])
    return (section_out, input_grad, param_grads[0], param_grads[1], param_grads[2], param_grads[3], param_grads[4], param_grads[5])
```

```python
import functools

import jax
import jax.numpy as jnp
from jax import lax
from jax.experimental import pallas as pl
from jax.experimental.pallas import tpu as pltpu
from jax.sharding import PartitionSpec as P

MESH = pl.DeviceIdType.MESH
HEAD_DIM = 64
EPSILON = 1e-06
MASKED_SCORE = -1e30
RING = 4
CHUNKS = 2
VMEM_LIMIT = 56 * 1024 * 1024
F32 = jnp.float32
BF16 = jnp.bfloat16


def vmem_spec():
    return pl.BlockSpec(memory_space=pltpu.VMEM)


def any_spec():
    return pl.BlockSpec(memory_space=pl.ANY)


def comm_params(cid):
    return pltpu.CompilerParams(
        collective_id=cid, has_side_effects=True, vmem_limit_bytes=VMEM_LIMIT
    )


def step(coord, by):
    return lax.rem(coord + by, RING)


def layer_norm(values, gain_row, shift_row):
    centre = values - jnp.mean(values, axis=-1, keepdims=True)
    spread = jnp.mean(centre * centre, axis=-1, keepdims=True)
    return centre * lax.rsqrt(spread + EPSILON) * gain_row + shift_row


def layer_norm_back(values, gain_row, grad):
    centre = values - jnp.mean(values, axis=-1, keepdims=True)
    spread = jnp.mean(centre * centre, axis=-1, keepdims=True)
    inverse = lax.rsqrt(spread + EPSILON)
    normed = centre * inverse
    scaled = grad * gain_row
    back = inverse * (
        scaled
        - jnp.mean(scaled, axis=-1, keepdims=True)
        - normed * jnp.mean(scaled * normed, axis=-1, keepdims=True)
    )
    return back, jnp.sum(grad * normed, axis=0, keepdims=True), jnp.sum(grad, axis=0, keepdims=True)


def tensor_kernel(function, n_rows, n_vecs, n_out, n_sums, reduce, gather, with_seg, *refs):
    refs = list(refs)
    take = lambda count: [refs.pop(0) for _ in range(count)]
    part = take(1)[0] if reduce else None
    rows_in = take(n_rows)
    vecs = take(n_vecs)
    seg_in = take(1)[0] if with_seg else None
    rows_out = take(n_out)
    sums_out = take(1)[0] if n_sums else None
    full = take(1)[0] if gather else None
    seg_out = take(1)[0] if with_seg else None
    landing = take(1)[0] if reduce else None
    send, recv, local = take(3)

    me = lax.axis_index("tensor")
    barrier = pltpu.get_barrier_semaphore()
    for k in range(1, RING):
        pl.semaphore_signal(
            barrier, inc=1, device_id={"tensor": step(me, k)}, device_id_type=MESH
        )
    pl.semaphore_wait(barrier, RING - 1)

    total_rows = (rows_in[0] if rows_in else part).shape[-2]
    chunk = total_rows // CHUNKS
    started = []

    def push(source, target, kind, index, k):
        copy = pltpu.make_async_remote_copy(
            src_ref=source,
            dst_ref=target,
            send_sem=send.at[kind, index, k - 1],
            recv_sem=recv.at[kind, index, k - 1],
            device_id={"tensor": step(me, k)},
            device_id_type=MESH,
        )
        copy.start()
        started.append(copy)
        return copy

    reduces = {}
    if reduce:
        for c in range(CHUNKS):
            here = pl.ds(c * chunk, chunk)
            for k in range(1, RING):
                reduces[c, k] = push(
                    part.at[step(me, k), here], landing.at[k - 1, here], 0, c, k
                )
    last = []
    if with_seg:
        own = pltpu.make_async_copy(seg_in, seg_out.at[me], local)
        own.start()
        last += [push(seg_in, seg_out.at[me], 2, 0, k) for k in range(1, RING)]
    sums = [None] * n_sums
    for c in range(CHUNKS):
        here = pl.ds(c * chunk, chunk)
        total = None
        if reduce:
            for k in range(1, RING):
                reduces[c, k].wait_recv()
            total = part[me, here].astype(F32)
            for k in range(1, RING):
                total = total + landing[k - 1, here].astype(F32)
        spread, outs, parts = function(
            total, [ref[here].astype(F32) for ref in rows_in], vecs
        )
        if gather:
            full[me, here] = spread.astype(BF16)
            last += [push(full.at[me, here], full.at[me, here], 1, c, k) for k in range(1, RING)]
        for ref, value in zip(rows_out, outs):
            ref[here] = value.astype(ref.dtype)
        sums = [new if old is None else old + new for old, new in zip(sums, parts)]
    if n_sums:
        sums_out[...] = jnp.concatenate(
            sums + [jnp.zeros((8 - n_sums, sums[0].shape[1]), F32)], axis=0
        ) if n_sums < 8 else jnp.concatenate(sums, axis=0)
    for copy in last:
        copy.wait_recv()
    if with_seg:
        own.wait()
    for copy in started:
        copy.wait_send()


def tensor_call(cid, function, part, rows, vecs, outs, n_sums, gather, seg=None):
    height, width = rows[0].shape
    reduce = part is not None
    with_seg = seg is not None
    args = ([part] if reduce else []) + list(rows) + list(vecs) + ([seg] if with_seg else [])
    shapes = [jax.ShapeDtypeStruct((height, width), dtype) for dtype in outs]
    if n_sums:
        shapes.append(jax.ShapeDtypeStruct((8, width), F32))
    if gather:
        shapes.append(jax.ShapeDtypeStruct((RING, height, width), BF16))
    if with_seg:
        shapes.append(jax.ShapeDtypeStruct((RING,) + seg.shape, seg.dtype))
    scratch = [pltpu.VMEM((RING - 1, height, width), BF16)] if reduce else []
    scratch += [
        pltpu.SemaphoreType.DMA((3, CHUNKS, RING - 1)),
        pltpu.SemaphoreType.DMA((3, CHUNKS, RING - 1)),
        pltpu.SemaphoreType.DMA,
    ]
    return pl.pallas_call(
        functools.partial(
            tensor_kernel, function, len(rows), len(vecs), len(outs), n_sums, reduce, gather, with_seg
        ),
        out_shape=shapes,
        in_specs=[vmem_spec()] * len(args),
        out_specs=[vmem_spec()] * len(shapes),
        scratch_shapes=scratch,
        compiler_params=comm_params(cid),
    )(*args)


def row(ref, index):
    return ref[pl.ds(index, 1), :]


def first_rows(total, rows, vecs):
    return layer_norm(rows[0], row(vecs[0], 0), row(vecs[0], 1)), [], []


def middle_rows(total, rows, vecs):
    vec = vecs[0]
    attn_out = total + row(vec, 13)
    hidden = rows[0] + row(vec, 4) * attn_out
    return layer_norm(hidden, row(vec, 5), row(vec, 6)), [attn_out, hidden], []


def end_rows_first(total, rows, vecs):
    vec, after = vecs
    mlp_out = total + row(vec, 7)
    outputs = (rows[0] + row(vec, 8) * mlp_out).astype(BF16)
    inputs = outputs.astype(F32)
    return layer_norm(inputs, row(after, 0), row(after, 1)), [mlp_out, outputs], []


def end_rows_last(total, rows, vecs):
    vec = vecs[0]
    hidden, upstream = rows
    mlp_out = total + row(vec, 7)
    outputs = hidden + row(vec, 8) * mlp_out
    mlp_grad = row(vec, 8) * upstream
    sums = [
        jnp.sum(upstream * mlp_out, axis=0, keepdims=True),
        jnp.sum(mlp_grad, axis=0, keepdims=True),
    ]
    return mlp_grad, [outputs], sums


def back_middle_rows(total, rows, vecs):
    vec = vecs[0]
    upstream, hidden, attn_out = rows
    part, gain, shift = layer_norm_back(hidden, row(vec, 5), total)
    hidden_grad = upstream + part
    attn_grad = row(vec, 4) * hidden_grad
    sums = [
        gain,
        shift,
        jnp.sum(hidden_grad * attn_out, axis=0, keepdims=True),
        jnp.sum(attn_grad, axis=0, keepdims=True),
    ]
    return attn_grad, [hidden_grad], sums


def back_end_rows_last(total, rows, vecs):
    vec, before = vecs
    hidden_grad, inputs, mlp_out = rows
    part, gain, shift = layer_norm_back(inputs, row(vec, 0), total)
    input_grad = hidden_grad + part
    upstream = input_grad.astype(BF16).astype(F32)
    mlp_grad = row(before, 8) * upstream
    sums = [
        gain,
        shift,
        jnp.sum(upstream * mlp_out, axis=0, keepdims=True),
        jnp.sum(mlp_grad, axis=0, keepdims=True),
    ]
    return mlp_grad, [input_grad], sums


def back_end_rows_first(total, rows, vecs):
    hidden_grad, inputs = rows
    part, gain, shift = layer_norm_back(inputs, row(vecs[0], 0), total)
    return None, [hidden_grad + part], [gain, shift]


def place(lane_first, own, other):
    return (other, own) if lane_first else (own, other)


def dp_neighbour(y, z, along_z, k):
    if along_z:
        return {"dp": y * RING + step(z, k)}
    return {"dp": step(y, k) * RING + z}


def dp_barrier(y, z, section):
    barrier = pltpu.get_barrier_semaphore()
    count = 0
    for along_z in (True, False):
        for k in range(1, RING):
            pl.semaphore_signal(
                barrier, inc=1, device_id=dp_neighbour(y, z, along_z, k), device_id_type=MESH
            )
            count += 1
    if section is not None:
        pl.semaphore_signal(
            barrier, inc=1, device_id={"section": 1 - section}, device_id_type=MESH
        )
        count += 1
    return barrier, count


def gather_kernel(pieces, n_in, n_out, with_sibling, *refs):
    ins, outs = refs[:n_in], refs[n_in : n_in + n_out]
    send, recv, local = refs[n_in + n_out :]
    rank = lax.axis_index("dp")
    y, z = rank // RING, lax.rem(rank, RING)
    section = lax.axis_index("section") if with_sibling else None
    barrier, count = dp_barrier(y, z, section)
    pl.semaphore_wait(barrier, count)
    started = []

    def push(index, stage, k, source, target, device):
        copy = pltpu.make_async_remote_copy(
            src_ref=source,
            dst_ref=target,
            send_sem=send.at[index, stage, k],
            recv_sem=recv.at[index, stage, k],
            device_id=device,
            device_id_type=MESH,
        )
        copy.start()
        started.append(copy)
        return copy

    def block(index, ys, zs):
        number, pre, along_z = pieces[index]
        lead = ((section,) if with_sibling else ()) + pre
        return outs[number].at[lead + (ys, zs)]

    own, first, second, across = [], {}, {}, []
    for index, (number, pre, along_z) in enumerate(pieces):
        source = ins[number].at[pre] if pre else ins[number]
        copy = pltpu.make_async_copy(source, block(index, y, z), local.at[index])
        copy.start()
        own.append(copy)
        for k in range(1, RING):
            first[index, k] = push(
                index, 0, k, source, block(index, y, z), dp_neighbour(y, z, along_z, k)
            )

    def line(index, k):
        along_z = pieces[index][2]
        return block(index, step(y, k), slice(None)) if along_z else block(index, slice(None), step(z, k))

    for index, (number, pre, along_z) in enumerate(pieces):
        own[index].wait()
        for k in range(1, RING):
            first[index, k].wait_recv()
        for k in range(1, RING):
            second[index, k] = push(
                index, 1, k, line(index, 0), line(index, 0), dp_neighbour(y, z, not along_z, k)
            )
        if with_sibling:
            across.append(
                push(index, 2, 0, line(index, 0), line(index, 0), {"section": 1 - section})
            )
    for index in range(len(pieces)):
        for k in range(1, RING):
            second[index, k].wait_recv()
            if with_sibling:
                came = line(index, RING - k)
                across.append(push(index, 2, k, came, came, {"section": 1 - section}))
    for copy in across:
        copy.wait_recv()
    for copy in started:
        copy.wait_send()


def gather_call(cid, pieces, ins, outs, with_sibling):
    return pl.pallas_call(
        functools.partial(gather_kernel, pieces, len(ins), len(outs), with_sibling),
        out_shape=outs,
        in_specs=[vmem_spec()] * len(ins),
        out_specs=[any_spec()] * len(outs),
        scratch_shapes=[
            pltpu.SemaphoreType.DMA((len(pieces), 3, RING)),
            pltpu.SemaphoreType.DMA((len(pieces), 3, RING)),
            pltpu.SemaphoreType.DMA((len(pieces),)),
        ],
        compiler_params=comm_params(cid),
    )(*ins)


def rows_loop(height, size, body):
    if height <= size:
        body(pl.ds(0, height))
        return

    def each(number, carry):
        body(pl.ds(pl.multiple_of(number * size, size), size))
        return carry

    lax.fori_loop(0, height // size, each, 0)


def scatter_first(index, along_z, source, landing, y, z, push):
    copies = []
    for k in range(1, RING):
        line = (
            source.at[:, step(z, k)] if along_z else source.at[step(y, k)]
        )
        copies.append(
            push(index, 0, k, line, landing.at[k - 1], dp_neighbour(y, z, along_z, k))
        )
    return copies


def scatter_second(index, along_z, source, landing, middle, arrivals, y, z, push, copies):
    for copy in copies:
        copy.wait_recv()
    height, width = source.shape[-2:]
    size = max(8, min(height, 65536 // width))
    second = []
    for k in list(range(1, RING)) + [0]:
        at = step(y, k) if along_z else step(z, k)

        def add(here):
            value = (source[at, z, here] if along_z else source[y, at, here]).astype(F32)
            for slot in range(RING - 1):
                value = value + landing[slot, at, here].astype(F32)
            middle[k, here] = value.astype(middle.dtype)

        rows_loop(height, size, add)
        if k:
            second.append(
                push(index, 1, k, middle.at[k], arrivals.at[k - 1], dp_neighbour(y, z, not along_z, k))
            )
    return second


def scatter_last(middle, arrivals, out, copies):
    for copy in copies:
        copy.wait_recv()
    height, width = middle.shape[-2:]
    size = max(8, min(height, 65536 // width))

    def add(here):
        value = middle[0, here].astype(F32)
        for slot in range(RING - 1):
            value = value + arrivals[slot, here].astype(F32)
        out[here] = value

    rows_loop(height, size, add)


def pusher(send, recv, started):
    def push(index, stage, k, source, target, device):
        copy = pltpu.make_async_remote_copy(
            src_ref=source,
            dst_ref=target,
            send_sem=send.at[index, stage, k],
            recv_sem=recv.at[index, stage, k],
            device_id=device,
            device_id_type=MESH,
        )
        copy.start()
        started.append(copy)
        return copy

    return push


def scatter_kernel(orders, *refs):
    n = len(orders)
    ins, outs = refs[:n], refs[n : 2 * n]
    landings, middles, arrivals = refs[2 * n : 3 * n], refs[3 * n : 4 * n], refs[4 * n : 5 * n]
    send, recv = refs[5 * n :]
    rank = lax.axis_index("dp")
    y, z = rank // RING, lax.rem(rank, RING)
    barrier, count = dp_barrier(y, z, None)
    pl.semaphore_wait(barrier, count)
    started = []
    push = pusher(send, recv, started)
    first = [
        scatter_first(i, orders[i], ins[i], landings[i], y, z, push) for i in range(n)
    ]
    second = [
        scatter_second(i, orders[i], ins[i], landings[i], middles[i], arrivals[i], y, z, push, first[i])
        for i in range(n)
    ]
    for i in range(n):
        scatter_last(middles[i], arrivals[i], outs[i], second[i])
    for copy in started:
        copy.wait_send()


def scatter_scratch(block, dtype):
    return (
        pltpu.VMEM((RING - 1, RING) + block, dtype),
        pltpu.VMEM((RING,) + block, dtype),
        pltpu.VMEM((RING - 1,) + block, dtype),
    )


def scatter_call(cid, orders, ins):
    blocks = [value.shape[2:] for value in ins]
    sets = [scatter_scratch(block, BF16) for block in blocks]
    return pl.pallas_call(
        functools.partial(scatter_kernel, orders),
        out_shape=[jax.ShapeDtypeStruct(block, F32) for block in blocks],
        in_specs=[vmem_spec()] * len(ins),
        out_specs=[vmem_spec()] * len(ins),
        scratch_shapes=[group[i] for i in range(3) for group in sets]
        + [
            pltpu.SemaphoreType.DMA((len(ins), 2, RING)),
            pltpu.SemaphoreType.DMA((len(ins), 2, RING)),
        ],
        compiler_params=comm_params(cid),
    )(*ins)


def final_kernel(orders, n_extra, *refs):
    n = len(orders)
    refs = list(refs)
    take = lambda count: [refs.pop(0) for _ in range(count)]
    ins, extras = take(n), take(n_extra)
    outs, extra_outs = take(n), take(n_extra)
    siblings, owns, landings, middles, arrivals = take(n), take(n), take(n), take(n), take(n)
    vector_own, vector_parts = take(2)
    send, recv, local, extra_send, extra_recv = take(5)
    rank = lax.axis_index("dp")
    y, z = rank // RING, lax.rem(rank, RING)
    section = lax.axis_index("section")
    me = lax.axis_index("tensor")
    barrier, count = dp_barrier(y, z, section)
    for k in range(1, RING):
        pl.semaphore_signal(
            barrier, inc=1, device_id={"tensor": step(me, k)}, device_id_type=MESH
        )
    pl.semaphore_wait(barrier, count + RING - 1)
    started = []
    push = pusher(send, recv, started)
    other = {"section": 1 - section}
    across, local_copies = [], []
    for i in range(n):
        across.append(push(i, 2, 0, ins[i].at[1 - section], siblings[i], other))
        copy = pltpu.make_async_copy(ins[i].at[section], owns[i], local.at[i])
        copy.start()
        local_copies.append(copy)
    extra_copies = []
    for i in range(n_extra):
        copy = pltpu.make_async_remote_copy(
            src_ref=extras[i],
            dst_ref=extra_outs[i],
            send_sem=extra_send.at[i],
            recv_sem=extra_recv.at[i],
            device_id=other,
            device_id_type=MESH,
        )
        copy.start()
        extra_copies.append(copy)
    first = []
    for i in range(n):
        local_copies[i].wait()
        across[i].wait_recv()
        own, sibling = owns[i], siblings[i]

        def add(number, carry):
            at_y, at_z = number // RING, lax.rem(number, RING)
            own[at_y, at_z] = (
                own[at_y, at_z].astype(F32) + sibling[at_y, at_z].astype(F32)
            ).astype(own.dtype)
            return carry

        lax.fori_loop(0, RING * RING, add, 0)
        first.append(scatter_first(i, orders[i], own, landings[i], y, z, push))
    second = [
        scatter_second(i, orders[i], owns[i], landings[i], middles[i], arrivals[i], y, z, push, first[i])
        for i in range(n)
    ]
    for i in range(n):
        scatter_last(
            middles[i], arrivals[i], vector_own if i == 0 else outs[i], second[i]
        )
        if i == 0:
            vector_parts[me] = vector_own[...]
            vector_copies = [
                push(
                    0, 3, k, vector_own, vector_parts.at[me], {"tensor": step(me, k)}
                )
                for k in range(1, RING)
            ]
    for copy in vector_copies:
        copy.wait_recv()
    total = vector_parts[0]
    for k in range(1, RING):
        total = total + vector_parts[k]
    outs[0][...] = total
    for copy in extra_copies:
        copy.wait()
    for copy in started:
        copy.wait_send()


def final_call(cid, orders, ins, extras):
    blocks = [value.shape[3:] for value in ins]
    sets = [scatter_scratch(block, value.dtype) for block, value in zip(blocks, ins)]
    square = [
        pltpu.VMEM((RING, RING) + block, value.dtype) for block, value in zip(blocks, ins)
    ]
    count, extra = len(ins), len(extras)
    return pl.pallas_call(
        functools.partial(final_kernel, orders, extra),
        out_shape=[jax.ShapeDtypeStruct(block, F32) for block in blocks]
        + [jax.ShapeDtypeStruct(value.shape, value.dtype) for value in extras],
        in_specs=[any_spec()] * count + [vmem_spec()] * extra,
        out_specs=[vmem_spec()] * (count + extra),
        scratch_shapes=square
        + square
        + [group[i] for i in range(3) for group in sets]
        + [
            pltpu.VMEM(blocks[0], F32),
            pltpu.VMEM((RING,) + blocks[0], F32),
            pltpu.SemaphoreType.DMA((count, 4, RING)),
            pltpu.SemaphoreType.DMA((count, 4, RING)),
            pltpu.SemaphoreType.DMA((count,)),
            pltpu.SemaphoreType.DMA((extra,)),
            pltpu.SemaphoreType.DMA((extra,)),
        ],
        compiler_params=comm_params(cid),
    )(*ins, *extras)


def gelu_exact(values):
    return jax.nn.gelu(values, approximate=False)


def flat_dot(former, latter):
    return lax.dot_general(former, latter, (((1,), (1,)), ((), ())), preferred_element_type=F32)


def rows_dot(former, latter):
    return lax.dot_general(former, latter, (((0,), (0,)), ((), ())), preferred_element_type=F32)


def attention_weights(queries, keys_full, seg_rows, seg_keys):
    heads_here = queries.shape[1] // HEAD_DIM
    query_heads = queries.reshape(queries.shape[0], heads_here, HEAD_DIM)
    key_heads = keys_full.reshape(keys_full.shape[0], heads_here, HEAD_DIM)
    raw_scores = jnp.einsum(
        "rhd,shd->hrs", query_heads, key_heads, preferred_element_type=F32
    ) * HEAD_DIM ** (-0.5)
    allowed = seg_rows[:, None] == seg_keys[None, :]
    masked = jnp.where(allowed[None], raw_scores, MASKED_SCORE)
    highest = jnp.max(masked, axis=-1, keepdims=True)
    exponent = jnp.exp(masked - highest)
    total = jnp.sum(exponent, axis=-1, keepdims=True)
    return exponent / total


def attention_forward(queries, keys_full, values_full, seg_rows, seg_keys):
    heads_here = queries.shape[1] // HEAD_DIM
    soft = attention_weights(queries, keys_full, seg_rows, seg_keys)
    mixed = jnp.einsum(
        "hrs,shd->rhd",
        soft.astype(BF16),
        values_full.reshape(-1, heads_here, HEAD_DIM),
        preferred_element_type=F32,
    )
    return mixed.reshape(queries.shape).astype(BF16)


def attention_backward(queries, keys_full, values_full, mixed_grad, seg_rows, seg_keys):
    local_width = queries.shape[1]
    heads_here = local_width // HEAD_DIM
    head_scale = HEAD_DIM ** (-0.5)
    soft = attention_weights(queries, keys_full, seg_rows, seg_keys)
    mixed_split = mixed_grad.reshape(-1, heads_here, HEAD_DIM)
    value_heads = values_full.reshape(-1, heads_here, HEAD_DIM)
    key_heads = keys_full.reshape(-1, heads_here, HEAD_DIM)
    query_heads = queries.reshape(-1, heads_here, HEAD_DIM)
    prob_grad = jnp.einsum("rhd,shd->hrs", mixed_split, value_heads, preferred_element_type=F32)
    row_delta = jnp.sum(prob_grad * soft, axis=-1)
    score_grad = soft * (prob_grad - row_delta[..., None])
    score_low = (score_grad * head_scale).astype(BF16)
    query_grad = jnp.einsum(
        "hrs,shd->rhd", score_low, key_heads, preferred_element_type=F32
    ).reshape(-1, local_width)
    values_grad = jnp.einsum(
        "hrs,rhd->shd", soft.astype(BF16), mixed_split, preferred_element_type=F32
    ).reshape(-1, local_width)
    keys_grad = jnp.einsum(
        "hrs,rhd->shd", score_low, query_heads, preferred_element_type=F32
    ).reshape(-1, local_width)
    return query_grad, keys_grad.astype(BF16), values_grad.astype(BF16)


WEIGHT_PIECES = (
    (0, (0,), True),
    (0, (1,), False),
    (0, (2,), True),
    (1, (), False),
    (4, (), True),
    (2, (), True),
    (3, (), False),
)


def shards(tokens, segment_ids, w_qkv, w_out, w_up, w_down, vectors, out_bias, cotangent):
    section = lax.axis_index("section")
    tensor_rank = lax.axis_index("tensor")
    own = lambda pair: jnp.where(section == 0, pair[0], pair[1])
    rows = tokens.shape[1]
    width = tokens.shape[2]
    group = rows * RING
    square = (RING, RING)
    local_width = w_qkv.shape[3]
    local_hidden = w_up.shape[2]

    depth = w_out.shape[1]
    small = jnp.pad(
        jnp.concatenate([vectors[0], out_bias], axis=0),
        ((0, 2), (0, 128 - depth)),
    )
    shape = lambda *dims: jax.ShapeDtypeStruct(dims, BF16)
    full_qkv, full_out, full_up, full_down, full_small = gather_call(
        0,
        WEIGHT_PIECES,
        [w_qkv[0], w_out[0], w_up[0], w_down[0], small],
        [
            shape(2, 3, *square, depth, local_width),
            shape(2, *square, depth, local_width),
            shape(2, *square, depth, local_hidden),
            shape(2, *square, depth, local_hidden),
            shape(2, *square, 16, 128),
        ],
        True,
    )
    full_qkv = full_qkv.reshape(2, 3, width, local_width)
    full_out = full_out.reshape(2, width, local_width)
    full_up = full_up.reshape(2, width, local_hidden)
    full_down = full_down.reshape(2, width, local_hidden)
    small_rows = (
        full_small.reshape(2, RING * RING, 16, 128)[..., :depth]
        .transpose(0, 2, 1, 3)
        .reshape(2, 16, width)
        .astype(F32)
    )

    my_tokens = own(tokens)
    my_cotangent = own(cotangent)
    my_segments = own(segment_ids)
    seg_block = jnp.zeros((8, 128), jnp.int32).at[0, :rows].set(my_segments)
    normed, seg_group = tensor_call(
        1, first_rows, None, [my_tokens], [small_rows[0]], [], 0, True, seg_block
    )
    seg_rows = seg_group[:, 0, :rows].reshape(group)
    seg_wide = jnp.broadcast_to(seg_rows[None], (8, group))
    inputs = my_tokens
    kept = []
    seg_keys = None
    for layer in range(2):
        vec = small_rows[layer]
        normed = normed.reshape(group, width)
        query_bias = lax.dynamic_slice_in_dim(vec[2], tensor_rank * local_width, local_width)
        value_bias = lax.dynamic_slice_in_dim(vec[3], tensor_rank * local_width, local_width)
        up_bias = lax.dynamic_slice_in_dim(
            vec[9:13].reshape(-1), tensor_rank * local_hidden, local_hidden
        )
        project = lambda which: jnp.dot(normed, full_qkv[layer, which], preferred_element_type=F32)
        queries = (project(0) + query_bias).astype(BF16)
        keys = project(1).astype(BF16)
        values = (project(2) + value_bias).astype(BF16)
        keys_full, values_full, seg_full = gather_call(
            2,
            ((2, (), True), (0, (), True), (1, (), False)),
            [keys, values, seg_wide],
            [
                shape(*square, group, local_width),
                shape(*square, group, local_width),
                jax.ShapeDtypeStruct(square + (8, group), jnp.int32),
            ],
            False,
        )
        keys_full = keys_full.reshape(-1, local_width)
        values_full = values_full.reshape(-1, local_width)
        if layer == 0:
            seg_keys = seg_full[:, :, 0].reshape(-1)
        mixed = attention_forward(queries, keys_full, values_full, seg_rows, seg_keys)
        part = flat_dot(mixed, full_out[layer]).astype(BF16).reshape(RING, rows, width)
        attn_out, hidden, normed_two = tensor_call(
            3, middle_rows, part, [inputs.astype(F32)], [vec], [F32, F32], 0, True
        )
        normed_two = normed_two.reshape(group, width)
        pre_act = jnp.dot(normed_two, full_up[layer], preferred_element_type=F32) + up_bias
        activated = gelu_exact(pre_act).astype(BF16)
        part = flat_dot(activated, full_down[layer]).astype(BF16).reshape(RING, rows, width)
        step_kept = [inputs, normed, queries, keys_full, values_full, mixed, attn_out, hidden]
        step_kept += [normed_two, pre_act, activated]
        if layer == 0:
            mlp_first, between, normed = tensor_call(
                4, end_rows_first, part, [hidden], [vec, small_rows[1]], [F32, BF16], 0, True
            )
            inputs = between
        else:
            outputs, sums_end, mlp_rows = tensor_call(
                5, end_rows_last, part, [hidden, my_cotangent], [vec], [BF16], 2, True
            )
        kept.append(step_kept)

    upstream = my_cotangent.astype(F32)
    grads = [None, None]
    scale_two, down_bias = sums_end[0], sums_end[1]
    for layer in (1, 0):
        vec = small_rows[layer]
        inputs, normed, queries, keys_full, values_full, mixed, attn_out, hidden = kept[layer][:8]
        normed_two, pre_act, activated = kept[layer][8:]
        mlp_rows = mlp_rows.reshape(group, width)
        act_grad = jnp.dot(mlp_rows, full_down[layer], preferred_element_type=F32)
        grad_down = rows_dot(mlp_rows, activated)
        pre_grad = jax.vjp(gelu_exact, pre_act)[1](act_grad)[0]
        up_bias_grad = jnp.sum(pre_grad, axis=0)
        pre_low = pre_grad.astype(BF16)
        grad_up = rows_dot(normed_two, pre_low)
        part = flat_dot(pre_low, full_up[layer]).astype(BF16).reshape(RING, rows, width)
        hidden_grad, sums_middle, attn_rows = tensor_call(
            6, back_middle_rows, part, [upstream, hidden, attn_out], [vec], [F32], 4, True
        )
        attn_rows = attn_rows.reshape(group, width)
        mixed_grad = jnp.dot(attn_rows, full_out[layer], preferred_element_type=F32).astype(BF16)
        grad_out = rows_dot(attn_rows, mixed)
        query_grad, keys_part, values_part = attention_backward(
            queries, keys_full, values_full, mixed_grad, seg_rows, seg_keys
        )
        keys_grad, values_grad = scatter_call(
            7,
            (True, False),
            [
                keys_part.reshape(*square, group, local_width),
                values_part.reshape(*square, group, local_width),
            ],
        )
        query_bias_grad = jnp.sum(query_grad, axis=0)
        value_bias_grad = jnp.sum(values_grad, axis=0)
        triple = [value.astype(BF16) for value in (query_grad, keys_grad, values_grad)]
        grad_qkv = [rows_dot(normed, value) for value in triple]
        part = sum(flat_dot(triple[which], full_qkv[layer, which]) for which in range(3))
        part = part.astype(BF16).reshape(RING, rows, width)
        if layer == 1:
            input_grad, sums_last, mlp_rows = tensor_call(
                8,
                back_end_rows_last,
                part,
                [hidden_grad, inputs.astype(F32), mlp_first],
                [vec, small_rows[0]],
                [F32],
                4,
                True,
            )
        else:
            input_grad, sums_last = tensor_call(
                9, back_end_rows_first, part, [hidden_grad, inputs.astype(F32)], [vec], [F32], 2, False
            )

        def placed(values, length):
            empty = jnp.zeros((length,), F32)
            return lax.dynamic_update_slice(empty, values, (tensor_rank * values.shape[0],))

        vector_rows = jnp.concatenate(
            [
                sums_last[0:2],
                placed(query_bias_grad, width)[None],
                placed(value_bias_grad, width)[None],
                sums_middle[2:3],
                sums_middle[0:2],
                down_bias[None],
                scale_two[None],
                placed(up_bias_grad, local_hidden * RING).reshape(-1, width),
                sums_middle[3:4],
                jnp.zeros((2, width), F32),
            ],
            axis=0,
        )
        vector_rows = jnp.pad(
            vector_rows.reshape(16, RING * RING, depth).transpose(1, 0, 2),
            ((0, 0), (0, 0), (0, 128 - depth)),
        ).reshape(*square, 16, 128)
        grads[layer] = [vector_rows] + [
            value.astype(BF16).reshape(*square, depth, value.shape[-1])
            for value in grad_qkv + [grad_out, grad_up, grad_down]
        ]
        if layer == 1:
            last_grad = input_grad
            upstream = input_grad.astype(BF16).astype(F32)
            scale_two, down_bias = sums_last[2], sums_last[3]
    first_grad = input_grad

    stacked = [jnp.stack(pair) for pair in zip(*grads)]
    extras = [
        jnp.where(section == 0, outputs, between),
        jnp.where(section == 0, last_grad, first_grad),
    ]
    results = final_call(10, (True, True, False, True, False, True, False), stacked, extras)
    small_sum, grad_q, grad_k, grad_v, grad_out, grad_up, grad_down, came_out, came_grad = results
    mine_out = jnp.where(section == 0, between, outputs)
    mine_grad = jnp.where(section == 0, first_grad, last_grad)
    pair = lambda mine, came: jnp.where(
        section == 0, jnp.stack([mine, came]), jnp.stack([came, mine])
    )[None]
    return (
        pair(mine_out, came_out),
        pair(mine_grad, came_grad),
        jnp.stack([grad_q, grad_k, grad_v])[None],
        grad_out[None],
        grad_up[None],
        grad_down[None],
        small_sum[:13, :depth][None],
        small_sum[13:14, :depth],
    )


def solution(mesh):
    in_specs = (
        P(None, ("dp", "tensor"), None),
        P(None, ("dp", "tensor")),
        P("section", None, "dp", "tensor"),
        P("section", "dp", "tensor"),
        P("section", "dp", "tensor"),
        P("section", "dp", "tensor"),
        P("section", None, "dp"),
        P("section", "dp"),
        P(None, ("dp", "tensor"), None),
    )
    out_specs = (
        P("section", None, ("dp", "tensor"), None),
        P("section", None, ("dp", "tensor"), None),
        P("section", None, "dp", "tensor"),
        P("section", "dp", "tensor"),
        P("section", "dp", "tensor"),
        P("section", "dp", "tensor"),
        P("section", None, "dp"),
        P("section", "dp"),
    )
    return jax.shard_map(shards, mesh=mesh, in_specs=in_specs, out_specs=out_specs, check_vma=False)
```

```python
import functools

import jax
import jax.numpy as jnp
from jax import lax
from jax.experimental import pallas as pl
from jax.experimental.pallas import tpu as pltpu
from jax.sharding import PartitionSpec as P

MESH = pl.DeviceIdType.MESH
HEAD_DIM = 64
EPSILON = 1e-06
MASKED_SCORE = -1e30
RING = 4
VMEM_LIMIT = 56 * 1024 * 1024
F32 = jnp.float32
BF16 = jnp.bfloat16


def vmem_spec():
    return pl.BlockSpec(memory_space=pltpu.VMEM)


def any_spec():
    return pl.BlockSpec(memory_space=pl.ANY)


def comm_params(cid):
    return pltpu.CompilerParams(
        collective_id=cid, has_side_effects=True, vmem_limit_bytes=VMEM_LIMIT
    )


def step(coord, by):
    return lax.rem(coord + by, RING)


def layer_norm(values, gain_row, shift_row):
    centre = values - jnp.mean(values, axis=-1, keepdims=True)
    spread = jnp.mean(centre * centre, axis=-1, keepdims=True)
    return centre * lax.rsqrt(spread + EPSILON) * gain_row + shift_row


def layer_norm_back(values, gain_row, grad):
    centre = values - jnp.mean(values, axis=-1, keepdims=True)
    spread = jnp.mean(centre * centre, axis=-1, keepdims=True)
    inverse = lax.rsqrt(spread + EPSILON)
    normed = centre * inverse
    scaled = grad * gain_row
    back = inverse * (
        scaled
        - jnp.mean(scaled, axis=-1, keepdims=True)
        - normed * jnp.mean(scaled * normed, axis=-1, keepdims=True)
    )
    return back, jnp.sum(grad * normed, axis=0, keepdims=True), jnp.sum(grad, axis=0, keepdims=True)


PLUS, FAR, MINUS = 1, 2, 3
SUBS = 2


def tensor_kernel(function, n_rows, n_vecs, n_out, n_sums, reduce, gather, with_seg, *refs):
    refs = list(refs)
    take = lambda count: [refs.pop(0) for _ in range(count)]
    part = take(1)[0] if reduce else None
    rows_in = take(n_rows)
    vecs = take(n_vecs)
    seg_in = take(1)[0] if with_seg else None
    rows_out = take(n_out)
    sums_out = take(1)[0] if n_sums else None
    full = take(1)[0] if gather else None
    seg_out = take(1)[0] if with_seg else None
    passing, joined, from_minus, from_plus = take(4) if reduce else [None] * 4
    send, recv, local = take(3)

    me = lax.axis_index("tensor")
    barrier = pltpu.get_barrier_semaphore()
    for k in (PLUS, MINUS):
        pl.semaphore_signal(
            barrier, inc=1, device_id={"tensor": step(me, k)}, device_id_type=MESH
        )
    pl.semaphore_wait(barrier, 2)

    chunk = rows_in[0].shape[0] // (2 * SUBS)
    started = []

    def push(source, target, kind, index, k):
        copy = pltpu.make_async_remote_copy(
            src_ref=source,
            dst_ref=target,
            send_sem=send.at[kind, index],
            recv_sem=recv.at[kind, index],
            device_id={"tensor": step(me, k)},
            device_id_type=MESH,
        )
        copy.start()
        started.append(copy)
        return copy

    chunks = range(2 * SUBS)
    here = lambda c: pl.ds(c * chunk, chunk)
    onward = lambda c: PLUS if c % 2 == 0 else MINUS
    aside = lambda c: MINUS if c % 2 == 0 else PLUS
    side_of = {PLUS: from_minus, MINUS: from_plus}
    way, straight, summed = {}, {}, {}
    if reduce:
        for c in chunks:
            way[c] = push(part.at[step(me, FAR), here(c)], passing.at[here(c)], 0, c, onward(c))
        for c in chunks:
            straight[c] = push(
                part.at[step(me, aside(c)), here(c)], side_of[aside(c)].at[here(c)], 1, c, aside(c)
            )
        for c in chunks:
            way[c].wait_recv()
            joined[here(c)] = (
                part[step(me, onward(c)), here(c)].astype(F32) + passing[here(c)].astype(F32)
            ).astype(BF16)
            summed[c] = push(joined.at[here(c)], side_of[onward(c)].at[here(c)], 2, c, onward(c))
    last = []
    if with_seg:
        own = pltpu.make_async_copy(seg_in, seg_out.at[me], local)
        own.start()
        seg_up = push(seg_in, seg_out.at[me], 6, 0, PLUS)
        seg_down = push(seg_in, seg_out.at[me], 6, 1, MINUS)
        last.append(seg_down)
    sums = [None] * n_sums
    ups, downs = {}, {}
    for c in chunks:
        total = None
        if reduce:
            straight[c].wait_recv()
            summed[c].wait_recv()
            total = (
                part[me, here(c)].astype(F32)
                + from_minus[here(c)].astype(F32)
                + from_plus[here(c)].astype(F32)
            )
        spread, outs, parts = function(
            total, [ref[here(c)].astype(F32) for ref in rows_in], vecs
        )
        if gather:
            full[me, here(c)] = spread.astype(BF16)
            ups[c] = push(full.at[me, here(c)], full.at[me, here(c)], 3, c, PLUS)
            downs[c] = push(full.at[me, here(c)], full.at[me, here(c)], 4, c, MINUS)
        for ref, value in zip(rows_out, outs):
            ref[here(c)] = value.astype(ref.dtype)
        sums = [new if old is None else old + new for old, new in zip(sums, parts)]
    if gather:
        for c in chunks:
            (ups if c % 2 == 0 else downs)[c].wait_recv()
            came = full.at[step(me, aside(c)), here(c)]
            last.append(push(came, came, 5, c, onward(c)))
            last.append((downs if c % 2 == 0 else ups)[c])
    if n_sums:
        sums_out[...] = jnp.concatenate(
            sums + [jnp.zeros((8 - n_sums, sums[0].shape[1]), F32)], axis=0
        )
    if with_seg:
        own.wait()
        seg_up.wait_recv()
        came = seg_out.at[step(me, MINUS)]
        last.append(push(came, came, 6, 2, PLUS))
    for copy in last:
        copy.wait_recv()
    for copy in started:
        copy.wait_send()


def tensor_call(cid, function, part, rows, vecs, outs, n_sums, gather, seg=None):
    height, width = rows[0].shape
    reduce = part is not None
    with_seg = seg is not None
    args = ([part] if reduce else []) + list(rows) + list(vecs) + ([seg] if with_seg else [])
    shapes = [jax.ShapeDtypeStruct((height, width), dtype) for dtype in outs]
    if n_sums:
        shapes.append(jax.ShapeDtypeStruct((8, width), F32))
    if gather:
        shapes.append(jax.ShapeDtypeStruct((RING, height, width), BF16))
    if with_seg:
        shapes.append(jax.ShapeDtypeStruct((RING,) + seg.shape, seg.dtype))
    scratch = [pltpu.VMEM((height, width), BF16)] * 4 if reduce else []
    scratch += [
        pltpu.SemaphoreType.DMA((7, 2 * SUBS)),
        pltpu.SemaphoreType.DMA((7, 2 * SUBS)),
        pltpu.SemaphoreType.DMA,
    ]
    return pl.pallas_call(
        functools.partial(
            tensor_kernel, function, len(rows), len(vecs), len(outs), n_sums, reduce, gather, with_seg
        ),
        out_shape=shapes,
        in_specs=[vmem_spec()] * len(args),
        out_specs=[vmem_spec()] * len(shapes),
        scratch_shapes=scratch,
        compiler_params=comm_params(cid),
    )(*args)


def row(ref, index):
    return ref[pl.ds(index, 1), :]


def first_rows(total, rows, vecs):
    return layer_norm(rows[0], row(vecs[0], 0), row(vecs[0], 1)), [], []


def middle_rows(total, rows, vecs):
    vec = vecs[0]
    attn_out = total + row(vec, 13)
    hidden = rows[0] + row(vec, 4) * attn_out
    return layer_norm(hidden, row(vec, 5), row(vec, 6)), [attn_out, hidden], []


def end_rows_first(total, rows, vecs):
    vec, after = vecs
    mlp_out = total + row(vec, 7)
    outputs = (rows[0] + row(vec, 8) * mlp_out).astype(BF16)
    inputs = outputs.astype(F32)
    return layer_norm(inputs, row(after, 0), row(after, 1)), [mlp_out, outputs], []


def end_rows_last(total, rows, vecs):
    vec = vecs[0]
    hidden, upstream = rows
    mlp_out = total + row(vec, 7)
    outputs = hidden + row(vec, 8) * mlp_out
    mlp_grad = row(vec, 8) * upstream
    sums = [
        jnp.sum(upstream * mlp_out, axis=0, keepdims=True),
        jnp.sum(mlp_grad, axis=0, keepdims=True),
    ]
    return mlp_grad, [outputs], sums


def back_middle_rows(total, rows, vecs):
    vec = vecs[0]
    upstream, hidden, attn_out = rows
    part, gain, shift = layer_norm_back(hidden, row(vec, 5), total)
    hidden_grad = upstream + part
    attn_grad = row(vec, 4) * hidden_grad
    sums = [
        gain,
        shift,
        jnp.sum(hidden_grad * attn_out, axis=0, keepdims=True),
        jnp.sum(attn_grad, axis=0, keepdims=True),
    ]
    return attn_grad, [hidden_grad], sums


def back_end_rows_last(total, rows, vecs):
    vec, before = vecs
    hidden_grad, inputs, mlp_out = rows
    part, gain, shift = layer_norm_back(inputs, row(vec, 0), total)
    input_grad = hidden_grad + part
    upstream = input_grad.astype(BF16).astype(F32)
    mlp_grad = row(before, 8) * upstream
    sums = [
        gain,
        shift,
        jnp.sum(upstream * mlp_out, axis=0, keepdims=True),
        jnp.sum(mlp_grad, axis=0, keepdims=True),
    ]
    return mlp_grad, [input_grad], sums


def back_end_rows_first(total, rows, vecs):
    hidden_grad, inputs = rows
    part, gain, shift = layer_norm_back(inputs, row(vecs[0], 0), total)
    return None, [hidden_grad + part], [gain, shift]


def dp_neighbour(y, z, along_z, k):
    if along_z:
        return {"dp": y * RING + step(z, k)}
    return {"dp": step(y, k) * RING + z}


def dp_barrier(y, z, section):
    barrier = pltpu.get_barrier_semaphore()
    count = 0
    for along_z in (True, False):
        for k in (PLUS, MINUS):
            pl.semaphore_signal(
                barrier, inc=1, device_id=dp_neighbour(y, z, along_z, k), device_id_type=MESH
            )
            count += 1
    if section is not None:
        pl.semaphore_signal(
            barrier, inc=1, device_id={"section": 1 - section}, device_id_type=MESH
        )
        count += 1
    return barrier, count


def pusher(send, recv, started):
    def push(index, kind, k, source, target, device):
        copy = pltpu.make_async_remote_copy(
            src_ref=source,
            dst_ref=target,
            send_sem=send.at[index, kind, k],
            recv_sem=recv.at[index, kind, k],
            device_id=device,
            device_id_type=MESH,
        )
        copy.start()
        started.append(copy)
        return copy

    return push


def gather_kernel(pieces, n_in, n_out, with_sibling, *refs):
    ins, outs = refs[:n_in], refs[n_in : n_in + n_out]
    send, recv, local = refs[n_in + n_out :]
    rank = lax.axis_index("dp")
    y, z = rank // RING, lax.rem(rank, RING)
    section = lax.axis_index("section") if with_sibling else None
    barrier, count = dp_barrier(y, z, section)
    pl.semaphore_wait(barrier, count)
    started = []
    push = pusher(send, recv, started)
    every = range(len(pieces))

    def block(i, along, across, rows=None):
        number, pre, along_z = pieces[i]
        lead = ((section,) if with_sibling else ()) + pre
        ys, zs = (across, along) if along_z else (along, across)
        ys = ys if isinstance(ys, slice) else step(y, ys) if ys else y
        zs = zs if isinstance(zs, slice) else step(z, zs) if zs else z
        return outs[number].at[lead + (ys, zs) + (() if rows is None else (rows,))]

    def first_way(i, k):
        return dp_neighbour(y, z, pieces[i][2], k)

    def second_way(i, k):
        return dp_neighbour(y, z, not pieces[i][2], k)

    def halves(i):
        height = outs[pieces[i][0]].shape[-2]
        if height < 32:
            return {PLUS: None}
        return {PLUS: pl.ds(0, height // 2), MINUS: pl.ds(height // 2, height // 2)}

    own, first, onward, second, relayed = {}, {}, {}, {}, {}

    def spread(i, offset, source):
        for k in (PLUS, MINUS):
            second[i, offset, k] = push(
                i, 2 if k == PLUS else 3, offset, source, block(i, offset, 0), second_way(i, k)
            )

    for i in every:
        number, pre, _ = pieces[i]
        source = ins[number].at[pre] if pre else ins[number]
        for k in (PLUS, MINUS):
            first[i, k] = push(i, 0, k, source, block(i, 0, 0), first_way(i, k))
        spread(i, 0, source)
        own[i] = pltpu.make_async_copy(source, block(i, 0, 0), local.at[i])
        own[i].start()
    for i in every:
        split = halves(i)
        for k in (PLUS, MINUS):
            first[i, k].wait_recv()
            came = RING - k
            if k in split:
                onward[i, k] = push(
                    i, 1, k, block(i, came, 0, split[k]), block(i, came, 0, split[k]), first_way(i, k)
                )
            spread(i, came, block(i, came, 0))
    ways = {0: PLUS, MINUS: MINUS, PLUS: PLUS, FAR: MINUS}

    def relay(i, offset):
        k = ways[offset]
        second[i, offset, k].wait_recv()
        came = block(i, offset, RING - k)
        relayed[i, offset] = push(i, 4, offset, came, came, second_way(i, k))

    for i in every:
        relay(i, 0)
    for i in every:
        for k in halves(i):
            onward[i, k].wait_recv()
        spread(i, FAR, block(i, FAR, 0))
    across = []

    def pass_on(i, line):
        came = block(i, slice(None), line)
        across.append(push(i, 5, line, came, came, {"section": 1 - section}))

    for i in every:
        relay(i, MINUS)
        relay(i, PLUS)
        own[i].wait()
        if with_sibling:
            pass_on(i, 0)
    for i in every:
        relay(i, FAR)
        for offset, k in ways.items():
            second[i, offset, RING - k].wait_recv()
        if with_sibling:
            pass_on(i, PLUS)
            pass_on(i, MINUS)
    for i in every:
        for offset in range(RING):
            relayed[i, offset].wait_recv()
        if with_sibling:
            pass_on(i, FAR)
    for copy in across:
        copy.wait_recv()
    for copy in started:
        copy.wait_send()


def gather_call(cid, pieces, ins, outs, with_sibling):
    return pl.pallas_call(
        functools.partial(gather_kernel, pieces, len(ins), len(outs), with_sibling),
        out_shape=outs,
        in_specs=[vmem_spec()] * len(ins),
        out_specs=[any_spec()] * len(outs),
        scratch_shapes=[
            pltpu.SemaphoreType.DMA((len(pieces), 6, RING)),
            pltpu.SemaphoreType.DMA((len(pieces), 6, RING)),
            pltpu.SemaphoreType.DMA((len(pieces),)),
        ],
        compiler_params=comm_params(cid),
    )(*ins)


class Scatter:
    ORDER = (FAR, PLUS, MINUS, 0)
    WAYS = {FAR: PLUS, 0: PLUS, PLUS: MINUS, MINUS: MINUS}

    def __init__(self, index, along_z, source, buffers, y, z, push):
        self.index, self.along_z, self.source = index, along_z, source
        self.passing, self.joined, self.summed, self.straight, self.middle = buffers[:5]
        self.far_two, self.joined_two, self.summed_two, self.straight_two = buffers[5:]
        self.y, self.z, self.push = y, z, push
        self.height, self.width = source.shape[-2:]

    def at(self, along, across):
        ys, zs = (across, along) if self.along_z else (along, across)
        return step(self.y, ys), step(self.z, zs)

    def way(self, first, k):
        return dp_neighbour(self.y, self.z, self.along_z == first, k)

    def add(self, target, terms, top=0, height=None):
        height = self.height if height is None else height
        size = max(8, min(height, 32768 // self.width))

        def part(here):
            value = terms[0](here).astype(F32)
            for term in terms[1:]:
                value = value + term(here).astype(F32)
            target[here] = value.astype(target.dtype)

        if height <= size:
            part(pl.ds(top, height))
            return

        def each(number, carry):
            part(pl.ds(pl.multiple_of(top + number * size, size), size))
            return carry

        lax.fori_loop(0, height // size, each, 0)

    def begin(self):
        self.via, self.direct, self.after = {}, {}, {}
        for j in self.ORDER:
            self.via[j] = self.push(
                self.index, 0, j, self.source.at[self.at(FAR, j)], self.passing.at[j],
                self.way(True, self.WAYS[j]),
            )
        for j in self.ORDER:
            k = RING - self.WAYS[j]
            self.direct[j] = self.push(
                self.index, 1, j, self.source.at[self.at(k, j)], self.straight.at[j],
                self.way(True, k),
            )

    def join(self):
        for j in self.ORDER:
            self.via[j].wait_recv()
            k = self.WAYS[j]
            at_y, at_z = self.at(k, j)
            self.add(
                self.joined.at[j],
                [lambda h: self.source[at_y, at_z, h], lambda h: self.passing[j, h]],
            )
            self.after[j] = self.push(
                self.index, 2, j, self.joined.at[j], self.summed.at[j], self.way(True, k)
            )

    def turn(self):
        half = self.height // 2
        low, high = pl.ds(0, half), pl.ds(half, half)
        send = lambda kind, slot, source, target, k: self.push(
            self.index, kind, slot, source, target, self.way(False, k)
        )
        for j in self.ORDER:
            self.direct[j].wait_recv()
            self.after[j].wait_recv()
            at_y, at_z = self.at(0, j)
            self.add(
                self.middle.at[j],
                [
                    lambda h: self.source[at_y, at_z, h],
                    lambda h: self.summed[j, h],
                    lambda h: self.straight[j, h],
                ],
            )
            if j == FAR:
                self.via_two = [
                    send(3, 0, self.middle.at[j, low], self.far_two.at[low], PLUS),
                    send(3, 1, self.middle.at[j, high], self.far_two.at[high], MINUS),
                ]
            if j == PLUS:
                high_copy = send(4, 1, self.middle.at[j, high], self.straight_two.at[high], PLUS)
            if j == MINUS:
                low_copy = send(4, 0, self.middle.at[j, low], self.straight_two.at[low], MINUS)
        self.direct_two = [low_copy, high_copy]

    def join_two(self):
        half = self.height // 2
        self.after_two = []
        for number, (top, k) in enumerate(((0, PLUS), (half, MINUS))):
            self.via_two[number].wait_recv()
            self.add(
                self.joined_two,
                [lambda h: self.middle[k, h], lambda h: self.far_two[h]],
                top,
                half,
            )
            here = pl.ds(top, half)
            self.after_two.append(
                self.push(
                    self.index, 5, number, self.joined_two.at[here], self.summed_two.at[here],
                    self.way(False, k),
                )
            )

    def finish(self, out):
        for copy in self.direct_two + self.after_two:
            copy.wait_recv()
        self.add(
            out,
            [
                lambda h: self.middle[0, h],
                lambda h: self.summed_two[h],
                lambda h: self.straight_two[h],
            ],
        )

    @staticmethod
    def scratch(block, dtype):
        return [pltpu.VMEM((RING,) + block, dtype)] * 5 + [pltpu.VMEM(block, dtype)] * 4


SCATTER_BUFFERS = 9


def scatter_kernel(orders, *refs):
    n = len(orders)
    ins, outs = refs[:n], refs[n : 2 * n]
    buffers = refs[2 * n : 2 * n + n * SCATTER_BUFFERS]
    send, recv = refs[2 * n + n * SCATTER_BUFFERS :]
    rank = lax.axis_index("dp")
    y, z = rank // RING, lax.rem(rank, RING)
    barrier, count = dp_barrier(y, z, None)
    pl.semaphore_wait(barrier, count)
    started = []
    push = pusher(send, recv, started)
    parts = [
        Scatter(
            i, orders[i], ins[i], buffers[i * SCATTER_BUFFERS : (i + 1) * SCATTER_BUFFERS], y, z, push
        )
        for i in range(n)
    ]
    for part in parts:
        part.begin()
    for part in parts:
        part.join()
    for part in parts:
        part.turn()
    for part in parts:
        part.join_two()
    for part, out in zip(parts, outs):
        part.finish(out)
    for copy in started:
        copy.wait_send()


def scatter_call(cid, orders, ins):
    blocks = [value.shape[2:] for value in ins]
    return pl.pallas_call(
        functools.partial(scatter_kernel, orders),
        out_shape=[jax.ShapeDtypeStruct(block, F32) for block in blocks],
        in_specs=[vmem_spec()] * len(ins),
        out_specs=[vmem_spec()] * len(ins),
        scratch_shapes=[one for block in blocks for one in Scatter.scratch(block, BF16)]
        + [
            pltpu.SemaphoreType.DMA((len(ins), 6, RING)),
            pltpu.SemaphoreType.DMA((len(ins), 6, RING)),
        ],
        compiler_params=comm_params(cid),
    )(*ins)


def final_kernel(orders, n_extra, *refs):
    n = len(orders)
    refs = list(refs)
    take = lambda count: [refs.pop(0) for _ in range(count)]
    ins, extras = take(n), take(n_extra)
    outs, extra_outs = take(n), take(n_extra)
    siblings, owns = take(n), take(n)
    buffers = [take(SCATTER_BUFFERS) for _ in range(n)]
    vector_own, vector_parts = take(2)
    send, recv, local, extra_send, extra_recv = take(5)
    rank = lax.axis_index("dp")
    y, z = rank // RING, lax.rem(rank, RING)
    section = lax.axis_index("section")
    me = lax.axis_index("tensor")
    barrier, count = dp_barrier(y, z, section)
    for k in range(1, RING):
        pl.semaphore_signal(
            barrier, inc=1, device_id={"tensor": step(me, k)}, device_id_type=MESH
        )
    pl.semaphore_wait(barrier, count + RING - 1)
    started = []
    push = pusher(send, recv, started)
    other = {"section": 1 - section}
    across, local_copies = [], []
    for i in range(n):
        across.append(push(i, 6, 0, ins[i].at[1 - section], siblings[i], other))
        copy = pltpu.make_async_copy(ins[i].at[section], owns[i], local.at[i])
        copy.start()
        local_copies.append(copy)
    extra_copies = []
    for i in range(n_extra):
        copy = pltpu.make_async_remote_copy(
            src_ref=extras[i],
            dst_ref=extra_outs[i],
            send_sem=extra_send.at[i],
            recv_sem=extra_recv.at[i],
            device_id=other,
            device_id_type=MESH,
        )
        copy.start()
        extra_copies.append(copy)
    parts = []
    for i in range(n):
        local_copies[i].wait()
        across[i].wait_recv()
        own, sibling = owns[i], siblings[i]

        def add(number, carry):
            at_y, at_z = number // RING, lax.rem(number, RING)
            own[at_y, at_z] = (
                own[at_y, at_z].astype(F32) + sibling[at_y, at_z].astype(F32)
            ).astype(own.dtype)
            return carry

        lax.fori_loop(0, RING * RING, add, 0)
        parts.append(Scatter(i, orders[i], own, buffers[i], y, z, push))
        parts[i].begin()
    for part in parts:
        part.join()
    for part in parts:
        part.turn()
    for part in parts:
        part.join_two()
    for i, part in enumerate(parts):
        part.finish(vector_own if i == 0 else outs[i])
        if i == 0:
            vector_parts[me] = vector_own[...]
            vector_copies = [
                push(0, 7, k, vector_own, vector_parts.at[me], {"tensor": step(me, k)})
                for k in range(1, RING)
            ]
    for copy in vector_copies:
        copy.wait_recv()
    total = vector_parts[0]
    for k in range(1, RING):
        total = total + vector_parts[k]
    outs[0][...] = total
    for copy in extra_copies:
        copy.wait()
    for copy in started:
        copy.wait_send()


def final_call(cid, orders, ins, extras):
    blocks = [value.shape[3:] for value in ins]
    square = [
        pltpu.VMEM((RING, RING) + block, value.dtype) for block, value in zip(blocks, ins)
    ]
    count, extra = len(ins), len(extras)
    return pl.pallas_call(
        functools.partial(final_kernel, orders, extra),
        out_shape=[jax.ShapeDtypeStruct(block, F32) for block in blocks]
        + [jax.ShapeDtypeStruct(value.shape, value.dtype) for value in extras],
        in_specs=[any_spec()] * count + [vmem_spec()] * extra,
        out_specs=[vmem_spec()] * (count + extra),
        scratch_shapes=square
        + square
        + [one for block, value in zip(blocks, ins) for one in Scatter.scratch(block, value.dtype)]
        + [
            pltpu.VMEM(blocks[0], F32),
            pltpu.VMEM((RING,) + blocks[0], F32),
            pltpu.SemaphoreType.DMA((count, 8, RING)),
            pltpu.SemaphoreType.DMA((count, 8, RING)),
            pltpu.SemaphoreType.DMA((count,)),
            pltpu.SemaphoreType.DMA((extra,)),
            pltpu.SemaphoreType.DMA((extra,)),
        ],
        compiler_params=comm_params(cid),
    )(*ins, *extras)


def gelu_exact(values):
    return jax.nn.gelu(values, approximate=False)


def flat_dot(former, latter):
    return lax.dot_general(former, latter, (((1,), (1,)), ((), ())), preferred_element_type=F32)


def rows_dot(former, latter):
    return lax.dot_general(former, latter, (((0,), (0,)), ((), ())), preferred_element_type=F32)


KEY_BLOCK = 256


def head_stack(values, scale):
    column = lax.broadcasted_iota(jnp.int32, values.shape, 1) // HEAD_DIM
    heads_here = values.shape[1] // HEAD_DIM
    zero = jnp.zeros_like(values)
    scaled = values * jnp.asarray(scale, values.dtype)
    return jnp.concatenate(
        [jnp.where(column == head, scaled, zero) for head in range(heads_here)], axis=0
    )


def block_scores(key_block, stack, seg_column, seg_wide):
    scores = flat_dot(key_block, stack)
    return jnp.where(seg_column == seg_wide, scores, MASKED_SCORE)


def attention_forward_kernel(q_ref, k_ref, v_ref, seg_q_ref, seg_k_ref, mixed_ref, wide_ref, lse_ref, stack, acc):
    group, width = q_ref.shape
    heads_here = width // HEAD_DIM
    stack[...] = head_stack(q_ref[...], HEAD_DIM ** (-0.5))
    acc[...] = jnp.zeros_like(acc)
    seg_wide = jnp.concatenate([seg_q_ref[0:1, :]] * heads_here, axis=1)
    seq = k_ref.shape[0]

    def each(number, carry):
        highest, total = carry
        here = pl.ds(pl.multiple_of(number * KEY_BLOCK, KEY_BLOCK), KEY_BLOCK)
        scores = block_scores(k_ref[here, :], stack[...], seg_k_ref[here, 0:1], seg_wide)
        above = jnp.maximum(highest, jnp.max(scores, axis=0, keepdims=True))
        weights = jnp.exp(scores - above)
        fade = jnp.exp(highest - above)
        total = total * fade + jnp.sum(weights, axis=0, keepdims=True)
        low = weights.astype(BF16)
        turned = v_ref[here, :].T
        for head in range(heads_here):
            rows = pl.ds(head * HEAD_DIM, HEAD_DIM)
            lanes = slice(head * group, (head + 1) * group)
            term = jnp.dot(
                turned[head * HEAD_DIM : (head + 1) * HEAD_DIM], low[:, lanes],
                preferred_element_type=F32,
            )
            acc[rows, :] = acc[rows, :] * fade[:, lanes] + term
        return above, total

    start = jnp.full((1, group * heads_here), MASKED_SCORE, F32)
    highest, total = lax.fori_loop(
        0, seq // KEY_BLOCK, each, (start, jnp.zeros_like(start))
    )
    inverse = 1.0 / total
    for head in range(heads_here):
        rows = pl.ds(head * HEAD_DIM, HEAD_DIM)
        wide_ref[rows, :] = acc[rows, :] * inverse[:, head * group : (head + 1) * group]
    mixed_ref[...] = wide_ref[...].T.astype(BF16)
    lse_ref[...] = jnp.broadcast_to(highest + jnp.log(total), lse_ref.shape)


def local_params():
    return pltpu.CompilerParams(vmem_limit_bytes=VMEM_LIMIT)


def attention_forward(queries, keys_full, values_full, seg_wide, seg_column):
    group, width = queries.shape
    heads_here = width // HEAD_DIM
    return pl.pallas_call(
        attention_forward_kernel,
        out_shape=[
            jax.ShapeDtypeStruct((group, width), BF16),
            jax.ShapeDtypeStruct((width, group), F32),
            jax.ShapeDtypeStruct((8, group * heads_here), F32),
        ],
        in_specs=[vmem_spec()] * 5,
        out_specs=[vmem_spec()] * 3,
        scratch_shapes=[
            pltpu.VMEM((group * heads_here, width), BF16),
            pltpu.VMEM((width, group), F32),
        ],
        compiler_params=local_params(),
    )(queries, keys_full, values_full, seg_wide, seg_column)


def attention_backward_kernel(
    q_ref, k_ref, v_ref, grad_ref, wide_ref, lse_ref, seg_q_ref, seg_k_ref,
    dq_ref, dk_ref, dv_ref,
    stack, plain, grad_stack, grad_plain, acc,
):
    group, width = q_ref.shape
    heads_here = width // HEAD_DIM
    scale = HEAD_DIM ** (-0.5)
    stack[...] = head_stack(q_ref[...], scale)
    plain[...] = head_stack(q_ref[...], 1.0)
    grad_stack[...] = head_stack(grad_ref[...], scale)
    grad_plain[...] = head_stack(grad_ref[...], 1.0)
    acc[...] = jnp.zeros_like(acc)
    seg_wide = jnp.concatenate([seg_q_ref[0:1, :]] * heads_here, axis=1)
    seq = k_ref.shape[0]
    product = grad_ref[...].astype(F32).T * wide_ref[...]
    delta = scale * jnp.concatenate(
        [
            jnp.sum(product[head * HEAD_DIM : (head + 1) * HEAD_DIM], axis=0, keepdims=True)
            for head in range(heads_here)
        ],
        axis=1,
    )
    lse = lse_ref[0:1, :]

    def each(number, carry):
        here = pl.ds(pl.multiple_of(number * KEY_BLOCK, KEY_BLOCK), KEY_BLOCK)
        key_block = k_ref[here, :]
        scores = block_scores(key_block, stack[...], seg_k_ref[here, 0:1], seg_wide)
        weights = jnp.exp(scores - lse)
        dv_ref[here, :] = jnp.dot(
            weights.astype(BF16), grad_plain[...], preferred_element_type=F32
        ).astype(BF16)
        prob_grad = flat_dot(v_ref[here, :], grad_stack[...])
        low = (weights * (prob_grad - delta)).astype(BF16)
        dk_ref[here, :] = jnp.dot(low, plain[...], preferred_element_type=F32).astype(BF16)
        turned = key_block.T
        for head in range(heads_here):
            rows = pl.ds(head * HEAD_DIM, HEAD_DIM)
            acc[rows, :] += jnp.dot(
                turned[head * HEAD_DIM : (head + 1) * HEAD_DIM],
                low[:, head * group : (head + 1) * group],
                preferred_element_type=F32,
            )
        return carry

    lax.fori_loop(0, seq // KEY_BLOCK, each, 0)
    dq_ref[...] = acc[...].T


def attention_backward(queries, keys_full, values_full, mixed_grad, wide, lse, seg_wide, seg_column):
    group, width = queries.shape
    heads_here = width // HEAD_DIM
    seq = keys_full.shape[0]
    return pl.pallas_call(
        attention_backward_kernel,
        out_shape=[
            jax.ShapeDtypeStruct((group, width), F32),
            jax.ShapeDtypeStruct((seq, width), BF16),
            jax.ShapeDtypeStruct((seq, width), BF16),
        ],
        in_specs=[vmem_spec()] * 8,
        out_specs=[vmem_spec()] * 3,
        scratch_shapes=[pltpu.VMEM((group * heads_here, width), BF16)] * 4
        + [pltpu.VMEM((width, group), F32)],
        compiler_params=local_params(),
    )(queries, keys_full, values_full, mixed_grad, wide, lse, seg_wide, seg_column)


WEIGHT_PIECES = (
    (0, (0,), True),
    (0, (1,), False),
    (0, (2,), True),
    (1, (), False),
    (4, (), True),
    (2, (), True),
    (3, (), False),
)


def shards(tokens, segment_ids, w_qkv, w_out, w_up, w_down, vectors, out_bias, cotangent):
    section = lax.axis_index("section")
    tensor_rank = lax.axis_index("tensor")
    own = lambda pair: jnp.where(section == 0, pair[0], pair[1])
    rows = tokens.shape[1]
    width = tokens.shape[2]
    group = rows * RING
    square = (RING, RING)
    local_width = w_qkv.shape[3]
    local_hidden = w_up.shape[2]

    depth = w_out.shape[1]
    small = jnp.pad(
        jnp.concatenate([vectors[0], out_bias], axis=0),
        ((0, 2), (0, 128 - depth)),
    )
    shape = lambda *dims: jax.ShapeDtypeStruct(dims, BF16)
    full_qkv, full_out, full_up, full_down, full_small = gather_call(
        0,
        WEIGHT_PIECES,
        [w_qkv[0], w_out[0], w_up[0], w_down[0], small],
        [
            shape(2, 3, *square, depth, local_width),
            shape(2, *square, depth, local_width),
            shape(2, *square, depth, local_hidden),
            shape(2, *square, depth, local_hidden),
            shape(2, *square, 16, 128),
        ],
        True,
    )
    full_qkv = full_qkv.reshape(2, 3, width, local_width)
    full_out = full_out.reshape(2, width, local_width)
    full_up = full_up.reshape(2, width, local_hidden)
    full_down = full_down.reshape(2, width, local_hidden)
    small_rows = (
        full_small.reshape(2, RING * RING, 16, 128)[..., :depth]
        .transpose(0, 2, 1, 3)
        .reshape(2, 16, width)
        .astype(F32)
    )

    my_tokens = own(tokens)
    my_cotangent = own(cotangent)
    my_segments = own(segment_ids)
    seg_block = jnp.zeros((8, 128), jnp.int32).at[0, :rows].set(my_segments)
    normed, seg_group = tensor_call(
        1, first_rows, None, [my_tokens], [small_rows[0]], [], 0, True, seg_block
    )
    seg_rows = seg_group[:, 0, :rows].reshape(group)
    seg_wide = jnp.broadcast_to(seg_rows[None], (8, group))
    inputs = my_tokens
    kept = []
    for layer in range(2):
        vec = small_rows[layer]
        normed = normed.reshape(group, width)
        query_bias = lax.dynamic_slice_in_dim(vec[2], tensor_rank * local_width, local_width)
        value_bias = lax.dynamic_slice_in_dim(vec[3], tensor_rank * local_width, local_width)
        up_bias = lax.dynamic_slice_in_dim(
            vec[9:13].reshape(-1), tensor_rank * local_hidden, local_hidden
        )
        project = lambda which: jnp.dot(normed, full_qkv[layer, which], preferred_element_type=F32)
        queries = (project(0) + query_bias).astype(BF16)
        keys = project(1).astype(BF16)
        values = (project(2) + value_bias).astype(BF16)
        keys_full, values_full, seg_full = gather_call(
            2,
            ((2, (), True), (0, (), True), (1, (), False)),
            [keys, values, seg_wide],
            [
                shape(*square, group, local_width),
                shape(*square, group, local_width),
                jax.ShapeDtypeStruct(square + (8, group), jnp.int32),
            ],
            False,
        )
        keys_full = keys_full.reshape(-1, local_width)
        values_full = values_full.reshape(-1, local_width)
        if layer == 0:
            seg_column = jnp.broadcast_to(
                seg_full[:, :, 0].reshape(-1)[:, None], (keys_full.shape[0], 128)
            )
        mixed, wide, lse = attention_forward(queries, keys_full, values_full, seg_wide, seg_column)
        part = flat_dot(mixed, full_out[layer]).astype(BF16).reshape(RING, rows, width)
        attn_out, hidden, normed_two = tensor_call(
            3, middle_rows, part, [inputs.astype(F32)], [vec], [F32, F32], 0, True
        )
        normed_two = normed_two.reshape(group, width)
        pre_act = jnp.dot(normed_two, full_up[layer], preferred_element_type=F32) + up_bias
        activated = gelu_exact(pre_act).astype(BF16)
        part = flat_dot(activated, full_down[layer]).astype(BF16).reshape(RING, rows, width)
        step_kept = [inputs, normed, queries, keys_full, values_full, mixed, attn_out, hidden]
        step_kept += [normed_two, pre_act, activated, wide, lse]
        if layer == 0:
            mlp_first, between, normed = tensor_call(
                4, end_rows_first, part, [hidden], [vec, small_rows[1]], [F32, BF16], 0, True
            )
            inputs = between
        else:
            outputs, sums_end, mlp_rows = tensor_call(
                5, end_rows_last, part, [hidden, my_cotangent], [vec], [BF16], 2, True
            )
        kept.append(step_kept)

    upstream = my_cotangent.astype(F32)
    grads = [None, None]
    scale_two, down_bias = sums_end[0], sums_end[1]
    for layer in (1, 0):
        vec = small_rows[layer]
        inputs, normed, queries, keys_full, values_full, mixed, attn_out, hidden = kept[layer][:8]
        normed_two, pre_act, activated, wide, lse = kept[layer][8:]
        mlp_rows = mlp_rows.reshape(group, width)
        act_grad = jnp.dot(mlp_rows, full_down[layer], preferred_element_type=F32)
        grad_down = rows_dot(mlp_rows, activated)
        pre_grad = jax.vjp(gelu_exact, pre_act)[1](act_grad)[0]
        up_bias_grad = jnp.sum(pre_grad, axis=0)
        pre_low = pre_grad.astype(BF16)
        grad_up = rows_dot(normed_two, pre_low)
        part = flat_dot(pre_low, full_up[layer]).astype(BF16).reshape(RING, rows, width)
        hidden_grad, sums_middle, attn_rows = tensor_call(
            6, back_middle_rows, part, [upstream, hidden, attn_out], [vec], [F32], 4, True
        )
        attn_rows = attn_rows.reshape(group, width)
        mixed_grad = jnp.dot(attn_rows, full_out[layer], preferred_element_type=F32).astype(BF16)
        grad_out = rows_dot(attn_rows, mixed)
        query_grad, keys_part, values_part = attention_backward(
            queries, keys_full, values_full, mixed_grad, wide, lse, seg_wide, seg_column
        )
        keys_grad, values_grad = scatter_call(
            7,
            (True, False),
            [
                keys_part.reshape(*square, group, local_width),
                values_part.reshape(*square, group, local_width),
            ],
        )
        query_bias_grad = jnp.sum(query_grad, axis=0)
        value_bias_grad = jnp.sum(values_grad, axis=0)
        triple = [value.astype(BF16) for value in (query_grad, keys_grad, values_grad)]
        grad_qkv = [rows_dot(normed, value) for value in triple]
        part = sum(flat_dot(triple[which], full_qkv[layer, which]) for which in range(3))
        part = part.astype(BF16).reshape(RING, rows, width)
        if layer == 1:
            input_grad, sums_last, mlp_rows = tensor_call(
                8,
                back_end_rows_last,
                part,
                [hidden_grad, inputs.astype(F32), mlp_first],
                [vec, small_rows[0]],
                [F32],
                4,
                True,
            )
        else:
            input_grad, sums_last = tensor_call(
                9, back_end_rows_first, part, [hidden_grad, inputs.astype(F32)], [vec], [F32], 2, False
            )

        def placed(values, length):
            empty = jnp.zeros((length,), F32)
            return lax.dynamic_update_slice(empty, values, (tensor_rank * values.shape[0],))

        vector_rows = jnp.concatenate(
            [
                sums_last[0:2],
                placed(query_bias_grad, width)[None],
                placed(value_bias_grad, width)[None],
                sums_middle[2:3],
                sums_middle[0:2],
                down_bias[None],
                scale_two[None],
                placed(up_bias_grad, local_hidden * RING).reshape(-1, width),
                sums_middle[3:4],
                jnp.zeros((2, width), F32),
            ],
            axis=0,
        )
        vector_rows = jnp.pad(
            vector_rows.reshape(16, RING * RING, depth).transpose(1, 0, 2),
            ((0, 0), (0, 0), (0, 128 - depth)),
        ).reshape(*square, 16, 128)
        grads[layer] = [vector_rows] + [
            value.astype(BF16).reshape(*square, depth, value.shape[-1])
            for value in grad_qkv + [grad_out, grad_up, grad_down]
        ]
        if layer == 1:
            last_grad = input_grad
            upstream = input_grad.astype(BF16).astype(F32)
            scale_two, down_bias = sums_last[2], sums_last[3]
    first_grad = input_grad

    stacked = [jnp.stack(pair) for pair in zip(*grads)]
    extras = [
        jnp.where(section == 0, outputs, between),
        jnp.where(section == 0, last_grad, first_grad),
    ]
    results = final_call(10, (True, True, False, True, False, True, False), stacked, extras)
    small_sum, grad_q, grad_k, grad_v, grad_out, grad_up, grad_down, came_out, came_grad = results
    mine_out = jnp.where(section == 0, between, outputs)
    mine_grad = jnp.where(section == 0, first_grad, last_grad)
    pair = lambda mine, came: jnp.where(
        section == 0, jnp.stack([mine, came]), jnp.stack([came, mine])
    )[None]
    return (
        pair(mine_out, came_out),
        pair(mine_grad, came_grad),
        jnp.stack([grad_q, grad_k, grad_v])[None],
        grad_out[None],
        grad_up[None],
        grad_down[None],
        small_sum[:13, :depth][None],
        small_sum[13:14, :depth],
    )


def solution(mesh):
    in_specs = (
        P(None, ("dp", "tensor"), None),
        P(None, ("dp", "tensor")),
        P("section", None, "dp", "tensor"),
        P("section", "dp", "tensor"),
        P("section", "dp", "tensor"),
        P("section", "dp", "tensor"),
        P("section", None, "dp"),
        P("section", "dp"),
        P(None, ("dp", "tensor"), None),
    )
    out_specs = (
        P("section", None, ("dp", "tensor"), None),
        P("section", None, ("dp", "tensor"), None),
        P("section", None, "dp", "tensor"),
        P("section", "dp", "tensor"),
        P("section", "dp", "tensor"),
        P("section", "dp", "tensor"),
        P("section", None, "dp"),
        P("section", "dp"),
    )
    return jax.shard_map(shards, mesh=mesh, in_specs=in_specs, out_specs=out_specs, check_vma=False)
```

```python
import functools

import jax
import jax.numpy as jnp
from jax import lax
from jax.experimental import pallas as pl
from jax.experimental.pallas import tpu as pltpu
from jax.sharding import PartitionSpec as P

MESH = pl.DeviceIdType.MESH
HEAD_DIM = 64
EPSILON = 1e-06
MASKED_SCORE = -1e30
RING = 4
VMEM_LIMIT = 56 * 1024 * 1024
F32 = jnp.float32
BF16 = jnp.bfloat16


def vmem_spec():
    return pl.BlockSpec(memory_space=pltpu.VMEM)


def any_spec():
    return pl.BlockSpec(memory_space=pl.ANY)


def comm_params(cid):
    return pltpu.CompilerParams(
        collective_id=cid, has_side_effects=True, vmem_limit_bytes=VMEM_LIMIT
    )


def step(coord, by):
    return lax.rem(coord + by, RING)


def layer_norm(values, gain_row, shift_row):
    centre = values - jnp.mean(values, axis=-1, keepdims=True)
    spread = jnp.mean(centre * centre, axis=-1, keepdims=True)
    return centre * lax.rsqrt(spread + EPSILON) * gain_row + shift_row


def layer_norm_back(values, gain_row, grad):
    centre = values - jnp.mean(values, axis=-1, keepdims=True)
    spread = jnp.mean(centre * centre, axis=-1, keepdims=True)
    inverse = lax.rsqrt(spread + EPSILON)
    normed = centre * inverse
    scaled = grad * gain_row
    back = inverse * (
        scaled
        - jnp.mean(scaled, axis=-1, keepdims=True)
        - normed * jnp.mean(scaled * normed, axis=-1, keepdims=True)
    )
    return back, jnp.sum(grad * normed, axis=0, keepdims=True), jnp.sum(grad, axis=0, keepdims=True)


PLUS, FAR, MINUS = 1, 2, 3
SUBS = 2


def tensor_kernel(function, n_rows, n_vecs, n_out, n_sums, reduce, gather, with_seg, *refs):
    refs = list(refs)
    take = lambda count: [refs.pop(0) for _ in range(count)]
    part = take(1)[0] if reduce else None
    rows_in = take(n_rows)
    vecs = take(n_vecs)
    seg_in = take(1)[0] if with_seg else None
    rows_out = take(n_out)
    sums_out = take(1)[0] if n_sums else None
    full = take(1)[0] if gather else None
    seg_out = take(1)[0] if with_seg else None
    passing, joined, from_minus, from_plus = take(4) if reduce else [None] * 4
    send, recv, local = take(3)

    me = lax.axis_index("tensor")
    barrier = pltpu.get_barrier_semaphore()
    for k in (PLUS, MINUS):
        pl.semaphore_signal(
            barrier, inc=1, device_id={"tensor": step(me, k)}, device_id_type=MESH
        )
    pl.semaphore_wait(barrier, 2)

    chunk = rows_in[0].shape[0] // (2 * SUBS)
    started = []

    def push(source, target, kind, index, k):
        copy = pltpu.make_async_remote_copy(
            src_ref=source,
            dst_ref=target,
            send_sem=send.at[kind, index],
            recv_sem=recv.at[kind, index],
            device_id={"tensor": step(me, k)},
            device_id_type=MESH,
        )
        copy.start()
        started.append(copy)
        return copy

    chunks = range(2 * SUBS)
    here = lambda c: pl.ds(c * chunk, chunk)
    onward = lambda c: PLUS if c % 2 == 0 else MINUS
    aside = lambda c: MINUS if c % 2 == 0 else PLUS
    side_of = {PLUS: from_minus, MINUS: from_plus}
    way, straight, summed = {}, {}, {}
    if reduce:
        for c in chunks:
            way[c] = push(part.at[step(me, FAR), here(c)], passing.at[here(c)], 0, c, onward(c))
        for c in chunks:
            straight[c] = push(
                part.at[step(me, aside(c)), here(c)], side_of[aside(c)].at[here(c)], 1, c, aside(c)
            )
        for c in chunks:
            way[c].wait_recv()
            joined[here(c)] = (
                part[step(me, onward(c)), here(c)].astype(F32) + passing[here(c)].astype(F32)
            ).astype(BF16)
            summed[c] = push(joined.at[here(c)], side_of[onward(c)].at[here(c)], 2, c, onward(c))
    last = []
    if with_seg:
        own = pltpu.make_async_copy(seg_in, seg_out.at[me], local)
        own.start()
        seg_up = push(seg_in, seg_out.at[me], 6, 0, PLUS)
        seg_down = push(seg_in, seg_out.at[me], 6, 1, MINUS)
        last.append(seg_down)
    sums = [None] * n_sums
    ups, downs = {}, {}
    for c in chunks:
        total = None
        if reduce:
            straight[c].wait_recv()
            summed[c].wait_recv()
            total = (
                part[me, here(c)].astype(F32)
                + from_minus[here(c)].astype(F32)
                + from_plus[here(c)].astype(F32)
            )
        spread, outs, parts = function(
            total, [ref[here(c)].astype(F32) for ref in rows_in], vecs
        )
        if gather:
            full[me, here(c)] = spread.astype(BF16)
            ups[c] = push(full.at[me, here(c)], full.at[me, here(c)], 3, c, PLUS)
            downs[c] = push(full.at[me, here(c)], full.at[me, here(c)], 4, c, MINUS)
        for ref, value in zip(rows_out, outs):
            ref[here(c)] = value.astype(ref.dtype)
        sums = [new if old is None else old + new for old, new in zip(sums, parts)]
    if gather:
        for c in chunks:
            (ups if c % 2 == 0 else downs)[c].wait_recv()
            came = full.at[step(me, aside(c)), here(c)]
            last.append(push(came, came, 5, c, onward(c)))
            last.append((downs if c % 2 == 0 else ups)[c])
    if n_sums:
        sums_out[...] = jnp.concatenate(
            sums + [jnp.zeros((8 - n_sums, sums[0].shape[1]), F32)], axis=0
        )
    if with_seg:
        own.wait()
        seg_up.wait_recv()
        came = seg_out.at[step(me, MINUS)]
        last.append(push(came, came, 6, 2, PLUS))
    for copy in last:
        copy.wait_recv()
    for copy in started:
        copy.wait_send()


def tensor_call(cid, function, part, rows, vecs, outs, n_sums, gather, seg=None):
    height, width = rows[0].shape
    reduce = part is not None
    with_seg = seg is not None
    args = ([part] if reduce else []) + list(rows) + list(vecs) + ([seg] if with_seg else [])
    shapes = [jax.ShapeDtypeStruct((height, width), dtype) for dtype in outs]
    if n_sums:
        shapes.append(jax.ShapeDtypeStruct((8, width), F32))
    if gather:
        shapes.append(jax.ShapeDtypeStruct((RING, height, width), BF16))
    if with_seg:
        shapes.append(jax.ShapeDtypeStruct((RING,) + seg.shape, seg.dtype))
    scratch = [pltpu.VMEM((height, width), BF16)] * 4 if reduce else []
    scratch += [
        pltpu.SemaphoreType.DMA((7, 2 * SUBS)),
        pltpu.SemaphoreType.DMA((7, 2 * SUBS)),
        pltpu.SemaphoreType.DMA,
    ]
    return pl.pallas_call(
        functools.partial(
            tensor_kernel, function, len(rows), len(vecs), len(outs), n_sums, reduce, gather, with_seg
        ),
        out_shape=shapes,
        in_specs=[vmem_spec()] * len(args),
        out_specs=[vmem_spec()] * len(shapes),
        scratch_shapes=scratch,
        compiler_params=comm_params(cid),
    )(*args)


def row(ref, index):
    return ref[pl.ds(index, 1), :]


def first_rows(total, rows, vecs):
    return layer_norm(rows[0], row(vecs[0], 0), row(vecs[0], 1)), [], []


def middle_rows(total, rows, vecs):
    vec = vecs[0]
    attn_out = total + row(vec, 13)
    hidden = rows[0] + row(vec, 4) * attn_out
    return layer_norm(hidden, row(vec, 5), row(vec, 6)), [attn_out, hidden], []


def end_rows_first(total, rows, vecs):
    vec, after = vecs
    mlp_out = total + row(vec, 7)
    outputs = (rows[0] + row(vec, 8) * mlp_out).astype(BF16)
    inputs = outputs.astype(F32)
    return layer_norm(inputs, row(after, 0), row(after, 1)), [mlp_out, outputs], []


def end_rows_last(total, rows, vecs):
    vec = vecs[0]
    hidden, upstream = rows
    mlp_out = total + row(vec, 7)
    outputs = hidden + row(vec, 8) * mlp_out
    mlp_grad = row(vec, 8) * upstream
    sums = [
        jnp.sum(upstream * mlp_out, axis=0, keepdims=True),
        jnp.sum(mlp_grad, axis=0, keepdims=True),
    ]
    return mlp_grad, [outputs], sums


def back_middle_rows(total, rows, vecs):
    vec = vecs[0]
    upstream, hidden, attn_out = rows
    part, gain, shift = layer_norm_back(hidden, row(vec, 5), total)
    hidden_grad = upstream + part
    attn_grad = row(vec, 4) * hidden_grad
    sums = [
        gain,
        shift,
        jnp.sum(hidden_grad * attn_out, axis=0, keepdims=True),
        jnp.sum(attn_grad, axis=0, keepdims=True),
    ]
    return attn_grad, [hidden_grad], sums


def back_end_rows_last(total, rows, vecs):
    vec, before = vecs
    hidden_grad, inputs, mlp_out = rows
    part, gain, shift = layer_norm_back(inputs, row(vec, 0), total)
    input_grad = hidden_grad + part
    upstream = input_grad.astype(BF16).astype(F32)
    mlp_grad = row(before, 8) * upstream
    sums = [
        gain,
        shift,
        jnp.sum(upstream * mlp_out, axis=0, keepdims=True),
        jnp.sum(mlp_grad, axis=0, keepdims=True),
    ]
    return mlp_grad, [input_grad], sums


def back_end_rows_first(total, rows, vecs):
    hidden_grad, inputs = rows
    part, gain, shift = layer_norm_back(inputs, row(vecs[0], 0), total)
    return None, [hidden_grad + part], [gain, shift]


def dp_neighbour(y, z, along_z, k):
    if along_z:
        return {"dp": y * RING + step(z, k)}
    return {"dp": step(y, k) * RING + z}


def dp_barrier(y, z, section):
    barrier = pltpu.get_barrier_semaphore()
    count = 0
    for along_z in (True, False):
        for k in (PLUS, MINUS):
            pl.semaphore_signal(
                barrier, inc=1, device_id=dp_neighbour(y, z, along_z, k), device_id_type=MESH
            )
            count += 1
    if section is not None:
        pl.semaphore_signal(
            barrier, inc=1, device_id={"section": 1 - section}, device_id_type=MESH
        )
        count += 1
    return barrier, count


def pusher(send, recv, started):
    def push(index, kind, k, source, target, device):
        copy = pltpu.make_async_remote_copy(
            src_ref=source,
            dst_ref=target,
            send_sem=send.at[index, kind, k],
            recv_sem=recv.at[index, kind, k],
            device_id=device,
            device_id_type=MESH,
        )
        copy.start()
        started.append(copy)
        return copy

    return push


class Gather:
    WAYS = {0: 1, 3: 1, 1: 1, 2: 3}

    def __init__(self, pieces, outs, y, z, lead, push):
        self.pieces, self.outs, self.y, self.z = pieces, outs, y, z
        self.lead, self.push = lead, push
        self.every = range(len(pieces))
        self.first, self.onward, self.second, self.relayed = {}, {}, {}, {}

    def block(self, i, along, across, rows=None):
        number, pre, along_z = self.pieces[i]
        ys, zs = (across, along) if along_z else (along, across)
        ys = ys if isinstance(ys, slice) else step(self.y, ys) if ys else self.y
        zs = zs if isinstance(zs, slice) else step(self.z, zs) if zs else self.z
        return self.outs[number].at[self.lead + pre + (ys, zs) + (() if rows is None else (rows,))]

    def way(self, i, first, k):
        return dp_neighbour(self.y, self.z, self.pieces[i][2] == first, k)

    def halves(self, i):
        height = self.outs[self.pieces[i][0]].shape[-2]
        if height < 32:
            return {PLUS: None}
        return {PLUS: pl.ds(0, height // 2), MINUS: pl.ds(height // 2, height // 2)}

    def spread(self, i, offset, source):
        for k in (PLUS, MINUS):
            self.second[i, offset, k] = self.push(
                i, 2 if k == PLUS else 3, offset, source, self.block(i, offset, 0), self.way(i, False, k)
            )

    def begin(self, i, source):
        for k in (PLUS, MINUS):
            self.first[i, k] = self.push(i, 0, k, source, self.block(i, 0, 0), self.way(i, True, k))
        self.spread(i, 0, source)

    def near(self):
        for i in self.every:
            split = self.halves(i)
            for k in (PLUS, MINUS):
                self.first[i, k].wait_recv()
                came = RING - k
                if k in split:
                    self.onward[i, k] = self.push(
                        i, 1, k, self.block(i, came, 0, split[k]), self.block(i, came, 0, split[k]),
                        self.way(i, True, k),
                    )
                self.spread(i, came, self.block(i, came, 0))

    def relay(self, i, offset):
        k = self.WAYS[offset]
        self.second[i, offset, k].wait_recv()
        came = self.block(i, offset, RING - k)
        self.relayed[i, offset] = self.push(i, 4, offset, came, came, self.way(i, False, k))

    def other(self, i, offset):
        self.second[i, offset, RING - self.WAYS[offset]].wait_recv()

    def far(self, i):
        for k in self.halves(i):
            self.onward[i, k].wait_recv()
        self.spread(i, FAR, self.block(i, FAR, 0))


def gather_kernel(pieces, n_in, n_out, with_sibling, *refs):
    ins, outs = refs[:n_in], refs[n_in : n_in + n_out]
    send, recv, local = refs[n_in + n_out :]
    rank = lax.axis_index("dp")
    y, z = rank // RING, lax.rem(rank, RING)
    section = lax.axis_index("section")
    barrier, count = dp_barrier(y, z, section)
    pl.semaphore_wait(barrier, count)
    started = []
    push = pusher(send, recv, started)
    ring = Gather(pieces, outs, y, z, (section,), push)
    own = {}
    for i, (number, pre, _) in enumerate(pieces):
        source = ins[number].at[pre] if pre else ins[number]
        ring.begin(i, source)
        own[i] = pltpu.make_async_copy(source, ring.block(i, 0, 0), local.at[i])
        own[i].start()
    across = []

    def pass_on(i, line):
        came = ring.block(i, slice(None), line)
        across.append(push(i, 5, line, came, came, {"section": 1 - section}))

    ring.near()
    for i in ring.every:
        ring.relay(i, 0)
    for i in ring.every:
        ring.far(i)
    for i in ring.every:
        ring.relay(i, MINUS)
        ring.relay(i, PLUS)
        own[i].wait()
        pass_on(i, 0)
    for i in ring.every:
        ring.relay(i, FAR)
        for offset in range(RING):
            ring.other(i, offset)
        pass_on(i, PLUS)
        pass_on(i, MINUS)
    for i in ring.every:
        for offset in range(RING):
            ring.relayed[i, offset].wait_recv()
        pass_on(i, FAR)
    for copy in across:
        copy.wait_recv()
    for copy in started:
        copy.wait_send()


def gather_call(cid, pieces, ins, outs, with_sibling):
    return pl.pallas_call(
        functools.partial(gather_kernel, pieces, len(ins), len(outs), with_sibling),
        out_shape=outs,
        in_specs=[vmem_spec()] * len(ins),
        out_specs=[any_spec()] * len(outs),
        scratch_shapes=[
            pltpu.SemaphoreType.DMA((len(pieces), 6, RING)),
            pltpu.SemaphoreType.DMA((len(pieces), 6, RING)),
            pltpu.SemaphoreType.DMA((len(pieces),)),
        ],
        compiler_params=comm_params(cid),
    )(*ins)


class Scatter:
    ORDER = (FAR, PLUS, MINUS, 0)
    WAYS = {FAR: PLUS, 0: PLUS, PLUS: MINUS, MINUS: MINUS}

    def __init__(self, index, along_z, source, buffers, y, z, push):
        self.index, self.along_z, self.source = index, along_z, source
        self.passing, self.joined, self.summed, self.straight, self.middle = buffers[:5]
        self.far_two, self.joined_two, self.summed_two, self.straight_two = buffers[5:]
        self.y, self.z, self.push = y, z, push
        self.height, self.width = source.shape[-2:]
        self.via, self.direct, self.after = {}, {}, {}

    def at(self, along, across):
        ys, zs = (across, along) if self.along_z else (along, across)
        return step(self.y, ys), step(self.z, zs)

    def way(self, first, k):
        return dp_neighbour(self.y, self.z, self.along_z == first, k)

    def add(self, target, terms, top=0, height=None):
        height = self.height if height is None else height
        size = max(8, min(height, 32768 // self.width))

        def part(here):
            value = terms[0](here).astype(F32)
            for term in terms[1:]:
                value = value + term(here).astype(F32)
            target[here] = value.astype(target.dtype)

        if height <= size:
            part(pl.ds(top, height))
            return

        def each(number, carry):
            part(pl.ds(pl.multiple_of(top + number * size, size), size))
            return carry

        lax.fori_loop(0, height // size, each, 0)

    def send_via(self, j):
        self.via[j] = self.push(
            self.index, 0, j, self.source.at[self.at(FAR, j)], self.passing.at[j],
            self.way(True, self.WAYS[j]),
        )

    def send_direct(self, j):
        k = RING - self.WAYS[j]
        self.direct[j] = self.push(
            self.index, 1, j, self.source.at[self.at(k, j)], self.straight.at[j], self.way(True, k)
        )

    def begin(self):
        for j in self.ORDER:
            self.send_via(j)
        for j in self.ORDER:
            self.send_direct(j)

    def join_one(self, j):
        self.via[j].wait_recv()
        k = self.WAYS[j]
        at_y, at_z = self.at(k, j)
        self.add(
            self.joined.at[j],
            [lambda h: self.source[at_y, at_z, h], lambda h: self.passing[j, h]],
        )
        self.after[j] = self.push(
            self.index, 2, j, self.joined.at[j], self.summed.at[j], self.way(True, k)
        )

    def join(self):
        for j in self.ORDER:
            self.join_one(j)

    def turn(self):
        half = self.height // 2
        low, high = pl.ds(0, half), pl.ds(half, half)
        send = lambda kind, slot, source, target, k: self.push(
            self.index, kind, slot, source, target, self.way(False, k)
        )
        for j in self.ORDER:
            self.direct[j].wait_recv()
            self.after[j].wait_recv()
            at_y, at_z = self.at(0, j)
            self.add(
                self.middle.at[j],
                [
                    lambda h: self.source[at_y, at_z, h],
                    lambda h: self.summed[j, h],
                    lambda h: self.straight[j, h],
                ],
            )
            if j == FAR:
                self.via_two = [
                    send(3, 0, self.middle.at[j, low], self.far_two.at[low], PLUS),
                    send(3, 1, self.middle.at[j, high], self.far_two.at[high], MINUS),
                ]
            if j == PLUS:
                high_copy = send(4, 1, self.middle.at[j, high], self.straight_two.at[high], PLUS)
            if j == MINUS:
                low_copy = send(4, 0, self.middle.at[j, low], self.straight_two.at[low], MINUS)
        self.direct_two = [low_copy, high_copy]

    def join_two(self):
        half = self.height // 2
        self.after_two = []
        for number, (top, k) in enumerate(((0, PLUS), (half, MINUS))):
            self.via_two[number].wait_recv()
            self.add(
                self.joined_two,
                [lambda h: self.middle[k, h], lambda h: self.far_two[h]],
                top,
                half,
            )
            here = pl.ds(top, half)
            self.after_two.append(
                self.push(
                    self.index, 5, number, self.joined_two.at[here], self.summed_two.at[here],
                    self.way(False, k),
                )
            )

    def finish(self, out):
        for copy in self.direct_two + self.after_two:
            copy.wait_recv()
        self.add(
            out,
            [
                lambda h: self.middle[0, h],
                lambda h: self.summed_two[h],
                lambda h: self.straight_two[h],
            ],
        )

    @staticmethod
    def scratch(block, dtype):
        return [pltpu.VMEM((RING,) + block, dtype)] * 5 + [pltpu.VMEM(block, dtype)] * 4


SCATTER_BUFFERS = 9


def final_kernel(orders, n_extra, *refs):
    n = len(orders)
    refs = list(refs)
    take = lambda count: [refs.pop(0) for _ in range(count)]
    ins, extras = take(n), take(n_extra)
    outs, extra_outs = take(n), take(n_extra)
    siblings, owns = take(n), take(n)
    buffers = [take(SCATTER_BUFFERS) for _ in range(n)]
    vector_own, vector_parts = take(2)
    send, recv, local, extra_send, extra_recv = take(5)
    rank = lax.axis_index("dp")
    y, z = rank // RING, lax.rem(rank, RING)
    section = lax.axis_index("section")
    me = lax.axis_index("tensor")
    barrier, count = dp_barrier(y, z, section)
    for k in range(1, RING):
        pl.semaphore_signal(
            barrier, inc=1, device_id={"tensor": step(me, k)}, device_id_type=MESH
        )
    pl.semaphore_wait(barrier, count + RING - 1)
    started = []
    push = pusher(send, recv, started)
    other = {"section": 1 - section}
    across, local_copies = [], []
    for i in range(n):
        across.append(push(i, 6, 0, ins[i].at[1 - section], siblings[i], other))
        copy = pltpu.make_async_copy(ins[i].at[section], owns[i], local.at[i])
        copy.start()
        local_copies.append(copy)
    extra_copies = []
    for i in range(n_extra):
        copy = pltpu.make_async_remote_copy(
            src_ref=extras[i],
            dst_ref=extra_outs[i],
            send_sem=extra_send.at[i],
            recv_sem=extra_recv.at[i],
            device_id=other,
            device_id_type=MESH,
        )
        copy.start()
        extra_copies.append(copy)
    parts = []
    for i in range(n):
        local_copies[i].wait()
        across[i].wait_recv()
        own, sibling = owns[i], siblings[i]

        def add(number, carry):
            at_y, at_z = number // RING, lax.rem(number, RING)
            own[at_y, at_z] = (
                own[at_y, at_z].astype(F32) + sibling[at_y, at_z].astype(F32)
            ).astype(own.dtype)
            return carry

        lax.fori_loop(0, RING * RING, add, 0)
        parts.append(Scatter(i, orders[i], own, buffers[i], y, z, push))
        parts[i].begin()
    for part in parts:
        part.join()
    for part in parts:
        part.turn()
    for part in parts:
        part.join_two()
    for i, part in enumerate(parts):
        part.finish(vector_own if i == 0 else outs[i])
        if i == 0:
            vector_parts[me] = vector_own[...]
            vector_copies = [
                push(0, 7, k, vector_own, vector_parts.at[me], {"tensor": step(me, k)})
                for k in range(1, RING)
            ]
    for copy in vector_copies:
        copy.wait_recv()
    total = vector_parts[0]
    for k in range(1, RING):
        total = total + vector_parts[k]
    outs[0][...] = total
    for copy in extra_copies:
        copy.wait()
    for copy in started:
        copy.wait_send()


def final_call(cid, orders, ins, extras):
    blocks = [value.shape[3:] for value in ins]
    square = [
        pltpu.VMEM((RING, RING) + block, value.dtype) for block, value in zip(blocks, ins)
    ]
    count, extra = len(ins), len(extras)
    return pl.pallas_call(
        functools.partial(final_kernel, orders, extra),
        out_shape=[jax.ShapeDtypeStruct(block, F32) for block in blocks]
        + [jax.ShapeDtypeStruct(value.shape, value.dtype) for value in extras],
        in_specs=[any_spec()] * count + [vmem_spec()] * extra,
        out_specs=[vmem_spec()] * (count + extra),
        scratch_shapes=square
        + square
        + [one for block, value in zip(blocks, ins) for one in Scatter.scratch(block, value.dtype)]
        + [
            pltpu.VMEM(blocks[0], F32),
            pltpu.VMEM((RING,) + blocks[0], F32),
            pltpu.SemaphoreType.DMA((count, 8, RING)),
            pltpu.SemaphoreType.DMA((count, 8, RING)),
            pltpu.SemaphoreType.DMA((count,)),
            pltpu.SemaphoreType.DMA((extra,)),
            pltpu.SemaphoreType.DMA((extra,)),
        ],
        compiler_params=comm_params(cid),
    )(*ins, *extras)


def gelu_exact(values):
    return jax.nn.gelu(values, approximate=False)


def flat_dot(former, latter):
    return lax.dot_general(former, latter, (((1,), (1,)), ((), ())), preferred_element_type=F32)


def rows_dot(former, latter):
    return lax.dot_general(former, latter, (((0,), (0,)), ((), ())), preferred_element_type=F32)


def head_stack(values, scale):
    column = lax.broadcasted_iota(jnp.int32, values.shape, 1) // HEAD_DIM
    heads_here = values.shape[1] // HEAD_DIM
    zero = jnp.zeros_like(values)
    scaled = values * jnp.asarray(scale, values.dtype)
    return jnp.concatenate(
        [jnp.where(column == head, scaled, zero) for head in range(heads_here)], axis=0
    )


def block_scores(key_block, stack, seg_column, seg_wide):
    scores = flat_dot(key_block, stack)
    return jnp.where(seg_column == seg_wide, scores, MASKED_SCORE)


def attend_kernel(
    layer, normed_ref, qkv_any, out_any, bias_ref, seg_q_ref, seg_k_ref,
    q_ref, k_ref, v_ref, mixed_ref, wide_ref, lse_ref, part_ref,
    qkv_ref, out_ref, stack, acc, top_ref, total_ref, send, recv, local,
):
    group, width = q_ref.shape
    heads_here = width // HEAD_DIM
    loads = [
        pltpu.make_async_copy(qkv_any.at[layer, which], qkv_ref.at[which], local.at[which])
        for which in range(3)
    ]
    loads.append(pltpu.make_async_copy(out_any.at[layer], out_ref, local.at[3]))
    for which in (1, 2, 0, 3):
        loads[which].start()
    rank = lax.axis_index("dp")
    y, z = rank // RING, lax.rem(rank, RING)
    barrier, count = dp_barrier(y, z, None)
    normed = normed_ref[...]
    loads[1].wait()
    k_ref[y, z] = jnp.dot(normed, qkv_ref[1], preferred_element_type=F32).astype(BF16)
    pl.semaphore_wait(barrier, count)
    started = []
    ring = Gather(((0, (), True), (1, (), False)), (k_ref, v_ref), y, z, (), pusher(send, recv, started))
    ring.begin(0, k_ref.at[y, z])
    loads[2].wait()
    v_ref[y, z] = (
        jnp.dot(normed, qkv_ref[2], preferred_element_type=F32) + bias_ref[1:2, :]
    ).astype(BF16)
    ring.begin(1, v_ref.at[y, z])
    loads[0].wait()
    q_ref[...] = (
        jnp.dot(normed, qkv_ref[0], preferred_element_type=F32) + bias_ref[0:1, :]
    ).astype(BF16)
    stack[...] = head_stack(q_ref[...], HEAD_DIM ** (-0.5))
    acc[...] = jnp.zeros_like(acc)
    top_ref[...] = jnp.full_like(top_ref, MASKED_SCORE)
    total_ref[...] = jnp.zeros_like(total_ref)
    seg_wide = jnp.concatenate([seg_q_ref[0:1, :]] * heads_here, axis=1)

    def attend(offset_y, offset_z):
        at_y, at_z = step(y, offset_y), step(z, offset_z)
        highest = top_ref[0:1, :]
        scores = block_scores(
            k_ref[at_y, at_z], stack[...], seg_k_ref[at_y, at_z, :, 0:1], seg_wide
        )
        above = jnp.maximum(highest, jnp.max(scores, axis=0, keepdims=True))
        weights = jnp.exp(scores - above)
        fade = jnp.exp(highest - above)
        total_ref[0:1, :] = total_ref[0:1, :] * fade + jnp.sum(weights, axis=0, keepdims=True)
        top_ref[0:1, :] = above
        low = weights.astype(BF16)
        turned = v_ref[at_y, at_z].T
        for head in range(heads_here):
            rows = pl.ds(head * HEAD_DIM, HEAD_DIM)
            lanes = slice(head * group, (head + 1) * group)
            term = jnp.dot(
                turned[head * HEAD_DIM : (head + 1) * HEAD_DIM], low[:, lanes],
                preferred_element_type=F32,
            )
            acc[rows, :] = acc[rows, :] * fade[:, lanes] + term

    def attend_all(count, offsets):
        def each(number, carry):
            attend(*offsets(number))
            return carry

        lax.fori_loop(0, count, each, 0)

    side = lambda t: 1 + 2 * lax.rem(t, 2)
    attend_all(1, lambda t: (t, t))
    ring.near()
    for i in ring.every:
        ring.relay(i, 0)
        ring.other(i, 0)
    attend_all(2, lambda t: (t * 0, side(t)))
    for i in ring.every:
        ring.far(i)
    attend_all(2, lambda t: (side(t), t * 0))
    for i in ring.every:
        ring.relay(i, MINUS)
        ring.relay(i, PLUS)
    for i in ring.every:
        ring.other(i, MINUS)
        ring.other(i, PLUS)
    attend_all(4, lambda t: (side(t // 2), side(t)))
    for i in ring.every:
        ring.relay(i, FAR)
        ring.relayed[i, 0].wait_recv()
    attend_all(2, lambda t: (2 * t, 2 - 2 * t))
    for i in ring.every:
        ring.other(i, FAR)
        ring.relayed[i, MINUS].wait_recv()
        ring.relayed[i, PLUS].wait_recv()
    attend_all(
        4,
        lambda t: (
            2 * (t // 2) + side(t) * (1 - t // 2),
            2 * (1 - t // 2) + side(t) * (t // 2),
        ),
    )
    for i in ring.every:
        ring.relayed[i, FAR].wait_recv()
    attend_all(1, lambda t: (t + FAR, t + FAR))

    total = total_ref[0:1, :]
    inverse = 1.0 / total
    for head in range(heads_here):
        rows = pl.ds(head * HEAD_DIM, HEAD_DIM)
        wide_ref[rows, :] = acc[rows, :] * inverse[:, head * group : (head + 1) * group]
    mixed_ref[...] = wide_ref[...].T.astype(BF16)
    lse_ref[...] = jnp.broadcast_to(top_ref[0:1, :] + jnp.log(total), lse_ref.shape)
    loads[3].wait()
    part = flat_dot(mixed_ref[...], out_ref[...]).astype(BF16)
    part_ref[...] = part.reshape(part_ref.shape)
    for copy in started:
        copy.wait_send()


def attend_call(cid, layer, normed, full_qkv, full_out, biases, seg_wide, seg_column):
    group, model = normed.shape
    width = full_out.shape[2]
    heads_here = width // HEAD_DIM
    square = (RING, RING, group, width)
    return pl.pallas_call(
        functools.partial(attend_kernel, layer),
        out_shape=[
            jax.ShapeDtypeStruct((group, width), BF16),
            jax.ShapeDtypeStruct(square, BF16),
            jax.ShapeDtypeStruct(square, BF16),
            jax.ShapeDtypeStruct((group, width), BF16),
            jax.ShapeDtypeStruct((width, group), F32),
            jax.ShapeDtypeStruct((8, group * heads_here), F32),
            jax.ShapeDtypeStruct((RING, group // RING, model), BF16),
        ],
        in_specs=[vmem_spec(), any_spec(), any_spec()] + [vmem_spec()] * 3,
        out_specs=[vmem_spec()] * 7,
        scratch_shapes=[
            pltpu.VMEM((3, model, width), BF16),
            pltpu.VMEM((model, width), BF16),
            pltpu.VMEM((group * heads_here, width), BF16),
            pltpu.VMEM((width, group), F32),
            pltpu.VMEM((8, group * heads_here), F32),
            pltpu.VMEM((8, group * heads_here), F32),
            pltpu.SemaphoreType.DMA((2, 5, RING)),
            pltpu.SemaphoreType.DMA((2, 5, RING)),
            pltpu.SemaphoreType.DMA((4,)),
        ],
        compiler_params=comm_params(cid),
    )(normed, full_qkv, full_out, biases, seg_wide, seg_column)


def attend_back_kernel(
    layer, rows_ref, qkv_any, out_any, q_ref, k_ref, v_ref, wide_ref, lse_ref, seg_q_ref, seg_k_ref,
    triple_ref, sums_ref, part_ref, *scratch,
):
    (
        qkv_ref, out_ref, grad_ref, stack, plain, grad_stack, grad_plain, acc, delta_ref,
        dk_ref, dv_ref, total_ref,
    ) = scratch[:12]
    buffers = scratch[12 : 12 + 2 * SCATTER_BUFFERS]
    send, recv, local = scratch[12 + 2 * SCATTER_BUFFERS :]
    group, width = q_ref.shape
    heads_here = width // HEAD_DIM
    scale = HEAD_DIM ** (-0.5)
    load_out = pltpu.make_async_copy(out_any.at[layer], out_ref, local.at[0])
    load_qkv = pltpu.make_async_copy(qkv_any.at[layer], qkv_ref, local.at[1])
    load_out.start()
    load_qkv.start()
    rank = lax.axis_index("dp")
    y, z = rank // RING, lax.rem(rank, RING)
    barrier, count = dp_barrier(y, z, None)
    stack[...] = head_stack(q_ref[...], scale)
    plain[...] = head_stack(q_ref[...], 1.0)
    load_out.wait()
    grad_ref[...] = jnp.dot(rows_ref[...], out_ref[...], preferred_element_type=F32).astype(BF16)
    grad_stack[...] = head_stack(grad_ref[...], scale)
    grad_plain[...] = head_stack(grad_ref[...], 1.0)
    acc[...] = jnp.zeros_like(acc)
    seg_wide = jnp.concatenate([seg_q_ref[0:1, :]] * heads_here, axis=1)
    product = grad_ref[...].astype(F32).T * wide_ref[...]
    for head in range(heads_here):
        delta_ref[0:1, pl.ds(head * group, group)] = scale * jnp.sum(
            product[head * HEAD_DIM : (head + 1) * HEAD_DIM], axis=0, keepdims=True
        )
    pl.semaphore_wait(barrier, count)
    started = []
    push = pusher(send, recv, started)
    keys = Scatter(0, True, dk_ref, buffers[:SCATTER_BUFFERS], y, z, push)
    values = Scatter(1, False, dv_ref, buffers[SCATTER_BUFFERS:], y, z, push)

    def attend(offset_y, offset_z):
        at_y, at_z = step(y, offset_y), step(z, offset_z)
        key_block = k_ref[at_y, at_z]
        scores = block_scores(key_block, stack[...], seg_k_ref[at_y, at_z, :, 0:1], seg_wide)
        weights = jnp.exp(scores - lse_ref[0:1, :])
        dv_ref[at_y, at_z] = jnp.dot(
            weights.astype(BF16), grad_plain[...], preferred_element_type=F32
        ).astype(BF16)
        prob_grad = flat_dot(v_ref[at_y, at_z], grad_stack[...])
        low = (weights * (prob_grad - delta_ref[0:1, :])).astype(BF16)
        dk_ref[at_y, at_z] = jnp.dot(low, plain[...], preferred_element_type=F32).astype(BF16)
        turned = key_block.T
        for head in range(heads_here):
            rows = pl.ds(head * HEAD_DIM, HEAD_DIM)
            acc[rows, :] += jnp.dot(
                turned[head * HEAD_DIM : (head + 1) * HEAD_DIM],
                low[:, head * group : (head + 1) * group],
                preferred_element_type=F32,
            )

    def attend_all(first, count, offsets):
        def each(number, carry):
            attend(*offsets(number))
            return carry

        lax.fori_loop(first, count, each, 0)

    attend_all(0, 4, lambda t: (t * 0 + FAR, step(t, FAR)))
    for j in Scatter.ORDER:
        values.send_via(j)
    keys.send_direct(FAR)
    attend_all(1, 4, lambda t: (step(t, FAR), t * 0 + FAR))
    for j in Scatter.ORDER:
        keys.send_via(j)
    values.send_direct(FAR)
    attend_all(1, 4, lambda t: (t * 0 + PLUS, step(t, FAR)))
    keys.send_direct(PLUS)
    values.send_direct(PLUS)
    values.send_direct(MINUS)
    attend_all(1, 4, lambda t: (t * 0 + MINUS, step(t, FAR)))
    keys.send_direct(MINUS)
    values.send_direct(0)
    values.join()
    for j in (FAR, PLUS, MINUS):
        keys.join_one(j)
    attend_all(1, 4, lambda t: (t * 0, step(t, FAR)))
    keys.send_direct(0)
    keys.join_one(0)
    values.turn()
    keys.turn()
    values.join_two()
    keys.join_two()
    sums_ref[...] = jnp.zeros_like(sums_ref)
    query_grad = acc[...].T
    sums_ref[0:1, :] = jnp.sum(query_grad, axis=0, keepdims=True)
    triple_ref[0] = query_grad.astype(BF16)
    load_qkv.wait()
    part = flat_dot(triple_ref[0], qkv_ref[0])
    values.finish(total_ref)
    triple_ref[2] = total_ref[...].astype(BF16)
    sums_ref[1:2, :] = jnp.sum(total_ref[...], axis=0, keepdims=True)
    part = part + flat_dot(triple_ref[2], qkv_ref[2])
    keys.finish(total_ref)
    triple_ref[1] = total_ref[...].astype(BF16)
    part = part + flat_dot(triple_ref[1], qkv_ref[1])
    part_ref[...] = part.astype(BF16).reshape(part_ref.shape)
    for copy in started:
        copy.wait_send()


def attend_back_call(cid, layer, attn_rows, full_qkv, full_out, queries, keys, values, wide, lse, seg_wide, seg_column):
    group, model = attn_rows.shape
    width = queries.shape[1]
    heads_here = width // HEAD_DIM
    block = (group, width)
    stacked = pltpu.VMEM((group * heads_here, width), BF16)
    return pl.pallas_call(
        functools.partial(attend_back_kernel, layer),
        out_shape=[
            jax.ShapeDtypeStruct((3, group, width), BF16),
            jax.ShapeDtypeStruct((8, width), F32),
            jax.ShapeDtypeStruct((RING, group // RING, model), BF16),
        ],
        in_specs=[vmem_spec(), any_spec(), any_spec()] + [vmem_spec()] * 7,
        out_specs=[vmem_spec()] * 3,
        scratch_shapes=[
            pltpu.VMEM((3, model, width), BF16),
            pltpu.VMEM((model, width), BF16),
            pltpu.VMEM(block, BF16),
            stacked,
            stacked,
            stacked,
            stacked,
            pltpu.VMEM((width, group), F32),
            pltpu.VMEM((8, group * heads_here), F32),
            pltpu.VMEM((RING, RING) + block, BF16),
            pltpu.VMEM((RING, RING) + block, BF16),
            pltpu.VMEM(block, F32),
        ]
        + Scatter.scratch(block, BF16)
        + Scatter.scratch(block, BF16)
        + [
            pltpu.SemaphoreType.DMA((2, 6, RING)),
            pltpu.SemaphoreType.DMA((2, 6, RING)),
            pltpu.SemaphoreType.DMA((2,)),
        ],
        compiler_params=comm_params(cid),
    )(attn_rows, full_qkv, full_out, queries, keys, values, wide, lse, seg_wide, seg_column)


WEIGHT_PIECES = (
    (0, (0,), True),
    (0, (1,), False),
    (0, (2,), True),
    (1, (), False),
    (4, (), True),
    (5, (), False),
    (2, (), True),
    (3, (), False),
)


def shards(tokens, segment_ids, w_qkv, w_out, w_up, w_down, vectors, out_bias, cotangent):
    section = lax.axis_index("section")
    tensor_rank = lax.axis_index("tensor")
    own = lambda pair: jnp.where(section == 0, pair[0], pair[1])
    rows = tokens.shape[1]
    width = tokens.shape[2]
    group = rows * RING
    square = (RING, RING)
    local_width = w_qkv.shape[3]
    local_hidden = w_up.shape[2]

    depth = w_out.shape[1]
    small = jnp.pad(
        jnp.concatenate([vectors[0], out_bias], axis=0),
        ((0, 2), (0, 128 - depth)),
    )
    shape = lambda *dims: jax.ShapeDtypeStruct(dims, BF16)
    my_segments = own(segment_ids)
    seg_block = jnp.zeros((8, 128), jnp.int32).at[0, :rows].set(my_segments)
    full_qkv, full_out, full_up, full_down, full_small, full_seg = gather_call(
        0,
        WEIGHT_PIECES,
        [w_qkv[0], w_out[0], w_up[0], w_down[0], small, seg_block],
        [
            shape(2, 3, *square, depth, local_width),
            shape(2, *square, depth, local_width),
            shape(2, *square, depth, local_hidden),
            shape(2, *square, depth, local_hidden),
            shape(2, *square, 16, 128),
            jax.ShapeDtypeStruct((2,) + square + (8, 128), jnp.int32),
        ],
        True,
    )
    full_qkv = full_qkv.reshape(2, 3, width, local_width)
    full_out = full_out.reshape(2, width, local_width)
    full_up = full_up.reshape(2, width, local_hidden)
    full_down = full_down.reshape(2, width, local_hidden)
    small_rows = (
        full_small.reshape(2, RING * RING, 16, 128)[..., :depth]
        .transpose(0, 2, 1, 3)
        .reshape(2, 16, width)
        .astype(F32)
    )

    my_tokens = own(tokens)
    my_cotangent = own(cotangent)
    seg_mine = own(full_seg)[:, :, 0, :rows].reshape(8, 128)
    normed, seg_group = tensor_call(
        1, first_rows, None, [my_tokens], [small_rows[0]], [], 0, True, seg_mine
    )
    seg_all = seg_group.reshape(RING, RING * RING, rows).transpose(1, 0, 2).reshape(-1, group)
    seg_rows = lax.dynamic_index_in_dim(seg_all, lax.axis_index("dp"), 0, keepdims=False)
    seg_wide = jnp.broadcast_to(seg_rows[None], (8, group))
    seg_column = jnp.broadcast_to(seg_all.reshape(*square, group)[..., None], square + (group, 128))
    inputs = my_tokens
    kept = []
    for layer in range(2):
        vec = small_rows[layer]
        normed = normed.reshape(group, width)
        query_bias = lax.dynamic_slice_in_dim(vec[2], tensor_rank * local_width, local_width)
        value_bias = lax.dynamic_slice_in_dim(vec[3], tensor_rank * local_width, local_width)
        up_bias = lax.dynamic_slice_in_dim(
            vec[9:13].reshape(-1), tensor_rank * local_hidden, local_hidden
        )
        biases = jnp.zeros((8, local_width), F32).at[0].set(query_bias).at[1].set(value_bias)
        queries, keys_full, values_full, mixed, wide, lse, part = attend_call(
            2 + 12 * layer, layer, normed, full_qkv, full_out, biases, seg_wide, seg_column
        )
        attn_out, hidden, normed_two = tensor_call(
            3, middle_rows, part, [inputs.astype(F32)], [vec], [F32, F32], 0, True
        )
        normed_two = normed_two.reshape(group, width)
        pre_act = jnp.dot(normed_two, full_up[layer], preferred_element_type=F32) + up_bias
        activated = gelu_exact(pre_act).astype(BF16)
        part = flat_dot(activated, full_down[layer]).astype(BF16).reshape(RING, rows, width)
        step_kept = [inputs, normed, queries, keys_full, values_full, mixed, attn_out, hidden]
        step_kept += [normed_two, pre_act, activated, wide, lse]
        if layer == 0:
            mlp_first, between, normed = tensor_call(
                4, end_rows_first, part, [hidden], [vec, small_rows[1]], [F32, BF16], 0, True
            )
            inputs = between
        else:
            outputs, sums_end, mlp_rows = tensor_call(
                5, end_rows_last, part, [hidden, my_cotangent], [vec], [BF16], 2, True
            )
        kept.append(step_kept)

    upstream = my_cotangent.astype(F32)
    grads = [None, None]
    scale_two, down_bias = sums_end[0], sums_end[1]
    for layer in (1, 0):
        vec = small_rows[layer]
        inputs, normed, queries, keys_full, values_full, mixed, attn_out, hidden = kept[layer][:8]
        normed_two, pre_act, activated, wide, lse = kept[layer][8:]
        mlp_rows = mlp_rows.reshape(group, width)
        act_grad = jnp.dot(mlp_rows, full_down[layer], preferred_element_type=F32)
        grad_down = rows_dot(mlp_rows, activated)
        pre_grad = jax.vjp(gelu_exact, pre_act)[1](act_grad)[0]
        up_bias_grad = jnp.sum(pre_grad, axis=0)
        pre_low = pre_grad.astype(BF16)
        grad_up = rows_dot(normed_two, pre_low)
        part = flat_dot(pre_low, full_up[layer]).astype(BF16).reshape(RING, rows, width)
        hidden_grad, sums_middle, attn_rows = tensor_call(
            6, back_middle_rows, part, [upstream, hidden, attn_out], [vec], [F32], 4, True
        )
        attn_rows = attn_rows.reshape(group, width)
        grad_out = rows_dot(attn_rows, mixed)
        triple, sums_attend, part = attend_back_call(
            7 + 12 * layer, layer, attn_rows, full_qkv, full_out, queries, keys_full, values_full,
            wide, lse, seg_wide, seg_column,
        )
        query_bias_grad, value_bias_grad = sums_attend[0], sums_attend[1]
        grad_qkv = [rows_dot(normed, triple[which]) for which in range(3)]
        if layer == 1:
            input_grad, sums_last, mlp_rows = tensor_call(
                8,
                back_end_rows_last,
                part,
                [hidden_grad, inputs.astype(F32), mlp_first],
                [vec, small_rows[0]],
                [F32],
                4,
                True,
            )
        else:
            input_grad, sums_last = tensor_call(
                9, back_end_rows_first, part, [hidden_grad, inputs.astype(F32)], [vec], [F32], 2, False
            )

        def placed(values, length):
            empty = jnp.zeros((length,), F32)
            return lax.dynamic_update_slice(empty, values, (tensor_rank * values.shape[0],))

        vector_rows = jnp.concatenate(
            [
                sums_last[0:2],
                placed(query_bias_grad, width)[None],
                placed(value_bias_grad, width)[None],
                sums_middle[2:3],
                sums_middle[0:2],
                down_bias[None],
                scale_two[None],
                placed(up_bias_grad, local_hidden * RING).reshape(-1, width),
                sums_middle[3:4],
                jnp.zeros((2, width), F32),
            ],
            axis=0,
        )
        vector_rows = jnp.pad(
            vector_rows.reshape(16, RING * RING, depth).transpose(1, 0, 2),
            ((0, 0), (0, 0), (0, 128 - depth)),
        ).reshape(*square, 16, 128)
        grads[layer] = [vector_rows] + [
            value.astype(BF16).reshape(*square, depth, value.shape[-1])
            for value in grad_qkv + [grad_out, grad_up, grad_down]
        ]
        if layer == 1:
            last_grad = input_grad
            upstream = input_grad.astype(BF16).astype(F32)
            scale_two, down_bias = sums_last[2], sums_last[3]
    first_grad = input_grad

    stacked = [jnp.stack(pair) for pair in zip(*grads)]
    extras = [
        jnp.where(section == 0, outputs, between),
        jnp.where(section == 0, last_grad, first_grad),
    ]
    results = final_call(10, (True, True, False, True, False, True, False), stacked, extras)
    small_sum, grad_q, grad_k, grad_v, grad_out, grad_up, grad_down, came_out, came_grad = results
    mine_out = jnp.where(section == 0, between, outputs)
    mine_grad = jnp.where(section == 0, first_grad, last_grad)
    pair = lambda mine, came: jnp.where(
        section == 0, jnp.stack([mine, came]), jnp.stack([came, mine])
    )[None]
    return (
        pair(mine_out, came_out),
        pair(mine_grad, came_grad),
        jnp.stack([grad_q, grad_k, grad_v])[None],
        grad_out[None],
        grad_up[None],
        grad_down[None],
        small_sum[:13, :depth][None],
        small_sum[13:14, :depth],
    )


def solution(mesh):
    in_specs = (
        P(None, ("dp", "tensor"), None),
        P(None, ("dp", "tensor")),
        P("section", None, "dp", "tensor"),
        P("section", "dp", "tensor"),
        P("section", "dp", "tensor"),
        P("section", "dp", "tensor"),
        P("section", None, "dp"),
        P("section", "dp"),
        P(None, ("dp", "tensor"), None),
    )
    out_specs = (
        P("section", None, ("dp", "tensor"), None),
        P("section", None, ("dp", "tensor"), None),
        P("section", None, "dp", "tensor"),
        P("section", "dp", "tensor"),
        P("section", "dp", "tensor"),
        P("section", "dp", "tensor"),
        P("section", None, "dp"),
        P("section", "dp"),
    )
    return jax.shard_map(shards, mesh=mesh, in_specs=in_specs, out_specs=out_specs, check_vma=False)
```

```python
import functools

import jax
import jax.numpy as jnp
from jax import lax
from jax.experimental import pallas as pl
from jax.experimental.pallas import tpu as pltpu
from jax.sharding import PartitionSpec as P

MESH = pl.DeviceIdType.MESH
HEAD_DIM = 64
EPSILON = 1e-06
MASKED_SCORE = -1e30
RING = 4
VMEM_LIMIT = 56 * 1024 * 1024
F32 = jnp.float32
BF16 = jnp.bfloat16


def vmem_spec():
    return pl.BlockSpec(memory_space=pltpu.VMEM)


def any_spec():
    return pl.BlockSpec(memory_space=pl.ANY)


def comm_params(cid):
    return pltpu.CompilerParams(
        collective_id=cid, has_side_effects=True, vmem_limit_bytes=VMEM_LIMIT
    )


def step(coord, by):
    return lax.rem(coord + by, RING)


def layer_norm(values, gain_row, shift_row):
    centre = values - jnp.mean(values, axis=-1, keepdims=True)
    spread = jnp.mean(centre * centre, axis=-1, keepdims=True)
    return centre * lax.rsqrt(spread + EPSILON) * gain_row + shift_row


def layer_norm_back(values, gain_row, grad):
    centre = values - jnp.mean(values, axis=-1, keepdims=True)
    spread = jnp.mean(centre * centre, axis=-1, keepdims=True)
    inverse = lax.rsqrt(spread + EPSILON)
    normed = centre * inverse
    scaled = grad * gain_row
    back = inverse * (
        scaled
        - jnp.mean(scaled, axis=-1, keepdims=True)
        - normed * jnp.mean(scaled * normed, axis=-1, keepdims=True)
    )
    return back, jnp.sum(grad * normed, axis=0, keepdims=True), jnp.sum(grad, axis=0, keepdims=True)


PLUS, FAR, MINUS = 1, 2, 3
CHUNKS = 2


class Rider:
    def __init__(self, build, ins, in_specs, outs, out_specs, scratch):
        self.build, self.ins, self.in_specs = build, ins, in_specs
        self.outs, self.out_specs, self.scratch = outs, out_specs, scratch


def tensor_barrier(me):
    barrier = pltpu.get_barrier_semaphore()
    for k in range(1, RING):
        pl.semaphore_signal(
            barrier, inc=1, device_id={"tensor": step(me, k)}, device_id_type=MESH
        )
    return barrier, RING - 1


def tensor_kernel(function, n_rows, n_vecs, n_out, n_sums, reduce, gather, with_seg, rider, *refs):
    refs = list(refs)
    take = lambda count: [refs.pop(0) for _ in range(count)]
    part = take(1)[0] if reduce else None
    rows_in = take(n_rows)
    vecs = take(n_vecs)
    seg_in = take(1)[0] if with_seg else None
    rider_ins = take(len(rider.ins)) if rider else []
    rows_out = take(n_out)
    sums_out = take(1)[0] if n_sums else None
    full = take(1)[0] if gather else None
    seg_out = take(1)[0] if with_seg else None
    rider_outs = take(len(rider.outs)) if rider else []
    landing = take(1)[0] if reduce else None
    send, recv, local = take(3)

    me = lax.axis_index("tensor")
    barrier, count = tensor_barrier(me)
    stages = []
    if rider:
        rank = lax.axis_index("dp")
        y, z = rank // RING, lax.rem(rank, RING)
        section = lax.axis_index("section")
        count += dp_barrier(y, z, section)[1]
        stages = rider.build(y, z, section, rider_ins, rider_outs, refs)
    pl.semaphore_wait(barrier, count)

    chunk = rows_in[0].shape[0] // CHUNKS
    started = []

    def push(source, target, kind, index, k):
        copy = pltpu.make_async_remote_copy(
            src_ref=source,
            dst_ref=target,
            send_sem=send.at[kind, index, k - 1],
            recv_sem=recv.at[kind, index, k - 1],
            device_id={"tensor": step(me, k)},
            device_id_type=MESH,
        )
        copy.start()
        started.append(copy)
        return copy

    def ride():
        if stages:
            stages.pop(0)()

    reduces = {}
    if reduce:
        for c in range(CHUNKS):
            here = pl.ds(c * chunk, chunk)
            for k in range(1, RING):
                reduces[c, k] = push(
                    part.at[step(me, k), here], landing.at[k - 1, here], 0, c, k
                )
    last = []
    if with_seg:
        own = pltpu.make_async_copy(seg_in, seg_out.at[me], local)
        own.start()
        last += [push(seg_in, seg_out.at[me], 2, 0, k) for k in range(1, RING)]
    ride()
    sums = [None] * n_sums
    for c in range(CHUNKS):
        here = pl.ds(c * chunk, chunk)
        total = None
        if reduce:
            for k in range(1, RING):
                reduces[c, k].wait_recv()
            total = part[me, here].astype(F32)
            for k in range(1, RING):
                total = total + landing[k - 1, here].astype(F32)
        spread, outs, parts = function(
            total, [ref[here].astype(F32) for ref in rows_in], vecs
        )
        if gather:
            full[me, here] = spread.astype(BF16)
            last += [push(full.at[me, here], full.at[me, here], 1, c, k) for k in range(1, RING)]
        for ref, value in zip(rows_out, outs):
            ref[here] = value.astype(ref.dtype)
        sums = [new if old is None else old + new for old, new in zip(sums, parts)]
        ride()
    if n_sums:
        sums_out[...] = jnp.concatenate(
            sums + [jnp.zeros((8 - n_sums, sums[0].shape[1]), F32)], axis=0
        )
    while stages:
        ride()
    for copy in last:
        copy.wait_recv()
    if with_seg:
        own.wait()
    for copy in started:
        copy.wait_send()


def tensor_call(cid, function, part, rows, vecs, outs, n_sums, gather, seg=None, rider=None):
    height, width = rows[0].shape
    reduce = part is not None
    with_seg = seg is not None
    args = ([part] if reduce else []) + list(rows) + list(vecs) + ([seg] if with_seg else [])
    shapes = [jax.ShapeDtypeStruct((height, width), dtype) for dtype in outs]
    if n_sums:
        shapes.append(jax.ShapeDtypeStruct((8, width), F32))
    if gather:
        shapes.append(jax.ShapeDtypeStruct((RING, height, width), BF16))
    if with_seg:
        shapes.append(jax.ShapeDtypeStruct((RING,) + seg.shape, seg.dtype))
    in_specs, out_specs = [vmem_spec()] * len(args), [vmem_spec()] * len(shapes)
    scratch = [pltpu.VMEM((RING - 1, height, width), BF16)] if reduce else []
    scratch += [
        pltpu.SemaphoreType.DMA((3, CHUNKS, RING - 1)),
        pltpu.SemaphoreType.DMA((3, CHUNKS, RING - 1)),
        pltpu.SemaphoreType.DMA,
    ]
    if rider:
        args, in_specs = args + rider.ins, in_specs + rider.in_specs
        shapes, out_specs = shapes + rider.outs, out_specs + rider.out_specs
        scratch = scratch + rider.scratch
    return pl.pallas_call(
        functools.partial(
            tensor_kernel, function, len(rows), len(vecs), len(outs), n_sums, reduce, gather, with_seg,
            rider,
        ),
        out_shape=shapes,
        in_specs=in_specs,
        out_specs=out_specs,
        scratch_shapes=scratch,
        compiler_params=comm_params(cid),
    )(*args)


def row(ref, index):
    return ref[pl.ds(index, 1), :]


def first_rows(total, rows, vecs):
    return layer_norm(rows[0], row(vecs[0], 0), row(vecs[0], 1)), [], []


def middle_rows(total, rows, vecs):
    vec = vecs[0]
    attn_out = total + row(vec, 13)
    hidden = rows[0] + row(vec, 4) * attn_out
    return layer_norm(hidden, row(vec, 5), row(vec, 6)), [attn_out, hidden], []


def end_rows_first(total, rows, vecs):
    vec, after = vecs
    mlp_out = total + row(vec, 7)
    outputs = (rows[0] + row(vec, 8) * mlp_out).astype(BF16)
    inputs = outputs.astype(F32)
    return layer_norm(inputs, row(after, 0), row(after, 1)), [mlp_out, outputs], []


def end_rows_last(total, rows, vecs):
    vec = vecs[0]
    hidden, upstream = rows
    mlp_out = total + row(vec, 7)
    outputs = hidden + row(vec, 8) * mlp_out
    mlp_grad = row(vec, 8) * upstream
    sums = [
        jnp.sum(upstream * mlp_out, axis=0, keepdims=True),
        jnp.sum(mlp_grad, axis=0, keepdims=True),
    ]
    return mlp_grad, [outputs], sums


def back_middle_rows(total, rows, vecs):
    vec = vecs[0]
    upstream, hidden, attn_out = rows
    part, gain, shift = layer_norm_back(hidden, row(vec, 5), total)
    hidden_grad = upstream + part
    attn_grad = row(vec, 4) * hidden_grad
    sums = [
        gain,
        shift,
        jnp.sum(hidden_grad * attn_out, axis=0, keepdims=True),
        jnp.sum(attn_grad, axis=0, keepdims=True),
    ]
    return attn_grad, [hidden_grad], sums


def back_end_rows_last(total, rows, vecs):
    vec, before = vecs
    hidden_grad, inputs, mlp_out = rows
    part, gain, shift = layer_norm_back(inputs, row(vec, 0), total)
    input_grad = hidden_grad + part
    upstream = input_grad.astype(BF16).astype(F32)
    mlp_grad = row(before, 8) * upstream
    sums = [
        gain,
        shift,
        jnp.sum(upstream * mlp_out, axis=0, keepdims=True),
        jnp.sum(mlp_grad, axis=0, keepdims=True),
    ]
    return mlp_grad, [input_grad], sums


def back_end_rows_first(total, rows, vecs):
    hidden_grad, inputs = rows
    part, gain, shift = layer_norm_back(inputs, row(vecs[0], 0), total)
    return None, [hidden_grad + part], [gain, shift]


def dp_neighbour(y, z, along_z, k):
    if along_z:
        return {"dp": y * RING + step(z, k)}
    return {"dp": step(y, k) * RING + z}


def dp_barrier(y, z, section):
    barrier = pltpu.get_barrier_semaphore()
    count = 0
    for along_z in (True, False):
        for k in (PLUS, MINUS):
            pl.semaphore_signal(
                barrier, inc=1, device_id=dp_neighbour(y, z, along_z, k), device_id_type=MESH
            )
            count += 1
    if section is not None:
        pl.semaphore_signal(
            barrier, inc=1, device_id={"section": 1 - section}, device_id_type=MESH
        )
        count += 1
    return barrier, count


def pusher(send, recv, started):
    def push(index, kind, k, source, target, device):
        copy = pltpu.make_async_remote_copy(
            src_ref=source,
            dst_ref=target,
            send_sem=send.at[index, kind, k],
            recv_sem=recv.at[index, kind, k],
            device_id=device,
            device_id_type=MESH,
        )
        copy.start()
        started.append(copy)
        return copy

    return push


class Gather:
    WAYS = {0: 1, 3: 1, 1: 1, 2: 3}

    def __init__(self, pieces, outs, y, z, lead, push):
        self.pieces, self.outs, self.y, self.z = pieces, outs, y, z
        self.lead, self.push = lead, push
        self.every = range(len(pieces))
        self.first, self.onward, self.second, self.relayed = {}, {}, {}, {}

    def block(self, i, along, across, rows=None):
        number, pre, along_z = self.pieces[i]
        ys, zs = (across, along) if along_z else (along, across)
        ys = ys if isinstance(ys, slice) else step(self.y, ys) if ys else self.y
        zs = zs if isinstance(zs, slice) else step(self.z, zs) if zs else self.z
        return self.outs[number].at[self.lead + pre + (ys, zs) + (() if rows is None else (rows,))]

    def way(self, i, first, k):
        return dp_neighbour(self.y, self.z, self.pieces[i][2] == first, k)

    def halves(self, i):
        height = self.outs[self.pieces[i][0]].shape[-2]
        if height < 32:
            return {PLUS: None}
        return {PLUS: pl.ds(0, height // 2), MINUS: pl.ds(height // 2, height // 2)}

    def spread(self, i, offset, source):
        for k in (PLUS, MINUS):
            self.second[i, offset, k] = self.push(
                i, 2 if k == PLUS else 3, offset, source, self.block(i, offset, 0), self.way(i, False, k)
            )

    def begin(self, i, source):
        for k in (PLUS, MINUS):
            self.first[i, k] = self.push(i, 0, k, source, self.block(i, 0, 0), self.way(i, True, k))
        self.spread(i, 0, source)

    def near(self):
        for i in self.every:
            split = self.halves(i)
            for k in (PLUS, MINUS):
                self.first[i, k].wait_recv()
                came = RING - k
                if k in split:
                    self.onward[i, k] = self.push(
                        i, 1, k, self.block(i, came, 0, split[k]), self.block(i, came, 0, split[k]),
                        self.way(i, True, k),
                    )
                self.spread(i, came, self.block(i, came, 0))

    def relay(self, i, offset):
        k = self.WAYS[offset]
        self.second[i, offset, k].wait_recv()
        came = self.block(i, offset, RING - k)
        self.relayed[i, offset] = self.push(i, 4, offset, came, came, self.way(i, False, k))

    def other(self, i, offset):
        self.second[i, offset, RING - self.WAYS[offset]].wait_recv()

    def far(self, i):
        for k in self.halves(i):
            self.onward[i, k].wait_recv()
        self.spread(i, FAR, self.block(i, FAR, 0))


def half_of(section, height):
    return pl.ds(pl.multiple_of(section * height, height), height)


def spread_stages(ring, sources, local, section, push):
    own, across = {}, []

    def pass_on(i, line):
        came = ring.block(i, slice(None), line)
        across.append(push(i, 5, line, came, came, {"section": 1 - section}))

    def begin():
        for i in ring.every:
            ring.begin(i, sources[i])
            own[i] = pltpu.make_async_copy(sources[i], ring.block(i, 0, 0), local.at[i])
            own[i].start()

    def near():
        ring.near()
        for i in ring.every:
            ring.relay(i, 0)

    def middle():
        for i in ring.every:
            ring.far(i)
        for i in ring.every:
            ring.relay(i, MINUS)
            ring.relay(i, PLUS)
            own[i].wait()
            pass_on(i, 0)

    def end():
        for i in ring.every:
            ring.relay(i, FAR)
            for offset in range(RING):
                ring.other(i, offset)
            pass_on(i, PLUS)
            pass_on(i, MINUS)
        for i in ring.every:
            for offset in range(RING):
                ring.relayed[i, offset].wait_recv()
            pass_on(i, FAR)
        for copy in across:
            copy.wait_recv()

    return [begin, near, middle, end]


def out_views(ref, rows):
    if len(ref.shape) == 5:
        return [ref.at[which, :, :, rows] for which in range(ref.shape[0])]
    return [ref.at[:, :, rows]]


def in_views(ref):
    if len(ref.shape) == 3:
        return [ref.at[which] for which in range(ref.shape[0])]
    return [ref]


def weight_pieces(count):
    return tuple((i, (), i % 2 == 0) for i in range(count))


def weight_rider(halves):
    count = sum(3 if value.ndim == 3 else 1 for value in halves)
    height = halves[0].shape[-2]

    def build(y, z, section, ins, outs, scratch):
        send, recv, local = scratch
        started = []
        push = pusher(send, recv, started)
        rows = half_of(section, height)
        views = [view for ref in outs for view in out_views(ref, rows)]
        sources = [view for ref in ins for view in in_views(ref)]
        ring = Gather(weight_pieces(count), views, y, z, (), push)

        def finish():
            for copy in started:
                copy.wait_send()

        return spread_stages(ring, sources, local, section, push) + [finish]

    outs = [
        jax.ShapeDtypeStruct(
            value.shape[:-2] + (RING, RING, 2 * height, value.shape[-1]), value.dtype
        )
        for value in halves
    ]
    return Rider(
        build,
        list(halves),
        [vmem_spec()] * len(halves),
        outs,
        [any_spec()] * len(outs),
        [
            pltpu.SemaphoreType.DMA((count, 6, RING)),
            pltpu.SemaphoreType.DMA((count, 6, RING)),
            pltpu.SemaphoreType.DMA((count,)),
        ],
    )


def first_kernel(
    qkv_in, out_in, up_in, down_in, small_in, seg_in,
    qkv_half, out_half, up_half, down_half, qkv_out, out_out, rows_out, seg_out,
    small_all, send, recv, local, swap_send, swap_recv, swap_local,
):
    rank = lax.axis_index("dp")
    y, z = rank // RING, lax.rem(rank, RING)
    section = lax.axis_index("section")
    barrier, count = dp_barrier(y, z, section)
    height = out_half.shape[-2]
    mine, other = half_of(section, height), half_of(1 - section, height)
    lead = lambda ref: (slice(None),) * (len(ref.shape) - 2)
    pl.semaphore_wait(barrier, count)
    started, swaps = [], []
    for i, (source, target) in enumerate(
        ((qkv_in, qkv_half), (out_in, out_half), (up_in, up_half), (down_in, down_half))
    ):
        copy = pltpu.make_async_remote_copy(
            src_ref=source.at[lead(source) + (other,)],
            dst_ref=target.at[section],
            send_sem=swap_send.at[i],
            recv_sem=swap_recv.at[i],
            device_id={"section": 1 - section},
            device_id_type=MESH,
        )
        copy.start()
        started.append(copy)
        kept = pltpu.make_async_copy(
            source.at[lead(source) + (mine,)], target.at[section], swap_local.at[i]
        )
        kept.start()
        swaps.append((copy, kept))
    push = pusher(send, recv, started)
    views = [small_all.at[section], seg_out.at[section]]
    views += [qkv_out.at[which, :, :, mine] for which in range(3)] + [out_out.at[:, :, mine]]
    sources = [small_in, seg_in]
    sources += [qkv_half.at[0, which] for which in range(3)] + [out_half.at[0]]
    ring = Gather(weight_pieces(6), views, y, z, (), push)
    stages = spread_stages(ring, sources, local, section, push)
    for copy, kept in swaps[:2]:
        copy.wait_recv()
        kept.wait()
    for stage in stages:
        stage()
    depth = rows_out.shape[-1] // (RING * RING)
    for layer in range(2):
        for number in range(RING * RING):
            block = small_all[layer, number // RING, number % RING]
            rows_out[layer, :, number * depth : (number + 1) * depth] = block[:, :depth].astype(F32)
    for copy, kept in swaps[2:]:
        copy.wait_recv()
        kept.wait()
    for copy in started:
        copy.wait_send()


def first_call(cid, w_qkv, w_out, w_up, w_down, small, seg):
    depth, width = w_out.shape
    hidden = w_up.shape[1]
    half = depth // 2
    shape = lambda *dims: jax.ShapeDtypeStruct(dims, BF16)
    return pl.pallas_call(
        first_kernel,
        out_shape=[
            shape(2, 3, half, width),
            shape(2, half, width),
            shape(2, half, hidden),
            shape(2, half, hidden),
            shape(3, RING, RING, depth, width),
            shape(RING, RING, depth, width),
            jax.ShapeDtypeStruct((2, 16, RING * RING * depth), F32),
            jax.ShapeDtypeStruct((2, RING, RING) + seg.shape, seg.dtype),
        ],
        in_specs=[vmem_spec()] * 6,
        out_specs=[vmem_spec()] * 4 + [any_spec()] * 2 + [vmem_spec()] * 2,
        scratch_shapes=[
            pltpu.VMEM((2, RING, RING) + small.shape, BF16),
            pltpu.SemaphoreType.DMA((6, 6, RING)),
            pltpu.SemaphoreType.DMA((6, 6, RING)),
            pltpu.SemaphoreType.DMA((6,)),
            pltpu.SemaphoreType.DMA((4,)),
            pltpu.SemaphoreType.DMA((4,)),
            pltpu.SemaphoreType.DMA((4,)),
        ],
        compiler_params=comm_params(cid),
    )(w_qkv, w_out, w_up, w_down, small, seg)


class Scatter:
    ORDER = (FAR, PLUS, MINUS, 0)
    WAYS = {FAR: PLUS, 0: PLUS, PLUS: MINUS, MINUS: MINUS}

    def __init__(self, index, along_z, source, buffers, y, z, push):
        self.index, self.along_z, self.source = index, along_z, source
        self.passing, self.joined, self.summed, self.straight, self.middle = buffers[:5]
        self.far_two, self.joined_two, self.summed_two, self.straight_two = buffers[5:]
        self.y, self.z, self.push = y, z, push
        self.height, self.width = source.shape[-2:]
        self.via, self.direct, self.after = {}, {}, {}

    def at(self, along, across):
        ys, zs = (across, along) if self.along_z else (along, across)
        return step(self.y, ys), step(self.z, zs)

    def way(self, first, k):
        return dp_neighbour(self.y, self.z, self.along_z == first, k)

    def add(self, target, terms, top=0, height=None):
        height = self.height if height is None else height
        size = max(8, min(height, 32768 // self.width))

        def part(here):
            value = terms[0](here).astype(F32)
            for term in terms[1:]:
                value = value + term(here).astype(F32)
            target[here] = value.astype(target.dtype)

        if height <= size:
            part(pl.ds(top, height))
            return

        def each(number, carry):
            part(pl.ds(pl.multiple_of(top + number * size, size), size))
            return carry

        lax.fori_loop(0, height // size, each, 0)

    def send_via(self, j):
        self.via[j] = self.push(
            self.index, 0, j, self.source.at[self.at(FAR, j)], self.passing.at[j],
            self.way(True, self.WAYS[j]),
        )

    def send_direct(self, j):
        k = RING - self.WAYS[j]
        self.direct[j] = self.push(
            self.index, 1, j, self.source.at[self.at(k, j)], self.straight.at[j], self.way(True, k)
        )

    def begin(self):
        for j in self.ORDER:
            self.send_via(j)
        for j in self.ORDER:
            self.send_direct(j)

    def join_one(self, j):
        self.via[j].wait_recv()
        k = self.WAYS[j]
        at_y, at_z = self.at(k, j)
        self.add(
            self.joined.at[j],
            [lambda h: self.source[at_y, at_z, h], lambda h: self.passing[j, h]],
        )
        self.after[j] = self.push(
            self.index, 2, j, self.joined.at[j], self.summed.at[j], self.way(True, k)
        )

    def join(self):
        for j in self.ORDER:
            self.join_one(j)

    def turn(self):
        half = self.height // 2
        low, high = pl.ds(0, half), pl.ds(half, half)
        send = lambda kind, slot, source, target, k: self.push(
            self.index, kind, slot, source, target, self.way(False, k)
        )
        for j in self.ORDER:
            self.direct[j].wait_recv()
            self.after[j].wait_recv()
            at_y, at_z = self.at(0, j)
            self.add(
                self.middle.at[j],
                [
                    lambda h: self.source[at_y, at_z, h],
                    lambda h: self.summed[j, h],
                    lambda h: self.straight[j, h],
                ],
            )
            if j == FAR:
                self.via_two = [
                    send(3, 0, self.middle.at[j, low], self.far_two.at[low], PLUS),
                    send(3, 1, self.middle.at[j, high], self.far_two.at[high], MINUS),
                ]
            if j == PLUS:
                high_copy = send(4, 1, self.middle.at[j, high], self.straight_two.at[high], PLUS)
            if j == MINUS:
                low_copy = send(4, 0, self.middle.at[j, low], self.straight_two.at[low], MINUS)
        self.direct_two = [low_copy, high_copy]

    def join_two(self):
        half = self.height // 2
        self.after_two = []
        for number, (top, k) in enumerate(((0, PLUS), (half, MINUS))):
            self.via_two[number].wait_recv()
            self.add(
                self.joined_two,
                [lambda h: self.middle[k, h], lambda h: self.far_two[h]],
                top,
                half,
            )
            here = pl.ds(top, half)
            self.after_two.append(
                self.push(
                    self.index, 5, number, self.joined_two.at[here], self.summed_two.at[here],
                    self.way(False, k),
                )
            )

    def finish(self, out):
        for copy in self.direct_two + self.after_two:
            copy.wait_recv()
        self.add(
            out,
            [
                lambda h: self.middle[0, h],
                lambda h: self.summed_two[h],
                lambda h: self.straight_two[h],
            ],
        )

    @staticmethod
    def scratch(block, dtype):
        return [pltpu.VMEM((RING,) + block, dtype)] * 5 + [pltpu.VMEM(block, dtype)] * 4


SCATTER_BUFFERS = 9


def gradient_scratch(values):
    scratch = []
    for value in values:
        block = (value.shape[2] // 2, value.shape[3])
        square = pltpu.VMEM((RING, RING) + block, value.dtype)
        scratch += [square, square] + Scatter.scratch(block, value.dtype)
    return scratch + [
        pltpu.SemaphoreType.DMA((len(values), 8, RING)),
        pltpu.SemaphoreType.DMA((len(values), 8, RING)),
    ]


def gradient_stages(y, z, section, ins, outs, scratch, shared):
    count = len(ins)
    size = 2 + SCATTER_BUFFERS
    send, recv = scratch[count * size :]
    started = []
    push = pusher(send, recv, started)
    other = {"section": 1 - section}
    siblings = [scratch[i * size] for i in range(count)]
    owns = [scratch[i * size + 1] for i in range(count)]
    parts = [
        Scatter(
            i, i % 2 == 0, owns[i], scratch[i * size + 2 : (i + 1) * size], y, z, push
        )
        for i in range(count)
    ]
    across, results = [], []

    def swap():
        for i in range(count):
            height = owns[i].shape[2]
            across.append(
                push(i, 6, 0, ins[i].at[:, :, half_of(1 - section, height)], siblings[i], other)
            )

    def begin():
        for i in range(count):
            across[i].wait_recv()
            mine = half_of(section, owns[i].shape[2])

            def add(number, carry):
                at_y, at_z = number // RING, lax.rem(number, RING)
                owns[i][at_y, at_z] = (
                    ins[i][at_y, at_z, mine].astype(F32) + siblings[i][at_y, at_z].astype(F32)
                ).astype(owns[i].dtype)
                return carry

            lax.fori_loop(0, RING * RING, add, 0)
            parts[i].begin()

    def join():
        for part in parts:
            part.join()

    def turn():
        for part in parts:
            part.turn()

    def join_two():
        for part in parts:
            part.join_two()

    def finish():
        for i in range(count):
            height = owns[i].shape[2]
            if shared[i]:
                mine = outs[i].at[half_of(section, height)]
                parts[i].finish(mine)
                results.append(push(i, 7, 0, mine, mine, other))
            else:
                parts[i].finish(outs[i])

    def end():
        for copy in results:
            copy.wait_recv()
        for copy in started:
            copy.wait_send()

    return [swap, begin, join, turn, join_two, finish, end]


def gradient_rider(values):
    def build(y, z, section, ins, outs, scratch):
        return gradient_stages(y, z, section, ins, outs, scratch, [True] * len(ins))

    return Rider(
        build,
        list(values),
        [vmem_spec()] * len(values),
        [jax.ShapeDtypeStruct(value.shape[2:], F32) for value in values],
        [vmem_spec()] * len(values),
        gradient_scratch(values),
    )


def final_kernel(n_extra, n_grad, *refs):
    refs = list(refs)
    take = lambda count: [refs.pop(0) for _ in range(count)]
    sums = [take(5), take(5)]
    ins, extras = take(n_grad), take(n_extra)
    small_out = take(1)[0]
    outs, extra_outs = take(n_grad), take(n_extra)
    small_in, small_rows, vector_own, vector_parts = take(4)
    vector_send, vector_recv, extra_send, extra_recv = take(4)
    rank = lax.axis_index("dp")
    y, z = rank // RING, lax.rem(rank, RING)
    section = lax.axis_index("section")
    me = lax.axis_index("tensor")
    barrier, count = tensor_barrier(me)
    count += dp_barrier(y, z, section)[1]
    small_rows[...] = jnp.zeros_like(small_rows)
    width = small_rows.shape[1]
    for layer in range(2):
        first, middle, end, attend, up = sums[layer]
        top = 16 * layer
        part = attend.shape[1]
        lanes = pl.ds(pl.multiple_of(me * part, part), part)
        small_rows[top : top + 2, :] = first[0:2, :]
        small_rows[top + 2 : top + 3, lanes] = attend[0:1, :]
        small_rows[top + 3 : top + 4, lanes] = attend[1:2, :]
        small_rows[top + 4 : top + 5, :] = middle[2:3, :]
        small_rows[top + 5 : top + 7, :] = middle[0:2, :]
        small_rows[top + 7 : top + 8, :] = end[1:2, :]
        small_rows[top + 8 : top + 9, :] = end[0:1, :]
        for rank_of in range(RING):
            small_rows[top + 9 + rank_of : top + 10 + rank_of, :] = jnp.where(
                me == rank_of, up[0:1, :], 0.0
            )
        small_rows[top + 13 : top + 14, :] = middle[3:4, :]
    small_in[...] = jnp.zeros_like(small_in)
    depth = width // (RING * RING)
    for number in range(RING * RING):
        small_in[number // RING, number % RING, :, 0:depth] = small_rows[
            :, number * depth : (number + 1) * depth
        ]
    pl.semaphore_wait(barrier, count)
    stages = gradient_stages(
        y, z, section, [small_in] + ins, [vector_own] + outs, refs, [False] + [True] * n_grad
    )
    stages[0]()
    extra_copies = []
    for i in range(n_extra):
        copy = pltpu.make_async_remote_copy(
            src_ref=extras[i],
            dst_ref=extra_outs[i],
            send_sem=extra_send.at[i],
            recv_sem=extra_recv.at[i],
            device_id={"section": 1 - section},
            device_id_type=MESH,
        )
        copy.start()
        extra_copies.append(copy)
    for stage in stages[1:6]:
        stage()
    vector_parts[me] = vector_own[...]
    vector_copies = []
    for k in range(1, RING):
        copy = pltpu.make_async_remote_copy(
            src_ref=vector_own,
            dst_ref=vector_parts.at[me],
            send_sem=vector_send.at[k],
            recv_sem=vector_recv.at[k],
            device_id={"tensor": step(me, k)},
            device_id_type=MESH,
        )
        copy.start()
        vector_copies.append(copy)
    stages[6]()
    for copy in vector_copies:
        copy.wait()
    total = vector_parts[0]
    for k in range(1, RING):
        total = total + vector_parts[k]
    small_out[...] = total
    for copy in extra_copies:
        copy.wait()


def final_call(cid, sums, grads, extras):
    extra = len(extras)
    width = sums[0].shape[1]
    small = jax.ShapeDtypeStruct((RING, RING, 32, 128), F32)
    args = list(sums) + list(grads) + list(extras)
    return pl.pallas_call(
        functools.partial(final_kernel, extra, len(grads)),
        out_shape=[jax.ShapeDtypeStruct((16, 128), F32)]
        + [jax.ShapeDtypeStruct(value.shape[2:], F32) for value in grads]
        + [jax.ShapeDtypeStruct(value.shape, value.dtype) for value in extras],
        in_specs=[vmem_spec()] * len(args),
        out_specs=[vmem_spec()] * (1 + len(grads) + extra),
        scratch_shapes=[
            pltpu.VMEM(small.shape, F32),
            pltpu.VMEM((32, width), F32),
            pltpu.VMEM((16, 128), F32),
            pltpu.VMEM((RING, 16, 128), F32),
            pltpu.SemaphoreType.DMA((RING,)),
            pltpu.SemaphoreType.DMA((RING,)),
            pltpu.SemaphoreType.DMA((extra,)),
            pltpu.SemaphoreType.DMA((extra,)),
        ]
        + gradient_scratch([small] + list(grads)),
        compiler_params=comm_params(cid),
    )(*args)


def gelu_exact(values):
    return jax.nn.gelu(values, approximate=False)


def flat_dot(former, latter):
    return lax.dot_general(former, latter, (((1,), (1,)), ((), ())), preferred_element_type=F32)


def rows_dot(former, latter):
    return lax.dot_general(former, latter, (((0,), (0,)), ((), ())), preferred_element_type=F32)


def head_stack(values, scale):
    column = lax.broadcasted_iota(jnp.int32, values.shape, 1) // HEAD_DIM
    heads_here = values.shape[1] // HEAD_DIM
    zero = jnp.zeros_like(values)
    scaled = values * jnp.asarray(scale, values.dtype)
    return jnp.concatenate(
        [jnp.where(column == head, scaled, zero) for head in range(heads_here)], axis=0
    )


def block_scores(key_block, stack, seg_column, seg_wide):
    scores = flat_dot(key_block, stack)
    return jnp.where(seg_column == seg_wide, scores, MASKED_SCORE)


def attend_kernel(
    normed_ref, qkv_any, out_any, bias_ref, seg_q_ref, seg_k_ref,
    q_ref, k_ref, v_ref, mixed_ref, wide_ref, lse_ref, part_ref,
    qkv_ref, out_ref, stack, acc, top_ref, total_ref, send, recv, local,
):
    group, width = q_ref.shape
    heads_here = width // HEAD_DIM
    loads = [
        pltpu.make_async_copy(qkv_any.at[which], qkv_ref.at[which], local.at[which])
        for which in range(3)
    ]
    loads.append(pltpu.make_async_copy(out_any, out_ref, local.at[3]))
    for which in (1, 2, 0, 3):
        loads[which].start()
    rank = lax.axis_index("dp")
    y, z = rank // RING, lax.rem(rank, RING)
    barrier, count = dp_barrier(y, z, None)
    normed = normed_ref[...]
    loads[1].wait()
    k_ref[y, z] = jnp.dot(normed, qkv_ref[1], preferred_element_type=F32).astype(BF16)
    pl.semaphore_wait(barrier, count)
    started = []
    ring = Gather(((0, (), True), (1, (), False)), (k_ref, v_ref), y, z, (), pusher(send, recv, started))
    ring.begin(0, k_ref.at[y, z])
    loads[2].wait()
    v_ref[y, z] = (
        jnp.dot(normed, qkv_ref[2], preferred_element_type=F32) + bias_ref[1:2, :]
    ).astype(BF16)
    ring.begin(1, v_ref.at[y, z])
    loads[0].wait()
    q_ref[...] = (
        jnp.dot(normed, qkv_ref[0], preferred_element_type=F32) + bias_ref[0:1, :]
    ).astype(BF16)
    stack[...] = head_stack(q_ref[...], HEAD_DIM ** (-0.5))
    acc[...] = jnp.zeros_like(acc)
    top_ref[...] = jnp.full_like(top_ref, MASKED_SCORE)
    total_ref[...] = jnp.zeros_like(total_ref)
    seg_wide = jnp.concatenate([seg_q_ref[0:1, :]] * heads_here, axis=1)

    def attend(offset_y, offset_z):
        at_y, at_z = step(y, offset_y), step(z, offset_z)
        highest = top_ref[0:1, :]
        scores = block_scores(
            k_ref[at_y, at_z], stack[...], seg_k_ref[at_y, at_z, :, 0:1], seg_wide
        )
        above = jnp.maximum(highest, jnp.max(scores, axis=0, keepdims=True))
        weights = jnp.exp(scores - above)
        fade = jnp.exp(highest - above)
        total_ref[0:1, :] = total_ref[0:1, :] * fade + jnp.sum(weights, axis=0, keepdims=True)
        top_ref[0:1, :] = above
        low = weights.astype(BF16)
        turned = v_ref[at_y, at_z].T
        for head in range(heads_here):
            rows = pl.ds(head * HEAD_DIM, HEAD_DIM)
            lanes = slice(head * group, (head + 1) * group)
            term = jnp.dot(
                turned[head * HEAD_DIM : (head + 1) * HEAD_DIM], low[:, lanes],
                preferred_element_type=F32,
            )
            acc[rows, :] = acc[rows, :] * fade[:, lanes] + term

    def attend_all(count, offsets):
        def each(number, carry):
            attend(*offsets(number))
            return carry

        lax.fori_loop(0, count, each, 0)

    side = lambda t: 1 + 2 * lax.rem(t, 2)
    attend_all(1, lambda t: (t, t))
    ring.near()
    for i in ring.every:
        ring.relay(i, 0)
        ring.other(i, 0)
    attend_all(2, lambda t: (t * 0, side(t)))
    for i in ring.every:
        ring.far(i)
    attend_all(2, lambda t: (side(t), t * 0))
    for i in ring.every:
        ring.relay(i, MINUS)
        ring.relay(i, PLUS)
    for i in ring.every:
        ring.other(i, MINUS)
        ring.other(i, PLUS)
    attend_all(4, lambda t: (side(t // 2), side(t)))
    for i in ring.every:
        ring.relay(i, FAR)
        ring.relayed[i, 0].wait_recv()
    attend_all(2, lambda t: (2 * t, 2 - 2 * t))
    for i in ring.every:
        ring.other(i, FAR)
        ring.relayed[i, MINUS].wait_recv()
        ring.relayed[i, PLUS].wait_recv()
    attend_all(
        4,
        lambda t: (
            2 * (t // 2) + side(t) * (1 - t // 2),
            2 * (1 - t // 2) + side(t) * (t // 2),
        ),
    )
    for i in ring.every:
        ring.relayed[i, FAR].wait_recv()
    attend_all(1, lambda t: (t + FAR, t + FAR))

    total = total_ref[0:1, :]
    inverse = 1.0 / total
    for head in range(heads_here):
        rows = pl.ds(head * HEAD_DIM, HEAD_DIM)
        wide_ref[rows, :] = acc[rows, :] * inverse[:, head * group : (head + 1) * group]
    mixed_ref[...] = wide_ref[...].T.astype(BF16)
    lse_ref[...] = jnp.broadcast_to(top_ref[0:1, :] + jnp.log(total), lse_ref.shape)
    loads[3].wait()
    part = flat_dot(mixed_ref[...], out_ref[...]).astype(BF16)
    part_ref[...] = part.reshape(part_ref.shape)
    for copy in started:
        copy.wait_send()


def attend_call(cid, normed, full_qkv, full_out, biases, seg_wide, seg_column):
    group, model = normed.shape
    width = full_out.shape[1]
    heads_here = width // HEAD_DIM
    square = (RING, RING, group, width)
    return pl.pallas_call(
        attend_kernel,
        out_shape=[
            jax.ShapeDtypeStruct((group, width), BF16),
            jax.ShapeDtypeStruct(square, BF16),
            jax.ShapeDtypeStruct(square, BF16),
            jax.ShapeDtypeStruct((group, width), BF16),
            jax.ShapeDtypeStruct((width, group), F32),
            jax.ShapeDtypeStruct((8, group * heads_here), F32),
            jax.ShapeDtypeStruct((RING, group // RING, model), BF16),
        ],
        in_specs=[vmem_spec(), any_spec(), any_spec()] + [vmem_spec()] * 3,
        out_specs=[vmem_spec()] * 7,
        scratch_shapes=[
            pltpu.VMEM((3, model, width), BF16),
            pltpu.VMEM((model, width), BF16),
            pltpu.VMEM((group * heads_here, width), BF16),
            pltpu.VMEM((width, group), F32),
            pltpu.VMEM((8, group * heads_here), F32),
            pltpu.VMEM((8, group * heads_here), F32),
            pltpu.SemaphoreType.DMA((2, 5, RING)),
            pltpu.SemaphoreType.DMA((2, 5, RING)),
            pltpu.SemaphoreType.DMA((4,)),
        ],
        compiler_params=comm_params(cid),
    )(normed, full_qkv, full_out, biases, seg_wide, seg_column)


def attend_back_kernel(
    rows_ref, qkv_any, out_any, q_ref, k_ref, v_ref, wide_ref, lse_ref, seg_q_ref, seg_k_ref,
    triple_ref, sums_ref, part_ref, *scratch,
):
    (
        qkv_ref, out_ref, grad_ref, stack, plain, grad_stack, grad_plain, acc, delta_ref,
        dk_ref, dv_ref, total_ref,
    ) = scratch[:12]
    buffers = scratch[12 : 12 + 2 * SCATTER_BUFFERS]
    send, recv, local = scratch[12 + 2 * SCATTER_BUFFERS :]
    group, width = q_ref.shape
    heads_here = width // HEAD_DIM
    scale = HEAD_DIM ** (-0.5)
    load_out = pltpu.make_async_copy(out_any, out_ref, local.at[0])
    load_qkv = pltpu.make_async_copy(qkv_any, qkv_ref, local.at[1])
    load_out.start()
    load_qkv.start()
    rank = lax.axis_index("dp")
    y, z = rank // RING, lax.rem(rank, RING)
    barrier, count = dp_barrier(y, z, None)
    stack[...] = head_stack(q_ref[...], scale)
    plain[...] = head_stack(q_ref[...], 1.0)
    load_out.wait()
    grad_ref[...] = jnp.dot(rows_ref[...], out_ref[...], preferred_element_type=F32).astype(BF16)
    grad_stack[...] = head_stack(grad_ref[...], scale)
    grad_plain[...] = head_stack(grad_ref[...], 1.0)
    acc[...] = jnp.zeros_like(acc)
    seg_wide = jnp.concatenate([seg_q_ref[0:1, :]] * heads_here, axis=1)
    product = grad_ref[...].astype(F32).T * wide_ref[...]
    for head in range(heads_here):
        delta_ref[0:1, pl.ds(head * group, group)] = scale * jnp.sum(
            product[head * HEAD_DIM : (head + 1) * HEAD_DIM], axis=0, keepdims=True
        )
    pl.semaphore_wait(barrier, count)
    started = []
    push = pusher(send, recv, started)
    keys = Scatter(0, True, dk_ref, buffers[:SCATTER_BUFFERS], y, z, push)
    values = Scatter(1, False, dv_ref, buffers[SCATTER_BUFFERS:], y, z, push)

    def attend(offset_y, offset_z):
        at_y, at_z = step(y, offset_y), step(z, offset_z)
        key_block = k_ref[at_y, at_z]
        scores = block_scores(key_block, stack[...], seg_k_ref[at_y, at_z, :, 0:1], seg_wide)
        weights = jnp.exp(scores - lse_ref[0:1, :])
        dv_ref[at_y, at_z] = jnp.dot(
            weights.astype(BF16), grad_plain[...], preferred_element_type=F32
        ).astype(BF16)
        prob_grad = flat_dot(v_ref[at_y, at_z], grad_stack[...])
        low = (weights * (prob_grad - delta_ref[0:1, :])).astype(BF16)
        dk_ref[at_y, at_z] = jnp.dot(low, plain[...], preferred_element_type=F32).astype(BF16)
        turned = key_block.T
        for head in range(heads_here):
            rows = pl.ds(head * HEAD_DIM, HEAD_DIM)
            acc[rows, :] += jnp.dot(
                turned[head * HEAD_DIM : (head + 1) * HEAD_DIM],
                low[:, head * group : (head + 1) * group],
                preferred_element_type=F32,
            )

    def attend_all(first, count, offsets):
        def each(number, carry):
            attend(*offsets(number))
            return carry

        lax.fori_loop(first, count, each, 0)

    attend_all(0, 4, lambda t: (t * 0 + FAR, step(t, FAR)))
    for j in Scatter.ORDER:
        values.send_via(j)
    keys.send_direct(FAR)
    attend_all(1, 4, lambda t: (step(t, FAR), t * 0 + FAR))
    for j in Scatter.ORDER:
        keys.send_via(j)
    values.send_direct(FAR)
    attend_all(1, 4, lambda t: (t * 0 + PLUS, step(t, FAR)))
    keys.send_direct(PLUS)
    values.send_direct(PLUS)
    values.send_direct(MINUS)
    attend_all(1, 4, lambda t: (t * 0 + MINUS, step(t, FAR)))
    keys.send_direct(MINUS)
    values.send_direct(0)
    values.join()
    for j in (FAR, PLUS, MINUS):
        keys.join_one(j)
    attend_all(1, 4, lambda t: (t * 0, step(t, FAR)))
    keys.send_direct(0)
    keys.join_one(0)
    values.turn()
    keys.turn()
    values.join_two()
    keys.join_two()
    sums_ref[...] = jnp.zeros_like(sums_ref)
    query_grad = acc[...].T
    sums_ref[0:1, :] = jnp.sum(query_grad, axis=0, keepdims=True)
    triple_ref[0] = query_grad.astype(BF16)
    load_qkv.wait()
    part = flat_dot(triple_ref[0], qkv_ref[0])
    values.finish(total_ref)
    triple_ref[2] = total_ref[...].astype(BF16)
    sums_ref[1:2, :] = jnp.sum(total_ref[...], axis=0, keepdims=True)
    part = part + flat_dot(triple_ref[2], qkv_ref[2])
    keys.finish(total_ref)
    triple_ref[1] = total_ref[...].astype(BF16)
    part = part + flat_dot(triple_ref[1], qkv_ref[1])
    part_ref[...] = part.astype(BF16).reshape(part_ref.shape)
    for copy in started:
        copy.wait_send()


def attend_back_call(cid, attn_rows, full_qkv, full_out, queries, keys, values, wide, lse, seg_wide, seg_column):
    group, model = attn_rows.shape
    width = queries.shape[1]
    heads_here = width // HEAD_DIM
    block = (group, width)
    stacked = pltpu.VMEM((group * heads_here, width), BF16)
    return pl.pallas_call(
        attend_back_kernel,
        out_shape=[
            jax.ShapeDtypeStruct((3, group, width), BF16),
            jax.ShapeDtypeStruct((8, width), F32),
            jax.ShapeDtypeStruct((RING, group // RING, model), BF16),
        ],
        in_specs=[vmem_spec(), any_spec(), any_spec()] + [vmem_spec()] * 7,
        out_specs=[vmem_spec()] * 3,
        scratch_shapes=[
            pltpu.VMEM((3, model, width), BF16),
            pltpu.VMEM((model, width), BF16),
            pltpu.VMEM(block, BF16),
            stacked,
            stacked,
            stacked,
            stacked,
            pltpu.VMEM((width, group), F32),
            pltpu.VMEM((8, group * heads_here), F32),
            pltpu.VMEM((RING, RING) + block, BF16),
            pltpu.VMEM((RING, RING) + block, BF16),
            pltpu.VMEM(block, F32),
        ]
        + Scatter.scratch(block, BF16)
        + Scatter.scratch(block, BF16)
        + [
            pltpu.SemaphoreType.DMA((2, 6, RING)),
            pltpu.SemaphoreType.DMA((2, 6, RING)),
            pltpu.SemaphoreType.DMA((2,)),
        ],
        compiler_params=comm_params(cid),
    )(attn_rows, full_qkv, full_out, queries, keys, values, wide, lse, seg_wide, seg_column)


def shards(tokens, segment_ids, w_qkv, w_out, w_up, w_down, vectors, out_bias, cotangent):
    section = lax.axis_index("section")
    tensor_rank = lax.axis_index("tensor")
    own = lambda pair: jnp.where(section == 0, pair[0], pair[1])
    rows = tokens.shape[1]
    width = tokens.shape[2]
    group = rows * RING
    square = (RING, RING)
    local_width = w_qkv.shape[3]
    local_hidden = w_up.shape[2]

    depth = w_out.shape[1]
    small = jnp.pad(
        jnp.concatenate([vectors[0], out_bias], axis=0),
        ((0, 2), (0, 128 - depth)),
    )
    my_segments = own(segment_ids)
    seg_block = jnp.pad(my_segments[None], ((0, 7), (0, 128 - rows)))
    qkv_half, out_half, up_half, down_half, qkv_first, out_first, small_rows, full_seg = first_call(
        0, w_qkv[0], w_out[0], w_up[0], w_down[0], small, seg_block
    )
    joined_qkv = lambda value: value.reshape(3, width, local_width)
    joined = lambda value: value.reshape(width, value.shape[-1])

    my_tokens = own(tokens)
    my_cotangent = own(cotangent)
    seg_mine = own(full_seg)[:, :, 0, :rows].reshape(8, 128)
    normed, seg_group, up_first, down_first = tensor_call(
        1, first_rows, None, [my_tokens], [small_rows[0]], [], 0, True, seg_mine,
        weight_rider([up_half[0], down_half[0]]),
    )
    full_qkv, full_out = [joined_qkv(qkv_first), None], [joined(out_first), None]
    full_up, full_down = [joined(up_first), None], [joined(down_first), None]
    seg_all = seg_group.reshape(RING, RING * RING, rows).transpose(1, 0, 2).reshape(-1, group)
    seg_rows = lax.dynamic_index_in_dim(seg_all, lax.axis_index("dp"), 0, keepdims=False)
    seg_wide = jnp.broadcast_to(seg_rows[None], (8, group))
    seg_column = jnp.broadcast_to(seg_all.reshape(*square, group)[..., None], square + (group, 128))
    inputs = my_tokens
    kept = []
    for layer in range(2):
        vec = small_rows[layer]
        normed = normed.reshape(group, width)
        query_bias = lax.dynamic_slice_in_dim(vec[2], tensor_rank * local_width, local_width)
        value_bias = lax.dynamic_slice_in_dim(vec[3], tensor_rank * local_width, local_width)
        up_bias = lax.dynamic_slice_in_dim(
            vec[9:13].reshape(-1), tensor_rank * local_hidden, local_hidden
        )
        biases = jnp.pad(jnp.stack([query_bias, value_bias]), ((0, 6), (0, 0)))
        queries, keys_full, values_full, mixed, wide, lse, part = attend_call(
            2 + 12 * layer, normed, full_qkv[layer], full_out[layer], biases, seg_wide, seg_column
        )
        rider = weight_rider([qkv_half[1], out_half[1]]) if layer == 0 else None
        results = tensor_call(
            3 + 12 * layer, middle_rows, part, [inputs.astype(F32)], [vec], [F32, F32], 0, True,
            None, rider,
        )
        attn_out, hidden, normed_two = results[:3]
        if layer == 0:
            full_qkv[1], full_out[1] = joined_qkv(results[3]), joined(results[4])
        normed_two = normed_two.reshape(group, width)
        pre_act = jnp.dot(normed_two, full_up[layer], preferred_element_type=F32) + up_bias
        activated = gelu_exact(pre_act).astype(BF16)
        part = flat_dot(activated, full_down[layer]).astype(BF16).reshape(RING, rows, width)
        step_kept = [inputs, normed, queries, keys_full, values_full, mixed, attn_out, hidden]
        step_kept += [normed_two, pre_act, activated, wide, lse]
        if layer == 0:
            mlp_first, between, normed, up_second, down_second = tensor_call(
                4, end_rows_first, part, [hidden], [vec, small_rows[1]], [F32, BF16], 0, True,
                None, weight_rider([up_half[1], down_half[1]]),
            )
            full_up[1], full_down[1] = joined(up_second), joined(down_second)
            inputs = between
        else:
            outputs, sums_end, mlp_rows = tensor_call(
                5, end_rows_last, part, [hidden, my_cotangent], [vec], [BF16], 2, True
            )
        kept.append(step_kept)

    upstream = my_cotangent.astype(F32)
    blocks = lambda value: value.astype(BF16).reshape(*square, depth, value.shape[-1])
    sums, waiting, summed = [None, None], None, [None, None]
    for layer in (1, 0):
        vec = small_rows[layer]
        inputs, normed, queries, keys_full, values_full, mixed, attn_out, hidden = kept[layer][:8]
        normed_two, pre_act, activated, wide, lse = kept[layer][8:]
        mlp_rows = mlp_rows.reshape(group, width)
        act_grad = jnp.dot(mlp_rows, full_down[layer], preferred_element_type=F32)
        grad_down = blocks(rows_dot(mlp_rows, activated))
        pre_grad = jax.vjp(gelu_exact, pre_act)[1](act_grad)[0]
        up_bias_grad = jnp.broadcast_to(jnp.sum(pre_grad, axis=0)[None], (8, local_hidden))
        pre_low = pre_grad.astype(BF16)
        grad_up = blocks(rows_dot(normed_two, pre_low))
        part = flat_dot(pre_low, full_up[layer]).astype(BF16).reshape(RING, rows, width)
        results = tensor_call(
            6 + 12 * layer, back_middle_rows, part, [upstream, hidden, attn_out], [vec], [F32], 4, True,
            None, gradient_rider(waiting) if layer == 0 else None,
        )
        hidden_grad, sums_middle, attn_rows = results[:3]
        if layer == 0:
            summed[1] = results[3:] + summed[1]
        attn_rows = attn_rows.reshape(group, width)
        grad_out = blocks(rows_dot(attn_rows, mixed))
        triple, sums_attend, part = attend_back_call(
            7 + 12 * layer, attn_rows, full_qkv[layer], full_out[layer], queries, keys_full, values_full,
            wide, lse, seg_wide, seg_column,
        )
        waiting = [blocks(rows_dot(normed, triple[which])) for which in range(3)]
        rider = gradient_rider([grad_up, grad_down, grad_out])
        if layer == 1:
            results = tensor_call(
                8,
                back_end_rows_last,
                part,
                [hidden_grad, inputs.astype(F32), mlp_first],
                [vec, small_rows[0]],
                [F32],
                4,
                True,
                None,
                rider,
            )
            input_grad, sums_last, mlp_rows = results[:3]
            summed[1] = results[3:]
        else:
            results = tensor_call(
                9, back_end_rows_first, part, [hidden_grad, inputs.astype(F32)], [vec], [F32], 2, False,
                None, rider,
            )
            input_grad, sums_last = results[:2]
            summed[0] = results[2:]
        sums[layer] = [sums_last, sums_middle, sums_end, sums_attend, up_bias_grad]
        if layer == 1:
            last_grad = input_grad
            upstream = input_grad.astype(BF16).astype(F32)
            sums_end = sums_last[2:]
    first_grad = input_grad

    extras = [
        jnp.where(section == 0, outputs, between),
        jnp.where(section == 0, last_grad, first_grad),
    ]
    results = final_call(10, sums[0] + sums[1], waiting, extras)
    small_sum, came_out, came_grad = results[0], results[4], results[5]
    summed[0] = results[1:4] + summed[0]
    mine_out = jnp.where(section == 0, between, outputs)
    mine_grad = jnp.where(section == 0, first_grad, last_grad)
    pair = lambda mine, came: jnp.where(
        section == 0, jnp.stack([mine, came]), jnp.stack([came, mine])
    )[None]
    pick = lambda which: jnp.where(section == 0, summed[0][which], summed[1][which])
    return (
        pair(mine_out, came_out),
        pair(mine_grad, came_grad),
        jnp.stack([pick(0), pick(1), pick(2)])[None],
        pick(5)[None],
        pick(3)[None],
        pick(4)[None],
        small_sum[:13, :depth][None],
        small_sum[13:14, :depth],
    )


def solution(mesh):
    in_specs = (
        P(None, ("dp", "tensor"), None),
        P(None, ("dp", "tensor")),
        P("section", None, "dp", "tensor"),
        P("section", "dp", "tensor"),
        P("section", "dp", "tensor"),
        P("section", "dp", "tensor"),
        P("section", None, "dp"),
        P("section", "dp"),
        P(None, ("dp", "tensor"), None),
    )
    out_specs = (
        P("section", None, ("dp", "tensor"), None),
        P("section", None, ("dp", "tensor"), None),
        P("section", None, "dp", "tensor"),
        P("section", "dp", "tensor"),
        P("section", "dp", "tensor"),
        P("section", "dp", "tensor"),
        P("section", None, "dp"),
        P("section", "dp"),
    )
    return jax.shard_map(shards, mesh=mesh, in_specs=in_specs, out_specs=out_specs, check_vma=False)
```

```python
import functools

import jax
import jax.numpy as jnp
from jax import lax
from jax.experimental import pallas as pl
from jax.experimental.pallas import tpu as pltpu
from jax.sharding import PartitionSpec as P

MESH = pl.DeviceIdType.MESH
HEAD_DIM = 64
EPSILON = 1e-06
MASKED_SCORE = -1e30
RING = 4
VMEM_LIMIT = 56 * 1024 * 1024
F32 = jnp.float32
BF16 = jnp.bfloat16


def vmem_spec():
    return pl.BlockSpec(memory_space=pltpu.VMEM)


def any_spec():
    return pl.BlockSpec(memory_space=pl.ANY)


def comm_params(cid):
    return pltpu.CompilerParams(
        collective_id=cid, has_side_effects=True, vmem_limit_bytes=VMEM_LIMIT
    )


def step(coord, by):
    return lax.rem(coord + by, RING)


def layer_norm(values, gain_row, shift_row):
    centre = values - jnp.mean(values, axis=-1, keepdims=True)
    spread = jnp.mean(centre * centre, axis=-1, keepdims=True)
    return centre * lax.rsqrt(spread + EPSILON) * gain_row + shift_row


def layer_norm_back(values, gain_row, grad):
    centre = values - jnp.mean(values, axis=-1, keepdims=True)
    spread = jnp.mean(centre * centre, axis=-1, keepdims=True)
    inverse = lax.rsqrt(spread + EPSILON)
    normed = centre * inverse
    scaled = grad * gain_row
    back = inverse * (
        scaled
        - jnp.mean(scaled, axis=-1, keepdims=True)
        - normed * jnp.mean(scaled * normed, axis=-1, keepdims=True)
    )
    return back, jnp.sum(grad * normed, axis=0, keepdims=True), jnp.sum(grad, axis=0, keepdims=True)


PLUS, FAR, MINUS = 1, 2, 3
CHUNKS = 2


def tensor_barrier(me):
    barrier = pltpu.get_barrier_semaphore()
    for k in range(1, RING):
        pl.semaphore_signal(
            barrier, inc=1, device_id={"tensor": step(me, k)}, device_id_type=MESH
        )
    return barrier, RING - 1


def tensor_kernel(function, n_rows, n_vecs, n_out, n_sums, reduce, gather, with_seg, *refs):
    refs = list(refs)
    take = lambda count: [refs.pop(0) for _ in range(count)]
    part = take(1)[0] if reduce else None
    rows_in = take(n_rows)
    vecs = take(n_vecs)
    seg_in = take(1)[0] if with_seg else None
    rows_out = take(n_out)
    sums_out = take(1)[0] if n_sums else None
    full = take(1)[0] if gather else None
    seg_out = take(1)[0] if with_seg else None
    landing = take(1)[0] if reduce else None
    send, recv, local = take(3)

    me = lax.axis_index("tensor")
    barrier, count = tensor_barrier(me)
    pl.semaphore_wait(barrier, count)

    chunk = rows_in[0].shape[0] // CHUNKS
    started = []

    def push(source, target, kind, index, k):
        copy = pltpu.make_async_remote_copy(
            src_ref=source,
            dst_ref=target,
            send_sem=send.at[kind, index, k - 1],
            recv_sem=recv.at[kind, index, k - 1],
            device_id={"tensor": step(me, k)},
            device_id_type=MESH,
        )
        copy.start()
        started.append(copy)
        return copy

    reduces = {}
    if reduce:
        for c in range(CHUNKS):
            here = pl.ds(c * chunk, chunk)
            for k in range(1, RING):
                reduces[c, k] = push(
                    part.at[step(me, k), here], landing.at[k - 1, here], 0, c, k
                )
    last = []
    if with_seg:
        own = pltpu.make_async_copy(seg_in, seg_out.at[me], local)
        own.start()
        last += [push(seg_in, seg_out.at[me], 2, 0, k) for k in range(1, RING)]
    sums = [None] * n_sums
    for c in range(CHUNKS):
        here = pl.ds(c * chunk, chunk)
        total = None
        if reduce:
            for k in range(1, RING):
                reduces[c, k].wait_recv()
            total = part[me, here].astype(F32)
            for k in range(1, RING):
                total = total + landing[k - 1, here].astype(F32)
        spread, outs, parts = function(
            total, [ref[here].astype(F32) for ref in rows_in], vecs
        )
        if gather:
            full[me, here] = spread.astype(BF16)
            last += [push(full.at[me, here], full.at[me, here], 1, c, k) for k in range(1, RING)]
        for ref, value in zip(rows_out, outs):
            ref[here] = value.astype(ref.dtype)
        sums = [new if old is None else old + new for old, new in zip(sums, parts)]
    if n_sums:
        sums_out[...] = jnp.concatenate(
            sums + [jnp.zeros((8 - n_sums, sums[0].shape[1]), F32)], axis=0
        )
    for copy in last:
        copy.wait_recv()
    if with_seg:
        own.wait()
    for copy in started:
        copy.wait_send()


def tensor_call(cid, function, part, rows, vecs, outs, n_sums, gather, seg=None):
    height, width = rows[0].shape
    reduce = part is not None
    with_seg = seg is not None
    args = ([part] if reduce else []) + list(rows) + list(vecs) + ([seg] if with_seg else [])
    shapes = [jax.ShapeDtypeStruct((height, width), dtype) for dtype in outs]
    if n_sums:
        shapes.append(jax.ShapeDtypeStruct((8, width), F32))
    if gather:
        shapes.append(jax.ShapeDtypeStruct((RING, height, width), BF16))
    if with_seg:
        shapes.append(jax.ShapeDtypeStruct((RING,) + seg.shape, seg.dtype))
    in_specs, out_specs = [vmem_spec()] * len(args), [vmem_spec()] * len(shapes)
    scratch = [pltpu.VMEM((RING - 1, height, width), BF16)] if reduce else []
    scratch += [
        pltpu.SemaphoreType.DMA((3, CHUNKS, RING - 1)),
        pltpu.SemaphoreType.DMA((3, CHUNKS, RING - 1)),
        pltpu.SemaphoreType.DMA,
    ]
    return pl.pallas_call(
        functools.partial(
            tensor_kernel, function, len(rows), len(vecs), len(outs), n_sums, reduce, gather, with_seg,
        ),
        out_shape=shapes,
        in_specs=in_specs,
        out_specs=out_specs,
        scratch_shapes=scratch,
        compiler_params=comm_params(cid),
    )(*args)


def row(ref, index):
    return ref[pl.ds(index, 1), :]


def first_rows(total, rows, vecs):
    return layer_norm(rows[0], row(vecs[0], 0), row(vecs[0], 1)), [], []


def middle_rows(total, rows, vecs):
    vec = vecs[0]
    attn_out = total + row(vec, 13)
    hidden = rows[0] + row(vec, 4) * attn_out
    return layer_norm(hidden, row(vec, 5), row(vec, 6)), [attn_out, hidden], []


def end_rows_first(total, rows, vecs):
    vec, after = vecs
    mlp_out = total + row(vec, 7)
    outputs = (rows[0] + row(vec, 8) * mlp_out).astype(BF16)
    inputs = outputs.astype(F32)
    return layer_norm(inputs, row(after, 0), row(after, 1)), [mlp_out, outputs], []


def end_rows_last(total, rows, vecs):
    vec = vecs[0]
    hidden, upstream = rows
    mlp_out = total + row(vec, 7)
    outputs = hidden + row(vec, 8) * mlp_out
    mlp_grad = row(vec, 8) * upstream
    sums = [
        jnp.sum(upstream * mlp_out, axis=0, keepdims=True),
        jnp.sum(mlp_grad, axis=0, keepdims=True),
    ]
    return mlp_grad, [outputs], sums


def back_middle_rows(total, rows, vecs):
    vec = vecs[0]
    upstream, hidden, attn_out = rows
    part, gain, shift = layer_norm_back(hidden, row(vec, 5), total)
    hidden_grad = upstream + part
    attn_grad = row(vec, 4) * hidden_grad
    sums = [
        gain,
        shift,
        jnp.sum(hidden_grad * attn_out, axis=0, keepdims=True),
        jnp.sum(attn_grad, axis=0, keepdims=True),
    ]
    return attn_grad, [hidden_grad], sums


def back_end_rows_last(total, rows, vecs):
    vec, before = vecs
    hidden_grad, inputs, mlp_out = rows
    part, gain, shift = layer_norm_back(inputs, row(vec, 0), total)
    input_grad = hidden_grad + part
    upstream = input_grad.astype(BF16).astype(F32)
    mlp_grad = row(before, 8) * upstream
    sums = [
        gain,
        shift,
        jnp.sum(upstream * mlp_out, axis=0, keepdims=True),
        jnp.sum(mlp_grad, axis=0, keepdims=True),
    ]
    return mlp_grad, [input_grad], sums


def back_end_rows_first(total, rows, vecs):
    hidden_grad, inputs = rows
    part, gain, shift = layer_norm_back(inputs, row(vecs[0], 0), total)
    return None, [hidden_grad + part], [gain, shift]


def dp_neighbour(y, z, along_z, k):
    if along_z:
        return {"dp": y * RING + step(z, k)}
    return {"dp": step(y, k) * RING + z}


def dp_barrier(y, z, section):
    barrier = pltpu.get_barrier_semaphore()
    count = 0
    for along_z in (True, False):
        for k in (PLUS, MINUS):
            pl.semaphore_signal(
                barrier, inc=1, device_id=dp_neighbour(y, z, along_z, k), device_id_type=MESH
            )
            count += 1
    if section is not None:
        pl.semaphore_signal(
            barrier, inc=1, device_id={"section": 1 - section}, device_id_type=MESH
        )
        count += 1
    return barrier, count


def pusher(send, recv, started):
    def push(index, kind, k, source, target, device):
        copy = pltpu.make_async_remote_copy(
            src_ref=source,
            dst_ref=target,
            send_sem=send.at[index, kind, k],
            recv_sem=recv.at[index, kind, k],
            device_id=device,
            device_id_type=MESH,
        )
        copy.start()
        started.append(copy)
        return copy

    return push


class Gather:
    WAYS = {0: 1, 3: 1, 1: 1, 2: 3}

    def __init__(self, pieces, outs, y, z, lead, push):
        self.pieces, self.outs, self.y, self.z = pieces, outs, y, z
        self.lead, self.push = lead, push
        self.every = range(len(pieces))
        self.first, self.onward, self.second, self.relayed = {}, {}, {}, {}

    def block(self, i, along, across, rows=None):
        number, pre, along_z = self.pieces[i]
        ys, zs = (across, along) if along_z else (along, across)
        ys = ys if isinstance(ys, slice) else step(self.y, ys) if ys else self.y
        zs = zs if isinstance(zs, slice) else step(self.z, zs) if zs else self.z
        return self.outs[number].at[self.lead + pre + (ys, zs) + (() if rows is None else (rows,))]

    def way(self, i, first, k):
        return dp_neighbour(self.y, self.z, self.pieces[i][2] == first, k)

    def halves(self, i):
        height = self.outs[self.pieces[i][0]].shape[-2]
        if height < 32:
            return {PLUS: None}
        half = height // 32 * 16
        return {PLUS: pl.ds(0, half), MINUS: pl.ds(half, height - half)}

    def spread(self, i, offset, source):
        for k in (PLUS, MINUS):
            self.second[i, offset, k] = self.push(
                i, 2 if k == PLUS else 3, offset, source, self.block(i, offset, 0), self.way(i, False, k)
            )

    def begin(self, i, source):
        for k in (PLUS, MINUS):
            self.first[i, k] = self.push(i, 0, k, source, self.block(i, 0, 0), self.way(i, True, k))
        self.spread(i, 0, source)

    def near(self):
        for i in self.every:
            split = self.halves(i)
            for k in (PLUS, MINUS):
                self.first[i, k].wait_recv()
                came = RING - k
                if k in split:
                    self.onward[i, k] = self.push(
                        i, 1, k, self.block(i, came, 0, split[k]), self.block(i, came, 0, split[k]),
                        self.way(i, True, k),
                    )
                self.spread(i, came, self.block(i, came, 0))

    def relay(self, i, offset):
        k = self.WAYS[offset]
        self.second[i, offset, k].wait_recv()
        came = self.block(i, offset, RING - k)
        self.relayed[i, offset] = self.push(i, 4, offset, came, came, self.way(i, False, k))

    def other(self, i, offset):
        self.second[i, offset, RING - self.WAYS[offset]].wait_recv()

    def far(self, i):
        for k in self.halves(i):
            self.onward[i, k].wait_recv()
        self.spread(i, FAR, self.block(i, FAR, 0))


def half_of(section, height):
    return pl.ds(pl.multiple_of(section * height, height), height)


def spread_stages(ring, sources, local, section, push):
    own, across = {}, []

    def pass_on(i, line):
        came = ring.block(i, slice(None), line)
        across.append(push(i, 5, line, came, came, {"section": 1 - section}))

    def begin():
        for i in ring.every:
            ring.begin(i, sources[i])
            own[i] = pltpu.make_async_copy(sources[i], ring.block(i, 0, 0), local.at[i])
            own[i].start()

    def near():
        ring.near()
        for i in ring.every:
            ring.relay(i, 0)

    def middle():
        for i in ring.every:
            ring.far(i)
        for i in ring.every:
            ring.relay(i, MINUS)
            ring.relay(i, PLUS)
            own[i].wait()
            pass_on(i, 0)

    def end():
        for i in ring.every:
            ring.relay(i, FAR)
            for offset in range(RING):
                ring.other(i, offset)
            pass_on(i, PLUS)
            pass_on(i, MINUS)
        for i in ring.every:
            for offset in range(RING):
                ring.relayed[i, offset].wait_recv()
            pass_on(i, FAR)
        for copy in across:
            copy.wait_recv()

    return [begin, near, middle, end]


PACKED = 192
SMALL = 16


def first_kernel(
    qkv_in, out_in, up_in, down_in, small_in, packed_out, small_all, rows_out,
    block, send, recv, local, pack_local, last_local,
):
    rank = lax.axis_index("dp")
    y, z = rank // RING, lax.rem(rank, RING)
    section = lax.axis_index("section")
    barrier, count = dp_barrier(y, z, section)
    depth, width = out_in.shape
    packs = [
        (qkv_in.at[which], block.at[0:depth, which * width : (which + 1) * width]) for which in range(3)
    ]
    packs += [
        (out_in, block.at[0:depth, 3 * width : 4 * width]),
        (up_in, block.at[depth : 2 * depth]),
        (down_in, block.at[2 * depth : 3 * depth]),
        (small_in, block.at[PACKED : PACKED + SMALL, 0 : small_in.shape[1]]),
    ]
    block[PACKED : PACKED + SMALL] = jnp.zeros((SMALL, block.shape[1]), BF16)
    copies = [
        pltpu.make_async_copy(source, target, pack_local.at[i])
        for i, (source, target) in enumerate(packs)
    ]
    for copy in copies:
        copy.start()
    for copy in copies:
        copy.wait()
    pl.semaphore_wait(barrier, count)
    started = []
    push = pusher(send, recv, started)
    low, high = pl.ds(0, PACKED // 2), pl.ds(PACKED // 2, PACKED // 2 + SMALL)
    views = [packed_out.at[section, :, :, low], packed_out.at[section, :, :, high]]
    ring = Gather(((0, (), True), (1, (), False)), views, y, z, (), push)
    for stage in spread_stages(ring, [block.at[low], block.at[high]], local, section, push):
        stage()
    last = pltpu.make_async_copy(
        packed_out.at[:, :, :, pl.ds(PACKED, SMALL), pl.ds(0, small_in.shape[1])], small_all, last_local
    )
    last.start()
    last.wait()
    for layer in range(2):
        for number in range(RING * RING):
            part = small_all[layer, number // RING, number % RING]
            rows_out[layer, :, number * depth : (number + 1) * depth] = part[:, :depth].astype(F32)
    for copy in started:
        copy.wait_send()


def first_call(cid, w_qkv, w_out, w_up, w_down, small):
    depth = w_out.shape[0]
    hidden = w_up.shape[1]
    return pl.pallas_call(
        first_kernel,
        out_shape=[
            jax.ShapeDtypeStruct((2, RING, RING, PACKED + SMALL, hidden), BF16),
            jax.ShapeDtypeStruct((2, RING, RING) + small.shape, BF16),
            jax.ShapeDtypeStruct((2, SMALL, RING * RING * depth), F32),
        ],
        in_specs=[vmem_spec()] * 5,
        out_specs=[any_spec(), vmem_spec(), vmem_spec()],
        scratch_shapes=[
            pltpu.VMEM((PACKED + SMALL, hidden), BF16),
            pltpu.SemaphoreType.DMA((2, 6, RING)),
            pltpu.SemaphoreType.DMA((2, 6, RING)),
            pltpu.SemaphoreType.DMA((2,)),
            pltpu.SemaphoreType.DMA((7,)),
            pltpu.SemaphoreType.DMA,
        ],
        compiler_params=comm_params(cid),
    )(w_qkv, w_out, w_up, w_down, small)


class Scatter:
    ORDER = (FAR, PLUS, MINUS, 0)
    WAYS = {FAR: PLUS, 0: PLUS, PLUS: MINUS, MINUS: MINUS}

    def __init__(self, index, along_z, source, buffers, y, z, push):
        self.index, self.along_z, self.source = index, along_z, source
        self.passing, self.joined, self.summed, self.straight, self.middle = buffers[:5]
        self.far_two, self.joined_two, self.summed_two, self.straight_two = buffers[5:]
        self.y, self.z, self.push = y, z, push
        self.height, self.width = source.shape[-2:]
        self.via, self.direct, self.after = {}, {}, {}

    def at(self, along, across):
        ys, zs = (across, along) if self.along_z else (along, across)
        return step(self.y, ys), step(self.z, zs)

    def way(self, first, k):
        return dp_neighbour(self.y, self.z, self.along_z == first, k)

    def add(self, target, terms, top=0, height=None):
        height = self.height if height is None else height
        size = max(8, min(height, 65536 // self.width))
        while height % size:
            size -= 16

        def part(here):
            value = terms[0](here).astype(F32)
            for term in terms[1:]:
                value = value + term(here).astype(F32)
            target[here] = value.astype(target.dtype)

        if height <= size:
            part(pl.ds(top, height))
            return

        def each(number, carry):
            part(pl.ds(pl.multiple_of(top + number * size, size), size))
            return carry

        lax.fori_loop(0, height // size, each, 0)

    def send_via(self, j):
        self.via[j] = self.push(
            self.index, 0, j, self.source.at[self.at(FAR, j)], self.passing.at[j],
            self.way(True, self.WAYS[j]),
        )

    def send_direct(self, j):
        k = RING - self.WAYS[j]
        self.direct[j] = self.push(
            self.index, 1, j, self.source.at[self.at(k, j)], self.straight.at[j], self.way(True, k)
        )

    def begin(self):
        for j in self.ORDER:
            self.send_via(j)
        for j in self.ORDER:
            self.send_direct(j)

    def join_one(self, j):
        self.via[j].wait_recv()
        k = self.WAYS[j]
        at_y, at_z = self.at(k, j)
        self.add(
            self.joined.at[j],
            [lambda h: self.source[at_y, at_z, h], lambda h: self.passing[j, h]],
        )
        self.after[j] = self.push(
            self.index, 2, j, self.joined.at[j], self.summed.at[j], self.way(True, k)
        )

    def join(self):
        for j in self.ORDER:
            self.join_one(j)

    def turn(self):
        half = self.height // 2
        low, high = pl.ds(0, half), pl.ds(half, half)
        send = lambda kind, slot, source, target, k: self.push(
            self.index, kind, slot, source, target, self.way(False, k)
        )
        for j in self.ORDER:
            self.direct[j].wait_recv()
            self.after[j].wait_recv()
            at_y, at_z = self.at(0, j)
            self.add(
                self.middle.at[j],
                [
                    lambda h: self.source[at_y, at_z, h],
                    lambda h: self.summed[j, h],
                    lambda h: self.straight[j, h],
                ],
            )
            if j == FAR:
                self.via_two = [
                    send(3, 0, self.middle.at[j, low], self.far_two.at[low], PLUS),
                    send(3, 1, self.middle.at[j, high], self.far_two.at[high], MINUS),
                ]
            if j == PLUS:
                high_copy = send(4, 1, self.middle.at[j, high], self.straight_two.at[high], PLUS)
            if j == MINUS:
                low_copy = send(4, 0, self.middle.at[j, low], self.straight_two.at[low], MINUS)
        self.direct_two = [low_copy, high_copy]

    def join_two(self):
        half = self.height // 2
        self.after_two = []
        for number, (top, k) in enumerate(((0, PLUS), (half, MINUS))):
            self.via_two[number].wait_recv()
            self.add(
                self.joined_two,
                [lambda h: self.middle[k, h], lambda h: self.far_two[h]],
                top,
                half,
            )
            here = pl.ds(top, half)
            self.after_two.append(
                self.push(
                    self.index, 5, number, self.joined_two.at[here], self.summed_two.at[here],
                    self.way(False, k),
                )
            )

    def finish(self, out):
        for copy in self.direct_two + self.after_two:
            copy.wait_recv()
        self.add(
            out,
            [
                lambda h: self.middle[0, h],
                lambda h: self.summed_two[h],
                lambda h: self.straight_two[h],
            ],
        )

    @staticmethod
    def scratch(block, dtype):
        return [pltpu.VMEM((RING,) + block, dtype)] * 5 + [pltpu.VMEM(block, dtype)] * 4


SCATTER_BUFFERS = 9


def scatter_buffers(block, dtype):
    square = pltpu.VMEM((RING, RING) + block, dtype)
    return [square, square] + Scatter.scratch(block, dtype)


def final_kernel(n_extra, *refs):
    refs = list(refs)
    take = lambda count: [refs.pop(0) for _ in range(count)]
    sums = [take(5), take(5)]
    grads = [take(6), take(6)]
    extras = take(n_extra)
    small_out, packed_out = take(2)
    extra_outs = take(n_extra)
    small_in, small_rows, vector_own, vector_parts, summed = take(5)
    buffers = [take(2 + SCATTER_BUFFERS) for _ in range(3)]
    send, recv, swap_send, swap_recv, keep_local = take(5)
    vector_send, vector_recv, extra_send, extra_recv, result_send, result_recv, result_local = take(7)
    rank = lax.axis_index("dp")
    y, z = rank // RING, lax.rem(rank, RING)
    section = lax.axis_index("section")
    me = lax.axis_index("tensor")
    other = {"section": 1 - section}
    barrier, count = tensor_barrier(me)
    count += dp_barrier(y, z, section)[1]

    depth, width = grads[0][0].shape[2:]
    hidden = grads[0][5].shape[3]
    half = depth // 2
    mine, others = half_of(section, half), half_of(1 - section, half)
    places = [(0, which * width, width) for which in range(4)]
    places += [(half, 0, hidden), (2 * half, 0, hidden)]
    keeps, swaps = [], []
    for layer in range(2):
        for i, (row, column, columns) in enumerate(places):
            region = (slice(None), slice(None), pl.ds(row, half), pl.ds(column, columns))
            copy = pltpu.make_async_copy(
                grads[layer][i].at[:, :, mine], buffers[layer][0].at[region], keep_local.at[layer, i]
            )
            copy.start()
            keeps.append(copy)

    small_rows[...] = jnp.zeros_like(small_rows)
    model = small_rows.shape[1]
    for layer in range(2):
        first, middle, end, attend, up = sums[layer]
        top = SMALL * layer
        part = attend.shape[1]
        lanes = pl.ds(pl.multiple_of(me * part, part), part)
        small_rows[top : top + 2, :] = first[0:2, :]
        small_rows[top + 2 : top + 3, lanes] = attend[0:1, :]
        small_rows[top + 3 : top + 4, lanes] = attend[1:2, :]
        small_rows[top + 4 : top + 5, :] = middle[2:3, :]
        small_rows[top + 5 : top + 7, :] = middle[0:2, :]
        small_rows[top + 7 : top + 8, :] = end[1:2, :]
        small_rows[top + 8 : top + 9, :] = end[0:1, :]
        for rank_of in range(RING):
            small_rows[top + 9 + rank_of : top + 10 + rank_of, :] = jnp.where(
                me == rank_of, up[0:1, :], 0.0
            )
        small_rows[top + 13 : top + 14, :] = middle[3:4, :]
    small_in[...] = jnp.zeros_like(small_in)
    for number in range(RING * RING):
        small_in[number // RING, number % RING, :, 0:depth] = small_rows[
            :, number * depth : (number + 1) * depth
        ]
    pl.semaphore_wait(barrier, count)
    started = []
    push = pusher(send, recv, started)
    for layer in range(2):
        for i, (row, column, columns) in enumerate(places):
            region = (slice(None), slice(None), pl.ds(row, half), pl.ds(column, columns))
            copy = pltpu.make_async_remote_copy(
                src_ref=grads[layer][i].at[:, :, others],
                dst_ref=buffers[layer][1].at[region],
                send_sem=swap_send.at[layer, i],
                recv_sem=swap_recv.at[layer, i],
                device_id=other,
                device_id_type=MESH,
            )
            copy.start()
            swaps.append(copy)
    started += swaps
    small_swap = push(2, 6, 0, small_in.at[:, :, half_of(1 - section, SMALL)], buffers[2][1], other)
    extra_copies = []
    for i in range(n_extra):
        copy = pltpu.make_async_remote_copy(
            src_ref=extras[i],
            dst_ref=extra_outs[i],
            send_sem=extra_send.at[i],
            recv_sem=extra_recv.at[i],
            device_id=other,
            device_id_type=MESH,
        )
        copy.start()
        extra_copies.append(copy)

    parts = []
    for piece in range(3):
        own, sibling = buffers[piece][:2]
        if piece == 2:
            small_swap.wait_recv()
            kept = small_in.at[:, :, half_of(section, SMALL)]
        else:
            for i in range(len(places)):
                keeps[piece * len(places) + i].wait()
                swaps[piece * len(places) + i].wait_recv()
            kept = own

        def add(number, carry):
            at_y, at_z = number // RING, lax.rem(number, RING)
            own[at_y, at_z] = (
                kept[at_y, at_z].astype(F32) + sibling[at_y, at_z].astype(F32)
            ).astype(own.dtype)
            return carry

        lax.fori_loop(0, RING * RING, add, 0)
        parts.append(Scatter(piece, piece != 1, own, buffers[piece][2:], y, z, push))
        parts[piece].begin()
    for part in parts:
        part.join()
    order = (parts[2], parts[0], parts[1])
    for part in order:
        part.turn()
    for part in order:
        part.join_two()
    parts[2].finish(vector_own)
    vector_parts[me] = vector_own[...]
    vector_copies = []
    for k in range(1, RING):
        copy = pltpu.make_async_remote_copy(
            src_ref=vector_own,
            dst_ref=vector_parts.at[me],
            send_sem=vector_send.at[k],
            recv_sem=vector_recv.at[k],
            device_id={"tensor": step(me, k)},
            device_id_type=MESH,
        )
        copy.start()
        vector_copies.append(copy)
    for layer in range(2):
        parts[layer].finish(summed.at[layer])
    result = pltpu.make_async_remote_copy(
        src_ref=summed.at[1 - section],
        dst_ref=packed_out.at[section],
        send_sem=result_send,
        recv_sem=result_recv,
        device_id=other,
        device_id_type=MESH,
    )
    result.start()
    own_result = pltpu.make_async_copy(summed.at[section], packed_out.at[section], result_local)
    own_result.start()
    own_result.wait()
    result.wait()
    for copy in vector_copies:
        copy.wait()
    total = vector_parts[0]
    for k in range(1, RING):
        total = total + vector_parts[k]
    small_out[...] = total
    for copy in extra_copies:
        copy.wait()
    for copy in started:
        copy.wait_send()


def final_call(cid, sums, grads, extras):
    extra = len(extras)
    width = sums[0].shape[1]
    hidden = grads[-1].shape[3]
    args = list(sums) + list(grads) + list(extras)
    block = (PACKED // 2, hidden)
    return pl.pallas_call(
        functools.partial(final_kernel, extra),
        out_shape=[
            jax.ShapeDtypeStruct((SMALL, 128), F32),
            jax.ShapeDtypeStruct((2, PACKED // 2, hidden), F32),
        ]
        + [jax.ShapeDtypeStruct(value.shape, value.dtype) for value in extras],
        in_specs=[vmem_spec()] * len(sums) + [any_spec()] * len(grads) + [vmem_spec()] * extra,
        out_specs=[vmem_spec()] * (2 + extra),
        scratch_shapes=[
            pltpu.VMEM((RING, RING, 2 * SMALL, 128), F32),
            pltpu.VMEM((2 * SMALL, width), F32),
            pltpu.VMEM((SMALL, 128), F32),
            pltpu.VMEM((RING, SMALL, 128), F32),
            pltpu.VMEM((2,) + block, F32),
        ]
        + scatter_buffers(block, BF16)
        + scatter_buffers(block, BF16)
        + scatter_buffers((SMALL, 128), F32)
        + [
            pltpu.SemaphoreType.DMA((3, 7, RING)),
            pltpu.SemaphoreType.DMA((3, 7, RING)),
            pltpu.SemaphoreType.DMA((2, 6)),
            pltpu.SemaphoreType.DMA((2, 6)),
            pltpu.SemaphoreType.DMA((2, 6)),
            pltpu.SemaphoreType.DMA((RING,)),
            pltpu.SemaphoreType.DMA((RING,)),
            pltpu.SemaphoreType.DMA((extra,)),
            pltpu.SemaphoreType.DMA((extra,)),
            pltpu.SemaphoreType.DMA,
            pltpu.SemaphoreType.DMA,
            pltpu.SemaphoreType.DMA,
        ],
        compiler_params=comm_params(cid),
    )(*args)


def gelu_exact(values):
    return jax.nn.gelu(values, approximate=False)


def flat_dot(former, latter):
    return lax.dot_general(former, latter, (((1,), (1,)), ((), ())), preferred_element_type=F32)


def rows_dot(former, latter):
    return lax.dot_general(former, latter, (((0,), (0,)), ((), ())), preferred_element_type=F32)


def head_stack(values, scale):
    column = lax.broadcasted_iota(jnp.int32, values.shape, 1) // HEAD_DIM
    heads_here = values.shape[1] // HEAD_DIM
    zero = jnp.zeros_like(values)
    scaled = values * jnp.asarray(scale, values.dtype)
    return jnp.concatenate(
        [jnp.where(column == head, scaled, zero) for head in range(heads_here)], axis=0
    )


def block_scores(key_block, stack, seg_column, seg_wide):
    scores = flat_dot(key_block, stack)
    return jnp.where(seg_column == seg_wide, scores, MASKED_SCORE)


def attend_kernel(
    layer, normed_ref, packed_any, bias_ref, seg_q_ref, seg_k_ref,
    q_ref, k_ref, v_ref, mixed_ref, wide_ref, lse_ref, part_ref,
    pack_ref, stack, acc, top_ref, total_ref, send, recv, local,
):
    group, width = q_ref.shape
    heads_here = width // HEAD_DIM
    depth = group // RING
    load = pltpu.make_async_copy(packed_any.at[layer, :, :, pl.ds(0, depth)], pack_ref, local)
    load.start()
    matrix = lambda which: pack_ref[:, :, :, which * width : (which + 1) * width].reshape(-1, width)
    rank = lax.axis_index("dp")
    y, z = rank // RING, lax.rem(rank, RING)
    barrier, count = dp_barrier(y, z, None)
    normed = normed_ref[...]
    load.wait()
    k_ref[y, z] = jnp.dot(normed, matrix(1), preferred_element_type=F32).astype(BF16)
    pl.semaphore_wait(barrier, count)
    started = []
    ring = Gather(((0, (), True), (1, (), False)), (k_ref, v_ref), y, z, (), pusher(send, recv, started))
    ring.begin(0, k_ref.at[y, z])
    v_ref[y, z] = (
        jnp.dot(normed, matrix(2), preferred_element_type=F32) + bias_ref[1:2, :]
    ).astype(BF16)
    ring.begin(1, v_ref.at[y, z])
    q_ref[...] = (
        jnp.dot(normed, matrix(0), preferred_element_type=F32) + bias_ref[0:1, :]
    ).astype(BF16)
    stack[...] = head_stack(q_ref[...], HEAD_DIM ** (-0.5))
    acc[...] = jnp.zeros_like(acc)
    top_ref[...] = jnp.full_like(top_ref, MASKED_SCORE)
    total_ref[...] = jnp.zeros_like(total_ref)
    seg_wide = jnp.concatenate([seg_q_ref[0:1, :]] * heads_here, axis=1)

    def attend(offset_y, offset_z):
        at_y, at_z = step(y, offset_y), step(z, offset_z)
        highest = top_ref[0:1, :]
        scores = block_scores(
            k_ref[at_y, at_z], stack[...], seg_k_ref[at_y, at_z, :, 0:1], seg_wide
        )
        above = jnp.maximum(highest, jnp.max(scores, axis=0, keepdims=True))
        weights = jnp.exp(scores - above)
        fade = jnp.exp(highest - above)
        total_ref[0:1, :] = total_ref[0:1, :] * fade + jnp.sum(weights, axis=0, keepdims=True)
        top_ref[0:1, :] = above
        low = weights.astype(BF16)
        turned = v_ref[at_y, at_z].T
        for head in range(heads_here):
            rows = pl.ds(head * HEAD_DIM, HEAD_DIM)
            lanes = slice(head * group, (head + 1) * group)
            term = jnp.dot(
                turned[head * HEAD_DIM : (head + 1) * HEAD_DIM], low[:, lanes],
                preferred_element_type=F32,
            )
            acc[rows, :] = acc[rows, :] * fade[:, lanes] + term

    def attend_all(count, offsets):
        def each(number, carry):
            attend(*offsets(number))
            return carry

        lax.fori_loop(0, count, each, 0)

    side = lambda t: 1 + 2 * lax.rem(t, 2)
    attend_all(1, lambda t: (t, t))
    ring.near()
    for i in ring.every:
        ring.relay(i, 0)
        ring.other(i, 0)
    attend_all(2, lambda t: (t * 0, side(t)))
    for i in ring.every:
        ring.far(i)
    attend_all(2, lambda t: (side(t), t * 0))
    for i in ring.every:
        ring.relay(i, MINUS)
        ring.relay(i, PLUS)
    for i in ring.every:
        ring.other(i, MINUS)
        ring.other(i, PLUS)
    attend_all(4, lambda t: (side(t // 2), side(t)))
    for i in ring.every:
        ring.relay(i, FAR)
        ring.relayed[i, 0].wait_recv()
    attend_all(2, lambda t: (2 * t, 2 - 2 * t))
    for i in ring.every:
        ring.other(i, FAR)
        ring.relayed[i, MINUS].wait_recv()
        ring.relayed[i, PLUS].wait_recv()
    attend_all(
        4,
        lambda t: (
            2 * (t // 2) + side(t) * (1 - t // 2),
            2 * (1 - t // 2) + side(t) * (t // 2),
        ),
    )
    for i in ring.every:
        ring.relayed[i, FAR].wait_recv()
    attend_all(1, lambda t: (t + FAR, t + FAR))

    total = total_ref[0:1, :]
    inverse = 1.0 / total
    for head in range(heads_here):
        rows = pl.ds(head * HEAD_DIM, HEAD_DIM)
        wide_ref[rows, :] = acc[rows, :] * inverse[:, head * group : (head + 1) * group]
    mixed_ref[...] = wide_ref[...].T.astype(BF16)
    lse_ref[...] = jnp.broadcast_to(top_ref[0:1, :] + jnp.log(total), lse_ref.shape)
    part = flat_dot(mixed_ref[...], matrix(3)).astype(BF16)
    part_ref[...] = part.reshape(part_ref.shape)
    for copy in started:
        copy.wait_send()


def attend_call(cid, layer, normed, packed, biases, seg_wide, seg_column):
    group, model = normed.shape
    width = biases.shape[1]
    heads_here = width // HEAD_DIM
    square = (RING, RING, group, width)
    return pl.pallas_call(
        functools.partial(attend_kernel, layer),
        out_shape=[
            jax.ShapeDtypeStruct((group, width), BF16),
            jax.ShapeDtypeStruct(square, BF16),
            jax.ShapeDtypeStruct(square, BF16),
            jax.ShapeDtypeStruct((group, width), BF16),
            jax.ShapeDtypeStruct((width, group), F32),
            jax.ShapeDtypeStruct((8, group * heads_here), F32),
            jax.ShapeDtypeStruct((RING, group // RING, model), BF16),
        ],
        in_specs=[vmem_spec(), any_spec()] + [vmem_spec()] * 3,
        out_specs=[vmem_spec()] * 7,
        scratch_shapes=[
            pltpu.VMEM((RING, RING, group // RING, model), BF16),
            pltpu.VMEM((group * heads_here, width), BF16),
            pltpu.VMEM((width, group), F32),
            pltpu.VMEM((8, group * heads_here), F32),
            pltpu.VMEM((8, group * heads_here), F32),
            pltpu.SemaphoreType.DMA((2, 5, RING)),
            pltpu.SemaphoreType.DMA((2, 5, RING)),
            pltpu.SemaphoreType.DMA,
        ],
        compiler_params=comm_params(cid),
    )(normed, packed, biases, seg_wide, seg_column)


def attend_back_kernel(
    layer, rows_ref, packed_any, q_ref, k_ref, v_ref, wide_ref, lse_ref, seg_q_ref, seg_k_ref,
    triple_ref, sums_ref, part_ref, *scratch,
):
    (
        pack_ref, grad_ref, stack, plain, grad_stack, grad_plain, acc, delta_ref,
        dk_ref, dv_ref, total_ref,
    ) = scratch[:11]
    buffers = scratch[11 : 11 + 2 * SCATTER_BUFFERS]
    send, recv, local = scratch[11 + 2 * SCATTER_BUFFERS :]
    group, width = q_ref.shape
    heads_here = width // HEAD_DIM
    scale = HEAD_DIM ** (-0.5)
    depth = group // RING
    load = pltpu.make_async_copy(packed_any.at[layer, :, :, pl.ds(0, depth)], pack_ref, local)
    load.start()
    matrix = lambda which: pack_ref[:, :, :, which * width : (which + 1) * width].reshape(-1, width)
    rank = lax.axis_index("dp")
    y, z = rank // RING, lax.rem(rank, RING)
    barrier, count = dp_barrier(y, z, None)
    stack[...] = head_stack(q_ref[...], scale)
    plain[...] = head_stack(q_ref[...], 1.0)
    load.wait()
    grad_ref[...] = jnp.dot(rows_ref[...], matrix(3), preferred_element_type=F32).astype(BF16)
    grad_stack[...] = head_stack(grad_ref[...], scale)
    grad_plain[...] = head_stack(grad_ref[...], 1.0)
    acc[...] = jnp.zeros_like(acc)
    seg_wide = jnp.concatenate([seg_q_ref[0:1, :]] * heads_here, axis=1)
    product = grad_ref[...].astype(F32).T * wide_ref[...]
    for head in range(heads_here):
        delta_ref[0:1, pl.ds(head * group, group)] = scale * jnp.sum(
            product[head * HEAD_DIM : (head + 1) * HEAD_DIM], axis=0, keepdims=True
        )
    pl.semaphore_wait(barrier, count)
    started = []
    push = pusher(send, recv, started)
    keys = Scatter(0, True, dk_ref, buffers[:SCATTER_BUFFERS], y, z, push)
    values = Scatter(1, False, dv_ref, buffers[SCATTER_BUFFERS:], y, z, push)

    def attend(offset_y, offset_z):
        at_y, at_z = step(y, offset_y), step(z, offset_z)
        key_block = k_ref[at_y, at_z]
        scores = block_scores(key_block, stack[...], seg_k_ref[at_y, at_z, :, 0:1], seg_wide)
        weights = jnp.exp(scores - lse_ref[0:1, :])
        dv_ref[at_y, at_z] = jnp.dot(
            weights.astype(BF16), grad_plain[...], preferred_element_type=F32
        ).astype(BF16)
        prob_grad = flat_dot(v_ref[at_y, at_z], grad_stack[...])
        low = (weights * (prob_grad - delta_ref[0:1, :])).astype(BF16)
        dk_ref[at_y, at_z] = jnp.dot(low, plain[...], preferred_element_type=F32).astype(BF16)
        turned = key_block.T
        for head in range(heads_here):
            rows = pl.ds(head * HEAD_DIM, HEAD_DIM)
            acc[rows, :] += jnp.dot(
                turned[head * HEAD_DIM : (head + 1) * HEAD_DIM],
                low[:, head * group : (head + 1) * group],
                preferred_element_type=F32,
            )

    def attend_all(first, count, offsets):
        def each(number, carry):
            attend(*offsets(number))
            return carry

        lax.fori_loop(first, count, each, 0)

    attend_all(0, 4, lambda t: (t * 0 + FAR, step(t, FAR)))
    for j in Scatter.ORDER:
        values.send_via(j)
    keys.send_direct(FAR)
    attend_all(1, 4, lambda t: (step(t, FAR), t * 0 + FAR))
    for j in Scatter.ORDER:
        keys.send_via(j)
    values.send_direct(FAR)
    attend_all(1, 4, lambda t: (t * 0 + PLUS, step(t, FAR)))
    keys.send_direct(PLUS)
    values.send_direct(PLUS)
    values.send_direct(MINUS)
    attend_all(1, 4, lambda t: (t * 0 + MINUS, step(t, FAR)))
    keys.send_direct(MINUS)
    values.send_direct(0)
    values.join()
    for j in (FAR, PLUS, MINUS):
        keys.join_one(j)
    attend_all(1, 4, lambda t: (t * 0, step(t, FAR)))
    keys.send_direct(0)
    keys.join_one(0)
    values.turn()
    keys.turn()
    values.join_two()
    keys.join_two()
    sums_ref[...] = jnp.zeros_like(sums_ref)
    query_grad = acc[...].T
    sums_ref[0:1, :] = jnp.sum(query_grad, axis=0, keepdims=True)
    triple_ref[0] = query_grad.astype(BF16)
    part = flat_dot(triple_ref[0], matrix(0))
    values.finish(total_ref)
    triple_ref[2] = total_ref[...].astype(BF16)
    sums_ref[1:2, :] = jnp.sum(total_ref[...], axis=0, keepdims=True)
    part = part + flat_dot(triple_ref[2], matrix(2))
    keys.finish(total_ref)
    triple_ref[1] = total_ref[...].astype(BF16)
    part = part + flat_dot(triple_ref[1], matrix(1))
    part_ref[...] = part.astype(BF16).reshape(part_ref.shape)
    for copy in started:
        copy.wait_send()


def attend_back_call(cid, layer, attn_rows, packed, queries, keys, values, wide, lse, seg_wide, seg_column):
    group, model = attn_rows.shape
    width = queries.shape[1]
    heads_here = width // HEAD_DIM
    block = (group, width)
    stacked = pltpu.VMEM((group * heads_here, width), BF16)
    return pl.pallas_call(
        functools.partial(attend_back_kernel, layer),
        out_shape=[
            jax.ShapeDtypeStruct((3, group, width), BF16),
            jax.ShapeDtypeStruct((8, width), F32),
            jax.ShapeDtypeStruct((RING, group // RING, model), BF16),
        ],
        in_specs=[vmem_spec(), any_spec()] + [vmem_spec()] * 7,
        out_specs=[vmem_spec()] * 3,
        scratch_shapes=[
            pltpu.VMEM((RING, RING, group // RING, model), BF16),
            pltpu.VMEM(block, BF16),
            stacked,
            stacked,
            stacked,
            stacked,
            pltpu.VMEM((width, group), F32),
            pltpu.VMEM((8, group * heads_here), F32),
            pltpu.VMEM((RING, RING) + block, BF16),
            pltpu.VMEM((RING, RING) + block, BF16),
            pltpu.VMEM(block, F32),
        ]
        + Scatter.scratch(block, BF16)
        + Scatter.scratch(block, BF16)
        + [
            pltpu.SemaphoreType.DMA((2, 6, RING)),
            pltpu.SemaphoreType.DMA((2, 6, RING)),
            pltpu.SemaphoreType.DMA,
        ],
        compiler_params=comm_params(cid),
    )(attn_rows, packed, queries, keys, values, wide, lse, seg_wide, seg_column)


def shards(tokens, segment_ids, w_qkv, w_out, w_up, w_down, vectors, out_bias, cotangent):
    section = lax.axis_index("section")
    tensor_rank = lax.axis_index("tensor")
    own = lambda pair: jnp.where(section == 0, pair[0], pair[1])
    rows = tokens.shape[1]
    width = tokens.shape[2]
    group = rows * RING
    square = (RING, RING)
    local_width = w_qkv.shape[3]
    local_hidden = w_up.shape[2]

    depth = w_out.shape[1]
    my_segments = own(segment_ids)
    wide_segments = jnp.pad(my_segments, (0, depth - rows)).astype(BF16)[None]
    small = jnp.pad(
        jnp.concatenate([vectors[0], out_bias, wide_segments], axis=0),
        ((0, 1), (0, 128 - depth)),
    )
    packed, small_all, small_rows = first_call(0, w_qkv[0], w_out[0], w_up[0], w_down[0], small)
    matrix = lambda layer, number: packed[
        layer, :, :, number * depth : (number + 1) * depth
    ].reshape(width, local_hidden)
    full_up = [matrix(layer, 1) for layer in range(2)]
    full_down = [matrix(layer, 2) for layer in range(2)]

    my_tokens = own(tokens)
    my_cotangent = own(cotangent)
    seg_mine = own(small_all)[:, :, 14, :rows].astype(jnp.int32).reshape(8, 128)
    normed, seg_group = tensor_call(
        1, first_rows, None, [my_tokens], [small_rows[0]], [], 0, True, seg_mine
    )
    seg_all = seg_group.reshape(RING, RING * RING, rows).transpose(1, 0, 2).reshape(-1, group)
    seg_rows = lax.dynamic_index_in_dim(seg_all, lax.axis_index("dp"), 0, keepdims=False)
    seg_wide = jnp.broadcast_to(seg_rows[None], (8, group))
    seg_column = jnp.broadcast_to(seg_all.reshape(*square, group)[..., None], square + (group, 128))
    inputs = my_tokens
    kept = []
    for layer in range(2):
        vec = small_rows[layer]
        normed = normed.reshape(group, width)
        query_bias = lax.dynamic_slice_in_dim(vec[2], tensor_rank * local_width, local_width)
        value_bias = lax.dynamic_slice_in_dim(vec[3], tensor_rank * local_width, local_width)
        up_bias = lax.dynamic_slice_in_dim(
            vec[9:13].reshape(-1), tensor_rank * local_hidden, local_hidden
        )
        biases = jnp.pad(jnp.stack([query_bias, value_bias]), ((0, 6), (0, 0)))
        queries, keys_full, values_full, mixed, wide, lse, part = attend_call(
            2 + 12 * layer, layer, normed, packed, biases, seg_wide, seg_column
        )
        attn_out, hidden, normed_two = tensor_call(
            3, middle_rows, part, [inputs.astype(F32)], [vec], [F32, F32], 0, True
        )
        normed_two = normed_two.reshape(group, width)
        pre_act = jnp.dot(normed_two, full_up[layer], preferred_element_type=F32) + up_bias
        activated = gelu_exact(pre_act).astype(BF16)
        part = flat_dot(activated, full_down[layer]).astype(BF16).reshape(RING, rows, width)
        step_kept = [inputs, normed, queries, keys_full, values_full, mixed, attn_out, hidden]
        step_kept += [normed_two, pre_act, activated, wide, lse]
        if layer == 0:
            mlp_first, between, normed = tensor_call(
                4, end_rows_first, part, [hidden], [vec, small_rows[1]], [F32, BF16], 0, True
            )
            inputs = between
        else:
            outputs, sums_end, mlp_rows = tensor_call(
                5, end_rows_last, part, [hidden, my_cotangent], [vec], [BF16], 2, True
            )
        kept.append(step_kept)

    upstream = my_cotangent.astype(F32)
    blocks = lambda value: value.astype(BF16).reshape(*square, depth, value.shape[-1])
    sums, grads = [None, None], [None, None]
    for layer in (1, 0):
        vec = small_rows[layer]
        inputs, normed, queries, keys_full, values_full, mixed, attn_out, hidden = kept[layer][:8]
        normed_two, pre_act, activated, wide, lse = kept[layer][8:]
        mlp_rows = mlp_rows.reshape(group, width)
        act_grad = jnp.dot(mlp_rows, full_down[layer], preferred_element_type=F32)
        grad_down = blocks(rows_dot(mlp_rows, activated))
        pre_grad = jax.vjp(gelu_exact, pre_act)[1](act_grad)[0]
        up_bias_grad = jnp.broadcast_to(jnp.sum(pre_grad, axis=0)[None], (8, local_hidden))
        pre_low = pre_grad.astype(BF16)
        grad_up = blocks(rows_dot(normed_two, pre_low))
        part = flat_dot(pre_low, full_up[layer]).astype(BF16).reshape(RING, rows, width)
        hidden_grad, sums_middle, attn_rows = tensor_call(
            6, back_middle_rows, part, [upstream, hidden, attn_out], [vec], [F32], 4, True
        )
        attn_rows = attn_rows.reshape(group, width)
        grad_out = blocks(rows_dot(attn_rows, mixed))
        triple, sums_attend, part = attend_back_call(
            7 + 12 * layer, layer, attn_rows, packed, queries, keys_full, values_full,
            wide, lse, seg_wide, seg_column,
        )
        grads[layer] = [blocks(rows_dot(normed, triple[which])) for which in range(3)]
        grads[layer] += [grad_out, grad_up, grad_down]
        if layer == 1:
            input_grad, sums_last, mlp_rows = tensor_call(
                8,
                back_end_rows_last,
                part,
                [hidden_grad, inputs.astype(F32), mlp_first],
                [vec, small_rows[0]],
                [F32],
                4,
                True,
            )
        else:
            input_grad, sums_last = tensor_call(
                9, back_end_rows_first, part, [hidden_grad, inputs.astype(F32)], [vec], [F32], 2, False
            )
        sums[layer] = [sums_last, sums_middle, sums_end, sums_attend, up_bias_grad]
        if layer == 1:
            last_grad = input_grad
            upstream = input_grad.astype(BF16).astype(F32)
            sums_end = sums_last[2:]
    first_grad = input_grad

    extras = [
        jnp.where(section == 0, outputs, between),
        jnp.where(section == 0, last_grad, first_grad),
    ]
    small_sum, packed_sum, came_out, came_grad = final_call(
        10, sums[0] + sums[1], grads[0] + grads[1], extras
    )
    mine_out = jnp.where(section == 0, between, outputs)
    mine_grad = jnp.where(section == 0, first_grad, last_grad)
    pair = lambda mine, came: jnp.where(
        section == 0, jnp.stack([mine, came]), jnp.stack([came, mine])
    )[None]
    half = depth // 2
    columns = lambda which: packed_sum[
        :, :half, which * local_width : (which + 1) * local_width
    ].reshape(depth, local_width)
    return (
        pair(mine_out, came_out),
        pair(mine_grad, came_grad),
        jnp.stack([columns(0), columns(1), columns(2)])[None],
        columns(3)[None],
        packed_sum[:, half : 2 * half].reshape(1, depth, local_hidden),
        packed_sum[:, 2 * half :].reshape(1, depth, local_hidden),
        small_sum[:13, :depth][None],
        small_sum[13:14, :depth],
    )


def solution(mesh):
    in_specs = (
        P(None, ("dp", "tensor"), None),
        P(None, ("dp", "tensor")),
        P("section", None, "dp", "tensor"),
        P("section", "dp", "tensor"),
        P("section", "dp", "tensor"),
        P("section", "dp", "tensor"),
        P("section", None, "dp"),
        P("section", "dp"),
        P(None, ("dp", "tensor"), None),
    )
    out_specs = (
        P("section", None, ("dp", "tensor"), None),
        P("section", None, ("dp", "tensor"), None),
        P("section", None, "dp", "tensor"),
        P("section", "dp", "tensor"),
        P("section", "dp", "tensor"),
        P("section", "dp", "tensor"),
        P("section", None, "dp"),
        P("section", "dp"),
    )
    return jax.shard_map(shards, mesh=mesh, in_specs=in_specs, out_specs=out_specs, check_vma=False)
```

```python
import functools
from types import SimpleNamespace

import jax
import jax.numpy as jnp
from jax import lax
from jax.experimental import pallas as pl
from jax.experimental.pallas import tpu as pltpu
from jax.sharding import PartitionSpec as P

MESH = pl.DeviceIdType.MESH
HEAD_DIM = 64
EPSILON = 1e-06
MASKED_SCORE = -1e30
RING = 4
VMEM_LIMIT = 56 * 1024 * 1024
F32 = jnp.float32
BF16 = jnp.bfloat16


def vmem_spec():
    return pl.BlockSpec(memory_space=pltpu.VMEM)


def any_spec():
    return pl.BlockSpec(memory_space=pl.ANY)


def comm_params(cid):
    return pltpu.CompilerParams(
        collective_id=cid, has_side_effects=True, vmem_limit_bytes=VMEM_LIMIT
    )


def step(coord, by):
    return lax.rem(coord + by, RING)


def layer_norm(values, gain_row, shift_row):
    centre = values - jnp.mean(values, axis=-1, keepdims=True)
    spread = jnp.mean(centre * centre, axis=-1, keepdims=True)
    return centre * lax.rsqrt(spread + EPSILON) * gain_row + shift_row


def layer_norm_back(values, gain_row, grad):
    centre = values - jnp.mean(values, axis=-1, keepdims=True)
    spread = jnp.mean(centre * centre, axis=-1, keepdims=True)
    inverse = lax.rsqrt(spread + EPSILON)
    normed = centre * inverse
    scaled = grad * gain_row
    back = inverse * (
        scaled
        - jnp.mean(scaled, axis=-1, keepdims=True)
        - normed * jnp.mean(scaled * normed, axis=-1, keepdims=True)
    )
    return back, jnp.sum(grad * normed, axis=0, keepdims=True), jnp.sum(grad, axis=0, keepdims=True)


PLUS, FAR, MINUS = 1, 2, 3
CHUNKS = 2


def tensor_barrier(me):
    barrier = pltpu.get_barrier_semaphore()
    for k in range(1, RING):
        pl.semaphore_signal(
            barrier, inc=1, device_id={"tensor": step(me, k)}, device_id_type=MESH
        )
    return barrier, RING - 1


def tensor_kernel(function, n_rows, n_vecs, n_out, n_sums, reduce, gather, with_seg, *refs):
    refs = list(refs)
    take = lambda count: [refs.pop(0) for _ in range(count)]
    part = take(1)[0] if reduce else None
    rows_in = take(n_rows)
    vecs = take(n_vecs)
    seg_in = take(1)[0] if with_seg else None
    rows_out = take(n_out)
    sums_out = take(1)[0] if n_sums else None
    full = take(1)[0] if gather else None
    seg_out = take(1)[0] if with_seg else None
    landing = take(1)[0] if reduce else None
    send, recv, local = take(3)

    me = lax.axis_index("tensor")
    barrier, count = tensor_barrier(me)
    pl.semaphore_wait(barrier, count)

    chunk = rows_in[0].shape[0] // CHUNKS
    started = []

    def push(source, target, kind, index, k):
        copy = pltpu.make_async_remote_copy(
            src_ref=source,
            dst_ref=target,
            send_sem=send.at[kind, index, k - 1],
            recv_sem=recv.at[kind, index, k - 1],
            device_id={"tensor": step(me, k)},
            device_id_type=MESH,
        )
        copy.start()
        started.append(copy)
        return copy

    reduces = {}
    if reduce:
        for c in range(CHUNKS):
            here = pl.ds(c * chunk, chunk)
            for k in range(1, RING):
                reduces[c, k] = push(
                    part.at[step(me, k), here], landing.at[k - 1, here], 0, c, k
                )
    last = []
    if with_seg:
        own = pltpu.make_async_copy(seg_in, seg_out.at[me], local)
        own.start()
        last += [push(seg_in, seg_out.at[me], 2, 0, k) for k in range(1, RING)]
    sums = [None] * n_sums
    for c in range(CHUNKS):
        here = pl.ds(c * chunk, chunk)
        total = None
        if reduce:
            for k in range(1, RING):
                reduces[c, k].wait_recv()
            total = part[me, here].astype(F32)
            for k in range(1, RING):
                total = total + landing[k - 1, here].astype(F32)
        spread, outs, parts = function(
            total, [ref[here].astype(F32) for ref in rows_in], vecs
        )
        if gather:
            full[me, here] = spread.astype(BF16)
            last += [push(full.at[me, here], full.at[me, here], 1, c, k) for k in range(1, RING)]
        for ref, value in zip(rows_out, outs):
            ref[here] = value.astype(ref.dtype)
        sums = [new if old is None else old + new for old, new in zip(sums, parts)]
    if n_sums:
        sums_out[...] = jnp.concatenate(
            sums + [jnp.zeros((8 - n_sums, sums[0].shape[1]), F32)], axis=0
        )
    for copy in last:
        copy.wait_recv()
    if with_seg:
        own.wait()
    for copy in started:
        copy.wait_send()


def tensor_call(cid, function, part, rows, vecs, outs, n_sums, gather, seg=None):
    height, width = rows[0].shape
    reduce = part is not None
    with_seg = seg is not None
    args = ([part] if reduce else []) + list(rows) + list(vecs) + ([seg] if with_seg else [])
    shapes = [jax.ShapeDtypeStruct((height, width), dtype) for dtype in outs]
    if n_sums:
        shapes.append(jax.ShapeDtypeStruct((8, width), F32))
    if gather:
        shapes.append(jax.ShapeDtypeStruct((RING, height, width), BF16))
    if with_seg:
        shapes.append(jax.ShapeDtypeStruct((RING,) + seg.shape, seg.dtype))
    in_specs, out_specs = [vmem_spec()] * len(args), [vmem_spec()] * len(shapes)
    scratch = [pltpu.VMEM((RING - 1, height, width), BF16)] if reduce else []
    scratch += [
        pltpu.SemaphoreType.DMA((3, CHUNKS, RING - 1)),
        pltpu.SemaphoreType.DMA((3, CHUNKS, RING - 1)),
        pltpu.SemaphoreType.DMA,
    ]
    return pl.pallas_call(
        functools.partial(
            tensor_kernel, function, len(rows), len(vecs), len(outs), n_sums, reduce, gather, with_seg,
        ),
        out_shape=shapes,
        in_specs=in_specs,
        out_specs=out_specs,
        scratch_shapes=scratch,
        compiler_params=comm_params(cid),
    )(*args)


def row(ref, index):
    return ref[pl.ds(index, 1), :]


def first_rows(total, rows, vecs):
    return layer_norm(rows[0], row(vecs[0], 0), row(vecs[0], 1)), [], []


def middle_rows(total, rows, vecs):
    vec = vecs[0]
    attn_out = total + row(vec, 13)
    hidden = rows[0] + row(vec, 4) * attn_out
    return layer_norm(hidden, row(vec, 5), row(vec, 6)), [attn_out, hidden], []


def end_rows_first(total, rows, vecs):
    vec, after = vecs
    mlp_out = total + row(vec, 7)
    outputs = (rows[0] + row(vec, 8) * mlp_out).astype(BF16)
    inputs = outputs.astype(F32)
    return layer_norm(inputs, row(after, 0), row(after, 1)), [mlp_out, outputs], []


def end_rows_last(total, rows, vecs):
    vec = vecs[0]
    hidden, upstream = rows
    mlp_out = total + row(vec, 7)
    outputs = hidden + row(vec, 8) * mlp_out
    mlp_grad = row(vec, 8) * upstream
    sums = [
        jnp.sum(upstream * mlp_out, axis=0, keepdims=True),
        jnp.sum(mlp_grad, axis=0, keepdims=True),
    ]
    return mlp_grad, [outputs], sums


def back_middle_rows(total, rows, vecs):
    vec = vecs[0]
    upstream, hidden, attn_out = rows
    part, gain, shift = layer_norm_back(hidden, row(vec, 5), total)
    hidden_grad = upstream + part
    attn_grad = row(vec, 4) * hidden_grad
    sums = [
        gain,
        shift,
        jnp.sum(hidden_grad * attn_out, axis=0, keepdims=True),
        jnp.sum(attn_grad, axis=0, keepdims=True),
    ]
    return attn_grad, [hidden_grad], sums


def back_end_rows_last(total, rows, vecs):
    vec, before = vecs
    hidden_grad, inputs, mlp_out = rows
    part, gain, shift = layer_norm_back(inputs, row(vec, 0), total)
    input_grad = hidden_grad + part
    upstream = input_grad.astype(BF16).astype(F32)
    mlp_grad = row(before, 8) * upstream
    sums = [
        gain,
        shift,
        jnp.sum(upstream * mlp_out, axis=0, keepdims=True),
        jnp.sum(mlp_grad, axis=0, keepdims=True),
    ]
    return mlp_grad, [input_grad], sums


def back_end_rows_first(total, rows, vecs):
    hidden_grad, inputs = rows
    part, gain, shift = layer_norm_back(inputs, row(vecs[0], 0), total)
    return None, [hidden_grad + part], [gain, shift]


def dp_neighbour(y, z, along_z, k):
    if along_z:
        return {"dp": y * RING + step(z, k)}
    return {"dp": step(y, k) * RING + z}


def dp_barrier(y, z, section):
    barrier = pltpu.get_barrier_semaphore()
    count = 0
    for along_z in (True, False):
        for k in (PLUS, MINUS):
            pl.semaphore_signal(
                barrier, inc=1, device_id=dp_neighbour(y, z, along_z, k), device_id_type=MESH
            )
            count += 1
    if section is not None:
        pl.semaphore_signal(
            barrier, inc=1, device_id={"section": 1 - section}, device_id_type=MESH
        )
        count += 1
    return barrier, count


def pusher(send, recv, started):
    def push(index, kind, k, source, target, device):
        copy = pltpu.make_async_remote_copy(
            src_ref=source,
            dst_ref=target,
            send_sem=send.at[index, kind, k],
            recv_sem=recv.at[index, kind, k],
            device_id=device,
            device_id_type=MESH,
        )
        copy.start()
        started.append(copy)
        return copy

    return push


class Gather:
    WAYS = {0: 1, 3: 1, 1: 1, 2: 3}

    def __init__(self, pieces, outs, y, z, lead, push):
        self.pieces, self.outs, self.y, self.z = pieces, outs, y, z
        self.lead, self.push = lead, push
        self.every = range(len(pieces))
        self.first, self.onward, self.second, self.relayed = {}, {}, {}, {}

    def block(self, i, along, across, rows=None):
        number, pre, along_z = self.pieces[i]
        ys, zs = (across, along) if along_z else (along, across)
        ys = ys if isinstance(ys, slice) else step(self.y, ys) if ys else self.y
        zs = zs if isinstance(zs, slice) else step(self.z, zs) if zs else self.z
        return self.outs[number].at[self.lead + pre + (ys, zs) + (() if rows is None else (rows,))]

    def way(self, i, first, k):
        return dp_neighbour(self.y, self.z, self.pieces[i][2] == first, k)

    def halves(self, i):
        height = self.outs[self.pieces[i][0]].shape[-2]
        if height < 32:
            return {PLUS: None}
        half = height // 32 * 16
        return {PLUS: pl.ds(0, half), MINUS: pl.ds(half, height - half)}

    def spread(self, i, offset, source):
        for k in (PLUS, MINUS):
            self.second[i, offset, k] = self.push(
                i, 2 if k == PLUS else 3, offset, source, self.block(i, offset, 0), self.way(i, False, k)
            )

    def begin(self, i, source):
        for k in (PLUS, MINUS):
            self.first[i, k] = self.push(i, 0, k, source, self.block(i, 0, 0), self.way(i, True, k))
        self.spread(i, 0, source)

    def near(self):
        for i in self.every:
            split = self.halves(i)
            for k in (PLUS, MINUS):
                self.first[i, k].wait_recv()
                came = RING - k
                if k in split:
                    self.onward[i, k] = self.push(
                        i, 1, k, self.block(i, came, 0, split[k]), self.block(i, came, 0, split[k]),
                        self.way(i, True, k),
                    )
                self.spread(i, came, self.block(i, came, 0))

    def relay(self, i, offset):
        k = self.WAYS[offset]
        self.second[i, offset, k].wait_recv()
        came = self.block(i, offset, RING - k)
        self.relayed[i, offset] = self.push(i, 4, offset, came, came, self.way(i, False, k))

    def other(self, i, offset):
        self.second[i, offset, RING - self.WAYS[offset]].wait_recv()

    def far(self, i):
        for k in self.halves(i):
            self.onward[i, k].wait_recv()
        self.spread(i, FAR, self.block(i, FAR, 0))


def half_of(section, height):
    return pl.ds(pl.multiple_of(section * height, height), height)


def spread_stages(ring, sources, local, section, push):
    own, across = {}, []

    def pass_on(i, line):
        came = ring.block(i, slice(None), line)
        across.append(push(i, 5, line, came, came, {"section": 1 - section}))

    def begin():
        for i in ring.every:
            ring.begin(i, sources[i])
            own[i] = pltpu.make_async_copy(sources[i], ring.block(i, 0, 0), local.at[i])
            own[i].start()

    def near():
        ring.near()
        for i in ring.every:
            ring.relay(i, 0)

    def middle():
        for i in ring.every:
            ring.far(i)
        for i in ring.every:
            ring.relay(i, MINUS)
            ring.relay(i, PLUS)
            own[i].wait()
            pass_on(i, 0)

    def end():
        for i in ring.every:
            ring.relay(i, FAR)
            for offset in range(RING):
                ring.other(i, offset)
            pass_on(i, PLUS)
            pass_on(i, MINUS)

    def last():
        for i in ring.every:
            for offset in range(RING):
                ring.relayed[i, offset].wait_recv()
            pass_on(i, FAR)
        for copy in across:
            copy.wait_recv()

    return [begin, near, middle, end, last]


HALF_ROWS = 96
SMALL = 16


def half_places(half, width, hidden):
    return [(0, which * width, width) for which in range(4)] + [
        (half, 0, hidden),
        (2 * half, 0, hidden),
    ]


def first_kernel(
    qkv_in, out_in, up_in, down_in, small_in, packed_out, stage, small_all, rows_out,
    send, recv, local, swap_send, swap_recv, swap_local, last_local,
):
    rank = lax.axis_index("dp")
    y, z = rank // RING, lax.rem(rank, RING)
    section = lax.axis_index("section")
    barrier, count = dp_barrier(y, z, section)
    depth, width = out_in.shape
    half = depth // 2
    mine, others = half_of(section, half), half_of(1 - section, half)
    sources = [qkv_in.at[which] for which in range(3)] + [out_in, up_in, down_in]
    places = half_places(half, width, stage.shape[2])
    tail = pl.ds(HALF_ROWS, SMALL)
    stage[0, tail] = jnp.zeros((SMALL, stage.shape[2]), BF16)
    stage[1, tail] = jnp.zeros((SMALL, stage.shape[2]), BF16)
    kept = [
        pltpu.make_async_copy(
            small_in, stage.at[0, tail, pl.ds(0, small_in.shape[1])], swap_local.at[len(places)]
        )
    ]
    kept[0].start()
    pl.semaphore_wait(barrier, count)
    started = []
    push = pusher(send, recv, started)
    swaps = []
    for i, (source, (row, column, columns)) in enumerate(zip(sources, places)):
        target = stage.at[section, pl.ds(row, half), pl.ds(column, columns)]
        copy = pltpu.make_async_remote_copy(
            src_ref=source.at[others],
            dst_ref=target,
            send_sem=swap_send.at[i],
            recv_sem=swap_recv.at[i],
            device_id={"section": 1 - section},
            device_id_type=MESH,
        )
        copy.start()
        swaps.append(copy)
        copy = pltpu.make_async_copy(source.at[mine], target, swap_local.at[i])
        copy.start()
        kept.append(copy)
    for copy in kept:
        copy.wait()
    for copy in swaps:
        copy.wait_recv()
    low, high = pl.ds(0, HALF_ROWS // 2), pl.ds(HALF_ROWS // 2, HALF_ROWS // 2 + SMALL)
    views = [packed_out.at[section, :, :, low], packed_out.at[section, :, :, high]]
    ring = Gather(((0, (), True), (1, (), False)), views, y, z, (), push)
    for each in spread_stages(ring, [stage.at[0, low], stage.at[0, high]], local, section, push):
        each()
    last = pltpu.make_async_copy(
        packed_out.at[:, :, :, tail, pl.ds(0, small_in.shape[1])], small_all, last_local
    )
    last.start()
    last.wait()
    for layer in range(2):
        for number in range(RING * RING):
            part = small_all[layer, number // RING, number % RING]
            rows_out[layer, :, number * depth : (number + 1) * depth] = part[:, :depth].astype(F32)
    for copy in started + swaps:
        copy.wait_send()


def gather_scratch():
    return [
        pltpu.SemaphoreType.DMA((2, 6, RING)),
        pltpu.SemaphoreType.DMA((2, 6, RING)),
        pltpu.SemaphoreType.DMA((2,)),
    ]


def first_call(cid, w_qkv, w_out, w_up, w_down, small):
    depth = w_out.shape[0]
    hidden = w_up.shape[1]
    return pl.pallas_call(
        first_kernel,
        out_shape=[
            jax.ShapeDtypeStruct((2, RING, RING, HALF_ROWS + SMALL, hidden), BF16),
            jax.ShapeDtypeStruct((2, HALF_ROWS + SMALL, hidden), BF16),
            jax.ShapeDtypeStruct((2, RING, RING) + small.shape, BF16),
            jax.ShapeDtypeStruct((2, SMALL, RING * RING * depth), F32),
        ],
        in_specs=[vmem_spec()] * 5,
        out_specs=[any_spec(), vmem_spec(), vmem_spec(), vmem_spec()],
        scratch_shapes=gather_scratch()
        + [
            pltpu.SemaphoreType.DMA((6,)),
            pltpu.SemaphoreType.DMA((6,)),
            pltpu.SemaphoreType.DMA((7,)),
            pltpu.SemaphoreType.DMA,
        ],
        compiler_params=comm_params(cid),
    )(w_qkv, w_out, w_up, w_down, small)


class Scatter:
    ORDER = (FAR, PLUS, MINUS, 0)
    WAYS = {FAR: PLUS, 0: PLUS, PLUS: MINUS, MINUS: MINUS}

    def __init__(self, index, along_z, source, buffers, y, z, push):
        self.index, self.along_z, self.source = index, along_z, source
        self.passing, self.joined, self.summed, self.straight, self.middle = buffers[:5]
        self.far_two, self.joined_two, self.summed_two, self.straight_two = buffers[5:]
        self.y, self.z, self.push = y, z, push
        self.height, self.width = source.shape[-2:]
        self.via, self.direct, self.after = {}, {}, {}

    def at(self, along, across):
        ys, zs = (across, along) if self.along_z else (along, across)
        return step(self.y, ys), step(self.z, zs)

    def way(self, first, k):
        return dp_neighbour(self.y, self.z, self.along_z == first, k)

    def add(self, target, terms, top=0, height=None):
        height = self.height if height is None else height
        size = max(8, min(height, 65536 // self.width))
        while height % size:
            size -= 16

        def part(here):
            value = terms[0](here).astype(F32)
            for term in terms[1:]:
                value = value + term(here).astype(F32)
            target[here] = value.astype(target.dtype)

        if height <= size:
            part(pl.ds(top, height))
            return

        def each(number, carry):
            part(pl.ds(pl.multiple_of(top + number * size, size), size))
            return carry

        lax.fori_loop(0, height // size, each, 0)

    def send_via(self, j):
        self.via[j] = self.push(
            self.index, 0, j, self.source.at[self.at(FAR, j)], self.passing.at[j],
            self.way(True, self.WAYS[j]),
        )

    def send_direct(self, j):
        k = RING - self.WAYS[j]
        self.direct[j] = self.push(
            self.index, 1, j, self.source.at[self.at(k, j)], self.straight.at[j], self.way(True, k)
        )

    def begin(self):
        for j in self.ORDER:
            self.send_via(j)
        for j in self.ORDER:
            self.send_direct(j)

    def join_one(self, j):
        self.via[j].wait_recv()
        k = self.WAYS[j]
        at_y, at_z = self.at(k, j)
        self.add(
            self.joined.at[j],
            [lambda h: self.source[at_y, at_z, h], lambda h: self.passing[j, h]],
        )
        self.after[j] = self.push(
            self.index, 2, j, self.joined.at[j], self.summed.at[j], self.way(True, k)
        )

    def join(self):
        for j in self.ORDER:
            self.join_one(j)

    def turn(self):
        half = self.height // 2
        low, high = pl.ds(0, half), pl.ds(half, half)
        send = lambda kind, slot, source, target, k: self.push(
            self.index, kind, slot, source, target, self.way(False, k)
        )
        for j in self.ORDER:
            self.direct[j].wait_recv()
            self.after[j].wait_recv()
            at_y, at_z = self.at(0, j)
            self.add(
                self.middle.at[j],
                [
                    lambda h: self.source[at_y, at_z, h],
                    lambda h: self.summed[j, h],
                    lambda h: self.straight[j, h],
                ],
            )
            if j == FAR:
                self.via_two = [
                    send(3, 0, self.middle.at[j, low], self.far_two.at[low], PLUS),
                    send(3, 1, self.middle.at[j, high], self.far_two.at[high], MINUS),
                ]
            if j == PLUS:
                high_copy = send(4, 1, self.middle.at[j, high], self.straight_two.at[high], PLUS)
            if j == MINUS:
                low_copy = send(4, 0, self.middle.at[j, low], self.straight_two.at[low], MINUS)
        self.direct_two = [low_copy, high_copy]

    def join_two(self):
        half = self.height // 2
        self.after_two = []
        for number, (top, k) in enumerate(((0, PLUS), (half, MINUS))):
            self.via_two[number].wait_recv()
            self.add(
                self.joined_two,
                [lambda h: self.middle[k, h], lambda h: self.far_two[h]],
                top,
                half,
            )
            here = pl.ds(top, half)
            self.after_two.append(
                self.push(
                    self.index, 5, number, self.joined_two.at[here], self.summed_two.at[here],
                    self.way(False, k),
                )
            )

    def finish(self, out):
        for copy in self.direct_two + self.after_two:
            copy.wait_recv()
        self.add(
            out,
            [
                lambda h: self.middle[0, h],
                lambda h: self.summed_two[h],
                lambda h: self.straight_two[h],
            ],
        )

    @staticmethod
    def scratch(block, dtype):
        return [pltpu.VMEM((RING,) + block, dtype)] * 5 + [pltpu.VMEM(block, dtype)] * 4


SCATTER_BUFFERS = 9


def scatter_buffers(block, dtype):
    square = pltpu.VMEM((RING, RING) + block, dtype)
    return [square, square] + Scatter.scratch(block, dtype)


class LayerGradients:
    def __init__(self, grads, buffers, semaphores, y, z, section, push):
        self.grads, self.buffers, self.y, self.z = grads, buffers, y, z
        self.section, self.push = section, push
        self.swap_send, self.swap_recv, self.keep_local = semaphores
        depth, width = grads[0].shape[2:]
        hidden = grads[5].shape[3]
        self.half = depth // 2
        self.places = [(0, 0, which * width, width) for which in range(4)]
        self.places += [(1, 0, 0, hidden), (1, self.half, 0, hidden)]

    def region(self, which, place):
        piece, row, column, columns = place
        return self.buffers[piece][which].at[:, :, pl.ds(row, self.half), pl.ds(column, columns)]

    def keep(self):
        mine = half_of(self.section, self.half)
        self.keeps = []
        for i, place in enumerate(self.places):
            copy = pltpu.make_async_copy(
                self.grads[i].at[:, :, mine], self.region(0, place), self.keep_local.at[i]
            )
            copy.start()
            self.keeps.append(copy)

    def swap(self):
        others = half_of(1 - self.section, self.half)
        self.swaps = []
        for i, place in enumerate(self.places):
            copy = pltpu.make_async_remote_copy(
                src_ref=self.grads[i].at[:, :, others],
                dst_ref=self.region(1, place),
                send_sem=self.swap_send.at[i],
                recv_sem=self.swap_recv.at[i],
                device_id={"section": 1 - self.section},
                device_id_type=MESH,
            )
            copy.start()
            self.swaps.append(copy)

    def begin(self):
        self.parts = []
        for piece in range(2):
            for i, place in enumerate(self.places):
                if place[0] == piece:
                    self.keeps[i].wait()
                    self.swaps[i].wait_recv()
            own, sibling = self.buffers[piece][:2]
            add_blocks(own, own, sibling)
            self.parts.append(
                Scatter(piece, piece == 0, own, self.buffers[piece][2:], self.y, self.z, self.push)
            )
            self.parts[piece].begin()

    def join(self):
        for part in self.parts:
            part.join()

    def turn(self):
        for part in self.parts:
            part.turn()

    def join_two(self):
        for part in self.parts:
            part.join_two()

    def finish(self, out):
        self.parts[0].finish(out.at[pl.ds(0, self.half)])
        self.parts[1].finish(out.at[pl.ds(self.half, 2 * self.half)])

    def end(self):
        for copy in self.swaps:
            copy.wait_send()

    @staticmethod
    def scratch(half, hidden):
        return (
            scatter_buffers((half, hidden), BF16)
            + scatter_buffers((2 * half, hidden), BF16)
            + [pltpu.SemaphoreType.DMA((6,))] * 3
            + [pltpu.SemaphoreType.DMA((3, 7, RING))] * 2
        )


LAYER_SCRATCH = 2 * (2 + SCATTER_BUFFERS) + 5


def layer_gradients(grads, scratch, y, z, section, started):
    size = 2 + SCATTER_BUFFERS
    push = pusher(scratch[-2], scratch[-1], started)
    return LayerGradients(
        grads, [scratch[:size], scratch[size : 2 * size]], scratch[2 * size : 2 * size + 3],
        y, z, section, push,
    )


def add_blocks(out, former, latter):
    def add(number, carry):
        at_y, at_z = number // RING, lax.rem(number, RING)
        out[at_y, at_z] = (
            former[at_y, at_z].astype(F32) + latter[at_y, at_z].astype(F32)
        ).astype(out.dtype)
        return carry

    lax.fori_loop(0, RING * RING, add, 0)


def final_kernel(n_extra, *refs):
    refs = list(refs)
    take = lambda count: [refs.pop(0) for _ in range(count)]
    sums = [take(5), take(5)]
    grads, summed_last = take(6), take(1)[0]
    extras = take(n_extra)
    small_out, packed_out = take(2)
    extra_outs = take(n_extra)
    small_in, small_rows, vector_own, vector_parts, summed = take(5)
    small_buffers = take(2 + SCATTER_BUFFERS)
    layer_scratch = take(LAYER_SCRATCH)
    vector_send, vector_recv, extra_send, extra_recv, result_send, result_recv, result_local, hand_local = take(8)
    rank = lax.axis_index("dp")
    y, z = rank // RING, lax.rem(rank, RING)
    section = lax.axis_index("section")
    me = lax.axis_index("tensor")
    other = {"section": 1 - section}
    barrier, count = tensor_barrier(me)
    count += dp_barrier(y, z, section)[1]

    started = []
    first_layer = layer_gradients(grads, layer_scratch, y, z, section, started)
    push = first_layer.push
    first_layer.keep()
    handed = pltpu.make_async_copy(summed_last, summed.at[1], hand_local)
    handed.start()
    depth = grads[0].shape[2]

    small_rows[...] = jnp.zeros_like(small_rows)
    model = small_rows.shape[1]
    for layer in range(2):
        first, middle, end, attend, up = sums[layer]
        top = SMALL * layer
        part = attend.shape[1]
        lanes = pl.ds(pl.multiple_of(me * part, part), part)
        small_rows[top : top + 2, :] = first[0:2, :]
        small_rows[top + 2 : top + 3, lanes] = attend[0:1, :]
        small_rows[top + 3 : top + 4, lanes] = attend[1:2, :]
        small_rows[top + 4 : top + 5, :] = middle[2:3, :]
        small_rows[top + 5 : top + 7, :] = middle[0:2, :]
        small_rows[top + 7 : top + 8, :] = end[1:2, :]
        small_rows[top + 8 : top + 9, :] = end[0:1, :]
        for rank_of in range(RING):
            small_rows[top + 9 + rank_of : top + 10 + rank_of, :] = jnp.where(
                me == rank_of, up[0:1, :], 0.0
            )
        small_rows[top + 13 : top + 14, :] = middle[3:4, :]
    small_in[...] = jnp.zeros_like(small_in)
    for number in range(RING * RING):
        small_in[number // RING, number % RING, :, 0:depth] = small_rows[
            :, number * depth : (number + 1) * depth
        ]
    pl.semaphore_wait(barrier, count)
    first_layer.swap()
    small_swap = push(2, 6, 0, small_in.at[:, :, half_of(1 - section, SMALL)], small_buffers[1], other)
    extra_copies = []
    for i in range(n_extra):
        copy = pltpu.make_async_remote_copy(
            src_ref=extras[i],
            dst_ref=extra_outs[i],
            send_sem=extra_send.at[i],
            recv_sem=extra_recv.at[i],
            device_id=other,
            device_id_type=MESH,
        )
        copy.start()
        extra_copies.append(copy)

    first_layer.begin()
    small_swap.wait_recv()
    add_blocks(small_buffers[0], small_in.at[:, :, half_of(section, SMALL)], small_buffers[1])
    small_part = Scatter(2, True, small_buffers[0], small_buffers[2:], y, z, push)
    small_part.begin()
    first_layer.join()
    small_part.join()
    first_layer.turn()
    small_part.turn()
    first_layer.join_two()
    small_part.join_two()
    small_part.finish(vector_own)
    vector_parts[me] = vector_own[...]
    vector_copies = []
    for k in range(1, RING):
        copy = pltpu.make_async_remote_copy(
            src_ref=vector_own,
            dst_ref=vector_parts.at[me],
            send_sem=vector_send.at[k],
            recv_sem=vector_recv.at[k],
            device_id={"tensor": step(me, k)},
            device_id_type=MESH,
        )
        copy.start()
        vector_copies.append(copy)
    first_layer.finish(summed.at[0])
    handed.wait()
    result = pltpu.make_async_remote_copy(
        src_ref=summed.at[1 - section],
        dst_ref=packed_out.at[section],
        send_sem=result_send,
        recv_sem=result_recv,
        device_id=other,
        device_id_type=MESH,
    )
    result.start()
    own_result = pltpu.make_async_copy(summed.at[section], packed_out.at[section], result_local)
    own_result.start()
    own_result.wait()
    result.wait()
    for copy in vector_copies:
        copy.wait()
    total = vector_parts[0]
    for k in range(1, RING):
        total = total + vector_parts[k]
    small_out[...] = total
    for copy in extra_copies:
        copy.wait()
    first_layer.end()
    for copy in started:
        copy.wait_send()


def final_call(cid, sums, grads, summed_last, extras):
    extra = len(extras)
    width = sums[0].shape[1]
    hidden = grads[-1].shape[3]
    args = list(sums) + list(grads) + [summed_last] + list(extras)
    block = (HALF_ROWS, hidden)
    return pl.pallas_call(
        functools.partial(final_kernel, extra),
        out_shape=[
            jax.ShapeDtypeStruct((SMALL, 128), F32),
            jax.ShapeDtypeStruct((2, HALF_ROWS, hidden), F32),
        ]
        + [jax.ShapeDtypeStruct(value.shape, value.dtype) for value in extras],
        in_specs=[vmem_spec()] * len(sums) + [any_spec()] * (len(grads) + 1) + [vmem_spec()] * extra,
        out_specs=[vmem_spec()] * (2 + extra),
        scratch_shapes=[
            pltpu.VMEM((RING, RING, 2 * SMALL, 128), F32),
            pltpu.VMEM((2 * SMALL, width), F32),
            pltpu.VMEM((SMALL, 128), F32),
            pltpu.VMEM((RING, SMALL, 128), F32),
            pltpu.VMEM((2,) + block, F32),
        ]
        + scatter_buffers((SMALL, 128), F32)
        + LayerGradients.scratch(HALF_ROWS // 3, hidden)
        + [
            pltpu.SemaphoreType.DMA((RING,)),
            pltpu.SemaphoreType.DMA((RING,)),
            pltpu.SemaphoreType.DMA((extra,)),
            pltpu.SemaphoreType.DMA((extra,)),
            pltpu.SemaphoreType.DMA,
            pltpu.SemaphoreType.DMA,
            pltpu.SemaphoreType.DMA,
            pltpu.SemaphoreType.DMA,
        ],
        compiler_params=comm_params(cid),
    )(*args)


def flat_dot(former, latter):
    return lax.dot_general(former, latter, (((1,), (1,)), ((), ())), preferred_element_type=F32)


def rows_dot(former, latter):
    return lax.dot_general(former, latter, (((0,), (0,)), ((), ())), preferred_element_type=F32)


def head_stack(values, scale):
    column = lax.broadcasted_iota(jnp.int32, values.shape, 1) // HEAD_DIM
    heads_here = values.shape[1] // HEAD_DIM
    zero = jnp.zeros_like(values)
    scaled = values * jnp.asarray(scale, values.dtype)
    return jnp.concatenate(
        [jnp.where(column == head, scaled, zero) for head in range(heads_here)], axis=0
    )


def block_scores(key_block, stack, seg_column, seg_wide):
    scores = flat_dot(key_block, stack)
    return jnp.where(seg_column == seg_wide, scores, MASKED_SCORE)


def load_matrix(packed_any, target, number, half, semaphores):
    copies = []
    for which in range(2):
        copy = pltpu.make_async_copy(
            packed_any.at[which, :, :, pl.ds(number * half, half)],
            target.at[:, :, pl.ds(which * half, half)],
            semaphores.at[which],
        )
        copy.start()
        copies.append(copy)
    return copies


def attend_kernel(
    normed_ref, packed_any, bias_ref, seg_q_ref, seg_k_ref,
    q_ref, k_ref, v_ref, mixed_ref, wide_ref, lse_ref, part_ref,
    pack_ref, stack, acc, top_ref, total_ref, send, recv, local,
):
    group, width = q_ref.shape
    heads_here = width // HEAD_DIM
    depth = group // RING
    loads = load_matrix(packed_any, pack_ref, 0, depth // 2, local)
    matrix = lambda which: pack_ref[:, :, :, which * width : (which + 1) * width].reshape(-1, width)
    rank = lax.axis_index("dp")
    y, z = rank // RING, lax.rem(rank, RING)
    barrier, count = dp_barrier(y, z, None)
    normed = normed_ref[...]
    for load in loads:
        load.wait()
    k_ref[y, z] = jnp.dot(normed, matrix(1), preferred_element_type=F32).astype(BF16)
    pl.semaphore_wait(barrier, count)
    started = []
    ring = Gather(((0, (), True), (1, (), False)), (k_ref, v_ref), y, z, (), pusher(send, recv, started))
    ring.begin(0, k_ref.at[y, z])
    v_ref[y, z] = (
        jnp.dot(normed, matrix(2), preferred_element_type=F32) + bias_ref[1:2, :]
    ).astype(BF16)
    ring.begin(1, v_ref.at[y, z])
    q_ref[...] = (
        jnp.dot(normed, matrix(0), preferred_element_type=F32) + bias_ref[0:1, :]
    ).astype(BF16)
    stack[...] = head_stack(q_ref[...], HEAD_DIM ** (-0.5))
    acc[...] = jnp.zeros_like(acc)
    top_ref[...] = jnp.full_like(top_ref, MASKED_SCORE)
    total_ref[...] = jnp.zeros_like(total_ref)
    seg_wide = jnp.concatenate([seg_q_ref[0:1, :]] * heads_here, axis=1)

    def attend(offset_y, offset_z):
        at_y, at_z = step(y, offset_y), step(z, offset_z)
        highest = top_ref[0:1, :]
        scores = block_scores(
            k_ref[at_y, at_z], stack[...], seg_k_ref[at_y, at_z, :, 0:1], seg_wide
        )
        above = jnp.maximum(highest, jnp.max(scores, axis=0, keepdims=True))
        weights = jnp.exp(scores - above)
        fade = jnp.exp(highest - above)
        total_ref[0:1, :] = total_ref[0:1, :] * fade + jnp.sum(weights, axis=0, keepdims=True)
        top_ref[0:1, :] = above
        low = weights.astype(BF16)
        turned = v_ref[at_y, at_z].T
        for head in range(heads_here):
            rows = pl.ds(head * HEAD_DIM, HEAD_DIM)
            lanes = slice(head * group, (head + 1) * group)
            term = jnp.dot(
                turned[head * HEAD_DIM : (head + 1) * HEAD_DIM], low[:, lanes],
                preferred_element_type=F32,
            )
            acc[rows, :] = acc[rows, :] * fade[:, lanes] + term

    def attend_all(count, offsets):
        def each(number, carry):
            attend(*offsets(number))
            return carry

        lax.fori_loop(0, count, each, 0)

    side = lambda t: 1 + 2 * lax.rem(t, 2)
    attend_all(1, lambda t: (t, t))
    ring.near()
    for i in ring.every:
        ring.relay(i, 0)
        ring.other(i, 0)
    attend_all(2, lambda t: (t * 0, side(t)))
    for i in ring.every:
        ring.far(i)
    attend_all(2, lambda t: (side(t), t * 0))
    for i in ring.every:
        ring.relay(i, MINUS)
        ring.relay(i, PLUS)
    for i in ring.every:
        ring.other(i, MINUS)
        ring.other(i, PLUS)
    attend_all(4, lambda t: (side(t // 2), side(t)))
    for i in ring.every:
        ring.relay(i, FAR)
        ring.relayed[i, 0].wait_recv()
    attend_all(2, lambda t: (2 * t, 2 - 2 * t))
    for i in ring.every:
        ring.other(i, FAR)
        ring.relayed[i, MINUS].wait_recv()
        ring.relayed[i, PLUS].wait_recv()
    attend_all(
        4,
        lambda t: (
            2 * (t // 2) + side(t) * (1 - t // 2),
            2 * (1 - t // 2) + side(t) * (t // 2),
        ),
    )
    for i in ring.every:
        ring.relayed[i, FAR].wait_recv()
    attend_all(1, lambda t: (t + FAR, t + FAR))

    total = total_ref[0:1, :]
    inverse = 1.0 / total
    for head in range(heads_here):
        rows = pl.ds(head * HEAD_DIM, HEAD_DIM)
        wide_ref[rows, :] = acc[rows, :] * inverse[:, head * group : (head + 1) * group]
    mixed_ref[...] = wide_ref[...].T.astype(BF16)
    lse_ref[...] = jnp.broadcast_to(top_ref[0:1, :] + jnp.log(total), lse_ref.shape)
    part = flat_dot(mixed_ref[...], matrix(3)).astype(BF16)
    part_ref[...] = part.reshape(part_ref.shape)
    for copy in started:
        copy.wait_send()


def attend_call(cid, normed, packed, biases, seg_wide, seg_column):
    group, model = normed.shape
    width = biases.shape[1]
    heads_here = width // HEAD_DIM
    square = (RING, RING, group, width)
    return pl.pallas_call(
        attend_kernel,
        out_shape=[
            jax.ShapeDtypeStruct((group, width), BF16),
            jax.ShapeDtypeStruct(square, BF16),
            jax.ShapeDtypeStruct(square, BF16),
            jax.ShapeDtypeStruct((group, width), BF16),
            jax.ShapeDtypeStruct((width, group), F32),
            jax.ShapeDtypeStruct((8, group * heads_here), F32),
            jax.ShapeDtypeStruct((RING, group // RING, model), BF16),
        ],
        in_specs=[vmem_spec(), any_spec()] + [vmem_spec()] * 3,
        out_specs=[vmem_spec()] * 7,
        scratch_shapes=[
            pltpu.VMEM((RING, RING, group // RING, model), BF16),
            pltpu.VMEM((group * heads_here, width), BF16),
            pltpu.VMEM((width, group), F32),
            pltpu.VMEM((8, group * heads_here), F32),
            pltpu.VMEM((8, group * heads_here), F32),
            pltpu.SemaphoreType.DMA((2, 5, RING)),
            pltpu.SemaphoreType.DMA((2, 5, RING)),
            pltpu.SemaphoreType.DMA((2,)),
        ],
        compiler_params=comm_params(cid),
    )(normed, packed, biases, seg_wide, seg_column)


def attend_back_kernel(
    rows_ref, packed_any, q_ref, k_ref, v_ref, wide_ref, lse_ref, seg_q_ref, seg_k_ref,
    triple_ref, sums_ref, part_ref, *scratch,
):
    (
        pack_ref, grad_ref, stack, plain, grad_stack, grad_plain, acc, delta_ref,
        dk_ref, dv_ref, total_ref,
    ) = scratch[:11]
    buffers = scratch[11 : 11 + 2 * SCATTER_BUFFERS]
    send, recv, local = scratch[11 + 2 * SCATTER_BUFFERS :]
    group, width = q_ref.shape
    heads_here = width // HEAD_DIM
    scale = HEAD_DIM ** (-0.5)
    depth = group // RING
    loads = load_matrix(packed_any, pack_ref, 0, depth // 2, local)
    matrix = lambda which: pack_ref[:, :, :, which * width : (which + 1) * width].reshape(-1, width)
    rank = lax.axis_index("dp")
    y, z = rank // RING, lax.rem(rank, RING)
    barrier, count = dp_barrier(y, z, None)
    stack[...] = head_stack(q_ref[...], scale)
    plain[...] = head_stack(q_ref[...], 1.0)
    for load in loads:
        load.wait()
    grad_ref[...] = jnp.dot(rows_ref[...], matrix(3), preferred_element_type=F32).astype(BF16)
    grad_stack[...] = head_stack(grad_ref[...], scale)
    grad_plain[...] = head_stack(grad_ref[...], 1.0)
    acc[...] = jnp.zeros_like(acc)
    seg_wide = jnp.concatenate([seg_q_ref[0:1, :]] * heads_here, axis=1)
    product = grad_ref[...].astype(F32).T * wide_ref[...]
    for head in range(heads_here):
        delta_ref[0:1, pl.ds(head * group, group)] = scale * jnp.sum(
            product[head * HEAD_DIM : (head + 1) * HEAD_DIM], axis=0, keepdims=True
        )
    pl.semaphore_wait(barrier, count)
    started = []
    push = pusher(send, recv, started)
    keys = Scatter(0, True, dk_ref, buffers[:SCATTER_BUFFERS], y, z, push)
    values = Scatter(1, False, dv_ref, buffers[SCATTER_BUFFERS:], y, z, push)

    def attend(offset_y, offset_z):
        at_y, at_z = step(y, offset_y), step(z, offset_z)
        key_block = k_ref[at_y, at_z]
        scores = block_scores(key_block, stack[...], seg_k_ref[at_y, at_z, :, 0:1], seg_wide)
        weights = jnp.exp(scores - lse_ref[0:1, :])
        dv_ref[at_y, at_z] = jnp.dot(
            weights.astype(BF16), grad_plain[...], preferred_element_type=F32
        ).astype(BF16)
        prob_grad = flat_dot(v_ref[at_y, at_z], grad_stack[...])
        low = (weights * (prob_grad - delta_ref[0:1, :])).astype(BF16)
        dk_ref[at_y, at_z] = jnp.dot(low, plain[...], preferred_element_type=F32).astype(BF16)
        turned = key_block.T
        for head in range(heads_here):
            rows = pl.ds(head * HEAD_DIM, HEAD_DIM)
            acc[rows, :] += jnp.dot(
                turned[head * HEAD_DIM : (head + 1) * HEAD_DIM],
                low[:, head * group : (head + 1) * group],
                preferred_element_type=F32,
            )

    def attend_all(first, count, offsets):
        def each(number, carry):
            attend(*offsets(number))
            return carry

        lax.fori_loop(first, count, each, 0)

    attend_all(0, 4, lambda t: (t * 0 + FAR, step(t, FAR)))
    for j in Scatter.ORDER:
        values.send_via(j)
    keys.send_direct(FAR)
    attend_all(1, 4, lambda t: (step(t, FAR), t * 0 + FAR))
    for j in Scatter.ORDER:
        keys.send_via(j)
    values.send_direct(FAR)
    attend_all(1, 4, lambda t: (t * 0 + PLUS, step(t, FAR)))
    keys.send_direct(PLUS)
    values.send_direct(PLUS)
    values.send_direct(MINUS)
    attend_all(1, 4, lambda t: (t * 0 + MINUS, step(t, FAR)))
    keys.send_direct(MINUS)
    values.send_direct(0)
    values.join()
    for j in (FAR, PLUS, MINUS):
        keys.join_one(j)
    attend_all(1, 4, lambda t: (t * 0, step(t, FAR)))
    keys.send_direct(0)
    keys.join_one(0)
    values.turn()
    keys.turn()
    values.join_two()
    keys.join_two()
    sums_ref[...] = jnp.zeros_like(sums_ref)
    query_grad = acc[...].T
    sums_ref[0:1, :] = jnp.sum(query_grad, axis=0, keepdims=True)
    triple_ref[0] = query_grad.astype(BF16)
    part = flat_dot(triple_ref[0], matrix(0))
    values.finish(total_ref)
    triple_ref[2] = total_ref[...].astype(BF16)
    sums_ref[1:2, :] = jnp.sum(total_ref[...], axis=0, keepdims=True)
    part = part + flat_dot(triple_ref[2], matrix(2))
    keys.finish(total_ref)
    triple_ref[1] = total_ref[...].astype(BF16)
    part = part + flat_dot(triple_ref[1], matrix(1))
    part_ref[...] = part.astype(BF16).reshape(part_ref.shape)
    for copy in started:
        copy.wait_send()


def attend_back_call(cid, attn_rows, packed, queries, keys, values, wide, lse, seg_wide, seg_column):
    group, model = attn_rows.shape
    width = queries.shape[1]
    heads_here = width // HEAD_DIM
    block = (group, width)
    stacked = pltpu.VMEM((group * heads_here, width), BF16)
    return pl.pallas_call(
        attend_back_kernel,
        out_shape=[
            jax.ShapeDtypeStruct((3, group, width), BF16),
            jax.ShapeDtypeStruct((8, width), F32),
            jax.ShapeDtypeStruct((RING, group // RING, model), BF16),
        ],
        in_specs=[vmem_spec(), any_spec()] + [vmem_spec()] * 7,
        out_specs=[vmem_spec()] * 3,
        scratch_shapes=[
            pltpu.VMEM((RING, RING, group // RING, model), BF16),
            pltpu.VMEM(block, BF16),
            stacked,
            stacked,
            stacked,
            stacked,
            pltpu.VMEM((width, group), F32),
            pltpu.VMEM((8, group * heads_here), F32),
            pltpu.VMEM((RING, RING) + block, BF16),
            pltpu.VMEM((RING, RING) + block, BF16),
            pltpu.VMEM(block, F32),
        ]
        + Scatter.scratch(block, BF16)
        + Scatter.scratch(block, BF16)
        + [
            pltpu.SemaphoreType.DMA((2, 6, RING)),
            pltpu.SemaphoreType.DMA((2, 6, RING)),
            pltpu.SemaphoreType.DMA((2,)),
        ],
        compiler_params=comm_params(cid),
    )(attn_rows, packed, queries, keys, values, wide, lse, seg_wide, seg_column)


class Exchange:
    def __init__(self, me, send, recv, landing, started):
        self.me, self.send, self.recv, self.landing, self.started = me, send, recv, landing, started
        self.reduces = {}

    def push(self, source, target, kind, index, k):
        copy = pltpu.make_async_remote_copy(
            src_ref=source,
            dst_ref=target,
            send_sem=self.send.at[kind, index, k - 1],
            recv_sem=self.recv.at[kind, index, k - 1],
            device_id={"tensor": step(self.me, k)},
            device_id_type=MESH,
        )
        copy.start()
        self.started.append(copy)
        return copy

    def reduce(self, part, peers=(1, 2, 3)):
        chunk = part.shape[-2] // CHUNKS
        for c in range(CHUNKS):
            here = pl.ds(c * chunk, chunk)
            for k in peers:
                self.reduces[c, k] = self.push(
                    part.at[step(self.me, k), here], self.landing.at[k - 1, here], 0, c, k
                )

    def run(self, part, function, rows_in, vecs, rows_out, sums_out, full, side=()):
        side = list(side)
        me = self.me
        chunk = part.shape[-2] // CHUNKS
        if side:
            side.pop(0)()
        sums, last = None, []
        for c in range(CHUNKS):
            here = pl.ds(c * chunk, chunk)
            for k in range(1, RING):
                self.reduces[c, k].wait_recv()
            total = part[me, here].astype(F32)
            for k in range(1, RING):
                total = total + self.landing[k - 1, here].astype(F32)
            spread, outs, parts = function(total, [ref[here].astype(F32) for ref in rows_in], vecs)
            if full is not None:
                full[me, here] = spread.astype(BF16)
                last += [
                    self.push(full.at[me, here], full.at[me, here], 1, c, k) for k in range(1, RING)
                ]
            for ref, value in zip(rows_out, outs):
                ref[here] = value.astype(ref.dtype)
            sums = parts if sums is None else [old + new for old, new in zip(sums, parts)]
        if sums_out is not None:
            sums_out[...] = jnp.concatenate(
                sums + [jnp.zeros((8 - len(sums), sums[0].shape[1]), F32)], axis=0
            )
        for work in side:
            work()
        for copy in last:
            copy.wait_recv()


TILES = ((2, 1), (3, 0))


def rows_of(ref, me, tile):
    return jnp.concatenate([ref[step(me, k)] for k in tile], axis=0)


def put_rows(ref, me, tile, value):
    rows = ref.shape[1]
    for i, k in enumerate(tile):
        ref[step(me, k)] = value[i * rows : (i + 1) * rows].astype(ref.dtype)


def wide_of(pack_ref):
    return pack_ref[...].reshape(-1, pack_ref.shape[-1])


def mlp_forward(me, full, up_ref, down_ref, bias_ref, act_ref, slope_ref, part_ref, exchange):
    for tile in TILES:
        value = jnp.dot(rows_of(full, me, tile), wide_of(up_ref), preferred_element_type=F32)
        value = value + bias_ref[0:1, :]
        phi = 0.5 * (1.0 + lax.erf(value * (0.5**0.5)))
        act = (value * phi).astype(BF16)
        density = jnp.exp(-0.5 * value * value) * 0.3989422804014327
        put_rows(act_ref, me, tile, act)
        put_rows(slope_ref, me, tile, phi + value * density)
        put_rows(part_ref, me, tile, flat_dot(act, wide_of(down_ref)))
        exchange.reduce(part_ref, [k for k in tile if k])


def mlp_backward(me, full, up_ref, down_ref, slope_ref, pre_ref, bias_out, part_ref, exchange):
    total = None
    for tile in TILES:
        value = jnp.dot(rows_of(full, me, tile), wide_of(down_ref), preferred_element_type=F32)
        value = value * rows_of(slope_ref, me, tile)
        part = jnp.sum(value, axis=0, keepdims=True)
        total = part if total is None else total + part
        low = value.astype(BF16)
        put_rows(pre_ref, me, tile, low)
        put_rows(part_ref, me, tile, flat_dot(low, wide_of(up_ref)))
        exchange.reduce(part_ref, [k for k in tile if k])
    bias_out[...] = jnp.broadcast_to(total, bias_out.shape)


def product(former_ref, latter_ref, out_ref):
    def work():
        tokens = lambda ref: ref[...].reshape(-1, ref.shape[-1])
        size = 256

        def each(number, carry):
            columns = pl.ds(pl.multiple_of(number * size, size), size)
            left = former_ref[..., columns].reshape(-1, size)
            value = jnp.dot(left.T, tokens(latter_ref), preferred_element_type=F32)
            out_ref[number] = value.astype(BF16).reshape(out_ref.shape[1:])
            return carry

        lax.fori_loop(0, RING, each, 0)

    return work


def chain_call(cid, body, exchanges, packed_array, ins, outs, inside, any_names=(), extra=None):
    names = list(ins) + list(outs) + list(inside)
    rows, model = 64, 1024
    count = len(names)
    load_packed = packed_array is not None

    def kernel(*refs):
        refs = list(refs)
        packed = refs.pop(0) if load_packed else None
        env = SimpleNamespace(**dict(zip(names, refs[:count])))
        refs = refs[count:]
        me = lax.axis_index("tensor")
        barrier, peers = tensor_barrier(me)
        started = []
        loads = []
        if load_packed:
            env.up, env.down, local = refs[:3]
            refs = refs[3:]
            half = env.up.shape[2] // 2
            for i, matrix in enumerate((env.up, env.down)):
                loads += load_matrix(packed, matrix, i + 1, half, local.at[i])
        if extra is not None:
            env.extra = refs[3 * exchanges :]
            rank = lax.axis_index("dp")
            env.place = (rank // RING, lax.rem(rank, RING), lax.axis_index("section"))
            peers += dp_barrier(*env.place)[1]
        pl.semaphore_wait(barrier, peers)
        env.started = started
        rings = [
            Exchange(me, refs[3 * i + 1], refs[3 * i + 2], refs[3 * i], started)
            for i in range(exchanges)
        ]
        body(me, env, rings, loads)
        for copy in started:
            copy.wait_send()

    scratch = [pltpu.VMEM(shape, dtype) for shape, dtype in inside.values()]
    spec_of = lambda name: any_spec() if name in any_names else vmem_spec()
    args, in_specs = list(ins.values()), [spec_of(name) for name in ins]
    if load_packed:
        args, in_specs = [packed_array] + args, [any_spec()] + in_specs
        matrix = pltpu.VMEM((RING, RING, rows, model), BF16)
        scratch += [matrix, matrix, pltpu.SemaphoreType.DMA((2, 2))]
    for _ in range(exchanges):
        scratch += [
            pltpu.VMEM((RING - 1, rows, model), BF16),
            pltpu.SemaphoreType.DMA((2, CHUNKS, RING - 1)),
            pltpu.SemaphoreType.DMA((2, CHUNKS, RING - 1)),
        ]
    scratch += extra or []
    results = pl.pallas_call(
        kernel,
        out_shape=[jax.ShapeDtypeStruct(shape, dtype) for shape, dtype in outs.values()],
        in_specs=in_specs,
        out_specs=[spec_of(name) for name in outs],
        scratch_shapes=scratch,
        compiler_params=comm_params(cid),
    )(*args)
    return SimpleNamespace(**dict(zip(outs, results)))


def first_mlp_body(me, env, rings, loads):
    y, z, section = env.place
    send, recv, local = env.extra
    push = pusher(send, recv, env.started)
    halves = [pl.ds(0, HALF_ROWS // 2), pl.ds(HALF_ROWS // 2, HALF_ROWS // 2)]
    ring = Gather(
        ((0, (), True), (1, (), False)),
        [env.packed_next.at[section, :, :, half] for half in halves], y, z, (), push,
    )
    begin, near, middle, end, final = spread_stages(
        ring, [env.stage.at[1, half] for half in halves], local, section, push
    )
    rings[0].reduce(env.part)
    rings[0].run(
        env.part, middle_rows, [env.inputs], [env.vec],
        [env.attn_out, env.hidden], None, env.normed, [begin, near],
    )
    middle()
    for copy in loads:
        copy.wait()
    mlp_forward(
        me, env.normed, env.up, env.down, env.bias, env.act, env.slope, env.sent, rings[1],
    )
    end()
    rings[1].run(
        env.sent, end_rows_first, [env.hidden], [env.vec, env.after],
        [env.mlp_out, env.outputs], None, env.next, [lambda: None, final],
    )


def last_mlp_body(me, env, rings, loads):
    rings[0].reduce(env.part)
    rings[0].run(
        env.part, middle_rows, [env.inputs], [env.vec],
        [env.attn_out, env.hidden], None, env.normed,
    )
    for copy in loads:
        copy.wait()
    mlp_forward(
        me, env.normed, env.up, env.down, env.bias, env.act, env.slope,
        env.sent, rings[1],
    )
    rings[1].run(
        env.sent, end_rows_last, [env.hidden, env.upstream], [env.vec],
        [env.outputs], env.sums_end, env.mlp_rows,
    )
    mlp_backward(
        me, env.mlp_rows, env.up, env.down, env.slope, env.pre, env.bias_grad,
        env.sent_two, rings[2],
    )
    rings[2].run(
        env.sent_two, back_middle_rows, [env.upstream, env.hidden, env.attn_out],
        [env.vec], [env.hidden_grad], env.sums_middle, env.attn_rows,
        [
            product(env.mlp_rows, env.act, env.grad_down),
            product(env.normed, env.pre, env.grad_up),
        ],
    )


def attention_products(env):
    return [
        product(env.attn_rows_in, env.mixed, env.grad_out)
    ] + [
        product(env.normed_in, env.triple.at[which], env.grad_qkv.at[which])
        for which in range(3)
    ]


def between_body(me, env, rings, loads):
    y, z, section = env.place
    grads = [env.grad_qkv.at[which] for which in range(3)]
    grads += [env.grad_out, env.last_up, env.last_down]
    layer = layer_gradients(grads, env.extra, y, z, section, env.started)

    def swap():
        for work in attention_products(env):
            work()
        layer.keep()
        layer.swap()

    rings[0].reduce(env.part)
    rings[0].run(
        env.part, back_end_rows_last, [env.hidden_grad_in, env.inputs, env.mlp_out],
        [env.vec_last, env.vec], [env.input_grad], env.sums_last, env.mlp_rows,
        [swap, layer.begin],
    )
    for copy in loads:
        copy.wait()
    mlp_backward(
        me, env.mlp_rows, env.up, env.down, env.slope, env.pre, env.bias_grad, env.sent, rings[1],
    )
    layer.join()

    def products():
        product(env.mlp_rows, env.act, env.grad_down)()
        product(env.normed, env.pre, env.grad_up)()

    def rest():
        layer.turn()
        layer.join_two()
        layer.finish(env.summed)
        layer.end()

    rings[1].run(
        env.sent, back_middle_rows_low, [env.input_grad, env.hidden, env.attn_out],
        [env.vec], [env.hidden_grad], env.sums_middle, env.attn_rows, [products, rest],
    )


def back_middle_rows_low(total, rows, vecs):
    return back_middle_rows(total, [rows[0].astype(BF16).astype(F32)] + rows[1:], vecs)


def close_body(me, env, rings, loads):
    rings[0].reduce(env.part)
    rings[0].run(
        env.part, back_end_rows_first, [env.hidden_grad_in, env.inputs],
        [env.vec], [env.input_grad], env.sums_last, None, attention_products(env),
    )


def shards(tokens, segment_ids, w_qkv, w_out, w_up, w_down, vectors, out_bias, cotangent):
    section = lax.axis_index("section")
    tensor_rank = lax.axis_index("tensor")
    own = lambda pair: jnp.where(section == 0, pair[0], pair[1])
    rows = tokens.shape[1]
    width = tokens.shape[2]
    group = rows * RING
    square = (RING, RING)
    local_width = w_qkv.shape[3]
    local_hidden = w_up.shape[2]

    depth = w_out.shape[1]
    my_segments = own(segment_ids)
    wide_segments = jnp.pad(my_segments, (0, depth - rows)).astype(BF16)[None]
    small = jnp.pad(
        jnp.concatenate([vectors[0], out_bias, wide_segments], axis=0),
        ((0, 1), (0, 128 - depth)),
    )
    packed_first, stage, small_all, small_rows = first_call(0, w_qkv[0], w_out[0], w_up[0], w_down[0], small)
    my_tokens = own(tokens)
    my_cotangent = own(cotangent)
    seg_mine = own(small_all)[:, :, 14, :rows].astype(jnp.int32).reshape(8, 128)
    normed, seg_group = tensor_call(
        1, first_rows, None, [my_tokens], [small_rows[0]], [], 0, True, seg_mine
    )
    seg_all = seg_group.reshape(RING, RING * RING, rows).transpose(1, 0, 2).reshape(-1, group)
    seg_rows = lax.dynamic_index_in_dim(seg_all, lax.axis_index("dp"), 0, keepdims=False)
    seg_wide = jnp.broadcast_to(seg_rows[None], (8, group))
    seg_column = jnp.broadcast_to(seg_all.reshape(*square, group)[..., None], square + (group, 128))
    whole = (RING, rows, width)
    blocks = lambda columns: square + (depth, columns)
    spread = (RING, rows, local_hidden)
    row_shape = (rows, width)
    inputs = my_tokens.astype(F32)
    up_biases = [
        jnp.broadcast_to(
            lax.dynamic_slice_in_dim(
                small_rows[layer, 9:13].reshape(-1), tensor_rank * local_hidden, local_hidden
            )[None],
            (8, local_hidden),
        )
        for layer in range(2)
    ]

    def attend_layer(layer, normed, packed):
        vec = small_rows[layer]
        query_bias = lax.dynamic_slice_in_dim(vec[2], tensor_rank * local_width, local_width)
        value_bias = lax.dynamic_slice_in_dim(vec[3], tensor_rank * local_width, local_width)
        biases = jnp.pad(jnp.stack([query_bias, value_bias]), ((0, 6), (0, 0)))
        return attend_call(
            2 + 12 * layer, normed.reshape(group, width), packed, biases, seg_wide, seg_column
        )

    normed_first = normed
    *kept_first, part = attend_layer(0, normed_first, packed_first)
    first = chain_call(
        3, first_mlp_body, 2, packed_first,
        dict(
            part=part, inputs=inputs, vec=small_rows[0], after=small_rows[1],
            bias=up_biases[0], stage=stage,
        ),
        dict(
            attn_out=(row_shape, F32), hidden=(row_shape, F32), normed=(whole, BF16),
            act=(spread, BF16), slope=(spread, F32), mlp_out=(row_shape, F32),
            outputs=(row_shape, BF16), next=(whole, BF16),
            packed_next=((2,) + square + (HALF_ROWS, local_hidden), BF16),
        ),
        dict(sent=(whole, BF16)),
        ("packed_next",),
        gather_scratch(),
    )
    between = first.outputs
    packed_last = first.packed_next
    *kept_last, part = attend_layer(1, first.next, packed_last)
    last = chain_call(
        5, last_mlp_body, 3, packed_last,
        dict(
            part=part, inputs=between.astype(F32), vec=small_rows[1],
            bias=up_biases[1], upstream=my_cotangent.astype(F32),
        ),
        dict(
            outputs=(row_shape, BF16), sums_end=((8, width), F32),
            hidden_grad=(row_shape, F32), sums_middle=((8, width), F32),
            attn_rows=(whole, BF16), bias_grad=((8, local_hidden), F32),
            grad_up=(blocks(local_hidden), BF16), grad_down=(blocks(local_hidden), BF16),
        ),
        dict(
            attn_out=(row_shape, F32), hidden=(row_shape, F32), normed=(whole, BF16),
            act=(spread, BF16), slope=(spread, F32), pre=(spread, BF16),
            mlp_rows=(whole, BF16), sent=(whole, BF16), sent_two=(whole, BF16),
        ),
    )
    outputs = last.outputs

    def attend_back_layer(layer, attn_rows, kept, packed):
        queries, keys_full, values_full, mixed, wide, lse = kept
        return attend_back_call(
            7 + 12 * layer, attn_rows.reshape(group, width), packed, queries, keys_full,
            values_full, wide, lse, seg_wide, seg_column,
        )

    attention_grads = dict(
        grad_out=(blocks(local_width), BF16), grad_qkv=((3,) + blocks(local_width), BF16),
    )
    triple, attend_last, part = attend_back_layer(1, last.attn_rows, kept_last, packed_last)
    middle = chain_call(
        8, between_body, 2, packed_first,
        dict(
            part=part, hidden_grad_in=last.hidden_grad, inputs=between.astype(F32),
            mlp_out=first.mlp_out, vec_last=small_rows[1], vec=small_rows[0],
            slope=first.slope, act=first.act, normed=first.normed,
            hidden=first.hidden, attn_out=first.attn_out,
            attn_rows_in=last.attn_rows, mixed=kept_last[3], normed_in=first.next,
            triple=triple, last_up=last.grad_up, last_down=last.grad_down,
        ),
        dict(
            summed=((HALF_ROWS, local_hidden), F32),
            input_grad=(row_shape, F32), sums_last=((8, width), F32),
            hidden_grad=(row_shape, F32), sums_middle=((8, width), F32),
            attn_rows=(whole, BF16), bias_grad=((8, local_hidden), F32),
            grad_up=(blocks(local_hidden), BF16), grad_down=(blocks(local_hidden), BF16),
            **attention_grads,
        ),
        dict(pre=(spread, BF16), mlp_rows=(whole, BF16), sent=(whole, BF16)),
        ("last_up", "last_down"),
        LayerGradients.scratch(HALF_ROWS // 3, local_hidden),
    )
    last_grad = middle.input_grad
    triple, attend_first, part = attend_back_layer(0, middle.attn_rows, kept_first, packed_first)
    close = chain_call(
        9, close_body, 1, None,
        dict(
            part=part, hidden_grad_in=middle.hidden_grad, inputs=inputs,
            vec=small_rows[0], attn_rows_in=middle.attn_rows, mixed=kept_first[3],
            normed_in=normed_first, triple=triple,
        ),
        dict(input_grad=(row_shape, F32), sums_last=((8, width), F32), **attention_grads),
        dict(),
    )
    input_grad = close.input_grad
    sums = [
        [close.sums_last, middle.sums_middle, middle.sums_last[2:], attend_first, middle.bias_grad],
        [middle.sums_last, last.sums_middle, last.sums_end, attend_last, last.bias_grad],
    ]
    grads = [close.grad_qkv[which] for which in range(3)]
    grads += [close.grad_out, middle.grad_up, middle.grad_down]
    first_grad = input_grad

    extras = [
        jnp.where(section == 0, outputs, between),
        jnp.where(section == 0, last_grad, first_grad),
    ]
    small_sum, packed_sum, came_out, came_grad = final_call(
        10, sums[0] + sums[1], grads, middle.summed, extras
    )
    mine_out = jnp.where(section == 0, between, outputs)
    mine_grad = jnp.where(section == 0, first_grad, last_grad)
    pair = lambda mine, came: jnp.where(
        section == 0, jnp.stack([mine, came]), jnp.stack([came, mine])
    )[None]
    half = depth // 2
    columns = lambda which: packed_sum[
        :, :half, which * local_width : (which + 1) * local_width
    ].reshape(depth, local_width)
    return (
        pair(mine_out, came_out),
        pair(mine_grad, came_grad),
        jnp.stack([columns(0), columns(1), columns(2)])[None],
        columns(3)[None],
        packed_sum[:, half : 2 * half].reshape(1, depth, local_hidden),
        packed_sum[:, 2 * half :].reshape(1, depth, local_hidden),
        small_sum[:13, :depth][None],
        small_sum[13:14, :depth],
    )


def solution(mesh):
    in_specs = (
        P(None, ("dp", "tensor"), None),
        P(None, ("dp", "tensor")),
        P("section", None, "dp", "tensor"),
        P("section", "dp", "tensor"),
        P("section", "dp", "tensor"),
        P("section", "dp", "tensor"),
        P("section", None, "dp"),
        P("section", "dp"),
        P(None, ("dp", "tensor"), None),
    )
    out_specs = (
        P("section", None, ("dp", "tensor"), None),
        P("section", None, ("dp", "tensor"), None),
        P("section", None, "dp", "tensor"),
        P("section", "dp", "tensor"),
        P("section", "dp", "tensor"),
        P("section", "dp", "tensor"),
        P("section", None, "dp"),
        P("section", "dp"),
    )
    return jax.shard_map(shards, mesh=mesh, in_specs=in_specs, out_specs=out_specs, check_vma=False)
```

```python
import functools
from types import SimpleNamespace

import jax
import jax.numpy as jnp
from jax import lax
from jax.experimental import pallas as pl
from jax.experimental.pallas import tpu as pltpu
from jax.sharding import PartitionSpec as P

MESH = pl.DeviceIdType.MESH
HEAD_DIM = 64
EPSILON = 1e-06
MASKED_SCORE = -1e30
RING = 4
VMEM_LIMIT = 56 * 1024 * 1024
F32 = jnp.float32
BF16 = jnp.bfloat16


def vmem_spec():
    return pl.BlockSpec(memory_space=pltpu.VMEM)


def any_spec():
    return pl.BlockSpec(memory_space=pl.ANY)


def comm_params(cid):
    return pltpu.CompilerParams(
        collective_id=cid, has_side_effects=True, vmem_limit_bytes=VMEM_LIMIT
    )


def step(coord, by):
    return lax.rem(coord + by, RING)


def layer_norm(values, gain_row, shift_row):
    centre = values - jnp.mean(values, axis=-1, keepdims=True)
    spread = jnp.mean(centre * centre, axis=-1, keepdims=True)
    return centre * lax.rsqrt(spread + EPSILON) * gain_row + shift_row


def layer_norm_back(values, gain_row, grad):
    centre = values - jnp.mean(values, axis=-1, keepdims=True)
    spread = jnp.mean(centre * centre, axis=-1, keepdims=True)
    inverse = lax.rsqrt(spread + EPSILON)
    normed = centre * inverse
    scaled = grad * gain_row
    back = inverse * (
        scaled
        - jnp.mean(scaled, axis=-1, keepdims=True)
        - normed * jnp.mean(scaled * normed, axis=-1, keepdims=True)
    )
    return back, jnp.sum(grad * normed, axis=0, keepdims=True), jnp.sum(grad, axis=0, keepdims=True)


PLUS, FAR, MINUS = 1, 2, 3
CHUNKS = 2


def tensor_barrier(me):
    barrier = pltpu.get_barrier_semaphore()
    for k in range(1, RING):
        pl.semaphore_signal(
            barrier, inc=1, device_id={"tensor": step(me, k)}, device_id_type=MESH
        )
    return barrier, RING - 1


def row(ref, index):
    return ref[pl.ds(index, 1), :]


def middle_rows(total, rows, vecs):
    vec = vecs[0]
    attn_out = total + row(vec, 13)
    hidden = rows[0] + row(vec, 4) * attn_out
    return layer_norm(hidden, row(vec, 5), row(vec, 6)), [attn_out, hidden], []


def end_rows_first(total, rows, vecs):
    vec, after = vecs
    mlp_out = total + row(vec, 7)
    outputs = (rows[0] + row(vec, 8) * mlp_out).astype(BF16)
    inputs = outputs.astype(F32)
    return layer_norm(inputs, row(after, 0), row(after, 1)), [mlp_out, outputs], []


def end_rows_last(total, rows, vecs):
    vec = vecs[0]
    hidden, upstream = rows
    mlp_out = total + row(vec, 7)
    outputs = hidden + row(vec, 8) * mlp_out
    mlp_grad = row(vec, 8) * upstream
    sums = [
        jnp.sum(upstream * mlp_out, axis=0, keepdims=True),
        jnp.sum(mlp_grad, axis=0, keepdims=True),
    ]
    return mlp_grad, [outputs], sums


def back_middle_rows(total, rows, vecs):
    vec = vecs[0]
    upstream, hidden, attn_out = rows
    part, gain, shift = layer_norm_back(hidden, row(vec, 5), total)
    hidden_grad = upstream + part
    attn_grad = row(vec, 4) * hidden_grad
    sums = [
        gain,
        shift,
        jnp.sum(hidden_grad * attn_out, axis=0, keepdims=True),
        jnp.sum(attn_grad, axis=0, keepdims=True),
    ]
    return attn_grad, [hidden_grad], sums


def back_end_rows_last(total, rows, vecs):
    vec, before = vecs
    hidden_grad, inputs, mlp_out = rows
    part, gain, shift = layer_norm_back(inputs, row(vec, 0), total)
    input_grad = hidden_grad + part
    upstream = input_grad.astype(BF16).astype(F32)
    mlp_grad = row(before, 8) * upstream
    sums = [
        gain,
        shift,
        jnp.sum(upstream * mlp_out, axis=0, keepdims=True),
        jnp.sum(mlp_grad, axis=0, keepdims=True),
    ]
    return mlp_grad, [input_grad], sums


def back_end_rows_first(total, rows, vecs):
    hidden_grad, inputs = rows
    part, gain, shift = layer_norm_back(inputs, row(vecs[0], 0), total)
    return None, [hidden_grad + part], [gain, shift]


def dp_neighbour(y, z, along_z, k):
    if along_z:
        return {"dp": y * RING + step(z, k)}
    return {"dp": step(y, k) * RING + z}


def dp_barrier(y, z, section):
    barrier = pltpu.get_barrier_semaphore()
    count = 0
    for along_z in (True, False):
        for k in (PLUS, MINUS):
            pl.semaphore_signal(
                barrier, inc=1, device_id=dp_neighbour(y, z, along_z, k), device_id_type=MESH
            )
            count += 1
    if section is not None:
        pl.semaphore_signal(
            barrier, inc=1, device_id={"section": 1 - section}, device_id_type=MESH
        )
        count += 1
    return barrier, count


def pusher(send, recv, started):
    def push(index, kind, k, source, target, device):
        copy = pltpu.make_async_remote_copy(
            src_ref=source,
            dst_ref=target,
            send_sem=send.at[index, kind, k],
            recv_sem=recv.at[index, kind, k],
            device_id=device,
            device_id_type=MESH,
        )
        copy.start()
        started.append(copy)
        return copy

    return push


class Gather:
    WAYS = {0: 1, 3: 1, 1: 1, 2: 3}

    def __init__(self, pieces, outs, y, z, lead, push):
        self.pieces, self.outs, self.y, self.z = pieces, outs, y, z
        self.lead, self.push = lead, push
        self.every = range(len(pieces))
        self.first, self.onward, self.second, self.relayed = {}, {}, {}, {}

    def block(self, i, along, across, rows=None):
        number, pre, along_z = self.pieces[i]
        ys, zs = (across, along) if along_z else (along, across)
        ys = ys if isinstance(ys, slice) else step(self.y, ys) if ys else self.y
        zs = zs if isinstance(zs, slice) else step(self.z, zs) if zs else self.z
        return self.outs[number].at[self.lead + pre + (ys, zs) + (() if rows is None else (rows,))]

    def way(self, i, first, k):
        return dp_neighbour(self.y, self.z, self.pieces[i][2] == first, k)

    def halves(self, i):
        height = self.outs[self.pieces[i][0]].shape[-2]
        if height < 32:
            return {PLUS: None}
        half = height // 32 * 16
        return {PLUS: pl.ds(0, half), MINUS: pl.ds(half, height - half)}

    def spread(self, i, offset, source):
        for k in (PLUS, MINUS):
            self.second[i, offset, k] = self.push(
                i, 2 if k == PLUS else 3, offset, source, self.block(i, offset, 0), self.way(i, False, k)
            )

    def begin(self, i, source):
        for k in (PLUS, MINUS):
            self.first[i, k] = self.push(i, 0, k, source, self.block(i, 0, 0), self.way(i, True, k))
        self.spread(i, 0, source)

    def near(self):
        for i in self.every:
            split = self.halves(i)
            for k in (PLUS, MINUS):
                self.first[i, k].wait_recv()
                came = RING - k
                if k in split:
                    self.onward[i, k] = self.push(
                        i, 1, k, self.block(i, came, 0, split[k]), self.block(i, came, 0, split[k]),
                        self.way(i, True, k),
                    )
                self.spread(i, came, self.block(i, came, 0))

    def relay(self, i, offset):
        k = self.WAYS[offset]
        self.second[i, offset, k].wait_recv()
        came = self.block(i, offset, RING - k)
        self.relayed[i, offset] = self.push(i, 4, offset, came, came, self.way(i, False, k))

    def other(self, i, offset):
        self.second[i, offset, RING - self.WAYS[offset]].wait_recv()

    def far(self, i):
        for k in self.halves(i):
            self.onward[i, k].wait_recv()
        self.spread(i, FAR, self.block(i, FAR, 0))


def half_of(section, height):
    return pl.ds(pl.multiple_of(section * height, height), height)


def spread_stages(ring, sources, local, section, push):
    own, across = {}, []

    def pass_on(i, line):
        came = ring.block(i, slice(None), line)
        across.append(push(i, 5, line, came, came, {"section": 1 - section}))

    def begin():
        for i in ring.every:
            ring.begin(i, sources[i])
            own[i] = pltpu.make_async_copy(sources[i], ring.block(i, 0, 0), local.at[i])
            own[i].start()

    def near():
        ring.near()
        for i in ring.every:
            ring.relay(i, 0)

    def middle():
        for i in ring.every:
            ring.far(i)
        for i in ring.every:
            ring.relay(i, MINUS)
            ring.relay(i, PLUS)
            own[i].wait()
            pass_on(i, 0)

    def end():
        for i in ring.every:
            ring.relay(i, FAR)
            for offset in range(RING):
                ring.other(i, offset)
            pass_on(i, PLUS)
            pass_on(i, MINUS)

    def last():
        for i in ring.every:
            for offset in range(RING):
                ring.relayed[i, offset].wait_recv()
            pass_on(i, FAR)
        for copy in across:
            copy.wait_recv()

    return [begin, near, middle, end, last]


HALF_ROWS = 96
SMALL = 16


def half_places(half, width, hidden):
    return [(0, which * width, width) for which in range(4)] + [
        (half, 0, hidden),
        (2 * half, 0, hidden),
    ]


def first_kernel(
    tokens_in, cotangent_in, qkv_in, out_in, up_in, down_in, small_in,
    packed_out, stage, rows_out, full, tokens_out, cotangent_out, seg_wide, seg_column,
    small_all, seg_parts, seg_rows,
    send, recv, local, small_send, small_recv, small_local,
    swap_send, swap_recv, swap_local, tensor_send, tensor_recv,
):
    rank = lax.axis_index("dp")
    y, z = rank // RING, lax.rem(rank, RING)
    section = lax.axis_index("section")
    me = lax.axis_index("tensor")
    barrier, count = dp_barrier(y, z, section)
    count += tensor_barrier(me)[1]
    depth, width = out_in.shape
    half = depth // 2
    mine, others = half_of(section, half), half_of(1 - section, half)
    sources = [qkv_in.at[which] for which in range(3)] + [out_in, up_in, down_in]
    places = half_places(half, width, stage.shape[2])
    tokens_out[...] = jnp.where(section == 0, tokens_in[0], tokens_in[1])
    cotangent_out[...] = jnp.where(section == 0, cotangent_in[0], cotangent_in[1])
    seg_parts[me] = jnp.zeros(seg_parts.shape[1:], jnp.int32)
    pl.semaphore_wait(barrier, count)
    started = []
    push = pusher(send, recv, started)
    swaps, kept = [], []
    for i, (source, (row, column, columns)) in enumerate(zip(sources, places)):
        target = stage.at[section, pl.ds(row, half), pl.ds(column, columns)]
        copy = pltpu.make_async_remote_copy(
            src_ref=source.at[others],
            dst_ref=target,
            send_sem=swap_send.at[i],
            recv_sem=swap_recv.at[i],
            device_id={"section": 1 - section},
            device_id_type=MESH,
        )
        copy.start()
        swaps.append(copy)
        copy = pltpu.make_async_copy(source.at[mine], target, swap_local.at[i])
        copy.start()
        kept.append(copy)
    small_push = pusher(small_send, small_recv, started)
    small_ring = Gather(((0, (), True),), [small_all.at[section]], y, z, (), small_push)
    small_stages = spread_stages(small_ring, [small_in], small_local, section, small_push)
    small_stages[0]()
    for copy in kept:
        copy.wait()
    for copy in swaps:
        copy.wait_recv()
    halves = [pl.ds(0, HALF_ROWS // 2), pl.ds(HALF_ROWS // 2, HALF_ROWS // 2)]
    views = [packed_out.at[section, :, :, rows] for rows in halves]
    ring = Gather(((0, (), True), (1, (), False)), views, y, z, (), push)
    stages = spread_stages(ring, [stage.at[0, rows] for rows in halves], local, section, push)
    stages[0]()
    small_stages[1]()
    small_stages[2]()
    stages[1]()
    small_stages[3]()
    small_stages[4]()
    for layer in range(2):
        for number in range(RING * RING):
            part = small_all[layer, number // RING, number % RING]
            rows_out[layer, :, number * depth : (number + 1) * depth] = part[:, :depth].astype(F32)
    for number in range(RING * RING):
        part = small_all[section, number // RING, number % RING]
        seg_parts[me, number : number + 1, 0:depth] = (
            part[14:15, :depth].astype(F32).astype(jnp.int32)
        )
    full[me] = layer_norm(
        tokens_out[...].astype(F32), rows_out[0, 0:1, :], rows_out[0, 1:2, :]
    ).astype(BF16)
    tensor_copies = []
    for i, ref in enumerate((seg_parts, full)):
        for k in range(1, RING):
            copy = pltpu.make_async_remote_copy(
                src_ref=ref.at[me],
                dst_ref=ref.at[me],
                send_sem=tensor_send.at[i, k],
                recv_sem=tensor_recv.at[i, k],
                device_id={"tensor": step(me, k)},
                device_id_type=MESH,
            )
            copy.start()
            tensor_copies.append(copy)
    stages[2]()
    stages[3]()
    for copy in tensor_copies:
        copy.wait_recv()
    for number in range(RING):
        seg_rows[:, number * depth : (number + 1) * depth] = seg_parts[number][:, :depth]
    seg_wide[...] = jnp.broadcast_to(seg_rows[pl.ds(rank, 1), :], seg_wide.shape)
    turned = seg_rows[...].astype(F32).T
    for number in range(RING * RING):
        seg_column[number // RING, number % RING] = jnp.broadcast_to(
            turned[:, number : number + 1], seg_column.shape[2:]
        ).astype(jnp.int32)
    stages[4]()
    for copy in started + swaps + tensor_copies:
        copy.wait_send()


def gather_scratch():
    return [
        pltpu.SemaphoreType.DMA((2, 6, RING)),
        pltpu.SemaphoreType.DMA((2, 6, RING)),
        pltpu.SemaphoreType.DMA((2,)),
    ]


def first_call(cid, tokens, cotangent, w_qkv, w_out, w_up, w_down, small):
    depth = w_out.shape[0]
    hidden = w_up.shape[1]
    rows, width = tokens.shape[1:]
    group = RING * rows
    return pl.pallas_call(
        first_kernel,
        out_shape=[
            jax.ShapeDtypeStruct((2, RING, RING, HALF_ROWS, hidden), BF16),
            jax.ShapeDtypeStruct((2, HALF_ROWS, hidden), BF16),
            jax.ShapeDtypeStruct((2, SMALL, width), F32),
            jax.ShapeDtypeStruct((RING, rows, width), BF16),
            jax.ShapeDtypeStruct((rows, width), BF16),
            jax.ShapeDtypeStruct((rows, width), BF16),
            jax.ShapeDtypeStruct((8, group), jnp.int32),
            jax.ShapeDtypeStruct((RING, RING, group, 128), jnp.int32),
        ],
        in_specs=[vmem_spec()] * 7,
        out_specs=[any_spec()] + [vmem_spec()] * 7,
        scratch_shapes=[
            pltpu.VMEM((2, RING, RING) + small.shape, BF16),
            pltpu.VMEM((RING, RING * RING, 128), jnp.int32),
            pltpu.VMEM((RING * RING, group), jnp.int32),
        ]
        + gather_scratch()
        + gather_scratch()
        + [
            pltpu.SemaphoreType.DMA((6,)),
            pltpu.SemaphoreType.DMA((6,)),
            pltpu.SemaphoreType.DMA((6,)),
            pltpu.SemaphoreType.DMA((2, RING)),
            pltpu.SemaphoreType.DMA((2, RING)),
        ],
        compiler_params=comm_params(cid),
    )(tokens, cotangent, w_qkv, w_out, w_up, w_down, small)


class Scatter:
    ORDER = (FAR, PLUS, MINUS, 0)
    WAYS = {FAR: PLUS, 0: PLUS, PLUS: MINUS, MINUS: MINUS}

    def __init__(self, index, along_z, source, buffers, y, z, push):
        self.index, self.along_z, self.source = index, along_z, source
        self.passing, self.joined, self.summed, self.straight, self.middle = buffers[:5]
        self.far_two, self.joined_two, self.summed_two, self.straight_two = buffers[5:]
        self.y, self.z, self.push = y, z, push
        self.height, self.width = source.shape[-2:]
        self.via, self.direct, self.after = {}, {}, {}

    def at(self, along, across):
        ys, zs = (across, along) if self.along_z else (along, across)
        return step(self.y, ys), step(self.z, zs)

    def way(self, first, k):
        return dp_neighbour(self.y, self.z, self.along_z == first, k)

    def add(self, target, terms, top=0, height=None):
        height = self.height if height is None else height
        size = max(8, min(height, 65536 // self.width))
        while height % size:
            size -= 16

        def part(here):
            value = terms[0](here).astype(F32)
            for term in terms[1:]:
                value = value + term(here).astype(F32)
            target[here] = value.astype(target.dtype)

        if height <= size:
            part(pl.ds(top, height))
            return

        def each(number, carry):
            part(pl.ds(pl.multiple_of(top + number * size, size), size))
            return carry

        lax.fori_loop(0, height // size, each, 0)

    def send_via(self, j):
        self.via[j] = self.push(
            self.index, 0, j, self.source.at[self.at(FAR, j)], self.passing.at[j],
            self.way(True, self.WAYS[j]),
        )

    def send_direct(self, j):
        k = RING - self.WAYS[j]
        self.direct[j] = self.push(
            self.index, 1, j, self.source.at[self.at(k, j)], self.straight.at[j], self.way(True, k)
        )

    def begin(self):
        for j in self.ORDER:
            self.send_via(j)
        for j in self.ORDER:
            self.send_direct(j)

    def join_one(self, j):
        self.via[j].wait_recv()
        k = self.WAYS[j]
        at_y, at_z = self.at(k, j)
        self.add(
            self.joined.at[j],
            [lambda h: self.source[at_y, at_z, h], lambda h: self.passing[j, h]],
        )
        self.after[j] = self.push(
            self.index, 2, j, self.joined.at[j], self.summed.at[j], self.way(True, k)
        )

    def join(self):
        for j in self.ORDER:
            self.join_one(j)

    def turn(self):
        half = self.height // 2
        low, high = pl.ds(0, half), pl.ds(half, half)
        send = lambda kind, slot, source, target, k: self.push(
            self.index, kind, slot, source, target, self.way(False, k)
        )
        for j in self.ORDER:
            self.direct[j].wait_recv()
            self.after[j].wait_recv()
            at_y, at_z = self.at(0, j)
            self.add(
                self.middle.at[j],
                [
                    lambda h: self.source[at_y, at_z, h],
                    lambda h: self.summed[j, h],
                    lambda h: self.straight[j, h],
                ],
            )
            if j == FAR:
                self.via_two = [
                    send(3, 0, self.middle.at[j, low], self.far_two.at[low], PLUS),
                    send(3, 1, self.middle.at[j, high], self.far_two.at[high], MINUS),
                ]
            if j == PLUS:
                high_copy = send(4, 1, self.middle.at[j, high], self.straight_two.at[high], PLUS)
            if j == MINUS:
                low_copy = send(4, 0, self.middle.at[j, low], self.straight_two.at[low], MINUS)
        self.direct_two = [low_copy, high_copy]

    def join_two(self):
        half = self.height // 2
        self.after_two = []
        for number, (top, k) in enumerate(((0, PLUS), (half, MINUS))):
            self.via_two[number].wait_recv()
            self.add(
                self.joined_two,
                [lambda h: self.middle[k, h], lambda h: self.far_two[h]],
                top,
                half,
            )
            here = pl.ds(top, half)
            self.after_two.append(
                self.push(
                    self.index, 5, number, self.joined_two.at[here], self.summed_two.at[here],
                    self.way(False, k),
                )
            )

    def finish(self, out):
        for copy in self.direct_two + self.after_two:
            copy.wait_recv()
        self.add(
            out,
            [
                lambda h: self.middle[0, h],
                lambda h: self.summed_two[h],
                lambda h: self.straight_two[h],
            ],
        )

    @staticmethod
    def scratch(block, dtype):
        return [pltpu.VMEM((RING,) + block, dtype)] * 5 + [pltpu.VMEM(block, dtype)] * 4


SCATTER_BUFFERS = 9


def scatter_buffers(block, dtype):
    square = pltpu.VMEM((RING, RING) + block, dtype)
    return [square, square] + Scatter.scratch(block, dtype)


class LayerGradients:
    def __init__(self, grads, buffers, semaphores, y, z, section, push):
        self.grads, self.buffers, self.y, self.z = grads, buffers, y, z
        self.section, self.push = section, push
        self.swap_send, self.swap_recv, self.keep_local = semaphores
        depth, width = grads[0].shape[2:]
        hidden = grads[5].shape[3]
        self.half = depth // 2
        self.places = [(0, 0, which * width, width) for which in range(4)]
        self.places += [(1, 0, 0, hidden), (1, self.half, 0, hidden)]

    def region(self, which, place):
        piece, row, column, columns = place
        return self.buffers[piece][which].at[:, :, pl.ds(row, self.half), pl.ds(column, columns)]

    def keep(self):
        mine = half_of(self.section, self.half)
        self.keeps = []
        for i, place in enumerate(self.places):
            copy = pltpu.make_async_copy(
                self.grads[i].at[:, :, mine], self.region(0, place), self.keep_local.at[i]
            )
            copy.start()
            self.keeps.append(copy)

    def swap(self):
        others = half_of(1 - self.section, self.half)
        self.swaps = []
        for i, place in enumerate(self.places):
            copy = pltpu.make_async_remote_copy(
                src_ref=self.grads[i].at[:, :, others],
                dst_ref=self.region(1, place),
                send_sem=self.swap_send.at[i],
                recv_sem=self.swap_recv.at[i],
                device_id={"section": 1 - self.section},
                device_id_type=MESH,
            )
            copy.start()
            self.swaps.append(copy)

    def begin(self):
        self.parts = []
        for piece in range(2):
            for i, place in enumerate(self.places):
                if place[0] == piece:
                    self.keeps[i].wait()
                    self.swaps[i].wait_recv()
            own, sibling = self.buffers[piece][:2]
            add_blocks(own, own, sibling)
            self.parts.append(
                Scatter(piece, piece == 0, own, self.buffers[piece][2:], self.y, self.z, self.push)
            )
            self.parts[piece].begin()

    def join(self):
        for part in self.parts:
            part.join()

    def turn(self):
        for part in self.parts:
            part.turn()

    def join_two(self):
        for part in self.parts:
            part.join_two()

    def finish(self, out):
        self.parts[0].finish(out.at[pl.ds(0, self.half)])
        self.parts[1].finish(out.at[pl.ds(self.half, 2 * self.half)])

    def end(self):
        for copy in self.swaps:
            copy.wait_send()

    @staticmethod
    def scratch(half, hidden):
        return (
            scatter_buffers((half, hidden), BF16)
            + scatter_buffers((2 * half, hidden), BF16)
            + [pltpu.SemaphoreType.DMA((6,))] * 3
            + [pltpu.SemaphoreType.DMA((3, 7, RING))] * 2
        )


LAYER_SCRATCH = 2 * (2 + SCATTER_BUFFERS) + 5


def layer_gradients(grads, scratch, y, z, section, started):
    size = 2 + SCATTER_BUFFERS
    push = pusher(scratch[-2], scratch[-1], started)
    return LayerGradients(
        grads, [scratch[:size], scratch[size : 2 * size]], scratch[2 * size : 2 * size + 3],
        y, z, section, push,
    )


def add_blocks(out, former, latter):
    def add(number, carry):
        at_y, at_z = number // RING, lax.rem(number, RING)
        out[at_y, at_z] = (
            former[at_y, at_z].astype(F32) + latter[at_y, at_z].astype(F32)
        ).astype(out.dtype)
        return carry

    lax.fori_loop(0, RING * RING, add, 0)


def final_kernel(*refs):
    refs = list(refs)
    take = lambda count: [refs.pop(0) for _ in range(count)]
    sums = [take(5), take(5)]
    grads, summed_last = take(6), take(1)[0]
    extras = take(4)
    small_out, packed_out = take(2)
    extra_outs = take(2)
    small_in, small_rows, vector_own, vector_parts, summed = take(5)
    extra_sends = take(2)
    small_buffers = take(2 + SCATTER_BUFFERS)
    layer_scratch = take(LAYER_SCRATCH)
    vector_send, vector_recv, extra_send, extra_recv, result_send, result_recv, result_local, hand_local = take(8)
    rank = lax.axis_index("dp")
    y, z = rank // RING, lax.rem(rank, RING)
    section = lax.axis_index("section")
    me = lax.axis_index("tensor")
    other = {"section": 1 - section}
    barrier, count = tensor_barrier(me)
    count += dp_barrier(y, z, section)[1]

    started = []
    first_layer = layer_gradients(grads, layer_scratch, y, z, section, started)
    push = first_layer.push
    first_layer.keep()
    handed = pltpu.make_async_copy(summed_last, summed.at[1], hand_local)
    handed.start()
    depth = grads[0].shape[2]
    for i in range(2):
        last_value, first_value = extras[2 * i][...], extras[2 * i + 1][...]
        extra_outs[i][section] = jnp.where(section == 0, first_value, last_value)
        extra_sends[i][...] = jnp.where(section == 0, last_value, first_value)

    small_rows[...] = jnp.zeros_like(small_rows)
    model = small_rows.shape[1]
    for layer in range(2):
        first, middle, end, attend, up = sums[layer]
        top = SMALL * layer
        part = attend.shape[1]
        lanes = pl.ds(pl.multiple_of(me * part, part), part)
        small_rows[top : top + 2, :] = first[0:2, :]
        small_rows[top + 2 : top + 3, lanes] = attend[0:1, :]
        small_rows[top + 3 : top + 4, lanes] = attend[1:2, :]
        small_rows[top + 4 : top + 5, :] = middle[2:3, :]
        small_rows[top + 5 : top + 7, :] = middle[0:2, :]
        small_rows[top + 7 : top + 8, :] = end[1:2, :]
        small_rows[top + 8 : top + 9, :] = end[0:1, :]
        for rank_of in range(RING):
            small_rows[top + 9 + rank_of : top + 10 + rank_of, :] = jnp.where(
                me == rank_of, up[0:1, :], 0.0
            )
        small_rows[top + 13 : top + 14, :] = middle[3:4, :]
    small_in[...] = jnp.zeros_like(small_in)
    for number in range(RING * RING):
        small_in[number // RING, number % RING, :, 0:depth] = small_rows[
            :, number * depth : (number + 1) * depth
        ]
    pl.semaphore_wait(barrier, count)
    first_layer.swap()
    small_swap = push(2, 6, 0, small_in.at[:, :, half_of(1 - section, SMALL)], small_buffers[1], other)
    extra_copies = []
    for i in range(2):
        copy = pltpu.make_async_remote_copy(
            src_ref=extra_sends[i],
            dst_ref=extra_outs[i].at[section],
            send_sem=extra_send.at[i],
            recv_sem=extra_recv.at[i],
            device_id=other,
            device_id_type=MESH,
        )
        copy.start()
        extra_copies.append(copy)

    first_layer.begin()
    small_swap.wait_recv()
    add_blocks(small_buffers[0], small_in.at[:, :, half_of(section, SMALL)], small_buffers[1])
    small_part = Scatter(2, True, small_buffers[0], small_buffers[2:], y, z, push)
    small_part.begin()
    first_layer.join()
    small_part.join()
    first_layer.turn()
    small_part.turn()
    first_layer.join_two()
    small_part.join_two()
    small_part.finish(vector_own)
    vector_parts[me] = vector_own[...]
    vector_copies = []
    for k in range(1, RING):
        copy = pltpu.make_async_remote_copy(
            src_ref=vector_own,
            dst_ref=vector_parts.at[me],
            send_sem=vector_send.at[k],
            recv_sem=vector_recv.at[k],
            device_id={"tensor": step(me, k)},
            device_id_type=MESH,
        )
        copy.start()
        vector_copies.append(copy)
    first_layer.finish(summed.at[0])
    handed.wait()
    result = pltpu.make_async_remote_copy(
        src_ref=summed.at[1 - section],
        dst_ref=packed_out.at[section],
        send_sem=result_send,
        recv_sem=result_recv,
        device_id=other,
        device_id_type=MESH,
    )
    result.start()
    own_result = pltpu.make_async_copy(summed.at[section], packed_out.at[section], result_local)
    own_result.start()
    own_result.wait()
    result.wait()
    for copy in vector_copies:
        copy.wait()
    total = vector_parts[0]
    for k in range(1, RING):
        total = total + vector_parts[k]
    small_out[...] = total
    for copy in extra_copies:
        copy.wait()
    first_layer.end()
    for copy in started:
        copy.wait_send()


def final_call(cid, sums, grads, summed_last, extras):
    extra = len(extras)
    width = sums[0].shape[1]
    hidden = grads[-1].shape[3]
    args = list(sums) + list(grads) + [summed_last] + list(extras)
    block = (HALF_ROWS, hidden)
    return pl.pallas_call(
        final_kernel,
        out_shape=[
            jax.ShapeDtypeStruct((SMALL, 128), F32),
            jax.ShapeDtypeStruct((2, HALF_ROWS, hidden), F32),
        ]
        + [jax.ShapeDtypeStruct((2,) + value.shape, value.dtype) for value in extras[::2]],
        in_specs=[vmem_spec()] * len(sums) + [any_spec()] * (len(grads) + 1) + [vmem_spec()] * extra,
        out_specs=[vmem_spec()] * 4,
        scratch_shapes=[
            pltpu.VMEM((RING, RING, 2 * SMALL, 128), F32),
            pltpu.VMEM((2 * SMALL, width), F32),
            pltpu.VMEM((SMALL, 128), F32),
            pltpu.VMEM((RING, SMALL, 128), F32),
            pltpu.VMEM((2,) + block, F32),
        ]
        + [pltpu.VMEM(value.shape, value.dtype) for value in extras[::2]]
        + scatter_buffers((SMALL, 128), F32)
        + LayerGradients.scratch(HALF_ROWS // 3, hidden)
        + [
            pltpu.SemaphoreType.DMA((RING,)),
            pltpu.SemaphoreType.DMA((RING,)),
            pltpu.SemaphoreType.DMA((extra,)),
            pltpu.SemaphoreType.DMA((extra,)),
            pltpu.SemaphoreType.DMA,
            pltpu.SemaphoreType.DMA,
            pltpu.SemaphoreType.DMA,
            pltpu.SemaphoreType.DMA,
        ],
        compiler_params=comm_params(cid),
    )(*args)


def flat_dot(former, latter):
    return lax.dot_general(former, latter, (((1,), (1,)), ((), ())), preferred_element_type=F32)


def rows_dot(former, latter):
    return lax.dot_general(former, latter, (((0,), (0,)), ((), ())), preferred_element_type=F32)


def head_stack(values, scale):
    column = lax.broadcasted_iota(jnp.int32, values.shape, 1) // HEAD_DIM
    heads_here = values.shape[1] // HEAD_DIM
    zero = jnp.zeros_like(values)
    scaled = values * jnp.asarray(scale, values.dtype)
    return jnp.concatenate(
        [jnp.where(column == head, scaled, zero) for head in range(heads_here)], axis=0
    )


def block_scores(key_block, stack, seg_column, seg_wide):
    scores = flat_dot(key_block, stack)
    return jnp.where(seg_column == seg_wide, scores, MASKED_SCORE)


def load_matrix(packed_any, target, number, half, semaphores):
    copies = []
    for which in range(2):
        copy = pltpu.make_async_copy(
            packed_any.at[which, :, :, pl.ds(number * half, half)],
            target.at[:, :, pl.ds(which * half, half)],
            semaphores.at[which],
        )
        copy.start()
        copies.append(copy)
    return copies


def attend_kernel(
    layer, normed_ref, packed_any, vec_ref, seg_q_ref, seg_k_ref,
    q_ref, k_ref, v_ref, mixed_ref, wide_ref, lse_ref, part_ref,
    pack_ref, stack, acc, top_ref, total_ref, send, recv, local,
):
    group, width = q_ref.shape
    heads_here = width // HEAD_DIM
    depth = group // RING
    loads = load_matrix(packed_any, pack_ref, 0, depth // 2, local)
    matrix = lambda which: pack_ref[:, :, :, which * width : (which + 1) * width].reshape(-1, width)
    rank = lax.axis_index("dp")
    y, z = rank // RING, lax.rem(rank, RING)
    barrier, count = dp_barrier(y, z, None)
    normed = normed_ref[...]
    start = pl.multiple_of(lax.axis_index("tensor") * width, width)
    query_bias = vec_ref[layer, 2:3, pl.ds(start, width)]
    value_bias = vec_ref[layer, 3:4, pl.ds(start, width)]
    for load in loads:
        load.wait()
    k_ref[y, z] = jnp.dot(normed, matrix(1), preferred_element_type=F32).astype(BF16)
    pl.semaphore_wait(barrier, count)
    started = []
    ring = Gather(((0, (), True), (1, (), False)), (k_ref, v_ref), y, z, (), pusher(send, recv, started))
    ring.begin(0, k_ref.at[y, z])
    v_ref[y, z] = (
        jnp.dot(normed, matrix(2), preferred_element_type=F32) + value_bias
    ).astype(BF16)
    ring.begin(1, v_ref.at[y, z])
    q_ref[...] = (
        jnp.dot(normed, matrix(0), preferred_element_type=F32) + query_bias
    ).astype(BF16)
    stack[...] = head_stack(q_ref[...], HEAD_DIM ** (-0.5))
    acc[...] = jnp.zeros_like(acc)
    top_ref[...] = jnp.full_like(top_ref, MASKED_SCORE)
    total_ref[...] = jnp.zeros_like(total_ref)
    seg_wide = jnp.concatenate([seg_q_ref[0:1, :]] * heads_here, axis=1)

    def attend(offset_y, offset_z):
        at_y, at_z = step(y, offset_y), step(z, offset_z)
        highest = top_ref[0:1, :]
        scores = block_scores(
            k_ref[at_y, at_z], stack[...], seg_k_ref[at_y, at_z, :, 0:1], seg_wide
        )
        above = jnp.maximum(highest, jnp.max(scores, axis=0, keepdims=True))
        weights = jnp.exp(scores - above)
        fade = jnp.exp(highest - above)
        total_ref[0:1, :] = total_ref[0:1, :] * fade + jnp.sum(weights, axis=0, keepdims=True)
        top_ref[0:1, :] = above
        low = weights.astype(BF16)
        turned = v_ref[at_y, at_z].T
        for head in range(heads_here):
            rows = pl.ds(head * HEAD_DIM, HEAD_DIM)
            lanes = slice(head * group, (head + 1) * group)
            term = jnp.dot(
                turned[head * HEAD_DIM : (head + 1) * HEAD_DIM], low[:, lanes],
                preferred_element_type=F32,
            )
            acc[rows, :] = acc[rows, :] * fade[:, lanes] + term

    def attend_all(count, offsets):
        def each(number, carry):
            attend(*offsets(number))
            return carry

        lax.fori_loop(0, count, each, 0)

    side = lambda t: 1 + 2 * lax.rem(t, 2)
    attend_all(1, lambda t: (t, t))
    ring.near()
    for i in ring.every:
        ring.relay(i, 0)
        ring.other(i, 0)
    attend_all(2, lambda t: (t * 0, side(t)))
    for i in ring.every:
        ring.far(i)
    attend_all(2, lambda t: (side(t), t * 0))
    for i in ring.every:
        ring.relay(i, MINUS)
        ring.relay(i, PLUS)
    for i in ring.every:
        ring.other(i, MINUS)
        ring.other(i, PLUS)
    attend_all(4, lambda t: (side(t // 2), side(t)))
    for i in ring.every:
        ring.relay(i, FAR)
        ring.relayed[i, 0].wait_recv()
    attend_all(2, lambda t: (2 * t, 2 - 2 * t))
    for i in ring.every:
        ring.other(i, FAR)
        ring.relayed[i, MINUS].wait_recv()
        ring.relayed[i, PLUS].wait_recv()
    attend_all(
        4,
        lambda t: (
            2 * (t // 2) + side(t) * (1 - t // 2),
            2 * (1 - t // 2) + side(t) * (t // 2),
        ),
    )
    for i in ring.every:
        ring.relayed[i, FAR].wait_recv()
    attend_all(1, lambda t: (t + FAR, t + FAR))

    total = total_ref[0:1, :]
    inverse = 1.0 / total
    for head in range(heads_here):
        rows = pl.ds(head * HEAD_DIM, HEAD_DIM)
        wide_ref[rows, :] = acc[rows, :] * inverse[:, head * group : (head + 1) * group]
    mixed_ref[...] = wide_ref[...].T.astype(BF16)
    lse_ref[...] = jnp.broadcast_to(top_ref[0:1, :] + jnp.log(total), lse_ref.shape)
    part = flat_dot(mixed_ref[...], matrix(3)).astype(BF16)
    part_ref[...] = part.reshape(part_ref.shape)
    for copy in started:
        copy.wait_send()


def attend_call(cid, layer, normed, packed, vectors, seg_wide, seg_column):
    group, model = normed.shape
    width = model // RING
    heads_here = width // HEAD_DIM
    square = (RING, RING, group, width)
    return pl.pallas_call(
        functools.partial(attend_kernel, layer),
        out_shape=[
            jax.ShapeDtypeStruct((group, width), BF16),
            jax.ShapeDtypeStruct(square, BF16),
            jax.ShapeDtypeStruct(square, BF16),
            jax.ShapeDtypeStruct((group, width), BF16),
            jax.ShapeDtypeStruct((width, group), F32),
            jax.ShapeDtypeStruct((8, group * heads_here), F32),
            jax.ShapeDtypeStruct((RING, group // RING, model), BF16),
        ],
        in_specs=[vmem_spec(), any_spec()] + [vmem_spec()] * 3,
        out_specs=[vmem_spec()] * 7,
        scratch_shapes=[
            pltpu.VMEM((RING, RING, group // RING, model), BF16),
            pltpu.VMEM((group * heads_here, width), BF16),
            pltpu.VMEM((width, group), F32),
            pltpu.VMEM((8, group * heads_here), F32),
            pltpu.VMEM((8, group * heads_here), F32),
            pltpu.SemaphoreType.DMA((2, 5, RING)),
            pltpu.SemaphoreType.DMA((2, 5, RING)),
            pltpu.SemaphoreType.DMA((2,)),
        ],
        compiler_params=comm_params(cid),
    )(normed, packed, vectors, seg_wide, seg_column)


def attend_back_kernel(
    rows_ref, packed_any, q_ref, k_ref, v_ref, wide_ref, lse_ref, seg_q_ref, seg_k_ref,
    triple_ref, sums_ref, part_ref, *scratch,
):
    (
        pack_ref, grad_ref, stack, plain, grad_stack, grad_plain, acc, delta_ref,
        dk_ref, dv_ref, total_ref,
    ) = scratch[:11]
    buffers = scratch[11 : 11 + 2 * SCATTER_BUFFERS]
    send, recv, local = scratch[11 + 2 * SCATTER_BUFFERS :]
    group, width = q_ref.shape
    heads_here = width // HEAD_DIM
    scale = HEAD_DIM ** (-0.5)
    depth = group // RING
    loads = load_matrix(packed_any, pack_ref, 0, depth // 2, local)
    matrix = lambda which: pack_ref[:, :, :, which * width : (which + 1) * width].reshape(-1, width)
    rank = lax.axis_index("dp")
    y, z = rank // RING, lax.rem(rank, RING)
    barrier, count = dp_barrier(y, z, None)
    stack[...] = head_stack(q_ref[...], scale)
    plain[...] = head_stack(q_ref[...], 1.0)
    for load in loads:
        load.wait()
    grad_ref[...] = jnp.dot(rows_ref[...], matrix(3), preferred_element_type=F32).astype(BF16)
    grad_stack[...] = head_stack(grad_ref[...], scale)
    grad_plain[...] = head_stack(grad_ref[...], 1.0)
    acc[...] = jnp.zeros_like(acc)
    seg_wide = jnp.concatenate([seg_q_ref[0:1, :]] * heads_here, axis=1)
    product = grad_ref[...].astype(F32).T * wide_ref[...]
    for head in range(heads_here):
        delta_ref[0:1, pl.ds(head * group, group)] = scale * jnp.sum(
            product[head * HEAD_DIM : (head + 1) * HEAD_DIM], axis=0, keepdims=True
        )
    pl.semaphore_wait(barrier, count)
    started = []
    push = pusher(send, recv, started)
    keys = Scatter(0, True, dk_ref, buffers[:SCATTER_BUFFERS], y, z, push)
    values = Scatter(1, False, dv_ref, buffers[SCATTER_BUFFERS:], y, z, push)

    def attend(offset_y, offset_z):
        at_y, at_z = step(y, offset_y), step(z, offset_z)
        key_block = k_ref[at_y, at_z]
        scores = block_scores(key_block, stack[...], seg_k_ref[at_y, at_z, :, 0:1], seg_wide)
        weights = jnp.exp(scores - lse_ref[0:1, :])
        dv_ref[at_y, at_z] = jnp.dot(
            weights.astype(BF16), grad_plain[...], preferred_element_type=F32
        ).astype(BF16)
        prob_grad = flat_dot(v_ref[at_y, at_z], grad_stack[...])
        low = (weights * (prob_grad - delta_ref[0:1, :])).astype(BF16)
        dk_ref[at_y, at_z] = jnp.dot(low, plain[...], preferred_element_type=F32).astype(BF16)
        turned = key_block.T
        for head in range(heads_here):
            rows = pl.ds(head * HEAD_DIM, HEAD_DIM)
            acc[rows, :] += jnp.dot(
                turned[head * HEAD_DIM : (head + 1) * HEAD_DIM],
                low[:, head * group : (head + 1) * group],
                preferred_element_type=F32,
            )

    def attend_all(first, count, offsets):
        def each(number, carry):
            attend(*offsets(number))
            return carry

        lax.fori_loop(first, count, each, 0)

    attend_all(0, 4, lambda t: (t * 0 + FAR, step(t, FAR)))
    for j in Scatter.ORDER:
        values.send_via(j)
    keys.send_direct(FAR)
    attend_all(1, 4, lambda t: (step(t, FAR), t * 0 + FAR))
    for j in Scatter.ORDER:
        keys.send_via(j)
    values.send_direct(FAR)
    attend_all(1, 4, lambda t: (t * 0 + PLUS, step(t, FAR)))
    keys.send_direct(PLUS)
    values.send_direct(PLUS)
    values.send_direct(MINUS)
    attend_all(1, 4, lambda t: (t * 0 + MINUS, step(t, FAR)))
    keys.send_direct(MINUS)
    values.send_direct(0)
    values.join()
    for j in (FAR, PLUS, MINUS):
        keys.join_one(j)
    attend_all(1, 4, lambda t: (t * 0, step(t, FAR)))
    keys.send_direct(0)
    keys.join_one(0)
    values.turn()
    keys.turn()
    values.join_two()
    keys.join_two()
    sums_ref[...] = jnp.zeros_like(sums_ref)
    query_grad = acc[...].T
    sums_ref[0:1, :] = jnp.sum(query_grad, axis=0, keepdims=True)
    triple_ref[0] = query_grad.astype(BF16)
    part = flat_dot(triple_ref[0], matrix(0))
    values.finish(total_ref)
    triple_ref[2] = total_ref[...].astype(BF16)
    sums_ref[1:2, :] = jnp.sum(total_ref[...], axis=0, keepdims=True)
    part = part + flat_dot(triple_ref[2], matrix(2))
    keys.finish(total_ref)
    triple_ref[1] = total_ref[...].astype(BF16)
    part = part + flat_dot(triple_ref[1], matrix(1))
    part_ref[...] = part.astype(BF16).reshape(part_ref.shape)
    for copy in started:
        copy.wait_send()


def attend_back_call(cid, attn_rows, packed, queries, keys, values, wide, lse, seg_wide, seg_column):
    group, model = attn_rows.shape
    width = queries.shape[1]
    heads_here = width // HEAD_DIM
    block = (group, width)
    stacked = pltpu.VMEM((group * heads_here, width), BF16)
    return pl.pallas_call(
        attend_back_kernel,
        out_shape=[
            jax.ShapeDtypeStruct((3, group, width), BF16),
            jax.ShapeDtypeStruct((8, width), F32),
            jax.ShapeDtypeStruct((RING, group // RING, model), BF16),
        ],
        in_specs=[vmem_spec(), any_spec()] + [vmem_spec()] * 7,
        out_specs=[vmem_spec()] * 3,
        scratch_shapes=[
            pltpu.VMEM((RING, RING, group // RING, model), BF16),
            pltpu.VMEM(block, BF16),
            stacked,
            stacked,
            stacked,
            stacked,
            pltpu.VMEM((width, group), F32),
            pltpu.VMEM((8, group * heads_here), F32),
            pltpu.VMEM((RING, RING) + block, BF16),
            pltpu.VMEM((RING, RING) + block, BF16),
            pltpu.VMEM(block, F32),
        ]
        + Scatter.scratch(block, BF16)
        + Scatter.scratch(block, BF16)
        + [
            pltpu.SemaphoreType.DMA((2, 6, RING)),
            pltpu.SemaphoreType.DMA((2, 6, RING)),
            pltpu.SemaphoreType.DMA((2,)),
        ],
        compiler_params=comm_params(cid),
    )(attn_rows, packed, queries, keys, values, wide, lse, seg_wide, seg_column)


class Exchange:
    def __init__(self, me, send, recv, landing, started):
        self.me, self.send, self.recv, self.landing, self.started = me, send, recv, landing, started
        self.reduces = {}

    def push(self, source, target, kind, index, k):
        copy = pltpu.make_async_remote_copy(
            src_ref=source,
            dst_ref=target,
            send_sem=self.send.at[kind, index, k - 1],
            recv_sem=self.recv.at[kind, index, k - 1],
            device_id={"tensor": step(self.me, k)},
            device_id_type=MESH,
        )
        copy.start()
        self.started.append(copy)
        return copy

    def reduce(self, part, peers=(1, 2, 3)):
        chunk = part.shape[-2] // CHUNKS
        for c in range(CHUNKS):
            here = pl.ds(c * chunk, chunk)
            for k in peers:
                self.reduces[c, k] = self.push(
                    part.at[step(self.me, k), here], self.landing.at[k - 1, here], 0, c, k
                )

    def run(self, part, function, rows_in, vecs, rows_out, sums_out, full, side=()):
        side = list(side)
        me = self.me
        chunk = part.shape[-2] // CHUNKS
        if side:
            side.pop(0)()
        sums, last = None, []
        for c in range(CHUNKS):
            here = pl.ds(c * chunk, chunk)
            for k in range(1, RING):
                self.reduces[c, k].wait_recv()
            total = part[me, here].astype(F32)
            for k in range(1, RING):
                total = total + self.landing[k - 1, here].astype(F32)
            spread, outs, parts = function(total, [ref[here].astype(F32) for ref in rows_in], vecs)
            if full is not None:
                full[me, here] = spread.astype(BF16)
                last += [
                    self.push(full.at[me, here], full.at[me, here], 1, c, k) for k in range(1, RING)
                ]
            for ref, value in zip(rows_out, outs):
                ref[here] = value.astype(ref.dtype)
            sums = parts if sums is None else [old + new for old, new in zip(sums, parts)]
        if sums_out is not None:
            sums_out[...] = jnp.concatenate(
                sums + [jnp.zeros((8 - len(sums), sums[0].shape[1]), F32)], axis=0
            )
        for work in side:
            work()
        for copy in last:
            copy.wait_recv()


TILES = ((2, 1), (3, 0))


def rows_of(ref, me, tile):
    return jnp.concatenate([ref[step(me, k)] for k in tile], axis=0)


def put_rows(ref, me, tile, value):
    rows = ref.shape[1]
    for i, k in enumerate(tile):
        ref[step(me, k)] = value[i * rows : (i + 1) * rows].astype(ref.dtype)


def wide_of(pack_ref):
    return pack_ref[...].reshape(-1, pack_ref.shape[-1])


def mlp_forward(me, full, up_ref, down_ref, bias, act_ref, slope_ref, part_ref, exchange):
    for tile in TILES:
        value = jnp.dot(rows_of(full, me, tile), wide_of(up_ref), preferred_element_type=F32)
        value = value + bias
        phi = 0.5 * (1.0 + lax.erf(value * (0.5**0.5)))
        act = (value * phi).astype(BF16)
        density = jnp.exp(-0.5 * value * value) * 0.3989422804014327
        put_rows(act_ref, me, tile, act)
        put_rows(slope_ref, me, tile, phi + value * density)
        put_rows(part_ref, me, tile, flat_dot(act, wide_of(down_ref)))
        exchange.reduce(part_ref, [k for k in tile if k])


def mlp_backward(me, full, up_ref, down_ref, slope_ref, pre_ref, bias_out, part_ref, exchange):
    total = None
    for tile in TILES:
        value = jnp.dot(rows_of(full, me, tile), wide_of(down_ref), preferred_element_type=F32)
        value = value * rows_of(slope_ref, me, tile)
        part = jnp.sum(value, axis=0, keepdims=True)
        total = part if total is None else total + part
        low = value.astype(BF16)
        put_rows(pre_ref, me, tile, low)
        put_rows(part_ref, me, tile, flat_dot(low, wide_of(up_ref)))
        exchange.reduce(part_ref, [k for k in tile if k])
    bias_out[...] = jnp.broadcast_to(total, bias_out.shape)


def product(former_ref, latter_ref, out_ref):
    def work():
        tokens = lambda ref: ref[...].reshape(-1, ref.shape[-1])
        size = 256

        def each(number, carry):
            columns = pl.ds(pl.multiple_of(number * size, size), size)
            left = former_ref[..., columns].reshape(-1, size)
            value = jnp.dot(left.T, tokens(latter_ref), preferred_element_type=F32)
            out_ref[number] = value.astype(BF16).reshape(out_ref.shape[1:])
            return carry

        lax.fori_loop(0, RING, each, 0)

    return work


def chain_call(cid, body, exchanges, packed_array, ins, outs, inside, any_names=(), extra=None):
    names = list(ins) + list(outs) + list(inside)
    rows, model = 64, 1024
    count = len(names)
    load_packed = packed_array is not None

    def kernel(*refs):
        refs = list(refs)
        packed = refs.pop(0) if load_packed else None
        env = SimpleNamespace(**dict(zip(names, refs[:count])))
        refs = refs[count:]
        me = lax.axis_index("tensor")
        barrier, peers = tensor_barrier(me)
        started = []
        loads = []
        if load_packed:
            env.up, env.down, local = refs[:3]
            refs = refs[3:]
            half = env.up.shape[2] // 2
            for i, matrix in enumerate((env.up, env.down)):
                loads += load_matrix(packed, matrix, i + 1, half, local.at[i])
        if extra is not None:
            env.extra = refs[3 * exchanges :]
            rank = lax.axis_index("dp")
            env.place = (rank // RING, lax.rem(rank, RING), lax.axis_index("section"))
            peers += dp_barrier(*env.place)[1]
        pl.semaphore_wait(barrier, peers)
        env.started = started
        rings = [
            Exchange(me, refs[3 * i + 1], refs[3 * i + 2], refs[3 * i], started)
            for i in range(exchanges)
        ]
        body(me, env, rings, loads)
        for copy in started:
            copy.wait_send()

    scratch = [pltpu.VMEM(shape, dtype) for shape, dtype in inside.values()]
    spec_of = lambda name: any_spec() if name in any_names else vmem_spec()
    args, in_specs = list(ins.values()), [spec_of(name) for name in ins]
    if load_packed:
        args, in_specs = [packed_array] + args, [any_spec()] + in_specs
        matrix = pltpu.VMEM((RING, RING, rows, model), BF16)
        scratch += [matrix, matrix, pltpu.SemaphoreType.DMA((2, 2))]
    for _ in range(exchanges):
        scratch += [
            pltpu.VMEM((RING - 1, rows, model), BF16),
            pltpu.SemaphoreType.DMA((2, CHUNKS, RING - 1)),
            pltpu.SemaphoreType.DMA((2, CHUNKS, RING - 1)),
        ]
    scratch += extra or []
    results = pl.pallas_call(
        kernel,
        out_shape=[jax.ShapeDtypeStruct(shape, dtype) for shape, dtype in outs.values()],
        in_specs=in_specs,
        out_specs=[spec_of(name) for name in outs],
        scratch_shapes=scratch,
        compiler_params=comm_params(cid),
    )(*args)
    return SimpleNamespace(**dict(zip(outs, results)))


def first_mlp_body(me, env, rings, loads):
    y, z, section = env.place
    send, recv, local = env.extra
    push = pusher(send, recv, env.started)
    halves = [pl.ds(0, HALF_ROWS // 2), pl.ds(HALF_ROWS // 2, HALF_ROWS // 2)]
    ring = Gather(
        ((0, (), True), (1, (), False)),
        [env.packed_next.at[section, :, :, half] for half in halves], y, z, (), push,
    )
    begin, near, middle, end, final = spread_stages(
        ring, [env.stage.at[1, half] for half in halves], local, section, push
    )
    rings[0].reduce(env.part)
    rings[0].run(
        env.part, middle_rows, [env.inputs], [env.vectors.at[0]],
        [env.attn_out, env.hidden], None, env.normed, [begin, near],
    )
    middle()
    for copy in loads:
        copy.wait()
    mlp_forward(
        me, env.normed, env.up, env.down, env.vectors[0, pl.ds(9 + me, 1), :], env.act, env.slope, env.sent, rings[1],
    )
    end()
    rings[1].run(
        env.sent, end_rows_first, [env.hidden], [env.vectors.at[0], env.vectors.at[1]],
        [env.mlp_out, env.outputs], None, env.next, [lambda: None, final],
    )


def last_mlp_body(me, env, rings, loads):
    rings[0].reduce(env.part)
    rings[0].run(
        env.part, middle_rows, [env.inputs], [env.vectors.at[1]],
        [env.attn_out, env.hidden], None, env.normed,
    )
    for copy in loads:
        copy.wait()
    mlp_forward(
        me, env.normed, env.up, env.down, env.vectors[1, pl.ds(9 + me, 1), :], env.act, env.slope,
        env.sent, rings[1],
    )
    rings[1].run(
        env.sent, end_rows_last, [env.hidden, env.upstream], [env.vectors.at[1]],
        [env.outputs], env.sums_end, env.mlp_rows,
    )
    mlp_backward(
        me, env.mlp_rows, env.up, env.down, env.slope, env.pre, env.bias_grad,
        env.sent_two, rings[2],
    )
    rings[2].run(
        env.sent_two, back_middle_rows, [env.upstream, env.hidden, env.attn_out],
        [env.vectors.at[1]], [env.hidden_grad], env.sums_middle, env.attn_rows,
        [
            product(env.mlp_rows, env.act, env.grad_down),
            product(env.normed, env.pre, env.grad_up),
        ],
    )


def attention_products(env):
    return [
        product(env.attn_rows_in, env.mixed, env.grad_out)
    ] + [
        product(env.normed_in, env.triple.at[which], env.grad_qkv.at[which])
        for which in range(3)
    ]


def between_body(me, env, rings, loads):
    y, z, section = env.place
    grads = [env.grad_qkv.at[which] for which in range(3)]
    grads += [env.grad_out, env.last_up, env.last_down]
    layer = layer_gradients(grads, env.extra, y, z, section, env.started)

    def swap():
        for work in attention_products(env):
            work()
        layer.keep()
        layer.swap()

    rings[0].reduce(env.part)
    rings[0].run(
        env.part, back_end_rows_last, [env.hidden_grad_in, env.inputs, env.mlp_out],
        [env.vectors.at[1], env.vectors.at[0]], [env.input_grad], env.sums_last, env.mlp_rows,
        [swap, layer.begin],
    )
    for copy in loads:
        copy.wait()
    mlp_backward(
        me, env.mlp_rows, env.up, env.down, env.slope, env.pre, env.bias_grad, env.sent, rings[1],
    )
    layer.join()

    def products():
        product(env.mlp_rows, env.act, env.grad_down)()
        product(env.normed, env.pre, env.grad_up)()

    def rest():
        layer.turn()
        layer.join_two()
        layer.finish(env.summed)
        layer.end()

    rings[1].run(
        env.sent, back_middle_rows_low, [env.input_grad, env.hidden, env.attn_out],
        [env.vectors.at[0]], [env.hidden_grad], env.sums_middle, env.attn_rows, [products, rest],
    )


def back_middle_rows_low(total, rows, vecs):
    return back_middle_rows(total, [rows[0].astype(BF16).astype(F32)] + rows[1:], vecs)


def close_body(me, env, rings, loads):
    rings[0].reduce(env.part)
    rings[0].run(
        env.part, back_end_rows_first, [env.hidden_grad_in, env.inputs],
        [env.vectors.at[0]], [env.input_grad], env.sums_last, None, attention_products(env),
    )


def shards(tokens, segment_ids, w_qkv, w_out, w_up, w_down, vectors, out_bias, cotangent):
    section = lax.axis_index("section")
    tensor_rank = lax.axis_index("tensor")
    own = lambda pair: jnp.where(section == 0, pair[0], pair[1])
    rows = tokens.shape[1]
    width = tokens.shape[2]
    group = rows * RING
    square = (RING, RING)
    local_width = w_qkv.shape[3]
    local_hidden = w_up.shape[2]

    depth = w_out.shape[1]
    my_segments = own(segment_ids)
    wide_segments = jnp.pad(my_segments, (0, depth - rows)).astype(BF16)[None]
    small = jnp.pad(
        jnp.concatenate([vectors[0], out_bias, wide_segments], axis=0),
        ((0, 1), (0, 128 - depth)),
    )
    packed_first, stage, small_rows, normed, inputs, my_cotangent, seg_wide, seg_column = first_call(
        0, tokens, cotangent, w_qkv[0], w_out[0], w_up[0], w_down[0], small
    )

    whole = (RING, rows, width)
    blocks = lambda columns: square + (depth, columns)
    spread = (RING, rows, local_hidden)
    row_shape = (rows, width)
    def attend_layer(layer, normed, packed):
        return attend_call(
            2 + 12 * layer, layer, normed.reshape(group, width), packed, small_rows, seg_wide, seg_column
        )

    normed_first = normed
    *kept_first, part = attend_layer(0, normed_first, packed_first)
    first = chain_call(
        3, first_mlp_body, 2, packed_first,
        dict(
            part=part, inputs=inputs, vectors=small_rows, stage=stage,
        ),
        dict(
            attn_out=(row_shape, F32), hidden=(row_shape, F32), normed=(whole, BF16),
            act=(spread, BF16), slope=(spread, F32), mlp_out=(row_shape, F32),
            outputs=(row_shape, BF16), next=(whole, BF16),
            packed_next=((2,) + square + (HALF_ROWS, local_hidden), BF16),
        ),
        dict(sent=(whole, BF16)),
        ("packed_next",),
        gather_scratch(),
    )
    between = first.outputs
    packed_last = first.packed_next
    *kept_last, part = attend_layer(1, first.next, packed_last)
    last = chain_call(
        5, last_mlp_body, 3, packed_last,
        dict(
            part=part, inputs=between, vectors=small_rows, upstream=my_cotangent,
        ),
        dict(
            outputs=(row_shape, BF16), sums_end=((8, width), F32),
            hidden_grad=(row_shape, F32), sums_middle=((8, width), F32),
            attn_rows=(whole, BF16), bias_grad=((8, local_hidden), F32),
            grad_up=(blocks(local_hidden), BF16), grad_down=(blocks(local_hidden), BF16),
        ),
        dict(
            attn_out=(row_shape, F32), hidden=(row_shape, F32), normed=(whole, BF16),
            act=(spread, BF16), slope=(spread, F32), pre=(spread, BF16),
            mlp_rows=(whole, BF16), sent=(whole, BF16), sent_two=(whole, BF16),
        ),
    )
    outputs = last.outputs

    def attend_back_layer(layer, attn_rows, kept, packed):
        queries, keys_full, values_full, mixed, wide, lse = kept
        return attend_back_call(
            7 + 12 * layer, attn_rows.reshape(group, width), packed, queries, keys_full,
            values_full, wide, lse, seg_wide, seg_column,
        )

    attention_grads = dict(
        grad_out=(blocks(local_width), BF16), grad_qkv=((3,) + blocks(local_width), BF16),
    )
    triple, attend_last, part = attend_back_layer(1, last.attn_rows, kept_last, packed_last)
    middle = chain_call(
        8, between_body, 2, packed_first,
        dict(
            part=part, hidden_grad_in=last.hidden_grad, inputs=between,
            mlp_out=first.mlp_out, vectors=small_rows,
            slope=first.slope, act=first.act, normed=first.normed,
            hidden=first.hidden, attn_out=first.attn_out,
            attn_rows_in=last.attn_rows, mixed=kept_last[3], normed_in=first.next,
            triple=triple, last_up=last.grad_up, last_down=last.grad_down,
        ),
        dict(
            summed=((HALF_ROWS, local_hidden), F32),
            input_grad=(row_shape, F32), sums_last=((8, width), F32),
            hidden_grad=(row_shape, F32), sums_middle=((8, width), F32),
            attn_rows=(whole, BF16), bias_grad=((8, local_hidden), F32),
            grad_up=(blocks(local_hidden), BF16), grad_down=(blocks(local_hidden), BF16),
            **attention_grads,
        ),
        dict(pre=(spread, BF16), mlp_rows=(whole, BF16), sent=(whole, BF16)),
        ("last_up", "last_down"),
        LayerGradients.scratch(HALF_ROWS // 3, local_hidden),
    )
    last_grad = middle.input_grad
    triple, attend_first, part = attend_back_layer(0, middle.attn_rows, kept_first, packed_first)
    close = chain_call(
        9, close_body, 1, None,
        dict(
            part=part, hidden_grad_in=middle.hidden_grad, inputs=inputs,
            vectors=small_rows, attn_rows_in=middle.attn_rows, mixed=kept_first[3],
            normed_in=normed_first, triple=triple,
        ),
        dict(input_grad=(row_shape, F32), sums_last=((8, width), F32), **attention_grads),
        dict(),
    )
    input_grad = close.input_grad
    sums = [
        [close.sums_last, middle.sums_middle, middle.sums_last[2:], attend_first, middle.bias_grad],
        [middle.sums_last, last.sums_middle, last.sums_end, attend_last, last.bias_grad],
    ]
    grads = [close.grad_qkv[which] for which in range(3)]
    grads += [close.grad_out, middle.grad_up, middle.grad_down]
    first_grad = input_grad

    small_sum, packed_sum, out_pair, grad_pair = final_call(
        10, sums[0] + sums[1], grads, middle.summed, [outputs, between, last_grad, first_grad]
    )
    half = depth // 2
    columns = lambda which: packed_sum[
        :, :half, which * local_width : (which + 1) * local_width
    ].reshape(depth, local_width)
    return (
        out_pair[None],
        grad_pair[None],
        jnp.stack([columns(0), columns(1), columns(2)])[None],
        columns(3)[None],
        packed_sum[:, half : 2 * half].reshape(1, depth, local_hidden),
        packed_sum[:, 2 * half :].reshape(1, depth, local_hidden),
        small_sum[:13, :depth][None],
        small_sum[13:14, :depth],
    )


def solution(mesh):
    in_specs = (
        P(None, ("dp", "tensor"), None),
        P(None, ("dp", "tensor")),
        P("section", None, "dp", "tensor"),
        P("section", "dp", "tensor"),
        P("section", "dp", "tensor"),
        P("section", "dp", "tensor"),
        P("section", None, "dp"),
        P("section", "dp"),
        P(None, ("dp", "tensor"), None),
    )
    out_specs = (
        P("section", None, ("dp", "tensor"), None),
        P("section", None, ("dp", "tensor"), None),
        P("section", None, "dp", "tensor"),
        P("section", "dp", "tensor"),
        P("section", "dp", "tensor"),
        P("section", "dp", "tensor"),
        P("section", None, "dp"),
        P("section", "dp"),
    )
    return jax.shard_map(shards, mesh=mesh, in_specs=in_specs, out_specs=out_specs, check_vma=False)
```

```python
import functools
from types import SimpleNamespace

import jax
import jax.numpy as jnp
from jax import lax
from jax.experimental import pallas as pl
from jax.experimental.pallas import tpu as pltpu
from jax.sharding import PartitionSpec as P

MESH = pl.DeviceIdType.MESH
HEAD_DIM = 64
EPSILON = 1e-06
MASKED_SCORE = -1e30
RING = 4
VMEM_LIMIT = 56 * 1024 * 1024
F32 = jnp.float32
BF16 = jnp.bfloat16


def vmem_spec():
    return pl.BlockSpec(memory_space=pltpu.VMEM)


def any_spec():
    return pl.BlockSpec(memory_space=pl.ANY)


def comm_params(cid):
    return pltpu.CompilerParams(
        collective_id=cid, has_side_effects=True, vmem_limit_bytes=VMEM_LIMIT
    )


def step(coord, by):
    return lax.rem(coord + by, RING)


def layer_norm(values, gain_row, shift_row):
    centre = values - jnp.mean(values, axis=-1, keepdims=True)
    spread = jnp.mean(centre * centre, axis=-1, keepdims=True)
    return centre * lax.rsqrt(spread + EPSILON) * gain_row + shift_row


def layer_norm_back(values, gain_row, grad):
    centre = values - jnp.mean(values, axis=-1, keepdims=True)
    spread = jnp.mean(centre * centre, axis=-1, keepdims=True)
    inverse = lax.rsqrt(spread + EPSILON)
    normed = centre * inverse
    scaled = grad * gain_row
    back = inverse * (
        scaled
        - jnp.mean(scaled, axis=-1, keepdims=True)
        - normed * jnp.mean(scaled * normed, axis=-1, keepdims=True)
    )
    return back, jnp.sum(grad * normed, axis=0, keepdims=True), jnp.sum(grad, axis=0, keepdims=True)


PLUS, FAR, MINUS = 1, 2, 3
CHUNKS = 2


def tensor_barrier(me):
    barrier = pltpu.get_barrier_semaphore()
    for k in range(1, RING):
        pl.semaphore_signal(
            barrier, inc=1, device_id={"tensor": step(me, k)}, device_id_type=MESH
        )
    return barrier, RING - 1


def row(ref, index):
    return ref[pl.ds(index, 1), :]


def middle_rows(total, rows, vecs):
    vec = vecs[0]
    attn_out = total + row(vec, 13)
    hidden = rows[0] + row(vec, 4) * attn_out
    return layer_norm(hidden, row(vec, 5), row(vec, 6)), [attn_out, hidden], []


def end_rows_first(total, rows, vecs):
    vec, after = vecs
    mlp_out = total + row(vec, 7)
    outputs = (rows[0] + row(vec, 8) * mlp_out).astype(BF16)
    inputs = outputs.astype(F32)
    return layer_norm(inputs, row(after, 0), row(after, 1)), [mlp_out, outputs], []


def end_rows_last(total, rows, vecs):
    vec = vecs[0]
    hidden, upstream = rows
    mlp_out = total + row(vec, 7)
    outputs = hidden + row(vec, 8) * mlp_out
    mlp_grad = row(vec, 8) * upstream
    sums = [
        jnp.sum(upstream * mlp_out, axis=0, keepdims=True),
        jnp.sum(mlp_grad, axis=0, keepdims=True),
    ]
    return mlp_grad, [outputs], sums


def back_middle_rows(total, rows, vecs):
    vec = vecs[0]
    upstream, hidden, attn_out = rows
    part, gain, shift = layer_norm_back(hidden, row(vec, 5), total)
    hidden_grad = upstream + part
    attn_grad = row(vec, 4) * hidden_grad
    sums = [
        gain,
        shift,
        jnp.sum(hidden_grad * attn_out, axis=0, keepdims=True),
        jnp.sum(attn_grad, axis=0, keepdims=True),
    ]
    return attn_grad, [hidden_grad], sums


def back_end_rows_last(total, rows, vecs):
    vec, before = vecs
    hidden_grad, inputs, mlp_out = rows
    part, gain, shift = layer_norm_back(inputs, row(vec, 0), total)
    input_grad = hidden_grad + part
    upstream = input_grad.astype(BF16).astype(F32)
    mlp_grad = row(before, 8) * upstream
    sums = [
        gain,
        shift,
        jnp.sum(upstream * mlp_out, axis=0, keepdims=True),
        jnp.sum(mlp_grad, axis=0, keepdims=True),
    ]
    return mlp_grad, [input_grad], sums


def back_end_rows_first(total, rows, vecs):
    hidden_grad, inputs = rows
    part, gain, shift = layer_norm_back(inputs, row(vecs[0], 0), total)
    return None, [hidden_grad + part], [gain, shift]


def dp_neighbour(y, z, along_z, k):
    if along_z:
        return {"dp": y * RING + step(z, k)}
    return {"dp": step(y, k) * RING + z}


def dp_barrier(y, z, section):
    barrier = pltpu.get_barrier_semaphore()
    count = 0
    for along_z in (True, False):
        for k in (PLUS, MINUS):
            pl.semaphore_signal(
                barrier, inc=1, device_id=dp_neighbour(y, z, along_z, k), device_id_type=MESH
            )
            count += 1
    if section is not None:
        pl.semaphore_signal(
            barrier, inc=1, device_id={"section": 1 - section}, device_id_type=MESH
        )
        count += 1
    return barrier, count


def pusher(send, recv, started):
    def push(index, kind, k, source, target, device):
        copy = pltpu.make_async_remote_copy(
            src_ref=source,
            dst_ref=target,
            send_sem=send.at[index, kind, k],
            recv_sem=recv.at[index, kind, k],
            device_id=device,
            device_id_type=MESH,
        )
        copy.start()
        started.append(copy)
        return copy

    return push


class Gather:
    WAYS = {0: 1, 3: 1, 1: 1, 2: 3}

    def __init__(self, pieces, outs, y, z, lead, push):
        self.pieces, self.outs, self.y, self.z = pieces, outs, y, z
        self.lead, self.push = lead, push
        self.every = range(len(pieces))
        self.first, self.onward, self.second, self.relayed = {}, {}, {}, {}

    def block(self, i, along, across, rows=None):
        number, pre, along_z = self.pieces[i]
        ys, zs = (across, along) if along_z else (along, across)
        ys = ys if isinstance(ys, slice) else step(self.y, ys) if ys else self.y
        zs = zs if isinstance(zs, slice) else step(self.z, zs) if zs else self.z
        return self.outs[number].at[self.lead + pre + (ys, zs) + (() if rows is None else (rows,))]

    def way(self, i, first, k):
        return dp_neighbour(self.y, self.z, self.pieces[i][2] == first, k)

    def halves(self, i):
        height = self.outs[self.pieces[i][0]].shape[-2]
        if height < 32:
            return {PLUS: None}
        half = height // 32 * 16
        return {PLUS: pl.ds(0, half), MINUS: pl.ds(half, height - half)}

    def spread(self, i, offset, source):
        for k in (PLUS, MINUS):
            self.second[i, offset, k] = self.push(
                i, 2 if k == PLUS else 3, offset, source, self.block(i, offset, 0), self.way(i, False, k)
            )

    def begin(self, i, source):
        for k in (PLUS, MINUS):
            self.first[i, k] = self.push(i, 0, k, source, self.block(i, 0, 0), self.way(i, True, k))
        self.spread(i, 0, source)

    def near(self):
        for i in self.every:
            split = self.halves(i)
            for k in (PLUS, MINUS):
                self.first[i, k].wait_recv()
                came = RING - k
                if k in split:
                    self.onward[i, k] = self.push(
                        i, 1, k, self.block(i, came, 0, split[k]), self.block(i, came, 0, split[k]),
                        self.way(i, True, k),
                    )
                self.spread(i, came, self.block(i, came, 0))

    def relay(self, i, offset):
        k = self.WAYS[offset]
        self.second[i, offset, k].wait_recv()
        came = self.block(i, offset, RING - k)
        self.relayed[i, offset] = self.push(i, 4, offset, came, came, self.way(i, False, k))

    def other(self, i, offset):
        self.second[i, offset, RING - self.WAYS[offset]].wait_recv()

    def far(self, i):
        for k in self.halves(i):
            self.onward[i, k].wait_recv()
        self.spread(i, FAR, self.block(i, FAR, 0))


def half_of(section, height):
    return pl.ds(pl.multiple_of(section * height, height), height)


def spread_stages(ring, sources, local, section, push):
    own, across = {}, []

    def pass_on(i, line):
        came = ring.block(i, slice(None), line)
        across.append(push(i, 5, line, came, came, {"section": 1 - section}))

    def begin():
        for i in ring.every:
            ring.begin(i, sources[i])
            own[i] = pltpu.make_async_copy(sources[i], ring.block(i, 0, 0), local.at[i])
            own[i].start()

    def near():
        ring.near()
        for i in ring.every:
            ring.relay(i, 0)

    def middle():
        for i in ring.every:
            ring.far(i)
        for i in ring.every:
            ring.relay(i, MINUS)
            ring.relay(i, PLUS)
            own[i].wait()
            pass_on(i, 0)

    def end():
        for i in ring.every:
            ring.relay(i, FAR)
            for offset in range(RING):
                ring.other(i, offset)
            pass_on(i, PLUS)
            pass_on(i, MINUS)

    def last():
        for i in ring.every:
            for offset in range(RING):
                ring.relayed[i, offset].wait_recv()
            pass_on(i, FAR)
        for copy in across:
            copy.wait_recv()

    return [begin, near, middle, end, last]


HALF_ROWS = 96
SMALL = 16


def half_places(half, width, hidden):
    return [(0, which * width, width) for which in range(4)] + [
        (half, 0, hidden),
        (2 * half, 0, hidden),
    ]


def first_kernel(
    tokens_in, cotangent_in, qkv_in, out_in, up_in, down_in, small_in,
    packed_out, stage, rows_out, full, tokens_out, cotangent_out, seg_wide, seg_column,
    small_all, seg_parts, seg_rows,
    send, recv, local, small_send, small_recv, small_local,
    swap_send, swap_recv, swap_local, tensor_send, tensor_recv,
):
    rank = lax.axis_index("dp")
    y, z = rank // RING, lax.rem(rank, RING)
    section = lax.axis_index("section")
    me = lax.axis_index("tensor")
    barrier, count = dp_barrier(y, z, section)
    count += tensor_barrier(me)[1]
    depth, width = out_in.shape
    half = depth // 2
    mine, others = half_of(section, half), half_of(1 - section, half)
    sources = [qkv_in.at[which] for which in range(3)] + [out_in, up_in, down_in]
    places = half_places(half, width, stage.shape[2])
    tokens_out[...] = jnp.where(section == 0, tokens_in[0], tokens_in[1])
    cotangent_out[...] = jnp.where(section == 0, cotangent_in[0], cotangent_in[1])
    seg_parts[me] = jnp.zeros(seg_parts.shape[1:], jnp.int32)
    pl.semaphore_wait(barrier, count)
    started = []
    push = pusher(send, recv, started)
    swaps, kept = [], []
    for i, (source, (row, column, columns)) in enumerate(zip(sources, places)):
        target = stage.at[section, pl.ds(row, half), pl.ds(column, columns)]
        copy = pltpu.make_async_remote_copy(
            src_ref=source.at[others],
            dst_ref=target,
            send_sem=swap_send.at[i],
            recv_sem=swap_recv.at[i],
            device_id={"section": 1 - section},
            device_id_type=MESH,
        )
        copy.start()
        swaps.append(copy)
        copy = pltpu.make_async_copy(source.at[mine], target, swap_local.at[i])
        copy.start()
        kept.append(copy)
    small_push = pusher(small_send, small_recv, started)
    small_ring = Gather(((0, (), True),), [small_all.at[section]], y, z, (), small_push)
    small_stages = spread_stages(small_ring, [small_in], small_local, section, small_push)
    small_stages[0]()
    for copy in kept:
        copy.wait()
    for copy in swaps:
        copy.wait_recv()
    halves = [pl.ds(0, HALF_ROWS // 2), pl.ds(HALF_ROWS // 2, HALF_ROWS // 2)]
    views = [packed_out.at[section, :, :, rows] for rows in halves]
    ring = Gather(((0, (), True), (1, (), False)), views, y, z, (), push)
    stages = spread_stages(ring, [stage.at[0, rows] for rows in halves], local, section, push)
    stages[0]()
    small_stages[1]()
    small_stages[2]()
    stages[1]()
    small_stages[3]()
    small_stages[4]()
    for layer in range(2):
        for number in range(RING * RING):
            part = small_all[layer, number // RING, number % RING]
            rows_out[layer, :, number * depth : (number + 1) * depth] = part[:, :depth].astype(F32)
    for number in range(RING * RING):
        part = small_all[section, number // RING, number % RING]
        seg_parts[me, number : number + 1, 0:depth] = (
            part[14:15, :depth].astype(F32).astype(jnp.int32)
        )
    full[me] = layer_norm(
        tokens_out[...].astype(F32), rows_out[0, 0:1, :], rows_out[0, 1:2, :]
    ).astype(BF16)
    tensor_copies = []
    for i, ref in enumerate((seg_parts, full)):
        for k in range(1, RING):
            copy = pltpu.make_async_remote_copy(
                src_ref=ref.at[me],
                dst_ref=ref.at[me],
                send_sem=tensor_send.at[i, k],
                recv_sem=tensor_recv.at[i, k],
                device_id={"tensor": step(me, k)},
                device_id_type=MESH,
            )
            copy.start()
            tensor_copies.append(copy)
    stages[2]()
    stages[3]()
    for copy in tensor_copies:
        copy.wait_recv()
    for number in range(RING):
        seg_rows[:, number * depth : (number + 1) * depth] = seg_parts[number][:, :depth]
    seg_wide[...] = jnp.broadcast_to(seg_rows[pl.ds(rank, 1), :], seg_wide.shape)
    turned = seg_rows[...].astype(F32).T
    for number in range(RING * RING):
        seg_column[number // RING, number % RING] = jnp.broadcast_to(
            turned[:, number : number + 1], seg_column.shape[2:]
        ).astype(jnp.int32)
    stages[4]()
    for copy in started + swaps + tensor_copies:
        copy.wait_send()


def gather_scratch():
    return [
        pltpu.SemaphoreType.DMA((2, 6, RING)),
        pltpu.SemaphoreType.DMA((2, 6, RING)),
        pltpu.SemaphoreType.DMA((2,)),
    ]


def first_call(cid, tokens, cotangent, w_qkv, w_out, w_up, w_down, small):
    depth = w_out.shape[0]
    hidden = w_up.shape[1]
    rows, width = tokens.shape[1:]
    group = RING * rows
    return pl.pallas_call(
        first_kernel,
        out_shape=[
            jax.ShapeDtypeStruct((2, RING, RING, HALF_ROWS, hidden), BF16),
            jax.ShapeDtypeStruct((2, HALF_ROWS, hidden), BF16),
            jax.ShapeDtypeStruct((2, SMALL, width), F32),
            jax.ShapeDtypeStruct((RING, rows, width), BF16),
            jax.ShapeDtypeStruct((rows, width), BF16),
            jax.ShapeDtypeStruct((rows, width), BF16),
            jax.ShapeDtypeStruct((8, group), jnp.int32),
            jax.ShapeDtypeStruct((RING, RING, group, 128), jnp.int32),
        ],
        in_specs=[vmem_spec()] * 7,
        out_specs=[any_spec()] + [vmem_spec()] * 7,
        scratch_shapes=[
            pltpu.VMEM((2, RING, RING) + small.shape, BF16),
            pltpu.VMEM((RING, RING * RING, 128), jnp.int32),
            pltpu.VMEM((RING * RING, group), jnp.int32),
        ]
        + gather_scratch()
        + gather_scratch()
        + [
            pltpu.SemaphoreType.DMA((6,)),
            pltpu.SemaphoreType.DMA((6,)),
            pltpu.SemaphoreType.DMA((6,)),
            pltpu.SemaphoreType.DMA((2, RING)),
            pltpu.SemaphoreType.DMA((2, RING)),
        ],
        compiler_params=comm_params(cid),
    )(tokens, cotangent, w_qkv, w_out, w_up, w_down, small)


class Scatter:
    ORDER = (FAR, PLUS, MINUS, 0)
    WAYS = {FAR: PLUS, 0: PLUS, PLUS: MINUS, MINUS: MINUS}

    def __init__(self, index, along_z, source, buffers, y, z, push):
        self.index, self.along_z, self.source = index, along_z, source
        self.passing, self.joined, self.summed, self.straight, self.middle = buffers[:5]
        self.far_two, self.joined_two, self.summed_two, self.straight_two = buffers[5:]
        self.y, self.z, self.push = y, z, push
        self.height, self.width = source.shape[-2:]
        self.via, self.direct, self.after = {}, {}, {}

    def at(self, along, across):
        ys, zs = (across, along) if self.along_z else (along, across)
        return step(self.y, ys), step(self.z, zs)

    def way(self, first, k):
        return dp_neighbour(self.y, self.z, self.along_z == first, k)

    def add(self, target, terms, top=0, height=None):
        height = self.height if height is None else height
        size = max(8, min(height, 65536 // self.width))
        while height % size:
            size -= 16

        def part(here):
            value = terms[0](here).astype(F32)
            for term in terms[1:]:
                value = value + term(here).astype(F32)
            target[here] = value.astype(target.dtype)

        if height <= size:
            part(pl.ds(top, height))
            return

        def each(number, carry):
            part(pl.ds(pl.multiple_of(top + number * size, size), size))
            return carry

        lax.fori_loop(0, height // size, each, 0)

    def send_via(self, j):
        self.via[j] = self.push(
            self.index, 0, j, self.source.at[self.at(FAR, j)], self.passing.at[j],
            self.way(True, self.WAYS[j]),
        )

    def send_direct(self, j):
        k = RING - self.WAYS[j]
        self.direct[j] = self.push(
            self.index, 1, j, self.source.at[self.at(k, j)], self.straight.at[j], self.way(True, k)
        )

    def begin(self):
        for j in self.ORDER:
            self.send_via(j)
        for j in self.ORDER:
            self.send_direct(j)

    def join_one(self, j):
        self.via[j].wait_recv()
        k = self.WAYS[j]
        at_y, at_z = self.at(k, j)
        self.add(
            self.joined.at[j],
            [lambda h: self.source[at_y, at_z, h], lambda h: self.passing[j, h]],
        )
        self.after[j] = self.push(
            self.index, 2, j, self.joined.at[j], self.summed.at[j], self.way(True, k)
        )

    def join(self):
        for j in self.ORDER:
            self.join_one(j)

    def turn(self):
        half = self.height // 2
        low, high = pl.ds(0, half), pl.ds(half, half)
        send = lambda kind, slot, source, target, k: self.push(
            self.index, kind, slot, source, target, self.way(False, k)
        )
        for j in self.ORDER:
            self.direct[j].wait_recv()
            self.after[j].wait_recv()
            at_y, at_z = self.at(0, j)
            self.add(
                self.middle.at[j],
                [
                    lambda h: self.source[at_y, at_z, h],
                    lambda h: self.summed[j, h],
                    lambda h: self.straight[j, h],
                ],
            )
            if j == FAR:
                self.via_two = [
                    send(3, 0, self.middle.at[j, low], self.far_two.at[low], PLUS),
                    send(3, 1, self.middle.at[j, high], self.far_two.at[high], MINUS),
                ]
            if j == PLUS:
                high_copy = send(4, 1, self.middle.at[j, high], self.straight_two.at[high], PLUS)
            if j == MINUS:
                low_copy = send(4, 0, self.middle.at[j, low], self.straight_two.at[low], MINUS)
        self.direct_two = [low_copy, high_copy]

    def join_two(self):
        half = self.height // 2
        self.after_two = []
        for number, (top, k) in enumerate(((0, PLUS), (half, MINUS))):
            self.via_two[number].wait_recv()
            self.add(
                self.joined_two,
                [lambda h: self.middle[k, h], lambda h: self.far_two[h]],
                top,
                half,
            )
            here = pl.ds(top, half)
            self.after_two.append(
                self.push(
                    self.index, 5, number, self.joined_two.at[here], self.summed_two.at[here],
                    self.way(False, k),
                )
            )

    def finish(self, out):
        for copy in self.direct_two + self.after_two:
            copy.wait_recv()
        self.add(
            out,
            [
                lambda h: self.middle[0, h],
                lambda h: self.summed_two[h],
                lambda h: self.straight_two[h],
            ],
        )

    @staticmethod
    def scratch(block, dtype):
        return [pltpu.VMEM((RING,) + block, dtype)] * 5 + [pltpu.VMEM(block, dtype)] * 4


SCATTER_BUFFERS = 9


def scatter_buffers(block, dtype):
    square = pltpu.VMEM((RING, RING) + block, dtype)
    return [square, square] + Scatter.scratch(block, dtype)


class LayerGradients:
    def __init__(self, grads, buffers, semaphores, y, z, section, push):
        self.grads, self.buffers, self.y, self.z = grads, buffers, y, z
        self.section, self.push = section, push
        self.swap_send, self.swap_recv, self.keep_local = semaphores
        depth, width = grads[0].shape[2:]
        hidden = grads[5].shape[3]
        self.half = depth // 2
        self.places = [(0, 0, which * width, width) for which in range(4)]
        self.places += [(1, 0, 0, hidden), (1, self.half, 0, hidden)]

    def region(self, which, place):
        piece, row, column, columns = place
        return self.buffers[piece][which].at[:, :, pl.ds(row, self.half), pl.ds(column, columns)]

    def keep(self):
        mine = half_of(self.section, self.half)
        self.keeps = []
        for i, place in enumerate(self.places):
            copy = pltpu.make_async_copy(
                self.grads[i].at[:, :, mine], self.region(0, place), self.keep_local.at[i]
            )
            copy.start()
            self.keeps.append(copy)

    def swap(self):
        others = half_of(1 - self.section, self.half)
        self.swaps = []
        for i, place in enumerate(self.places):
            copy = pltpu.make_async_remote_copy(
                src_ref=self.grads[i].at[:, :, others],
                dst_ref=self.region(1, place),
                send_sem=self.swap_send.at[i],
                recv_sem=self.swap_recv.at[i],
                device_id={"section": 1 - self.section},
                device_id_type=MESH,
            )
            copy.start()
            self.swaps.append(copy)

    def begin(self):
        self.parts = []
        for piece in range(2):
            for i, place in enumerate(self.places):
                if place[0] == piece:
                    self.keeps[i].wait()
                    self.swaps[i].wait_recv()
            own, sibling = self.buffers[piece][:2]
            add_blocks(own, own, sibling)
            self.parts.append(
                Scatter(piece, piece == 0, own, self.buffers[piece][2:], self.y, self.z, self.push)
            )
            self.parts[piece].begin()

    def join(self):
        for part in self.parts:
            part.join()

    def turn(self):
        for part in self.parts:
            part.turn()

    def join_two(self):
        for part in self.parts:
            part.join_two()

    def finish(self, out):
        self.parts[0].finish(out.at[pl.ds(0, self.half)])
        self.parts[1].finish(out.at[pl.ds(self.half, 2 * self.half)])

    def end(self):
        for copy in self.swaps:
            copy.wait_send()

    @staticmethod
    def scratch(half, hidden):
        return (
            scatter_buffers((half, hidden), BF16)
            + scatter_buffers((2 * half, hidden), BF16)
            + [pltpu.SemaphoreType.DMA((6,))] * 3
            + [pltpu.SemaphoreType.DMA((3, 7, RING))] * 2
        )


LAYER_SCRATCH = 2 * (2 + SCATTER_BUFFERS) + 5


def layer_gradients(grads, scratch, y, z, section, started):
    size = 2 + SCATTER_BUFFERS
    push = pusher(scratch[-2], scratch[-1], started)
    return LayerGradients(
        grads, [scratch[:size], scratch[size : 2 * size]], scratch[2 * size : 2 * size + 3],
        y, z, section, push,
    )


def add_blocks(out, former, latter):
    def add(number, carry):
        at_y, at_z = number // RING, lax.rem(number, RING)
        out[at_y, at_z] = (
            former[at_y, at_z].astype(F32) + latter[at_y, at_z].astype(F32)
        ).astype(out.dtype)
        return carry

    lax.fori_loop(0, RING * RING, add, 0)


def final_kernel(*refs):
    refs = list(refs)
    take = lambda count: [refs.pop(0) for _ in range(count)]
    sums = [take(5), take(5)]
    grad_qkv, *grads = take(4)
    grads = [grad_qkv.at[which] for which in range(3)] + grads
    summed_last = take(1)[0]
    extras = take(4)
    small_out, qkv_out, *matrix_outs = take(5)
    targets = [qkv_out.at[which] for which in range(3)] + matrix_outs
    extra_outs = take(2)
    small_in, small_rows, vector_own, vector_parts, summed = take(5)
    extra_sends = take(2)
    small_buffers = take(2 + SCATTER_BUFFERS)
    layer_scratch = take(LAYER_SCRATCH)
    vector_send, vector_recv, extra_send, extra_recv, result_send, result_recv, result_local, hand_local = take(8)
    rank = lax.axis_index("dp")
    y, z = rank // RING, lax.rem(rank, RING)
    section = lax.axis_index("section")
    me = lax.axis_index("tensor")
    other = {"section": 1 - section}
    barrier, count = tensor_barrier(me)
    count += dp_barrier(y, z, section)[1]

    started = []
    first_layer = layer_gradients(grads, layer_scratch, y, z, section, started)
    push = first_layer.push
    first_layer.keep()
    handed = pltpu.make_async_copy(summed_last, summed.at[1], hand_local)
    handed.start()
    depth = grads[0].shape[2]
    for i in range(2):
        last_value, first_value = extras[2 * i][...], extras[2 * i + 1][...]
        extra_outs[i][section] = jnp.where(section == 0, first_value, last_value)
        extra_sends[i][...] = jnp.where(section == 0, last_value, first_value)

    small_rows[...] = jnp.zeros_like(small_rows)
    model = small_rows.shape[1]
    for layer in range(2):
        first, middle, end, attend, up = sums[layer]
        top = SMALL * layer
        part = attend.shape[1]
        lanes = pl.ds(pl.multiple_of(me * part, part), part)
        small_rows[top : top + 2, :] = first[0:2, :]
        small_rows[top + 2 : top + 3, lanes] = attend[0:1, :]
        small_rows[top + 3 : top + 4, lanes] = attend[1:2, :]
        small_rows[top + 4 : top + 5, :] = middle[2:3, :]
        small_rows[top + 5 : top + 7, :] = middle[0:2, :]
        small_rows[top + 7 : top + 8, :] = end[1:2, :]
        small_rows[top + 8 : top + 9, :] = end[0:1, :]
        for rank_of in range(RING):
            small_rows[top + 9 + rank_of : top + 10 + rank_of, :] = jnp.where(
                me == rank_of, up[0:1, :], 0.0
            )
        small_rows[top + 13 : top + 14, :] = middle[3:4, :]
    small_in[...] = jnp.zeros_like(small_in)
    for number in range(RING * RING):
        small_in[number // RING, number % RING, :, 0:depth] = small_rows[
            :, number * depth : (number + 1) * depth
        ]
    pl.semaphore_wait(barrier, count)
    first_layer.swap()
    small_swap = push(2, 6, 0, small_in.at[:, :, half_of(1 - section, SMALL)], small_buffers[1], other)
    extra_copies = []
    for i in range(2):
        copy = pltpu.make_async_remote_copy(
            src_ref=extra_sends[i],
            dst_ref=extra_outs[i].at[section],
            send_sem=extra_send.at[i],
            recv_sem=extra_recv.at[i],
            device_id=other,
            device_id_type=MESH,
        )
        copy.start()
        extra_copies.append(copy)

    first_layer.begin()
    small_swap.wait_recv()
    add_blocks(small_buffers[0], small_in.at[:, :, half_of(section, SMALL)], small_buffers[1])
    small_part = Scatter(2, True, small_buffers[0], small_buffers[2:], y, z, push)
    small_part.begin()
    first_layer.join()
    small_part.join()
    first_layer.turn()
    small_part.turn()
    first_layer.join_two()
    small_part.join_two()
    small_part.finish(vector_own)
    vector_parts[me] = vector_own[...]
    vector_copies = []
    for k in range(1, RING):
        copy = pltpu.make_async_remote_copy(
            src_ref=vector_own,
            dst_ref=vector_parts.at[me],
            send_sem=vector_send.at[k],
            recv_sem=vector_recv.at[k],
            device_id={"tensor": step(me, k)},
            device_id_type=MESH,
        )
        copy.start()
        vector_copies.append(copy)
    first_layer.finish(summed.at[0])
    handed.wait()
    half = depth // 2
    mine = half_of(section, half)
    results = []
    for i, (row, column, columns) in enumerate(half_places(half, qkv_out.shape[2], summed.shape[2])):
        area = (pl.ds(row, half), pl.ds(column, columns))
        copy = pltpu.make_async_remote_copy(
            src_ref=summed.at[(1 - section,) + area],
            dst_ref=targets[i].at[mine],
            send_sem=result_send.at[i],
            recv_sem=result_recv.at[i],
            device_id=other,
            device_id_type=MESH,
        )
        copy.start()
        results.append(copy)
        copy = pltpu.make_async_copy(
            summed.at[(section,) + area], targets[i].at[mine], result_local.at[i]
        )
        copy.start()
        results.append(copy)
    for copy in results:
        copy.wait()
    for copy in vector_copies:
        copy.wait()
    total = vector_parts[0]
    for k in range(1, RING):
        total = total + vector_parts[k]
    small_out[...] = total
    for copy in extra_copies:
        copy.wait()
    first_layer.end()
    for copy in started:
        copy.wait_send()


def final_call(cid, sums, grads, summed_last, extras):
    extra = len(extras)
    width = sums[0].shape[1]
    hidden = grads[-1].shape[3]
    args = list(sums) + list(grads) + [summed_last] + list(extras)
    block = (HALF_ROWS, hidden)
    return pl.pallas_call(
        final_kernel,
        out_shape=[
            jax.ShapeDtypeStruct((SMALL, 128), F32),
            jax.ShapeDtypeStruct((3,) + grads[1].shape[2:], F32),
        ]
        + [jax.ShapeDtypeStruct(value.shape[2:], F32) for value in grads[1:]]
        + [jax.ShapeDtypeStruct((2,) + value.shape, value.dtype) for value in extras[::2]],
        in_specs=[vmem_spec()] * len(sums) + [any_spec()] * (len(grads) + 1) + [vmem_spec()] * extra,
        out_specs=[vmem_spec()] * 7,
        scratch_shapes=[
            pltpu.VMEM((RING, RING, 2 * SMALL, 128), F32),
            pltpu.VMEM((2 * SMALL, width), F32),
            pltpu.VMEM((SMALL, 128), F32),
            pltpu.VMEM((RING, SMALL, 128), F32),
            pltpu.VMEM((2,) + block, F32),
        ]
        + [pltpu.VMEM(value.shape, value.dtype) for value in extras[::2]]
        + scatter_buffers((SMALL, 128), F32)
        + LayerGradients.scratch(HALF_ROWS // 3, hidden)
        + [
            pltpu.SemaphoreType.DMA((RING,)),
            pltpu.SemaphoreType.DMA((RING,)),
            pltpu.SemaphoreType.DMA((extra,)),
            pltpu.SemaphoreType.DMA((extra,)),
            pltpu.SemaphoreType.DMA((6,)),
            pltpu.SemaphoreType.DMA((6,)),
            pltpu.SemaphoreType.DMA((6,)),
            pltpu.SemaphoreType.DMA,
        ],
        compiler_params=comm_params(cid),
    )(*args)


def flat_dot(former, latter):
    return lax.dot_general(former, latter, (((1,), (1,)), ((), ())), preferred_element_type=F32)


def rows_dot(former, latter):
    return lax.dot_general(former, latter, (((0,), (0,)), ((), ())), preferred_element_type=F32)


def head_stack(values, scale):
    column = lax.broadcasted_iota(jnp.int32, values.shape, 1) // HEAD_DIM
    heads_here = values.shape[1] // HEAD_DIM
    zero = jnp.zeros_like(values)
    scaled = values * jnp.asarray(scale, values.dtype)
    return jnp.concatenate(
        [jnp.where(column == head, scaled, zero) for head in range(heads_here)], axis=0
    )


def block_scores(key_block, stack, seg_column, seg_wide):
    scores = flat_dot(key_block, stack)
    return jnp.where(seg_column == seg_wide, scores, MASKED_SCORE)


def load_matrix(packed_any, target, number, half, semaphores):
    copies = []
    for which in range(2):
        copy = pltpu.make_async_copy(
            packed_any.at[which, :, :, pl.ds(number * half, half)],
            target.at[:, :, pl.ds(which * half, half)],
            semaphores.at[which],
        )
        copy.start()
        copies.append(copy)
    return copies


def attend_kernel(
    layer, normed_ref, packed_any, vec_ref, seg_q_ref, seg_k_ref,
    q_ref, k_ref, v_ref, mixed_ref, wide_ref, lse_ref, part_ref,
    pack_ref, stack, acc, top_ref, total_ref, send, recv, local,
):
    group, width = q_ref.shape
    heads_here = width // HEAD_DIM
    depth = group // RING
    loads = load_matrix(packed_any, pack_ref, 0, depth // 2, local)
    matrix = lambda which: pack_ref[:, :, :, which * width : (which + 1) * width].reshape(-1, width)
    rank = lax.axis_index("dp")
    y, z = rank // RING, lax.rem(rank, RING)
    barrier, count = dp_barrier(y, z, None)
    normed = normed_ref[...]
    start = pl.multiple_of(lax.axis_index("tensor") * width, width)
    query_bias = vec_ref[layer, 2:3, pl.ds(start, width)]
    value_bias = vec_ref[layer, 3:4, pl.ds(start, width)]
    for load in loads:
        load.wait()
    k_ref[y, z] = jnp.dot(normed, matrix(1), preferred_element_type=F32).astype(BF16)
    pl.semaphore_wait(barrier, count)
    started = []
    ring = Gather(((0, (), True), (1, (), False)), (k_ref, v_ref), y, z, (), pusher(send, recv, started))
    ring.begin(0, k_ref.at[y, z])
    v_ref[y, z] = (
        jnp.dot(normed, matrix(2), preferred_element_type=F32) + value_bias
    ).astype(BF16)
    ring.begin(1, v_ref.at[y, z])
    q_ref[...] = (
        jnp.dot(normed, matrix(0), preferred_element_type=F32) + query_bias
    ).astype(BF16)
    stack[...] = head_stack(q_ref[...], HEAD_DIM ** (-0.5))
    acc[...] = jnp.zeros_like(acc)
    top_ref[...] = jnp.full_like(top_ref, MASKED_SCORE)
    total_ref[...] = jnp.zeros_like(total_ref)
    seg_wide = jnp.concatenate([seg_q_ref[0:1, :]] * heads_here, axis=1)

    def attend(offset_y, offset_z):
        at_y, at_z = step(y, offset_y), step(z, offset_z)
        highest = top_ref[0:1, :]
        scores = block_scores(
            k_ref[at_y, at_z], stack[...], seg_k_ref[at_y, at_z, :, 0:1], seg_wide
        )
        above = jnp.maximum(highest, jnp.max(scores, axis=0, keepdims=True))
        weights = jnp.exp(scores - above)
        fade = jnp.exp(highest - above)
        total_ref[0:1, :] = total_ref[0:1, :] * fade + jnp.sum(weights, axis=0, keepdims=True)
        top_ref[0:1, :] = above
        low = weights.astype(BF16)
        turned = v_ref[at_y, at_z].T
        for head in range(heads_here):
            rows = pl.ds(head * HEAD_DIM, HEAD_DIM)
            lanes = slice(head * group, (head + 1) * group)
            term = jnp.dot(
                turned[head * HEAD_DIM : (head + 1) * HEAD_DIM], low[:, lanes],
                preferred_element_type=F32,
            )
            acc[rows, :] = acc[rows, :] * fade[:, lanes] + term

    def attend_all(count, offsets):
        def each(number, carry):
            attend(*offsets(number))
            return carry

        lax.fori_loop(0, count, each, 0)

    side = lambda t: 1 + 2 * lax.rem(t, 2)
    attend_all(1, lambda t: (t, t))
    ring.near()
    for i in ring.every:
        ring.relay(i, 0)
    for i in ring.every:
        ring.far(i)
        ring.other(i, 0)
    attend_all(4, lambda t: (side(t) * (t // 2), side(t) * (1 - t // 2)))
    for i in ring.every:
        ring.relay(i, MINUS)
        ring.relay(i, PLUS)
    for i in ring.every:
        ring.other(i, MINUS)
        ring.other(i, PLUS)
    attend_all(2, lambda t: (t * 0 + PLUS, side(t)))
    for i in ring.every:
        ring.relay(i, FAR)
        ring.relayed[i, 0].wait_recv()
    attend_all(2, lambda t: (t * 0 + MINUS, side(t)))
    attend_all(2, lambda t: (2 * t, 2 - 2 * t))
    for i in ring.every:
        ring.other(i, FAR)
        ring.relayed[i, MINUS].wait_recv()
        ring.relayed[i, PLUS].wait_recv()
    attend_all(
        4,
        lambda t: (
            2 * (t // 2) + side(t) * (1 - t // 2),
            2 * (1 - t // 2) + side(t) * (t // 2),
        ),
    )
    for i in ring.every:
        ring.relayed[i, FAR].wait_recv()
    attend_all(1, lambda t: (t + FAR, t + FAR))

    total = total_ref[0:1, :]
    inverse = 1.0 / total
    for head in range(heads_here):
        rows = pl.ds(head * HEAD_DIM, HEAD_DIM)
        wide_ref[rows, :] = acc[rows, :] * inverse[:, head * group : (head + 1) * group]
    mixed_ref[...] = wide_ref[...].T.astype(BF16)
    lse_ref[...] = jnp.broadcast_to(top_ref[0:1, :] + jnp.log(total), lse_ref.shape)
    part = flat_dot(mixed_ref[...], matrix(3)).astype(BF16)
    part_ref[...] = part.reshape(part_ref.shape)
    for copy in started:
        copy.wait_send()


def attend_call(cid, layer, normed, packed, vectors, seg_wide, seg_column):
    group, model = normed.shape
    width = model // RING
    heads_here = width // HEAD_DIM
    square = (RING, RING, group, width)
    return pl.pallas_call(
        functools.partial(attend_kernel, layer),
        out_shape=[
            jax.ShapeDtypeStruct((group, width), BF16),
            jax.ShapeDtypeStruct(square, BF16),
            jax.ShapeDtypeStruct(square, BF16),
            jax.ShapeDtypeStruct((group, width), BF16),
            jax.ShapeDtypeStruct((width, group), F32),
            jax.ShapeDtypeStruct((8, group * heads_here), F32),
            jax.ShapeDtypeStruct((RING, group // RING, model), BF16),
        ],
        in_specs=[vmem_spec(), any_spec()] + [vmem_spec()] * 3,
        out_specs=[vmem_spec()] * 7,
        scratch_shapes=[
            pltpu.VMEM((RING, RING, group // RING, model), BF16),
            pltpu.VMEM((group * heads_here, width), BF16),
            pltpu.VMEM((width, group), F32),
            pltpu.VMEM((8, group * heads_here), F32),
            pltpu.VMEM((8, group * heads_here), F32),
            pltpu.SemaphoreType.DMA((2, 5, RING)),
            pltpu.SemaphoreType.DMA((2, 5, RING)),
            pltpu.SemaphoreType.DMA((2,)),
        ],
        compiler_params=comm_params(cid),
    )(normed, packed, vectors, seg_wide, seg_column)


def attend_back_kernel(
    rows_ref, packed_any, q_ref, k_ref, v_ref, wide_ref, lse_ref, seg_q_ref, seg_k_ref,
    triple_ref, sums_ref, part_ref, *scratch,
):
    (
        pack_ref, grad_ref, stack, plain, grad_stack, grad_plain, acc, delta_ref,
        dk_ref, dv_ref, total_ref,
    ) = scratch[:11]
    buffers = scratch[11 : 11 + 2 * SCATTER_BUFFERS]
    send, recv, local = scratch[11 + 2 * SCATTER_BUFFERS :]
    group, width = q_ref.shape
    heads_here = width // HEAD_DIM
    scale = HEAD_DIM ** (-0.5)
    depth = group // RING
    loads = load_matrix(packed_any, pack_ref, 0, depth // 2, local)
    matrix = lambda which: pack_ref[:, :, :, which * width : (which + 1) * width].reshape(-1, width)
    rank = lax.axis_index("dp")
    y, z = rank // RING, lax.rem(rank, RING)
    barrier, count = dp_barrier(y, z, None)
    stack[...] = head_stack(q_ref[...], scale)
    plain[...] = head_stack(q_ref[...], 1.0)
    for load in loads:
        load.wait()
    grad_ref[...] = jnp.dot(rows_ref[...], matrix(3), preferred_element_type=F32).astype(BF16)
    grad_stack[...] = head_stack(grad_ref[...], scale)
    grad_plain[...] = head_stack(grad_ref[...], 1.0)
    acc[...] = jnp.zeros_like(acc)
    seg_wide = jnp.concatenate([seg_q_ref[0:1, :]] * heads_here, axis=1)
    product = grad_ref[...].astype(F32).T * wide_ref[...]
    for head in range(heads_here):
        delta_ref[0:1, pl.ds(head * group, group)] = scale * jnp.sum(
            product[head * HEAD_DIM : (head + 1) * HEAD_DIM], axis=0, keepdims=True
        )
    pl.semaphore_wait(barrier, count)
    started = []
    push = pusher(send, recv, started)
    keys = Scatter(0, True, dk_ref, buffers[:SCATTER_BUFFERS], y, z, push)
    values = Scatter(1, False, dv_ref, buffers[SCATTER_BUFFERS:], y, z, push)

    def attend(offset_y, offset_z):
        at_y, at_z = step(y, offset_y), step(z, offset_z)
        key_block = k_ref[at_y, at_z]
        scores = block_scores(key_block, stack[...], seg_k_ref[at_y, at_z, :, 0:1], seg_wide)
        weights = jnp.exp(scores - lse_ref[0:1, :])
        dv_ref[at_y, at_z] = jnp.dot(
            weights.astype(BF16), grad_plain[...], preferred_element_type=F32
        ).astype(BF16)
        prob_grad = flat_dot(v_ref[at_y, at_z], grad_stack[...])
        low = (weights * (prob_grad - delta_ref[0:1, :])).astype(BF16)
        dk_ref[at_y, at_z] = jnp.dot(low, plain[...], preferred_element_type=F32).astype(BF16)
        turned = key_block.T
        for head in range(heads_here):
            rows = pl.ds(head * HEAD_DIM, HEAD_DIM)
            acc[rows, :] += jnp.dot(
                turned[head * HEAD_DIM : (head + 1) * HEAD_DIM],
                low[:, head * group : (head + 1) * group],
                preferred_element_type=F32,
            )

    def attend_all(first, count, offsets):
        def each(number, carry):
            attend(*offsets(number))
            return carry

        lax.fori_loop(first, count, each, 0)

    attend_all(0, 4, lambda t: (t * 0 + FAR, step(t, FAR)))
    for j in Scatter.ORDER:
        values.send_via(j)
    keys.send_direct(FAR)
    attend_all(1, 4, lambda t: (step(t, FAR), t * 0 + FAR))
    for j in Scatter.ORDER:
        keys.send_via(j)
    values.send_direct(FAR)
    attend_all(1, 4, lambda t: (t * 0 + PLUS, step(t, FAR)))
    keys.send_direct(PLUS)
    values.send_direct(PLUS)
    values.send_direct(MINUS)
    attend_all(1, 4, lambda t: (t * 0 + MINUS, step(t, FAR)))
    keys.send_direct(MINUS)
    values.send_direct(0)
    values.join()
    for j in (FAR, PLUS, MINUS):
        keys.join_one(j)
    attend_all(0, 2, lambda t: (t * 0, 1 + 2 * t))
    keys.send_direct(0)
    keys.join_one(0)
    attend_all(0, 1, lambda t: (t, t))
    values.turn()
    keys.turn()
    values.join_two()
    keys.join_two()
    sums_ref[...] = jnp.zeros_like(sums_ref)
    query_grad = acc[...].T
    sums_ref[0:1, :] = jnp.sum(query_grad, axis=0, keepdims=True)
    triple_ref[0] = query_grad.astype(BF16)
    part = flat_dot(triple_ref[0], matrix(0))
    values.finish(total_ref)
    triple_ref[2] = total_ref[...].astype(BF16)
    sums_ref[1:2, :] = jnp.sum(total_ref[...], axis=0, keepdims=True)
    part = part + flat_dot(triple_ref[2], matrix(2))
    keys.finish(total_ref)
    triple_ref[1] = total_ref[...].astype(BF16)
    part = part + flat_dot(triple_ref[1], matrix(1))
    part_ref[...] = part.astype(BF16).reshape(part_ref.shape)
    for copy in started:
        copy.wait_send()


def attend_back_call(cid, attn_rows, packed, queries, keys, values, wide, lse, seg_wide, seg_column):
    group, model = attn_rows.shape
    width = queries.shape[1]
    heads_here = width // HEAD_DIM
    block = (group, width)
    stacked = pltpu.VMEM((group * heads_here, width), BF16)
    return pl.pallas_call(
        attend_back_kernel,
        out_shape=[
            jax.ShapeDtypeStruct((3, group, width), BF16),
            jax.ShapeDtypeStruct((8, width), F32),
            jax.ShapeDtypeStruct((RING, group // RING, model), BF16),
        ],
        in_specs=[vmem_spec(), any_spec()] + [vmem_spec()] * 7,
        out_specs=[vmem_spec()] * 3,
        scratch_shapes=[
            pltpu.VMEM((RING, RING, group // RING, model), BF16),
            pltpu.VMEM(block, BF16),
            stacked,
            stacked,
            stacked,
            stacked,
            pltpu.VMEM((width, group), F32),
            pltpu.VMEM((8, group * heads_here), F32),
            pltpu.VMEM((RING, RING) + block, BF16),
            pltpu.VMEM((RING, RING) + block, BF16),
            pltpu.VMEM(block, F32),
        ]
        + Scatter.scratch(block, BF16)
        + Scatter.scratch(block, BF16)
        + [
            pltpu.SemaphoreType.DMA((2, 6, RING)),
            pltpu.SemaphoreType.DMA((2, 6, RING)),
            pltpu.SemaphoreType.DMA((2,)),
        ],
        compiler_params=comm_params(cid),
    )(attn_rows, packed, queries, keys, values, wide, lse, seg_wide, seg_column)


class Exchange:
    def __init__(self, me, send, recv, landing, started):
        self.me, self.send, self.recv, self.landing, self.started = me, send, recv, landing, started
        self.reduces = {}

    def push(self, source, target, kind, index, k):
        copy = pltpu.make_async_remote_copy(
            src_ref=source,
            dst_ref=target,
            send_sem=self.send.at[kind, index, k - 1],
            recv_sem=self.recv.at[kind, index, k - 1],
            device_id={"tensor": step(self.me, k)},
            device_id_type=MESH,
        )
        copy.start()
        self.started.append(copy)
        return copy

    def reduce(self, part, peers=(1, 2, 3)):
        chunk = part.shape[-2] // CHUNKS
        for c in range(CHUNKS):
            here = pl.ds(c * chunk, chunk)
            for k in peers:
                self.reduces[c, k] = self.push(
                    part.at[step(self.me, k), here], self.landing.at[k - 1, here], 0, c, k
                )

    def run(self, part, function, rows_in, vecs, rows_out, sums_out, full, side=()):
        side = list(side)
        me = self.me
        chunk = part.shape[-2] // CHUNKS
        if side:
            side.pop(0)()
        sums, last = None, []
        for c in range(CHUNKS):
            here = pl.ds(c * chunk, chunk)
            for k in range(1, RING):
                self.reduces[c, k].wait_recv()
            total = part[me, here].astype(F32)
            for k in range(1, RING):
                total = total + self.landing[k - 1, here].astype(F32)
            spread, outs, parts = function(total, [ref[here].astype(F32) for ref in rows_in], vecs)
            if full is not None:
                full[me, here] = spread.astype(BF16)
                last += [
                    self.push(full.at[me, here], full.at[me, here], 1, c, k) for k in range(1, RING)
                ]
            for ref, value in zip(rows_out, outs):
                ref[here] = value.astype(ref.dtype)
            sums = parts if sums is None else [old + new for old, new in zip(sums, parts)]
        if sums_out is not None:
            sums_out[...] = jnp.concatenate(
                sums + [jnp.zeros((8 - len(sums), sums[0].shape[1]), F32)], axis=0
            )
        for work in side:
            work()
        for copy in last:
            copy.wait_recv()


TILES = ((2, 1), (3, 0))


def rows_of(ref, me, tile):
    return jnp.concatenate([ref[step(me, k)] for k in tile], axis=0)


def put_rows(ref, me, tile, value):
    rows = ref.shape[1]
    for i, k in enumerate(tile):
        ref[step(me, k)] = value[i * rows : (i + 1) * rows].astype(ref.dtype)


def wide_of(pack_ref):
    return pack_ref[...].reshape(-1, pack_ref.shape[-1])


def mlp_forward(me, full, up_ref, down_ref, bias, act_ref, slope_ref, part_ref, exchange):
    for tile in TILES:
        value = jnp.dot(rows_of(full, me, tile), wide_of(up_ref), preferred_element_type=F32)
        value = value + bias
        phi = 0.5 * (1.0 + lax.erf(value * (0.5**0.5)))
        act = (value * phi).astype(BF16)
        density = jnp.exp(-0.5 * value * value) * 0.3989422804014327
        put_rows(act_ref, me, tile, act)
        put_rows(slope_ref, me, tile, phi + value * density)
        put_rows(part_ref, me, tile, flat_dot(act, wide_of(down_ref)))
        exchange.reduce(part_ref, [k for k in tile if k])


def mlp_backward(me, full, up_ref, down_ref, slope_ref, pre_ref, bias_out, part_ref, exchange):
    total = None
    for tile in TILES:
        value = jnp.dot(rows_of(full, me, tile), wide_of(down_ref), preferred_element_type=F32)
        value = value * rows_of(slope_ref, me, tile)
        part = jnp.sum(value, axis=0, keepdims=True)
        total = part if total is None else total + part
        low = value.astype(BF16)
        put_rows(pre_ref, me, tile, low)
        put_rows(part_ref, me, tile, flat_dot(low, wide_of(up_ref)))
        exchange.reduce(part_ref, [k for k in tile if k])
    bias_out[...] = jnp.broadcast_to(total, bias_out.shape)


def product(former_ref, latter_ref, out_ref):
    def work():
        tokens = lambda ref: ref[...].reshape(-1, ref.shape[-1])
        size = 256

        def each(number, carry):
            columns = pl.ds(pl.multiple_of(number * size, size), size)
            left = former_ref[..., columns].reshape(-1, size)
            value = jnp.dot(left.T, tokens(latter_ref), preferred_element_type=F32)
            out_ref[number] = value.astype(BF16).reshape(out_ref.shape[1:])
            return carry

        lax.fori_loop(0, RING, each, 0)

    return work


def chain_call(cid, body, exchanges, packed_array, ins, outs, inside, any_names=(), extra=None):
    names = list(ins) + list(outs) + list(inside)
    rows, model = 64, 1024
    count = len(names)
    load_packed = packed_array is not None

    def kernel(*refs):
        refs = list(refs)
        packed = refs.pop(0) if load_packed else None
        env = SimpleNamespace(**dict(zip(names, refs[:count])))
        refs = refs[count:]
        me = lax.axis_index("tensor")
        barrier, peers = tensor_barrier(me)
        started = []
        loads = []
        if load_packed:
            env.up, env.down, local = refs[:3]
            refs = refs[3:]
            half = env.up.shape[2] // 2
            for i, matrix in enumerate((env.up, env.down)):
                loads += load_matrix(packed, matrix, i + 1, half, local.at[i])
        if extra is not None:
            env.extra = refs[3 * exchanges :]
            rank = lax.axis_index("dp")
            env.place = (rank // RING, lax.rem(rank, RING), lax.axis_index("section"))
            peers += dp_barrier(*env.place)[1]
        pl.semaphore_wait(barrier, peers)
        env.started = started
        rings = [
            Exchange(me, refs[3 * i + 1], refs[3 * i + 2], refs[3 * i], started)
            for i in range(exchanges)
        ]
        body(me, env, rings, loads)
        for copy in started:
            copy.wait_send()

    scratch = [pltpu.VMEM(shape, dtype) for shape, dtype in inside.values()]
    spec_of = lambda name: any_spec() if name in any_names else vmem_spec()
    args, in_specs = list(ins.values()), [spec_of(name) for name in ins]
    if load_packed:
        args, in_specs = [packed_array] + args, [any_spec()] + in_specs
        matrix = pltpu.VMEM((RING, RING, rows, model), BF16)
        scratch += [matrix, matrix, pltpu.SemaphoreType.DMA((2, 2))]
    for _ in range(exchanges):
        scratch += [
            pltpu.VMEM((RING - 1, rows, model), BF16),
            pltpu.SemaphoreType.DMA((2, CHUNKS, RING - 1)),
            pltpu.SemaphoreType.DMA((2, CHUNKS, RING - 1)),
        ]
    scratch += extra or []
    results = pl.pallas_call(
        kernel,
        out_shape=[jax.ShapeDtypeStruct(shape, dtype) for shape, dtype in outs.values()],
        in_specs=in_specs,
        out_specs=[spec_of(name) for name in outs],
        scratch_shapes=scratch,
        compiler_params=comm_params(cid),
    )(*args)
    return SimpleNamespace(**dict(zip(outs, results)))


def first_mlp_body(me, env, rings, loads):
    y, z, section = env.place
    send, recv, local = env.extra
    push = pusher(send, recv, env.started)
    halves = [pl.ds(0, HALF_ROWS // 2), pl.ds(HALF_ROWS // 2, HALF_ROWS // 2)]
    ring = Gather(
        ((0, (), True), (1, (), False)),
        [env.packed_next.at[section, :, :, half] for half in halves], y, z, (), push,
    )
    begin, near, middle, end, final = spread_stages(
        ring, [env.stage.at[1, half] for half in halves], local, section, push
    )
    rings[0].reduce(env.part)
    rings[0].run(
        env.part, middle_rows, [env.inputs], [env.vectors.at[0]],
        [env.attn_out, env.hidden], None, env.normed, [begin, near],
    )
    middle()
    for copy in loads:
        copy.wait()
    mlp_forward(
        me, env.normed, env.up, env.down, env.vectors[0, pl.ds(9 + me, 1), :], env.act, env.slope, env.sent, rings[1],
    )
    end()
    rings[1].run(
        env.sent, end_rows_first, [env.hidden], [env.vectors.at[0], env.vectors.at[1]],
        [env.mlp_out, env.outputs], None, env.next, [lambda: None, final],
    )


def last_mlp_body(me, env, rings, loads):
    rings[0].reduce(env.part)
    rings[0].run(
        env.part, middle_rows, [env.inputs], [env.vectors.at[1]],
        [env.attn_out, env.hidden], None, env.normed,
    )
    for copy in loads:
        copy.wait()
    mlp_forward(
        me, env.normed, env.up, env.down, env.vectors[1, pl.ds(9 + me, 1), :], env.act, env.slope,
        env.sent, rings[1],
    )
    rings[1].run(
        env.sent, end_rows_last, [env.hidden, env.upstream], [env.vectors.at[1]],
        [env.outputs], env.sums_end, env.mlp_rows,
    )
    mlp_backward(
        me, env.mlp_rows, env.up, env.down, env.slope, env.pre, env.bias_grad,
        env.sent_two, rings[2],
    )
    rings[2].run(
        env.sent_two, back_middle_rows, [env.upstream, env.hidden, env.attn_out],
        [env.vectors.at[1]], [env.hidden_grad], env.sums_middle, env.attn_rows,
        [
            product(env.mlp_rows, env.act, env.grad_down),
            product(env.normed, env.pre, env.grad_up),
        ],
    )


def attention_products(env):
    return [
        product(env.attn_rows_in, env.mixed, env.grad_out)
    ] + [
        product(env.normed_in, env.triple.at[which], env.grad_qkv.at[which])
        for which in range(3)
    ]


def between_body(me, env, rings, loads):
    y, z, section = env.place
    grads = [env.grad_qkv.at[which] for which in range(3)]
    grads += [env.grad_out, env.last_up, env.last_down]
    layer = layer_gradients(grads, env.extra, y, z, section, env.started)

    def swap():
        for work in attention_products(env):
            work()
        layer.keep()
        layer.swap()

    rings[0].reduce(env.part)
    rings[0].run(
        env.part, back_end_rows_last, [env.hidden_grad_in, env.inputs, env.mlp_out],
        [env.vectors.at[1], env.vectors.at[0]], [env.input_grad], env.sums_last, env.mlp_rows,
        [swap, layer.begin],
    )
    for copy in loads:
        copy.wait()
    mlp_backward(
        me, env.mlp_rows, env.up, env.down, env.slope, env.pre, env.bias_grad, env.sent, rings[1],
    )
    layer.join()

    def products():
        product(env.mlp_rows, env.act, env.grad_down)()
        product(env.normed, env.pre, env.grad_up)()

    def rest():
        layer.turn()
        layer.join_two()
        layer.finish(env.summed)
        layer.end()

    rings[1].run(
        env.sent, back_middle_rows_low, [env.input_grad, env.hidden, env.attn_out],
        [env.vectors.at[0]], [env.hidden_grad], env.sums_middle, env.attn_rows, [products, rest],
    )


def back_middle_rows_low(total, rows, vecs):
    return back_middle_rows(total, [rows[0].astype(BF16).astype(F32)] + rows[1:], vecs)


def close_body(me, env, rings, loads):
    rings[0].reduce(env.part)
    rings[0].run(
        env.part, back_end_rows_first, [env.hidden_grad_in, env.inputs],
        [env.vectors.at[0]], [env.input_grad], env.sums_last, None, attention_products(env),
    )


def shards(tokens, segment_ids, w_qkv, w_out, w_up, w_down, vectors, out_bias, cotangent):
    section = lax.axis_index("section")
    tensor_rank = lax.axis_index("tensor")
    own = lambda pair: jnp.where(section == 0, pair[0], pair[1])
    rows = tokens.shape[1]
    width = tokens.shape[2]
    group = rows * RING
    square = (RING, RING)
    local_width = w_qkv.shape[3]
    local_hidden = w_up.shape[2]

    depth = w_out.shape[1]
    my_segments = own(segment_ids)
    wide_segments = jnp.pad(my_segments, (0, depth - rows)).astype(BF16)[None]
    small = jnp.pad(
        jnp.concatenate([vectors[0], out_bias, wide_segments], axis=0),
        ((0, 1), (0, 128 - depth)),
    )
    packed_first, stage, small_rows, normed, inputs, my_cotangent, seg_wide, seg_column = first_call(
        0, tokens, cotangent, w_qkv[0], w_out[0], w_up[0], w_down[0], small
    )

    whole = (RING, rows, width)
    blocks = lambda columns: square + (depth, columns)
    spread = (RING, rows, local_hidden)
    row_shape = (rows, width)
    def attend_layer(layer, normed, packed):
        return attend_call(
            2 + 12 * layer, layer, normed.reshape(group, width), packed, small_rows, seg_wide, seg_column
        )

    normed_first = normed
    *kept_first, part = attend_layer(0, normed_first, packed_first)
    first = chain_call(
        3, first_mlp_body, 2, packed_first,
        dict(
            part=part, inputs=inputs, vectors=small_rows, stage=stage,
        ),
        dict(
            attn_out=(row_shape, F32), hidden=(row_shape, F32), normed=(whole, BF16),
            act=(spread, BF16), slope=(spread, F32), mlp_out=(row_shape, F32),
            outputs=(row_shape, BF16), next=(whole, BF16),
            packed_next=((2,) + square + (HALF_ROWS, local_hidden), BF16),
        ),
        dict(sent=(whole, BF16)),
        ("packed_next",),
        gather_scratch(),
    )
    between = first.outputs
    packed_last = first.packed_next
    *kept_last, part = attend_layer(1, first.next, packed_last)
    last = chain_call(
        5, last_mlp_body, 3, packed_last,
        dict(
            part=part, inputs=between, vectors=small_rows, upstream=my_cotangent,
        ),
        dict(
            outputs=(row_shape, BF16), sums_end=((8, width), F32),
            hidden_grad=(row_shape, F32), sums_middle=((8, width), F32),
            attn_rows=(whole, BF16), bias_grad=((8, local_hidden), F32),
            grad_up=(blocks(local_hidden), BF16), grad_down=(blocks(local_hidden), BF16),
        ),
        dict(
            attn_out=(row_shape, F32), hidden=(row_shape, F32), normed=(whole, BF16),
            act=(spread, BF16), slope=(spread, F32), pre=(spread, BF16),
            mlp_rows=(whole, BF16), sent=(whole, BF16), sent_two=(whole, BF16),
        ),
    )
    outputs = last.outputs

    def attend_back_layer(layer, attn_rows, kept, packed):
        queries, keys_full, values_full, mixed, wide, lse = kept
        return attend_back_call(
            7 + 12 * layer, attn_rows.reshape(group, width), packed, queries, keys_full,
            values_full, wide, lse, seg_wide, seg_column,
        )

    attention_grads = dict(
        grad_out=(blocks(local_width), BF16), grad_qkv=((3,) + blocks(local_width), BF16),
    )
    triple, attend_last, part = attend_back_layer(1, last.attn_rows, kept_last, packed_last)
    middle = chain_call(
        8, between_body, 2, packed_first,
        dict(
            part=part, hidden_grad_in=last.hidden_grad, inputs=between,
            mlp_out=first.mlp_out, vectors=small_rows,
            slope=first.slope, act=first.act, normed=first.normed,
            hidden=first.hidden, attn_out=first.attn_out,
            attn_rows_in=last.attn_rows, mixed=kept_last[3], normed_in=first.next,
            triple=triple, last_up=last.grad_up, last_down=last.grad_down,
        ),
        dict(
            summed=((HALF_ROWS, local_hidden), F32),
            input_grad=(row_shape, F32), sums_last=((8, width), F32),
            hidden_grad=(row_shape, F32), sums_middle=((8, width), F32),
            attn_rows=(whole, BF16), bias_grad=((8, local_hidden), F32),
            grad_up=(blocks(local_hidden), BF16), grad_down=(blocks(local_hidden), BF16),
            **attention_grads,
        ),
        dict(pre=(spread, BF16), mlp_rows=(whole, BF16), sent=(whole, BF16)),
        ("last_up", "last_down"),
        LayerGradients.scratch(HALF_ROWS // 3, local_hidden),
    )
    last_grad = middle.input_grad
    triple, attend_first, part = attend_back_layer(0, middle.attn_rows, kept_first, packed_first)
    close = chain_call(
        9, close_body, 1, None,
        dict(
            part=part, hidden_grad_in=middle.hidden_grad, inputs=inputs,
            vectors=small_rows, attn_rows_in=middle.attn_rows, mixed=kept_first[3],
            normed_in=normed_first, triple=triple,
        ),
        dict(input_grad=(row_shape, F32), sums_last=((8, width), F32), **attention_grads),
        dict(),
    )
    input_grad = close.input_grad
    sums = [
        [close.sums_last, middle.sums_middle, middle.sums_last[2:], attend_first, middle.bias_grad],
        [middle.sums_last, last.sums_middle, last.sums_end, attend_last, last.bias_grad],
    ]
    grads = [close.grad_qkv, close.grad_out, middle.grad_up, middle.grad_down]
    first_grad = input_grad

    small_sum, sum_qkv, sum_out, sum_up, sum_down, out_pair, grad_pair = final_call(
        10, sums[0] + sums[1], grads, middle.summed, [outputs, between, last_grad, first_grad]
    )
    return (
        out_pair[None],
        grad_pair[None],
        sum_qkv[None],
        sum_out[None],
        sum_up[None],
        sum_down[None],
        small_sum[:13, :depth][None],
        small_sum[13:14, :depth],
    )


def solution(mesh):
    in_specs = (
        P(None, ("dp", "tensor"), None),
        P(None, ("dp", "tensor")),
        P("section", None, "dp", "tensor"),
        P("section", "dp", "tensor"),
        P("section", "dp", "tensor"),
        P("section", "dp", "tensor"),
        P("section", None, "dp"),
        P("section", "dp"),
        P(None, ("dp", "tensor"), None),
    )
    out_specs = (
        P("section", None, ("dp", "tensor"), None),
        P("section", None, ("dp", "tensor"), None),
        P("section", None, "dp", "tensor"),
        P("section", "dp", "tensor"),
        P("section", "dp", "tensor"),
        P("section", "dp", "tensor"),
        P("section", None, "dp"),
        P("section", "dp"),
    )
    return jax.shard_map(shards, mesh=mesh, in_specs=in_specs, out_specs=out_specs, check_vma=False)
```

```python
import functools
from types import SimpleNamespace

import jax
import jax.numpy as jnp
from jax import lax
from jax.experimental import pallas as pl
from jax.experimental.pallas import tpu as pltpu
from jax.sharding import PartitionSpec as P

MESH = pl.DeviceIdType.MESH
HEAD_DIM = 64
EPSILON = 1e-06
MASKED_SCORE = -1e30
RING = 4
VMEM_LIMIT = 56 * 1024 * 1024
F32 = jnp.float32
BF16 = jnp.bfloat16


def vmem_spec():
    return pl.BlockSpec(memory_space=pltpu.VMEM)


def any_spec():
    return pl.BlockSpec(memory_space=pl.ANY)


def comm_params(cid):
    return pltpu.CompilerParams(
        collective_id=cid, has_side_effects=True, vmem_limit_bytes=VMEM_LIMIT
    )


def step(coord, by):
    return lax.rem(coord + by, RING)


def layer_norm(values, gain_row, shift_row):
    centre = values - jnp.mean(values, axis=-1, keepdims=True)
    spread = jnp.mean(centre * centre, axis=-1, keepdims=True)
    return centre * lax.rsqrt(spread + EPSILON) * gain_row + shift_row


def layer_norm_back(values, gain_row, grad):
    centre = values - jnp.mean(values, axis=-1, keepdims=True)
    spread = jnp.mean(centre * centre, axis=-1, keepdims=True)
    inverse = lax.rsqrt(spread + EPSILON)
    normed = centre * inverse
    scaled = grad * gain_row
    back = inverse * (
        scaled
        - jnp.mean(scaled, axis=-1, keepdims=True)
        - normed * jnp.mean(scaled * normed, axis=-1, keepdims=True)
    )
    return back, jnp.sum(grad * normed, axis=0, keepdims=True), jnp.sum(grad, axis=0, keepdims=True)


PLUS, FAR, MINUS = 1, 2, 3
CHUNKS = 2


def tensor_barrier(me):
    barrier = pltpu.get_barrier_semaphore()
    for k in range(1, RING):
        pl.semaphore_signal(
            barrier, inc=1, device_id={"tensor": step(me, k)}, device_id_type=MESH
        )
    return barrier, RING - 1


def row(ref, index):
    return ref[pl.ds(index, 1), :]


def middle_rows(total, rows, vecs):
    vec = vecs[0]
    attn_out = total + row(vec, 13)
    hidden = rows[0] + row(vec, 4) * attn_out
    return layer_norm(hidden, row(vec, 5), row(vec, 6)), [attn_out, hidden], []


def end_rows_first(total, rows, vecs):
    vec, after = vecs
    mlp_out = total + row(vec, 7)
    outputs = (rows[0] + row(vec, 8) * mlp_out).astype(BF16)
    inputs = outputs.astype(F32)
    return layer_norm(inputs, row(after, 0), row(after, 1)), [mlp_out, outputs], []


def end_rows_last(total, rows, vecs):
    vec = vecs[0]
    hidden, upstream = rows
    mlp_out = total + row(vec, 7)
    outputs = hidden + row(vec, 8) * mlp_out
    mlp_grad = row(vec, 8) * upstream
    sums = [
        jnp.sum(upstream * mlp_out, axis=0, keepdims=True),
        jnp.sum(mlp_grad, axis=0, keepdims=True),
    ]
    return mlp_grad, [outputs], sums


def back_middle_rows(total, rows, vecs):
    vec = vecs[0]
    upstream, hidden, attn_out = rows
    part, gain, shift = layer_norm_back(hidden, row(vec, 5), total)
    hidden_grad = upstream + part
    attn_grad = row(vec, 4) * hidden_grad
    sums = [
        gain,
        shift,
        jnp.sum(hidden_grad * attn_out, axis=0, keepdims=True),
        jnp.sum(attn_grad, axis=0, keepdims=True),
    ]
    return attn_grad, [hidden_grad], sums


def back_end_rows_last(total, rows, vecs):
    vec, before = vecs
    hidden_grad, inputs, mlp_out = rows
    part, gain, shift = layer_norm_back(inputs, row(vec, 0), total)
    input_grad = hidden_grad + part
    upstream = input_grad.astype(BF16).astype(F32)
    mlp_grad = row(before, 8) * upstream
    sums = [
        gain,
        shift,
        jnp.sum(upstream * mlp_out, axis=0, keepdims=True),
        jnp.sum(mlp_grad, axis=0, keepdims=True),
    ]
    return mlp_grad, [input_grad], sums


def back_end_rows_first(total, rows, vecs):
    hidden_grad, inputs = rows
    part, gain, shift = layer_norm_back(inputs, row(vecs[0], 0), total)
    return None, [hidden_grad + part], [gain, shift]


def dp_neighbour(y, z, along_z, k):
    if along_z:
        return {"dp": y * RING + step(z, k)}
    return {"dp": step(y, k) * RING + z}


def dp_barrier(y, z, section):
    barrier = pltpu.get_barrier_semaphore()
    count = 0
    for along_z in (True, False):
        for k in (PLUS, MINUS):
            pl.semaphore_signal(
                barrier, inc=1, device_id=dp_neighbour(y, z, along_z, k), device_id_type=MESH
            )
            count += 1
    if section is not None:
        pl.semaphore_signal(
            barrier, inc=1, device_id={"section": 1 - section}, device_id_type=MESH
        )
        count += 1
    return barrier, count


def pusher(send, recv, started):
    def push(index, kind, k, source, target, device):
        copy = pltpu.make_async_remote_copy(
            src_ref=source,
            dst_ref=target,
            send_sem=send.at[index, kind, k],
            recv_sem=recv.at[index, kind, k],
            device_id=device,
            device_id_type=MESH,
        )
        copy.start()
        started.append(copy)
        return copy

    return push


class Gather:
    WAYS = {0: 1, 3: 1, 1: 1, 2: 3}

    def __init__(self, pieces, outs, y, z, lead, push):
        self.pieces, self.outs, self.y, self.z = pieces, outs, y, z
        self.lead, self.push = lead, push
        self.every = range(len(pieces))
        self.first, self.onward, self.second, self.relayed = {}, {}, {}, {}

    def block(self, i, along, across, rows=None):
        number, pre, along_z = self.pieces[i]
        ys, zs = (across, along) if along_z else (along, across)
        ys = ys if isinstance(ys, slice) else step(self.y, ys) if ys else self.y
        zs = zs if isinstance(zs, slice) else step(self.z, zs) if zs else self.z
        return self.outs[number].at[self.lead + pre + (ys, zs) + (() if rows is None else (rows,))]

    def way(self, i, first, k):
        return dp_neighbour(self.y, self.z, self.pieces[i][2] == first, k)

    def halves(self, i):
        height = self.outs[self.pieces[i][0]].shape[-2]
        if height < 32:
            return {PLUS: None}
        half = height // 32 * 16
        return {PLUS: pl.ds(0, half), MINUS: pl.ds(half, height - half)}

    def spread(self, i, offset, source):
        for k in (PLUS, MINUS):
            self.second[i, offset, k] = self.push(
                i, 2 if k == PLUS else 3, offset, source, self.block(i, offset, 0), self.way(i, False, k)
            )

    def begin(self, i, source):
        for k in (PLUS, MINUS):
            self.first[i, k] = self.push(i, 0, k, source, self.block(i, 0, 0), self.way(i, True, k))
        self.spread(i, 0, source)

    def near(self):
        for i in self.every:
            split = self.halves(i)
            for k in (PLUS, MINUS):
                self.first[i, k].wait_recv()
                came = RING - k
                if k in split:
                    self.onward[i, k] = self.push(
                        i, 1, k, self.block(i, came, 0, split[k]), self.block(i, came, 0, split[k]),
                        self.way(i, True, k),
                    )
                self.spread(i, came, self.block(i, came, 0))

    def relay(self, i, offset):
        k = self.WAYS[offset]
        self.second[i, offset, k].wait_recv()
        came = self.block(i, offset, RING - k)
        self.relayed[i, offset] = self.push(i, 4, offset, came, came, self.way(i, False, k))

    def other(self, i, offset):
        self.second[i, offset, RING - self.WAYS[offset]].wait_recv()

    def far(self, i):
        for k in self.halves(i):
            self.onward[i, k].wait_recv()
        self.spread(i, FAR, self.block(i, FAR, 0))


def half_of(section, height):
    return pl.ds(pl.multiple_of(section * height, height), height)


def spread_stages(ring, sources, local, section, push):
    own, across = {}, []

    def pass_on(i, line):
        came = ring.block(i, slice(None), line)
        across.append(push(i, 5, line, came, came, {"section": 1 - section}))

    def begin():
        for i in ring.every:
            ring.begin(i, sources[i])
            own[i] = pltpu.make_async_copy(sources[i], ring.block(i, 0, 0), local.at[i])
            own[i].start()

    def near():
        ring.near()
        for i in ring.every:
            ring.relay(i, 0)

    def middle():
        for i in ring.every:
            ring.far(i)
        for i in ring.every:
            ring.relay(i, MINUS)
            ring.relay(i, PLUS)
            own[i].wait()
            pass_on(i, 0)

    def end():
        for i in ring.every:
            ring.relay(i, FAR)
            for offset in range(RING):
                ring.other(i, offset)
            pass_on(i, PLUS)
            pass_on(i, MINUS)

    def last():
        for i in ring.every:
            for offset in range(RING):
                ring.relayed[i, offset].wait_recv()
            pass_on(i, FAR)
        for copy in across:
            copy.wait_recv()

    return [begin, near, middle, end, last]


HALF_ROWS = 96
SMALL = 16


def half_places(half, width, hidden):
    return [(0, which * width, width) for which in range(4)] + [
        (half, 0, hidden),
        (2 * half, 0, hidden),
    ]


def first_kernel(
    tokens_in, cotangent_in, qkv_in, out_in, up_in, down_in, small_in,
    packed_out, stage, rows_out, full, tokens_out, cotangent_out, seg_wide, seg_column,
    small_all, seg_parts, seg_rows,
    send, recv, local, small_send, small_recv, small_local,
    swap_send, swap_recv, swap_local, tensor_send, tensor_recv,
):
    rank = lax.axis_index("dp")
    y, z = rank // RING, lax.rem(rank, RING)
    section = lax.axis_index("section")
    me = lax.axis_index("tensor")
    barrier, count = dp_barrier(y, z, section)
    count += tensor_barrier(me)[1]
    depth, width = out_in.shape
    half = depth // 2
    mine, others = half_of(section, half), half_of(1 - section, half)
    sources = [qkv_in.at[which] for which in range(3)] + [out_in, up_in, down_in]
    places = half_places(half, width, stage.shape[2])
    tokens_out[...] = jnp.where(section == 0, tokens_in[0], tokens_in[1])
    cotangent_out[...] = jnp.where(section == 0, cotangent_in[0], cotangent_in[1])
    seg_parts[me] = jnp.zeros(seg_parts.shape[1:], jnp.int32)
    pl.semaphore_wait(barrier, count)
    started = []
    push = pusher(send, recv, started)
    swaps, kept = [], []
    for i, (source, (row, column, columns)) in enumerate(zip(sources, places)):
        target = stage.at[section, pl.ds(row, half), pl.ds(column, columns)]
        copy = pltpu.make_async_remote_copy(
            src_ref=source.at[others],
            dst_ref=target,
            send_sem=swap_send.at[i],
            recv_sem=swap_recv.at[i],
            device_id={"section": 1 - section},
            device_id_type=MESH,
        )
        copy.start()
        swaps.append(copy)
        copy = pltpu.make_async_copy(source.at[mine], target, swap_local.at[i])
        copy.start()
        kept.append(copy)
    small_push = pusher(small_send, small_recv, started)
    small_ring = Gather(((0, (), True),), [small_all.at[section]], y, z, (), small_push)
    small_stages = spread_stages(small_ring, [small_in], small_local, section, small_push)
    small_stages[0]()
    for copy in kept:
        copy.wait()
    for copy in swaps:
        copy.wait_recv()
    halves = [pl.ds(0, HALF_ROWS // 2), pl.ds(HALF_ROWS // 2, HALF_ROWS // 2)]
    views = [packed_out.at[section, :, :, rows] for rows in halves]
    ring = Gather(((0, (), True), (1, (), False)), views, y, z, (), push)
    stages = spread_stages(ring, [stage.at[0, rows] for rows in halves], local, section, push)
    stages[0]()
    small_stages[1]()
    small_stages[2]()
    stages[1]()
    small_stages[3]()
    small_stages[4]()
    for layer in range(2):
        for number in range(RING * RING):
            part = small_all[layer, number // RING, number % RING]
            rows_out[layer, :, number * depth : (number + 1) * depth] = part[:, :depth].astype(F32)
    for number in range(RING * RING):
        part = small_all[section, number // RING, number % RING]
        seg_parts[me, number : number + 1, 0:depth] = (
            part[14:15, :depth].astype(F32).astype(jnp.int32)
        )
    full[me] = layer_norm(
        tokens_out[...].astype(F32), rows_out[0, 0:1, :], rows_out[0, 1:2, :]
    ).astype(BF16)
    tensor_copies = []
    for i, ref in enumerate((seg_parts, full)):
        for k in range(1, RING):
            copy = pltpu.make_async_remote_copy(
                src_ref=ref.at[me],
                dst_ref=ref.at[me],
                send_sem=tensor_send.at[i, k],
                recv_sem=tensor_recv.at[i, k],
                device_id={"tensor": step(me, k)},
                device_id_type=MESH,
            )
            copy.start()
            tensor_copies.append(copy)
    stages[2]()
    stages[3]()
    for copy in tensor_copies:
        copy.wait_recv()
    for number in range(RING):
        seg_rows[:, number * depth : (number + 1) * depth] = seg_parts[number][:, :depth]
    seg_wide[...] = jnp.broadcast_to(seg_rows[pl.ds(rank, 1), :], seg_wide.shape)
    turned = seg_rows[...].astype(F32).T
    for number in range(RING * RING):
        seg_column[number // RING, number % RING] = jnp.broadcast_to(
            turned[:, number : number + 1], seg_column.shape[2:]
        ).astype(jnp.int32)
    stages[4]()
    for copy in started + swaps + tensor_copies:
        copy.wait_send()


def gather_scratch():
    return [
        pltpu.SemaphoreType.DMA((2, 6, RING)),
        pltpu.SemaphoreType.DMA((2, 6, RING)),
        pltpu.SemaphoreType.DMA((2,)),
    ]


def first_call(cid, tokens, cotangent, w_qkv, w_out, w_up, w_down, small):
    depth = w_out.shape[0]
    hidden = w_up.shape[1]
    rows, width = tokens.shape[1:]
    group = RING * rows
    return pl.pallas_call(
        first_kernel,
        out_shape=[
            jax.ShapeDtypeStruct((2, RING, RING, HALF_ROWS, hidden), BF16),
            jax.ShapeDtypeStruct((2, HALF_ROWS, hidden), BF16),
            jax.ShapeDtypeStruct((2, SMALL, width), F32),
            jax.ShapeDtypeStruct((RING, rows, width), BF16),
            jax.ShapeDtypeStruct((rows, width), BF16),
            jax.ShapeDtypeStruct((rows, width), BF16),
            jax.ShapeDtypeStruct((8, group), jnp.int32),
            jax.ShapeDtypeStruct((RING, RING, group, 128), jnp.int32),
        ],
        in_specs=[vmem_spec()] * 7,
        out_specs=[any_spec()] + [vmem_spec()] * 7,
        scratch_shapes=[
            pltpu.VMEM((2, RING, RING) + small.shape, BF16),
            pltpu.VMEM((RING, RING * RING, 128), jnp.int32),
            pltpu.VMEM((RING * RING, group), jnp.int32),
        ]
        + gather_scratch()
        + gather_scratch()
        + [
            pltpu.SemaphoreType.DMA((6,)),
            pltpu.SemaphoreType.DMA((6,)),
            pltpu.SemaphoreType.DMA((6,)),
            pltpu.SemaphoreType.DMA((2, RING)),
            pltpu.SemaphoreType.DMA((2, RING)),
        ],
        compiler_params=comm_params(cid),
    )(tokens, cotangent, w_qkv, w_out, w_up, w_down, small)


class Scatter:
    ORDER = (FAR, PLUS, MINUS, 0)
    WAYS = {FAR: PLUS, 0: PLUS, PLUS: MINUS, MINUS: MINUS}

    def __init__(self, index, along_z, source, buffers, y, z, push):
        self.index, self.along_z, self.source = index, along_z, source
        self.passing, self.joined, self.summed, self.straight, self.middle = buffers[:5]
        self.far_two, self.joined_two, self.summed_two, self.straight_two = buffers[5:]
        self.y, self.z, self.push = y, z, push
        self.height, self.width = source.shape[-2:]
        self.via, self.direct, self.after = {}, {}, {}

    def at(self, along, across):
        ys, zs = (across, along) if self.along_z else (along, across)
        return step(self.y, ys), step(self.z, zs)

    def way(self, first, k):
        return dp_neighbour(self.y, self.z, self.along_z == first, k)

    def add(self, target, terms, top=0, height=None):
        height = self.height if height is None else height
        size = max(8, min(height, 65536 // self.width))
        while height % size:
            size -= 16

        def part(here):
            value = terms[0](here).astype(F32)
            for term in terms[1:]:
                value = value + term(here).astype(F32)
            target[here] = value.astype(target.dtype)

        if height <= size:
            part(pl.ds(top, height))
            return

        def each(number, carry):
            part(pl.ds(pl.multiple_of(top + number * size, size), size))
            return carry

        lax.fori_loop(0, height // size, each, 0)

    def send_via(self, j):
        self.via[j] = self.push(
            self.index, 0, j, self.source.at[self.at(FAR, j)], self.passing.at[j],
            self.way(True, self.WAYS[j]),
        )

    def send_direct(self, j):
        k = RING - self.WAYS[j]
        self.direct[j] = self.push(
            self.index, 1, j, self.source.at[self.at(k, j)], self.straight.at[j], self.way(True, k)
        )

    def begin(self):
        for j in self.ORDER:
            self.send_via(j)
        for j in self.ORDER:
            self.send_direct(j)

    def join_one(self, j):
        self.via[j].wait_recv()
        k = self.WAYS[j]
        at_y, at_z = self.at(k, j)
        self.add(
            self.joined.at[j],
            [lambda h: self.source[at_y, at_z, h], lambda h: self.passing[j, h]],
        )
        self.after[j] = self.push(
            self.index, 2, j, self.joined.at[j], self.summed.at[j], self.way(True, k)
        )

    def join(self):
        for j in self.ORDER:
            self.join_one(j)

    def turn(self):
        half = self.height // 2
        low, high = pl.ds(0, half), pl.ds(half, half)
        send = lambda kind, slot, source, target, k: self.push(
            self.index, kind, slot, source, target, self.way(False, k)
        )
        for j in self.ORDER:
            self.direct[j].wait_recv()
            self.after[j].wait_recv()
            at_y, at_z = self.at(0, j)
            self.add(
                self.middle.at[j],
                [
                    lambda h: self.source[at_y, at_z, h],
                    lambda h: self.summed[j, h],
                    lambda h: self.straight[j, h],
                ],
            )
            if j == FAR:
                self.via_two = [
                    send(3, 0, self.middle.at[j, low], self.far_two.at[low], PLUS),
                    send(3, 1, self.middle.at[j, high], self.far_two.at[high], MINUS),
                ]
            if j == PLUS:
                high_copy = send(4, 1, self.middle.at[j, high], self.straight_two.at[high], PLUS)
            if j == MINUS:
                low_copy = send(4, 0, self.middle.at[j, low], self.straight_two.at[low], MINUS)
        self.direct_two = [low_copy, high_copy]

    def join_two(self):
        half = self.height // 2
        self.after_two = []
        for number, (top, k) in enumerate(((0, PLUS), (half, MINUS))):
            self.via_two[number].wait_recv()
            self.add(
                self.joined_two,
                [lambda h: self.middle[k, h], lambda h: self.far_two[h]],
                top,
                half,
            )
            here = pl.ds(top, half)
            self.after_two.append(
                self.push(
                    self.index, 5, number, self.joined_two.at[here], self.summed_two.at[here],
                    self.way(False, k),
                )
            )

    def finish(self, out):
        for copy in self.direct_two + self.after_two:
            copy.wait_recv()
        self.add(
            out,
            [
                lambda h: self.middle[0, h],
                lambda h: self.summed_two[h],
                lambda h: self.straight_two[h],
            ],
        )

    @staticmethod
    def scratch(block, dtype):
        return [pltpu.VMEM((RING,) + block, dtype)] * 5 + [pltpu.VMEM(block, dtype)] * 4


SCATTER_BUFFERS = 9


def scatter_buffers(block, dtype):
    square = pltpu.VMEM((RING, RING) + block, dtype)
    return [square, square] + Scatter.scratch(block, dtype)


class LayerGradients:
    def __init__(self, grads, buffers, semaphores, y, z, section, push):
        self.grads, self.buffers, self.y, self.z = grads, buffers, y, z
        self.section, self.push = section, push
        self.keeps, self.swaps, self.parts = {}, {}, {}
        self.swap_send, self.swap_recv, self.keep_local = semaphores
        depth, width = grads[0].shape[2:]
        hidden = grads[5].shape[3]
        self.half = depth // 2
        self.places = [(0, 0, which * width, width) for which in range(4)]
        self.places += [(1, 0, 0, hidden), (1, self.half, 0, hidden)]

    def region(self, which, place):
        piece, row, column, columns = place
        return self.buffers[piece][which].at[:, :, pl.ds(row, self.half), pl.ds(column, columns)]

    def keep(self, piece):
        mine = half_of(self.section, self.half)
        for i, place in enumerate(self.places):
            if place[0] == piece:
                self.keeps[i] = pltpu.make_async_copy(
                    self.grads[i].at[:, :, mine], self.region(0, place), self.keep_local.at[i]
                )
                self.keeps[i].start()

    def swap(self, piece):
        others = half_of(1 - self.section, self.half)
        for i, place in enumerate(self.places):
            if place[0] == piece:
                self.swaps[i] = pltpu.make_async_remote_copy(
                    src_ref=self.grads[i].at[:, :, others],
                    dst_ref=self.region(1, place),
                    send_sem=self.swap_send.at[i],
                    recv_sem=self.swap_recv.at[i],
                    device_id={"section": 1 - self.section},
                    device_id_type=MESH,
                )
                self.swaps[i].start()

    def begin(self, piece):
        for i, place in enumerate(self.places):
            if place[0] == piece:
                self.keeps[i].wait()
                self.swaps[i].wait_recv()
        own, sibling = self.buffers[piece][:2]
        add_blocks(own, own, sibling)
        self.parts[piece] = Scatter(
            piece, piece == 0, own, self.buffers[piece][2:], self.y, self.z, self.push
        )
        self.parts[piece].begin()

    def join(self):
        for piece in (1, 0):
            self.parts[piece].join()

    def turn(self):
        for piece in (1, 0):
            self.parts[piece].turn()

    def join_two(self):
        for piece in (1, 0):
            self.parts[piece].join_two()

    def finish(self, out):
        self.parts[0].finish(out.at[pl.ds(0, self.half)])
        self.parts[1].finish(out.at[pl.ds(self.half, 2 * self.half)])

    def end(self):
        for copy in self.swaps.values():
            copy.wait_send()

    @staticmethod
    def scratch(half, hidden):
        return (
            scatter_buffers((half, hidden), BF16)
            + scatter_buffers((2 * half, hidden), BF16)
            + [pltpu.SemaphoreType.DMA((6,))] * 3
            + [pltpu.SemaphoreType.DMA((3, 7, RING))] * 2
        )


LAYER_SCRATCH = 2 * (2 + SCATTER_BUFFERS) + 5


def layer_gradients(grads, scratch, y, z, section, started):
    size = 2 + SCATTER_BUFFERS
    push = pusher(scratch[-2], scratch[-1], started)
    return LayerGradients(
        grads, [scratch[:size], scratch[size : 2 * size]], scratch[2 * size : 2 * size + 3],
        y, z, section, push,
    )


def add_blocks(out, former, latter):
    def add(number, carry):
        at_y, at_z = number // RING, lax.rem(number, RING)
        out[at_y, at_z] = (
            former[at_y, at_z].astype(F32) + latter[at_y, at_z].astype(F32)
        ).astype(out.dtype)
        return carry

    lax.fori_loop(0, RING * RING, add, 0)


def final_kernel(*refs):
    refs = list(refs)
    take = lambda count: [refs.pop(0) for _ in range(count)]
    sums = [take(5), take(5)]
    grad_qkv, *grads = take(4)
    grads = [grad_qkv.at[which] for which in range(3)] + grads
    summed_last = take(1)[0]
    extras = take(4)
    small_out, qkv_out, *matrix_outs = take(5)
    targets = [qkv_out.at[which] for which in range(3)] + matrix_outs
    extra_outs = take(2)
    small_in, small_rows, vector_own, vector_parts, summed = take(5)
    extra_sends = take(2)
    small_buffers = take(2 + SCATTER_BUFFERS)
    layer_scratch = take(LAYER_SCRATCH)
    vector_send, vector_recv, extra_send, extra_recv, result_send, result_recv, result_local, hand_local = take(8)
    rank = lax.axis_index("dp")
    y, z = rank // RING, lax.rem(rank, RING)
    section = lax.axis_index("section")
    me = lax.axis_index("tensor")
    other = {"section": 1 - section}
    barrier, count = tensor_barrier(me)
    count += dp_barrier(y, z, section)[1]

    started = []
    first_layer = layer_gradients(grads, layer_scratch, y, z, section, started)
    push = first_layer.push
    first_layer.keep(1)
    first_layer.keep(0)
    handed = pltpu.make_async_copy(summed_last, summed.at[1], hand_local)
    handed.start()
    depth = grads[0].shape[2]
    for i in range(2):
        last_value, first_value = extras[2 * i][...], extras[2 * i + 1][...]
        extra_outs[i][section] = jnp.where(section == 0, first_value, last_value)
        extra_sends[i][...] = jnp.where(section == 0, last_value, first_value)

    small_rows[...] = jnp.zeros_like(small_rows)
    model = small_rows.shape[1]
    for layer in range(2):
        first, middle, end, attend, up = sums[layer]
        top = SMALL * layer
        part = attend.shape[1]
        lanes = pl.ds(pl.multiple_of(me * part, part), part)
        small_rows[top : top + 2, :] = first[0:2, :]
        small_rows[top + 2 : top + 3, lanes] = attend[0:1, :]
        small_rows[top + 3 : top + 4, lanes] = attend[1:2, :]
        small_rows[top + 4 : top + 5, :] = middle[2:3, :]
        small_rows[top + 5 : top + 7, :] = middle[0:2, :]
        small_rows[top + 7 : top + 8, :] = end[1:2, :]
        small_rows[top + 8 : top + 9, :] = end[0:1, :]
        for rank_of in range(RING):
            small_rows[top + 9 + rank_of : top + 10 + rank_of, :] = jnp.where(
                me == rank_of, up[0:1, :], 0.0
            )
        small_rows[top + 13 : top + 14, :] = middle[3:4, :]
    small_in[...] = jnp.zeros_like(small_in)
    for number in range(RING * RING):
        small_in[number // RING, number % RING, :, 0:depth] = small_rows[
            :, number * depth : (number + 1) * depth
        ]
    pl.semaphore_wait(barrier, count)
    first_layer.swap(1)
    first_layer.swap(0)
    small_swap = push(2, 6, 0, small_in.at[:, :, half_of(1 - section, SMALL)], small_buffers[1], other)
    extra_copies = []
    for i in range(2):
        copy = pltpu.make_async_remote_copy(
            src_ref=extra_sends[i],
            dst_ref=extra_outs[i].at[section],
            send_sem=extra_send.at[i],
            recv_sem=extra_recv.at[i],
            device_id=other,
            device_id_type=MESH,
        )
        copy.start()
        extra_copies.append(copy)

    first_layer.begin(1)
    first_layer.begin(0)
    small_swap.wait_recv()
    add_blocks(small_buffers[0], small_in.at[:, :, half_of(section, SMALL)], small_buffers[1])
    small_part = Scatter(2, True, small_buffers[0], small_buffers[2:], y, z, push)
    small_part.begin()
    first_layer.join()
    small_part.join()
    first_layer.turn()
    small_part.turn()
    first_layer.join_two()
    small_part.join_two()
    small_part.finish(vector_own)
    vector_parts[me] = vector_own[...]
    vector_copies = []
    for k in range(1, RING):
        copy = pltpu.make_async_remote_copy(
            src_ref=vector_own,
            dst_ref=vector_parts.at[me],
            send_sem=vector_send.at[k],
            recv_sem=vector_recv.at[k],
            device_id={"tensor": step(me, k)},
            device_id_type=MESH,
        )
        copy.start()
        vector_copies.append(copy)
    first_layer.finish(summed.at[0])
    handed.wait()
    half = depth // 2
    mine = half_of(section, half)
    results = []
    for i, (row, column, columns) in enumerate(half_places(half, qkv_out.shape[2], summed.shape[2])):
        area = (pl.ds(row, half), pl.ds(column, columns))
        copy = pltpu.make_async_remote_copy(
            src_ref=summed.at[(1 - section,) + area],
            dst_ref=targets[i].at[mine],
            send_sem=result_send.at[i],
            recv_sem=result_recv.at[i],
            device_id=other,
            device_id_type=MESH,
        )
        copy.start()
        results.append(copy)
        copy = pltpu.make_async_copy(
            summed.at[(section,) + area], targets[i].at[mine], result_local.at[i]
        )
        copy.start()
        results.append(copy)
    for copy in results:
        copy.wait()
    for copy in vector_copies:
        copy.wait()
    total = vector_parts[0]
    for k in range(1, RING):
        total = total + vector_parts[k]
    small_out[...] = total
    for copy in extra_copies:
        copy.wait()
    first_layer.end()
    for copy in started:
        copy.wait_send()


def final_call(cid, sums, grads, summed_last, extras):
    extra = len(extras)
    width = sums[0].shape[1]
    hidden = grads[-1].shape[3]
    args = list(sums) + list(grads) + [summed_last] + list(extras)
    block = (HALF_ROWS, hidden)
    return pl.pallas_call(
        final_kernel,
        out_shape=[
            jax.ShapeDtypeStruct((SMALL, 128), F32),
            jax.ShapeDtypeStruct((3,) + grads[1].shape[2:], F32),
        ]
        + [jax.ShapeDtypeStruct(value.shape[2:], F32) for value in grads[1:]]
        + [jax.ShapeDtypeStruct((2,) + value.shape, value.dtype) for value in extras[::2]],
        in_specs=[vmem_spec()] * len(sums) + [any_spec()] * (len(grads) + 1) + [vmem_spec()] * extra,
        out_specs=[vmem_spec()] * 7,
        scratch_shapes=[
            pltpu.VMEM((RING, RING, 2 * SMALL, 128), F32),
            pltpu.VMEM((2 * SMALL, width), F32),
            pltpu.VMEM((SMALL, 128), F32),
            pltpu.VMEM((RING, SMALL, 128), F32),
            pltpu.VMEM((2,) + block, F32),
        ]
        + [pltpu.VMEM(value.shape, value.dtype) for value in extras[::2]]
        + scatter_buffers((SMALL, 128), F32)
        + LayerGradients.scratch(HALF_ROWS // 3, hidden)
        + [
            pltpu.SemaphoreType.DMA((RING,)),
            pltpu.SemaphoreType.DMA((RING,)),
            pltpu.SemaphoreType.DMA((extra,)),
            pltpu.SemaphoreType.DMA((extra,)),
            pltpu.SemaphoreType.DMA((6,)),
            pltpu.SemaphoreType.DMA((6,)),
            pltpu.SemaphoreType.DMA((6,)),
            pltpu.SemaphoreType.DMA,
        ],
        compiler_params=comm_params(cid),
    )(*args)


def flat_dot(former, latter):
    return lax.dot_general(former, latter, (((1,), (1,)), ((), ())), preferred_element_type=F32)


def rows_dot(former, latter):
    return lax.dot_general(former, latter, (((0,), (0,)), ((), ())), preferred_element_type=F32)


def head_stack(values, scale):
    column = lax.broadcasted_iota(jnp.int32, values.shape, 1) // HEAD_DIM
    heads_here = values.shape[1] // HEAD_DIM
    zero = jnp.zeros_like(values)
    scaled = values * jnp.asarray(scale, values.dtype)
    return jnp.concatenate(
        [jnp.where(column == head, scaled, zero) for head in range(heads_here)], axis=0
    )


def block_scores(key_block, stack, seg_column, seg_wide):
    scores = flat_dot(key_block, stack)
    return jnp.where(seg_column == seg_wide, scores, MASKED_SCORE)


def load_matrix(packed_any, target, number, half, semaphores):
    copies = []
    for which in range(2):
        copy = pltpu.make_async_copy(
            packed_any.at[which, :, :, pl.ds(number * half, half)],
            target.at[:, :, pl.ds(which * half, half)],
            semaphores.at[which],
        )
        copy.start()
        copies.append(copy)
    return copies


def attend_kernel(
    layer, normed_ref, packed_any, vec_ref, seg_q_ref, seg_k_ref,
    q_ref, k_ref, v_ref, mixed_ref, wide_ref, lse_ref, part_ref,
    pack_ref, stack, acc, top_ref, total_ref, send, recv, local,
):
    group, width = q_ref.shape
    heads_here = width // HEAD_DIM
    depth = group // RING
    loads = load_matrix(packed_any, pack_ref, 0, depth // 2, local)
    matrix = lambda which: pack_ref[:, :, :, which * width : (which + 1) * width].reshape(-1, width)
    rank = lax.axis_index("dp")
    y, z = rank // RING, lax.rem(rank, RING)
    barrier, count = dp_barrier(y, z, None)
    normed = normed_ref[...]
    start = pl.multiple_of(lax.axis_index("tensor") * width, width)
    query_bias = vec_ref[layer, 2:3, pl.ds(start, width)]
    value_bias = vec_ref[layer, 3:4, pl.ds(start, width)]
    for load in loads:
        load.wait()
    k_ref[y, z] = jnp.dot(normed, matrix(1), preferred_element_type=F32).astype(BF16)
    pl.semaphore_wait(barrier, count)
    started = []
    ring = Gather(((0, (), True), (1, (), False)), (k_ref, v_ref), y, z, (), pusher(send, recv, started))
    ring.begin(0, k_ref.at[y, z])
    v_ref[y, z] = (
        jnp.dot(normed, matrix(2), preferred_element_type=F32) + value_bias
    ).astype(BF16)
    ring.begin(1, v_ref.at[y, z])
    q_ref[...] = (
        jnp.dot(normed, matrix(0), preferred_element_type=F32) + query_bias
    ).astype(BF16)
    stack[...] = head_stack(q_ref[...], HEAD_DIM ** (-0.5))
    acc[...] = jnp.zeros_like(acc)
    top_ref[...] = jnp.full_like(top_ref, MASKED_SCORE)
    total_ref[...] = jnp.zeros_like(total_ref)
    seg_wide = jnp.concatenate([seg_q_ref[0:1, :]] * heads_here, axis=1)

    def attend(offset_y, offset_z):
        at_y, at_z = step(y, offset_y), step(z, offset_z)
        highest = top_ref[0:1, :]
        scores = block_scores(
            k_ref[at_y, at_z], stack[...], seg_k_ref[at_y, at_z, :, 0:1], seg_wide
        )
        above = jnp.maximum(highest, jnp.max(scores, axis=0, keepdims=True))
        weights = jnp.exp(scores - above)
        fade = jnp.exp(highest - above)
        total_ref[0:1, :] = total_ref[0:1, :] * fade + jnp.sum(weights, axis=0, keepdims=True)
        top_ref[0:1, :] = above
        low = weights.astype(BF16)
        turned = v_ref[at_y, at_z].T
        for head in range(heads_here):
            rows = pl.ds(head * HEAD_DIM, HEAD_DIM)
            lanes = slice(head * group, (head + 1) * group)
            term = jnp.dot(
                turned[head * HEAD_DIM : (head + 1) * HEAD_DIM], low[:, lanes],
                preferred_element_type=F32,
            )
            acc[rows, :] = acc[rows, :] * fade[:, lanes] + term

    def attend_all(count, offsets):
        def each(number, carry):
            attend(*offsets(number))
            return carry

        lax.fori_loop(0, count, each, 0)

    side = lambda t: 1 + 2 * lax.rem(t, 2)
    attend_all(1, lambda t: (t, t))
    ring.near()
    for i in ring.every:
        ring.relay(i, 0)
    for i in ring.every:
        ring.far(i)
        ring.other(i, 0)
    attend_all(4, lambda t: (side(t) * (t // 2), side(t) * (1 - t // 2)))
    for i in ring.every:
        ring.relay(i, MINUS)
        ring.relay(i, PLUS)
    for i in ring.every:
        ring.other(i, MINUS)
        ring.other(i, PLUS)
    attend_all(2, lambda t: (t * 0 + PLUS, side(t)))
    for i in ring.every:
        ring.relay(i, FAR)
        ring.relayed[i, 0].wait_recv()
    attend_all(2, lambda t: (t * 0 + MINUS, side(t)))
    attend_all(2, lambda t: (2 * t, 2 - 2 * t))
    for i in ring.every:
        ring.other(i, FAR)
        ring.relayed[i, MINUS].wait_recv()
        ring.relayed[i, PLUS].wait_recv()
    attend_all(
        4,
        lambda t: (
            2 * (t // 2) + side(t) * (1 - t // 2),
            2 * (1 - t // 2) + side(t) * (t // 2),
        ),
    )
    for i in ring.every:
        ring.relayed[i, FAR].wait_recv()
    attend_all(1, lambda t: (t + FAR, t + FAR))

    total = total_ref[0:1, :]
    inverse = 1.0 / total
    for head in range(heads_here):
        rows = pl.ds(head * HEAD_DIM, HEAD_DIM)
        wide_ref[rows, :] = acc[rows, :] * inverse[:, head * group : (head + 1) * group]
    mixed_ref[...] = wide_ref[...].T.astype(BF16)
    lse_ref[...] = jnp.broadcast_to(top_ref[0:1, :] + jnp.log(total), lse_ref.shape)
    part = flat_dot(mixed_ref[...], matrix(3)).astype(BF16)
    part_ref[...] = part.reshape(part_ref.shape)
    for copy in started:
        copy.wait_send()


def attend_call(cid, layer, normed, packed, vectors, seg_wide, seg_column):
    group, model = normed.shape
    width = model // RING
    heads_here = width // HEAD_DIM
    square = (RING, RING, group, width)
    return pl.pallas_call(
        functools.partial(attend_kernel, layer),
        out_shape=[
            jax.ShapeDtypeStruct((group, width), BF16),
            jax.ShapeDtypeStruct(square, BF16),
            jax.ShapeDtypeStruct(square, BF16),
            jax.ShapeDtypeStruct((group, width), BF16),
            jax.ShapeDtypeStruct((width, group), F32),
            jax.ShapeDtypeStruct((8, group * heads_here), F32),
            jax.ShapeDtypeStruct((RING, group // RING, model), BF16),
        ],
        in_specs=[vmem_spec(), any_spec()] + [vmem_spec()] * 3,
        out_specs=[vmem_spec()] * 7,
        scratch_shapes=[
            pltpu.VMEM((RING, RING, group // RING, model), BF16),
            pltpu.VMEM((group * heads_here, width), BF16),
            pltpu.VMEM((width, group), F32),
            pltpu.VMEM((8, group * heads_here), F32),
            pltpu.VMEM((8, group * heads_here), F32),
            pltpu.SemaphoreType.DMA((2, 5, RING)),
            pltpu.SemaphoreType.DMA((2, 5, RING)),
            pltpu.SemaphoreType.DMA((2,)),
        ],
        compiler_params=comm_params(cid),
    )(normed, packed, vectors, seg_wide, seg_column)


def attend_back_kernel(
    rows_ref, packed_any, q_ref, k_ref, v_ref, wide_ref, lse_ref, seg_q_ref, seg_k_ref,
    triple_ref, sums_ref, part_ref, *scratch,
):
    (
        pack_ref, grad_ref, stack, plain, grad_stack, grad_plain, acc, delta_ref,
        dk_ref, dv_ref, total_ref,
    ) = scratch[:11]
    buffers = scratch[11 : 11 + 2 * SCATTER_BUFFERS]
    send, recv, local = scratch[11 + 2 * SCATTER_BUFFERS :]
    group, width = q_ref.shape
    heads_here = width // HEAD_DIM
    scale = HEAD_DIM ** (-0.5)
    depth = group // RING
    loads = load_matrix(packed_any, pack_ref, 0, depth // 2, local)
    matrix = lambda which: pack_ref[:, :, :, which * width : (which + 1) * width].reshape(-1, width)
    rank = lax.axis_index("dp")
    y, z = rank // RING, lax.rem(rank, RING)
    barrier, count = dp_barrier(y, z, None)
    stack[...] = head_stack(q_ref[...], scale)
    plain[...] = head_stack(q_ref[...], 1.0)
    for load in loads:
        load.wait()
    grad_ref[...] = jnp.dot(rows_ref[...], matrix(3), preferred_element_type=F32).astype(BF16)
    grad_stack[...] = head_stack(grad_ref[...], scale)
    grad_plain[...] = head_stack(grad_ref[...], 1.0)
    acc[...] = jnp.zeros_like(acc)
    seg_wide = jnp.concatenate([seg_q_ref[0:1, :]] * heads_here, axis=1)
    product = grad_ref[...].astype(F32).T * wide_ref[...]
    for head in range(heads_here):
        delta_ref[0:1, pl.ds(head * group, group)] = scale * jnp.sum(
            product[head * HEAD_DIM : (head + 1) * HEAD_DIM], axis=0, keepdims=True
        )
    pl.semaphore_wait(barrier, count)
    started = []
    push = pusher(send, recv, started)
    keys = Scatter(0, True, dk_ref, buffers[:SCATTER_BUFFERS], y, z, push)
    values = Scatter(1, False, dv_ref, buffers[SCATTER_BUFFERS:], y, z, push)

    def attend(offset_y, offset_z):
        at_y, at_z = step(y, offset_y), step(z, offset_z)
        key_block = k_ref[at_y, at_z]
        scores = block_scores(key_block, stack[...], seg_k_ref[at_y, at_z, :, 0:1], seg_wide)
        weights = jnp.exp(scores - lse_ref[0:1, :])
        dv_ref[at_y, at_z] = jnp.dot(
            weights.astype(BF16), grad_plain[...], preferred_element_type=F32
        ).astype(BF16)
        prob_grad = flat_dot(v_ref[at_y, at_z], grad_stack[...])
        low = (weights * (prob_grad - delta_ref[0:1, :])).astype(BF16)
        dk_ref[at_y, at_z] = jnp.dot(low, plain[...], preferred_element_type=F32).astype(BF16)
        turned = key_block.T
        for head in range(heads_here):
            rows = pl.ds(head * HEAD_DIM, HEAD_DIM)
            acc[rows, :] += jnp.dot(
                turned[head * HEAD_DIM : (head + 1) * HEAD_DIM],
                low[:, head * group : (head + 1) * group],
                preferred_element_type=F32,
            )

    def attend_all(first, count, offsets):
        def each(number, carry):
            attend(*offsets(number))
            return carry

        lax.fori_loop(first, count, each, 0)

    attend_all(0, 4, lambda t: (t * 0 + FAR, step(t, FAR)))
    for j in Scatter.ORDER:
        values.send_via(j)
    keys.send_direct(FAR)
    attend_all(1, 4, lambda t: (step(t, FAR), t * 0 + FAR))
    for j in Scatter.ORDER:
        keys.send_via(j)
    values.send_direct(FAR)
    attend_all(1, 4, lambda t: (t * 0 + PLUS, step(t, FAR)))
    keys.send_direct(PLUS)
    values.send_direct(PLUS)
    values.send_direct(MINUS)
    attend_all(1, 4, lambda t: (t * 0 + MINUS, step(t, FAR)))
    keys.send_direct(MINUS)
    values.send_direct(0)
    values.join()
    for j in (FAR, PLUS, MINUS):
        keys.join_one(j)
    attend_all(0, 2, lambda t: (t * 0, 1 + 2 * t))
    keys.send_direct(0)
    keys.join_one(0)
    attend_all(0, 1, lambda t: (t, t))
    values.turn()
    keys.turn()
    values.join_two()
    keys.join_two()
    sums_ref[...] = jnp.zeros_like(sums_ref)
    query_grad = acc[...].T
    sums_ref[0:1, :] = jnp.sum(query_grad, axis=0, keepdims=True)
    triple_ref[0] = query_grad.astype(BF16)
    part = flat_dot(triple_ref[0], matrix(0))
    values.finish(total_ref)
    triple_ref[2] = total_ref[...].astype(BF16)
    sums_ref[1:2, :] = jnp.sum(total_ref[...], axis=0, keepdims=True)
    part = part + flat_dot(triple_ref[2], matrix(2))
    keys.finish(total_ref)
    triple_ref[1] = total_ref[...].astype(BF16)
    part = part + flat_dot(triple_ref[1], matrix(1))
    part_ref[...] = part.astype(BF16).reshape(part_ref.shape)
    for copy in started:
        copy.wait_send()


def attend_back_call(cid, attn_rows, packed, queries, keys, values, wide, lse, seg_wide, seg_column):
    group, model = attn_rows.shape
    width = queries.shape[1]
    heads_here = width // HEAD_DIM
    block = (group, width)
    stacked = pltpu.VMEM((group * heads_here, width), BF16)
    return pl.pallas_call(
        attend_back_kernel,
        out_shape=[
            jax.ShapeDtypeStruct((3, group, width), BF16),
            jax.ShapeDtypeStruct((8, width), F32),
            jax.ShapeDtypeStruct((RING, group // RING, model), BF16),
        ],
        in_specs=[vmem_spec(), any_spec()] + [vmem_spec()] * 7,
        out_specs=[vmem_spec()] * 3,
        scratch_shapes=[
            pltpu.VMEM((RING, RING, group // RING, model), BF16),
            pltpu.VMEM(block, BF16),
            stacked,
            stacked,
            stacked,
            stacked,
            pltpu.VMEM((width, group), F32),
            pltpu.VMEM((8, group * heads_here), F32),
            pltpu.VMEM((RING, RING) + block, BF16),
            pltpu.VMEM((RING, RING) + block, BF16),
            pltpu.VMEM(block, F32),
        ]
        + Scatter.scratch(block, BF16)
        + Scatter.scratch(block, BF16)
        + [
            pltpu.SemaphoreType.DMA((2, 6, RING)),
            pltpu.SemaphoreType.DMA((2, 6, RING)),
            pltpu.SemaphoreType.DMA((2,)),
        ],
        compiler_params=comm_params(cid),
    )(attn_rows, packed, queries, keys, values, wide, lse, seg_wide, seg_column)


class Exchange:
    def __init__(self, me, send, recv, landing, started):
        self.me, self.send, self.recv, self.landing, self.started = me, send, recv, landing, started
        self.reduces = {}

    def push(self, source, target, kind, index, k):
        copy = pltpu.make_async_remote_copy(
            src_ref=source,
            dst_ref=target,
            send_sem=self.send.at[kind, index, k - 1],
            recv_sem=self.recv.at[kind, index, k - 1],
            device_id={"tensor": step(self.me, k)},
            device_id_type=MESH,
        )
        copy.start()
        self.started.append(copy)
        return copy

    def reduce(self, part, peers=(1, 2, 3)):
        chunk = part.shape[-2] // CHUNKS
        for c in range(CHUNKS):
            here = pl.ds(c * chunk, chunk)
            for k in peers:
                self.reduces[c, k] = self.push(
                    part.at[step(self.me, k), here], self.landing.at[k - 1, here], 0, c, k
                )

    def run(self, part, function, rows_in, vecs, rows_out, sums_out, full, side=()):
        side = list(side)
        me = self.me
        chunk = part.shape[-2] // CHUNKS
        if side:
            side.pop(0)()
        sums, last = None, []
        for c in range(CHUNKS):
            here = pl.ds(c * chunk, chunk)
            for k in range(1, RING):
                self.reduces[c, k].wait_recv()
            total = part[me, here].astype(F32)
            for k in range(1, RING):
                total = total + self.landing[k - 1, here].astype(F32)
            spread, outs, parts = function(total, [ref[here].astype(F32) for ref in rows_in], vecs)
            if full is not None:
                full[me, here] = spread.astype(BF16)
                last += [
                    self.push(full.at[me, here], full.at[me, here], 1, c, k) for k in range(1, RING)
                ]
            for ref, value in zip(rows_out, outs):
                ref[here] = value.astype(ref.dtype)
            sums = parts if sums is None else [old + new for old, new in zip(sums, parts)]
        if sums_out is not None:
            sums_out[...] = jnp.concatenate(
                sums + [jnp.zeros((8 - len(sums), sums[0].shape[1]), F32)], axis=0
            )
        for work in side:
            work()
        for copy in last:
            copy.wait_recv()


TILES = ((2, 1), (3, 0))


def rows_of(ref, me, tile):
    return jnp.concatenate([ref[step(me, k)] for k in tile], axis=0)


def put_rows(ref, me, tile, value):
    rows = ref.shape[1]
    for i, k in enumerate(tile):
        ref[step(me, k)] = value[i * rows : (i + 1) * rows].astype(ref.dtype)


def wide_of(pack_ref):
    return pack_ref[...].reshape(-1, pack_ref.shape[-1])


def mlp_forward(me, full, up_ref, down_ref, bias, act_ref, slope_ref, part_ref, exchange):
    for tile in TILES:
        value = jnp.dot(rows_of(full, me, tile), wide_of(up_ref), preferred_element_type=F32)
        value = value + bias
        phi = 0.5 * (1.0 + lax.erf(value * (0.5**0.5)))
        act = (value * phi).astype(BF16)
        density = jnp.exp(-0.5 * value * value) * 0.3989422804014327
        put_rows(act_ref, me, tile, act)
        put_rows(slope_ref, me, tile, phi + value * density)
        put_rows(part_ref, me, tile, flat_dot(act, wide_of(down_ref)))
        exchange.reduce(part_ref, [k for k in tile if k])


def mlp_backward(me, full, up_ref, down_ref, slope_ref, pre_ref, bias_out, part_ref, exchange):
    total = None
    for tile in TILES:
        value = jnp.dot(rows_of(full, me, tile), wide_of(down_ref), preferred_element_type=F32)
        value = value * rows_of(slope_ref, me, tile)
        part = jnp.sum(value, axis=0, keepdims=True)
        total = part if total is None else total + part
        low = value.astype(BF16)
        put_rows(pre_ref, me, tile, low)
        put_rows(part_ref, me, tile, flat_dot(low, wide_of(up_ref)))
        exchange.reduce(part_ref, [k for k in tile if k])
    bias_out[...] = jnp.broadcast_to(total, bias_out.shape)


def product(former_ref, latter_ref, out_ref):
    def work():
        tokens = lambda ref: ref[...].reshape(-1, ref.shape[-1])
        size = 256

        def each(number, carry):
            columns = pl.ds(pl.multiple_of(number * size, size), size)
            left = former_ref[..., columns].reshape(-1, size)
            value = jnp.dot(left.T, tokens(latter_ref), preferred_element_type=F32)
            out_ref[number] = value.astype(BF16).reshape(out_ref.shape[1:])
            return carry

        lax.fori_loop(0, RING, each, 0)

    return work


def chain_call(cid, body, exchanges, packed_array, ins, outs, inside, any_names=(), extra=None):
    names = list(ins) + list(outs) + list(inside)
    rows, model = 64, 1024
    count = len(names)
    load_packed = packed_array is not None

    def kernel(*refs):
        refs = list(refs)
        packed = refs.pop(0) if load_packed else None
        env = SimpleNamespace(**dict(zip(names, refs[:count])))
        refs = refs[count:]
        me = lax.axis_index("tensor")
        barrier, peers = tensor_barrier(me)
        started = []
        loads = []
        if load_packed:
            env.up, env.down, local = refs[:3]
            refs = refs[3:]
            half = env.up.shape[2] // 2
            for i, matrix in enumerate((env.up, env.down)):
                loads += load_matrix(packed, matrix, i + 1, half, local.at[i])
        if extra is not None:
            env.extra = refs[3 * exchanges :]
            rank = lax.axis_index("dp")
            env.place = (rank // RING, lax.rem(rank, RING), lax.axis_index("section"))
            peers += dp_barrier(*env.place)[1]
        pl.semaphore_wait(barrier, peers)
        env.started = started
        rings = [
            Exchange(me, refs[3 * i + 1], refs[3 * i + 2], refs[3 * i], started)
            for i in range(exchanges)
        ]
        body(me, env, rings, loads)
        for copy in started:
            copy.wait_send()

    scratch = [pltpu.VMEM(shape, dtype) for shape, dtype in inside.values()]
    spec_of = lambda name: any_spec() if name in any_names else vmem_spec()
    args, in_specs = list(ins.values()), [spec_of(name) for name in ins]
    if load_packed:
        args, in_specs = [packed_array] + args, [any_spec()] + in_specs
        matrix = pltpu.VMEM((RING, RING, rows, model), BF16)
        scratch += [matrix, matrix, pltpu.SemaphoreType.DMA((2, 2))]
    for _ in range(exchanges):
        scratch += [
            pltpu.VMEM((RING - 1, rows, model), BF16),
            pltpu.SemaphoreType.DMA((2, CHUNKS, RING - 1)),
            pltpu.SemaphoreType.DMA((2, CHUNKS, RING - 1)),
        ]
    scratch += extra or []
    results = pl.pallas_call(
        kernel,
        out_shape=[jax.ShapeDtypeStruct(shape, dtype) for shape, dtype in outs.values()],
        in_specs=in_specs,
        out_specs=[spec_of(name) for name in outs],
        scratch_shapes=scratch,
        compiler_params=comm_params(cid),
    )(*args)
    return SimpleNamespace(**dict(zip(outs, results)))


def first_mlp_body(me, env, rings, loads):
    y, z, section = env.place
    send, recv, local = env.extra
    push = pusher(send, recv, env.started)
    halves = [pl.ds(0, HALF_ROWS // 2), pl.ds(HALF_ROWS // 2, HALF_ROWS // 2)]
    ring = Gather(
        ((0, (), True), (1, (), False)),
        [env.packed_next.at[section, :, :, half] for half in halves], y, z, (), push,
    )
    begin, near, middle, end, final = spread_stages(
        ring, [env.stage.at[1, half] for half in halves], local, section, push
    )
    rings[0].reduce(env.part)
    rings[0].run(
        env.part, middle_rows, [env.inputs], [env.vectors.at[0]],
        [env.attn_out, env.hidden], None, env.normed, [begin, near],
    )
    middle()
    for copy in loads:
        copy.wait()
    mlp_forward(
        me, env.normed, env.up, env.down, env.vectors[0, pl.ds(9 + me, 1), :], env.act, env.slope, env.sent, rings[1],
    )
    end()
    rings[1].run(
        env.sent, end_rows_first, [env.hidden], [env.vectors.at[0], env.vectors.at[1]],
        [env.mlp_out, env.outputs], None, env.next, [lambda: None, final],
    )


def last_mlp_body(me, env, rings, loads):
    rings[0].reduce(env.part)
    rings[0].run(
        env.part, middle_rows, [env.inputs], [env.vectors.at[1]],
        [env.attn_out, env.hidden], None, env.normed,
    )
    for copy in loads:
        copy.wait()
    mlp_forward(
        me, env.normed, env.up, env.down, env.vectors[1, pl.ds(9 + me, 1), :], env.act, env.slope,
        env.sent, rings[1],
    )
    rings[1].run(
        env.sent, end_rows_last, [env.hidden, env.upstream], [env.vectors.at[1]],
        [env.outputs], env.sums_end, env.mlp_rows,
    )
    mlp_backward(
        me, env.mlp_rows, env.up, env.down, env.slope, env.pre, env.bias_grad,
        env.sent_two, rings[2],
    )
    rings[2].run(
        env.sent_two, back_middle_rows, [env.upstream, env.hidden, env.attn_out],
        [env.vectors.at[1]], [env.hidden_grad], env.sums_middle, env.attn_rows,
        [
            product(env.mlp_rows, env.act, env.grad_down),
            product(env.normed, env.pre, env.grad_up),
        ],
    )


def attention_products(env):
    return [
        product(env.attn_rows_in, env.mixed, env.grad_out)
    ] + [
        product(env.normed_in, env.triple.at[which], env.grad_qkv.at[which])
        for which in range(3)
    ]


def between_body(me, env, rings, loads):
    y, z, section = env.place
    grads = [env.grad_qkv.at[which] for which in range(3)]
    grads += [env.grad_out, env.last_up, env.last_down]
    layer = layer_gradients(grads, env.extra, y, z, section, env.started)

    def swap():
        for work in attention_products(env):
            work()
        layer.keep(0)
        layer.swap(0)
        layer.begin(1)

    layer.swap(1)
    layer.keep(1)
    rings[0].reduce(env.part)
    rings[0].run(
        env.part, back_end_rows_last, [env.hidden_grad_in, env.inputs, env.mlp_out],
        [env.vectors.at[1], env.vectors.at[0]], [env.input_grad], env.sums_last, env.mlp_rows,
        [swap, lambda: layer.begin(0)],
    )
    for copy in loads:
        copy.wait()
    mlp_backward(
        me, env.mlp_rows, env.up, env.down, env.slope, env.pre, env.bias_grad, env.sent, rings[1],
    )
    layer.join()

    def products():
        product(env.mlp_rows, env.act, env.grad_down)()
        product(env.normed, env.pre, env.grad_up)()

    def rest():
        layer.turn()
        layer.join_two()
        layer.finish(env.summed)
        layer.end()

    rings[1].run(
        env.sent, back_middle_rows_low, [env.input_grad, env.hidden, env.attn_out],
        [env.vectors.at[0]], [env.hidden_grad], env.sums_middle, env.attn_rows, [products, rest],
    )


def back_middle_rows_low(total, rows, vecs):
    return back_middle_rows(total, [rows[0].astype(BF16).astype(F32)] + rows[1:], vecs)


def close_body(me, env, rings, loads):
    rings[0].reduce(env.part)
    rings[0].run(
        env.part, back_end_rows_first, [env.hidden_grad_in, env.inputs],
        [env.vectors.at[0]], [env.input_grad], env.sums_last, None, attention_products(env),
    )


def shards(tokens, segment_ids, w_qkv, w_out, w_up, w_down, vectors, out_bias, cotangent):
    section = lax.axis_index("section")
    tensor_rank = lax.axis_index("tensor")
    own = lambda pair: jnp.where(section == 0, pair[0], pair[1])
    rows = tokens.shape[1]
    width = tokens.shape[2]
    group = rows * RING
    square = (RING, RING)
    local_width = w_qkv.shape[3]
    local_hidden = w_up.shape[2]

    depth = w_out.shape[1]
    my_segments = own(segment_ids)
    wide_segments = jnp.pad(my_segments, (0, depth - rows)).astype(BF16)[None]
    small = jnp.pad(
        jnp.concatenate([vectors[0], out_bias, wide_segments], axis=0),
        ((0, 1), (0, 128 - depth)),
    )
    packed_first, stage, small_rows, normed, inputs, my_cotangent, seg_wide, seg_column = first_call(
        0, tokens, cotangent, w_qkv[0], w_out[0], w_up[0], w_down[0], small
    )

    whole = (RING, rows, width)
    blocks = lambda columns: square + (depth, columns)
    spread = (RING, rows, local_hidden)
    row_shape = (rows, width)
    def attend_layer(layer, normed, packed):
        return attend_call(
            2 + 12 * layer, layer, normed.reshape(group, width), packed, small_rows, seg_wide, seg_column
        )

    normed_first = normed
    *kept_first, part = attend_layer(0, normed_first, packed_first)
    first = chain_call(
        3, first_mlp_body, 2, packed_first,
        dict(
            part=part, inputs=inputs, vectors=small_rows, stage=stage,
        ),
        dict(
            attn_out=(row_shape, F32), hidden=(row_shape, F32), normed=(whole, BF16),
            act=(spread, BF16), slope=(spread, F32), mlp_out=(row_shape, F32),
            outputs=(row_shape, BF16), next=(whole, BF16),
            packed_next=((2,) + square + (HALF_ROWS, local_hidden), BF16),
        ),
        dict(sent=(whole, BF16)),
        ("packed_next",),
        gather_scratch(),
    )
    between = first.outputs
    packed_last = first.packed_next
    *kept_last, part = attend_layer(1, first.next, packed_last)
    last = chain_call(
        5, last_mlp_body, 3, packed_last,
        dict(
            part=part, inputs=between, vectors=small_rows, upstream=my_cotangent,
        ),
        dict(
            outputs=(row_shape, BF16), sums_end=((8, width), F32),
            hidden_grad=(row_shape, F32), sums_middle=((8, width), F32),
            attn_rows=(whole, BF16), bias_grad=((8, local_hidden), F32),
            grad_up=(blocks(local_hidden), BF16), grad_down=(blocks(local_hidden), BF16),
        ),
        dict(
            attn_out=(row_shape, F32), hidden=(row_shape, F32), normed=(whole, BF16),
            act=(spread, BF16), slope=(spread, F32), pre=(spread, BF16),
            mlp_rows=(whole, BF16), sent=(whole, BF16), sent_two=(whole, BF16),
        ),
    )
    outputs = last.outputs

    def attend_back_layer(layer, attn_rows, kept, packed):
        queries, keys_full, values_full, mixed, wide, lse = kept
        return attend_back_call(
            7 + 12 * layer, attn_rows.reshape(group, width), packed, queries, keys_full,
            values_full, wide, lse, seg_wide, seg_column,
        )

    attention_grads = dict(
        grad_out=(blocks(local_width), BF16), grad_qkv=((3,) + blocks(local_width), BF16),
    )
    triple, attend_last, part = attend_back_layer(1, last.attn_rows, kept_last, packed_last)
    middle = chain_call(
        8, between_body, 2, packed_first,
        dict(
            part=part, hidden_grad_in=last.hidden_grad, inputs=between,
            mlp_out=first.mlp_out, vectors=small_rows,
            slope=first.slope, act=first.act, normed=first.normed,
            hidden=first.hidden, attn_out=first.attn_out,
            attn_rows_in=last.attn_rows, mixed=kept_last[3], normed_in=first.next,
            triple=triple, last_up=last.grad_up, last_down=last.grad_down,
        ),
        dict(
            summed=((HALF_ROWS, local_hidden), F32),
            input_grad=(row_shape, F32), sums_last=((8, width), F32),
            hidden_grad=(row_shape, F32), sums_middle=((8, width), F32),
            attn_rows=(whole, BF16), bias_grad=((8, local_hidden), F32),
            grad_up=(blocks(local_hidden), BF16), grad_down=(blocks(local_hidden), BF16),
            **attention_grads,
        ),
        dict(pre=(spread, BF16), mlp_rows=(whole, BF16), sent=(whole, BF16)),
        ("last_up", "last_down"),
        LayerGradients.scratch(HALF_ROWS // 3, local_hidden),
    )
    last_grad = middle.input_grad
    triple, attend_first, part = attend_back_layer(0, middle.attn_rows, kept_first, packed_first)
    close = chain_call(
        9, close_body, 1, None,
        dict(
            part=part, hidden_grad_in=middle.hidden_grad, inputs=inputs,
            vectors=small_rows, attn_rows_in=middle.attn_rows, mixed=kept_first[3],
            normed_in=normed_first, triple=triple,
        ),
        dict(input_grad=(row_shape, F32), sums_last=((8, width), F32), **attention_grads),
        dict(),
    )
    input_grad = close.input_grad
    sums = [
        [close.sums_last, middle.sums_middle, middle.sums_last[2:], attend_first, middle.bias_grad],
        [middle.sums_last, last.sums_middle, last.sums_end, attend_last, last.bias_grad],
    ]
    grads = [close.grad_qkv, close.grad_out, middle.grad_up, middle.grad_down]
    first_grad = input_grad

    small_sum, sum_qkv, sum_out, sum_up, sum_down, out_pair, grad_pair = final_call(
        10, sums[0] + sums[1], grads, middle.summed, [outputs, between, last_grad, first_grad]
    )
    return (
        out_pair[None],
        grad_pair[None],
        sum_qkv[None],
        sum_out[None],
        sum_up[None],
        sum_down[None],
        small_sum[:13, :depth][None],
        small_sum[13:14, :depth],
    )


def solution(mesh):
    in_specs = (
        P(None, ("dp", "tensor"), None),
        P(None, ("dp", "tensor")),
        P("section", None, "dp", "tensor"),
        P("section", "dp", "tensor"),
        P("section", "dp", "tensor"),
        P("section", "dp", "tensor"),
        P("section", None, "dp"),
        P("section", "dp"),
        P(None, ("dp", "tensor"), None),
    )
    out_specs = (
        P("section", None, ("dp", "tensor"), None),
        P("section", None, ("dp", "tensor"), None),
        P("section", None, "dp", "tensor"),
        P("section", "dp", "tensor"),
        P("section", "dp", "tensor"),
        P("section", "dp", "tensor"),
        P("section", None, "dp"),
        P("section", "dp"),
    )
    return jax.shard_map(shards, mesh=mesh, in_specs=in_specs, out_specs=out_specs, check_vma=False)
```

```python
import functools
from types import SimpleNamespace

import jax
import jax.numpy as jnp
from jax import lax
from jax.experimental import pallas as pl
from jax.experimental.pallas import tpu as pltpu
from jax.sharding import PartitionSpec as P

MESH = pl.DeviceIdType.MESH
HEAD_DIM = 64
EPSILON = 1e-06
MASKED_SCORE = -1e30
RING = 4
VMEM_LIMIT = 56 * 1024 * 1024
F32 = jnp.float32
BF16 = jnp.bfloat16


def vmem_spec():
    return pl.BlockSpec(memory_space=pltpu.VMEM)


def any_spec():
    return pl.BlockSpec(memory_space=pl.ANY)


def comm_params(cid):
    return pltpu.CompilerParams(
        collective_id=cid, has_side_effects=True, vmem_limit_bytes=VMEM_LIMIT
    )


def step(coord, by):
    return lax.rem(coord + by, RING)


def layer_norm(values, gain_row, shift_row):
    centre = values - jnp.mean(values, axis=-1, keepdims=True)
    spread = jnp.mean(centre * centre, axis=-1, keepdims=True)
    return centre * lax.rsqrt(spread + EPSILON) * gain_row + shift_row


def layer_norm_back(values, gain_row, grad):
    centre = values - jnp.mean(values, axis=-1, keepdims=True)
    spread = jnp.mean(centre * centre, axis=-1, keepdims=True)
    inverse = lax.rsqrt(spread + EPSILON)
    normed = centre * inverse
    scaled = grad * gain_row
    back = inverse * (
        scaled
        - jnp.mean(scaled, axis=-1, keepdims=True)
        - normed * jnp.mean(scaled * normed, axis=-1, keepdims=True)
    )
    return back, jnp.sum(grad * normed, axis=0, keepdims=True), jnp.sum(grad, axis=0, keepdims=True)


PLUS, FAR, MINUS = 1, 2, 3
CHUNKS = 2


def tensor_barrier(me):
    barrier = pltpu.get_barrier_semaphore()
    for k in range(1, RING):
        pl.semaphore_signal(
            barrier, inc=1, device_id={"tensor": step(me, k)}, device_id_type=MESH
        )
    return barrier, RING - 1


def row(ref, index):
    return ref[pl.ds(index, 1), :]


def middle_rows(total, rows, vecs):
    vec = vecs[0]
    attn_out = total + row(vec, 13)
    hidden = rows[0] + row(vec, 4) * attn_out
    return layer_norm(hidden, row(vec, 5), row(vec, 6)), [attn_out, hidden], []


def end_rows_first(total, rows, vecs):
    vec, after = vecs
    mlp_out = total + row(vec, 7)
    outputs = (rows[0] + row(vec, 8) * mlp_out).astype(BF16)
    inputs = outputs.astype(F32)
    return layer_norm(inputs, row(after, 0), row(after, 1)), [mlp_out, outputs], []


def end_rows_last(total, rows, vecs):
    vec = vecs[0]
    hidden, upstream = rows
    mlp_out = total + row(vec, 7)
    outputs = hidden + row(vec, 8) * mlp_out
    mlp_grad = row(vec, 8) * upstream
    sums = [
        jnp.sum(upstream * mlp_out, axis=0, keepdims=True),
        jnp.sum(mlp_grad, axis=0, keepdims=True),
    ]
    return mlp_grad, [outputs], sums


def back_middle_rows(total, rows, vecs):
    vec = vecs[0]
    upstream, hidden, attn_out = rows
    part, gain, shift = layer_norm_back(hidden, row(vec, 5), total)
    hidden_grad = upstream + part
    attn_grad = row(vec, 4) * hidden_grad
    sums = [
        gain,
        shift,
        jnp.sum(hidden_grad * attn_out, axis=0, keepdims=True),
        jnp.sum(attn_grad, axis=0, keepdims=True),
    ]
    return attn_grad, [hidden_grad], sums


def back_end_rows_last(total, rows, vecs):
    vec, before = vecs
    hidden_grad, inputs, mlp_out = rows
    part, gain, shift = layer_norm_back(inputs, row(vec, 0), total)
    input_grad = hidden_grad + part
    upstream = input_grad.astype(BF16).astype(F32)
    mlp_grad = row(before, 8) * upstream
    sums = [
        gain,
        shift,
        jnp.sum(upstream * mlp_out, axis=0, keepdims=True),
        jnp.sum(mlp_grad, axis=0, keepdims=True),
    ]
    return mlp_grad, [input_grad], sums


def back_end_rows_first(total, rows, vecs):
    hidden_grad, inputs = rows
    part, gain, shift = layer_norm_back(inputs, row(vecs[0], 0), total)
    return None, [hidden_grad + part], [gain, shift]


def dp_neighbour(y, z, along_z, k):
    if along_z:
        return {"dp": y * RING + step(z, k)}
    return {"dp": step(y, k) * RING + z}


def dp_barrier(y, z, section):
    barrier = pltpu.get_barrier_semaphore()
    count = 0
    for along_z in (True, False):
        for k in (PLUS, MINUS):
            pl.semaphore_signal(
                barrier, inc=1, device_id=dp_neighbour(y, z, along_z, k), device_id_type=MESH
            )
            count += 1
    if section is not None:
        pl.semaphore_signal(
            barrier, inc=1, device_id={"section": 1 - section}, device_id_type=MESH
        )
        count += 1
    return barrier, count


def pusher(send, recv, started):
    def push(index, kind, k, source, target, device):
        copy = pltpu.make_async_remote_copy(
            src_ref=source,
            dst_ref=target,
            send_sem=send.at[index, kind, k],
            recv_sem=recv.at[index, kind, k],
            device_id=device,
            device_id_type=MESH,
        )
        copy.start()
        started.append(copy)
        return copy

    return push


class Gather:
    WAYS = {0: 1, 3: 1, 1: 1, 2: 3}

    def __init__(self, pieces, outs, y, z, lead, push):
        self.pieces, self.outs, self.y, self.z = pieces, outs, y, z
        self.lead, self.push = lead, push
        self.every = range(len(pieces))
        self.first, self.onward, self.second, self.relayed = {}, {}, {}, {}

    def block(self, i, along, across, rows=None):
        number, pre, along_z = self.pieces[i]
        ys, zs = (across, along) if along_z else (along, across)
        ys = ys if isinstance(ys, slice) else step(self.y, ys) if ys else self.y
        zs = zs if isinstance(zs, slice) else step(self.z, zs) if zs else self.z
        return self.outs[number].at[self.lead + pre + (ys, zs) + (() if rows is None else (rows,))]

    def way(self, i, first, k):
        return dp_neighbour(self.y, self.z, self.pieces[i][2] == first, k)

    def halves(self, i):
        height = self.outs[self.pieces[i][0]].shape[-2]
        if height < 32:
            return {PLUS: None}
        half = height // 32 * 16
        return {PLUS: pl.ds(0, half), MINUS: pl.ds(half, height - half)}

    def spread(self, i, offset, source):
        for k in (PLUS, MINUS):
            self.second[i, offset, k] = self.push(
                i, 2 if k == PLUS else 3, offset, source, self.block(i, offset, 0), self.way(i, False, k)
            )

    def begin(self, i, source):
        for k in (PLUS, MINUS):
            self.first[i, k] = self.push(i, 0, k, source, self.block(i, 0, 0), self.way(i, True, k))
        self.spread(i, 0, source)

    def near(self):
        for i in self.every:
            split = self.halves(i)
            for k in (PLUS, MINUS):
                self.first[i, k].wait_recv()
                came = RING - k
                if k in split:
                    self.onward[i, k] = self.push(
                        i, 1, k, self.block(i, came, 0, split[k]), self.block(i, came, 0, split[k]),
                        self.way(i, True, k),
                    )
                self.spread(i, came, self.block(i, came, 0))

    def relay(self, i, offset):
        k = self.WAYS[offset]
        self.second[i, offset, k].wait_recv()
        came = self.block(i, offset, RING - k)
        self.relayed[i, offset] = self.push(i, 4, offset, came, came, self.way(i, False, k))

    def other(self, i, offset):
        self.second[i, offset, RING - self.WAYS[offset]].wait_recv()

    def far(self, i):
        for k in self.halves(i):
            self.onward[i, k].wait_recv()
        self.spread(i, FAR, self.block(i, FAR, 0))


def half_of(section, height):
    return pl.ds(pl.multiple_of(section * height, height), height)


def spread_stages(ring, sources, local, section, push):
    own, across = {}, []

    def pass_on(i, line):
        came = ring.block(i, slice(None), line)
        across.append(push(i, 5, line, came, came, {"section": 1 - section}))

    def begin():
        for i in ring.every:
            ring.begin(i, sources[i])
            own[i] = pltpu.make_async_copy(sources[i], ring.block(i, 0, 0), local.at[i])
            own[i].start()

    def near():
        ring.near()
        for i in ring.every:
            ring.relay(i, 0)

    def middle():
        for i in ring.every:
            ring.far(i)
        for i in ring.every:
            ring.relay(i, MINUS)
            ring.relay(i, PLUS)
            own[i].wait()
            pass_on(i, 0)

    def end():
        for i in ring.every:
            ring.relay(i, FAR)
            for offset in range(RING):
                ring.other(i, offset)
            pass_on(i, PLUS)
            pass_on(i, MINUS)

    def last():
        for i in ring.every:
            for offset in range(RING):
                ring.relayed[i, offset].wait_recv()
            pass_on(i, FAR)
        for copy in across:
            copy.wait_recv()

    return [begin, near, middle, end, last]


HALF_ROWS = 96
SMALL = 16


def half_places(half, width, hidden):
    return [(0, which * width, width) for which in range(4)] + [
        (half, 0, hidden),
        (2 * half, 0, hidden),
    ]


def first_kernel(
    tokens_in, cotangent_in, qkv_in, out_in, up_in, down_in, small_in,
    packed_out, stage, rows_out, full, tokens_out, cotangent_out, seg_wide, seg_column,
    small_all, seg_parts, seg_rows,
    send, recv, local, small_send, small_recv, small_local,
    swap_send, swap_recv, swap_local, tensor_send, tensor_recv,
):
    rank = lax.axis_index("dp")
    y, z = rank // RING, lax.rem(rank, RING)
    section = lax.axis_index("section")
    me = lax.axis_index("tensor")
    barrier, count = dp_barrier(y, z, section)
    count += tensor_barrier(me)[1]
    depth, width = out_in.shape
    half = depth // 2
    mine, others = half_of(section, half), half_of(1 - section, half)
    sources = [qkv_in.at[which] for which in range(3)] + [out_in, up_in, down_in]
    places = half_places(half, width, stage.shape[2])
    tokens_out[...] = jnp.where(section == 0, tokens_in[0], tokens_in[1])
    cotangent_out[...] = jnp.where(section == 0, cotangent_in[0], cotangent_in[1])
    seg_parts[me] = jnp.zeros(seg_parts.shape[1:], jnp.int32)
    pl.semaphore_wait(barrier, count)
    started = []
    push = pusher(send, recv, started)
    swaps, kept = [], []
    for i, (source, (row, column, columns)) in enumerate(zip(sources, places)):
        target = stage.at[section, pl.ds(row, half), pl.ds(column, columns)]
        copy = pltpu.make_async_remote_copy(
            src_ref=source.at[others],
            dst_ref=target,
            send_sem=swap_send.at[i],
            recv_sem=swap_recv.at[i],
            device_id={"section": 1 - section},
            device_id_type=MESH,
        )
        copy.start()
        swaps.append(copy)
        copy = pltpu.make_async_copy(source.at[mine], target, swap_local.at[i])
        copy.start()
        kept.append(copy)
    small_push = pusher(small_send, small_recv, started)
    small_ring = Gather(((0, (), True),), [small_all.at[section]], y, z, (), small_push)
    small_stages = spread_stages(small_ring, [small_in], small_local, section, small_push)
    small_stages[0]()
    for copy in kept:
        copy.wait()
    for copy in swaps:
        copy.wait_recv()
    halves = [pl.ds(0, HALF_ROWS // 2), pl.ds(HALF_ROWS // 2, HALF_ROWS // 2)]
    views = [packed_out.at[section, :, :, rows] for rows in halves]
    ring = Gather(((0, (), True), (1, (), False)), views, y, z, (), push)
    stages = spread_stages(ring, [stage.at[0, rows] for rows in halves], local, section, push)
    stages[0]()
    small_stages[1]()
    small_stages[2]()
    stages[1]()
    small_stages[3]()
    small_stages[4]()
    for layer in range(2):
        for number in range(RING * RING):
            part = small_all[layer, number // RING, number % RING]
            rows_out[layer, :, number * depth : (number + 1) * depth] = part[:, :depth].astype(F32)
    for number in range(RING * RING):
        part = small_all[section, number // RING, number % RING]
        seg_parts[me, number : number + 1, 0:depth] = (
            part[14:15, :depth].astype(F32).astype(jnp.int32)
        )
    full[me] = layer_norm(
        tokens_out[...].astype(F32), rows_out[0, 0:1, :], rows_out[0, 1:2, :]
    ).astype(BF16)
    tensor_copies = []
    for i, ref in enumerate((seg_parts, full)):
        for k in range(1, RING):
            copy = pltpu.make_async_remote_copy(
                src_ref=ref.at[me],
                dst_ref=ref.at[me],
                send_sem=tensor_send.at[i, k],
                recv_sem=tensor_recv.at[i, k],
                device_id={"tensor": step(me, k)},
                device_id_type=MESH,
            )
            copy.start()
            tensor_copies.append(copy)
    stages[2]()
    stages[3]()
    for copy in tensor_copies:
        copy.wait_recv()
    for number in range(RING):
        seg_rows[:, number * depth : (number + 1) * depth] = seg_parts[number][:, :depth]
    seg_wide[...] = jnp.broadcast_to(seg_rows[pl.ds(rank, 1), :], seg_wide.shape)
    turned = seg_rows[...].astype(F32).T
    for number in range(RING * RING):
        seg_column[number // RING, number % RING] = jnp.broadcast_to(
            turned[:, number : number + 1], seg_column.shape[2:]
        ).astype(jnp.int32)
    stages[4]()
    for copy in started + swaps + tensor_copies:
        copy.wait_send()


def gather_scratch():
    return [
        pltpu.SemaphoreType.DMA((2, 6, RING)),
        pltpu.SemaphoreType.DMA((2, 6, RING)),
        pltpu.SemaphoreType.DMA((2,)),
    ]


def first_call(cid, tokens, cotangent, w_qkv, w_out, w_up, w_down, small):
    depth = w_out.shape[0]
    hidden = w_up.shape[1]
    rows, width = tokens.shape[1:]
    group = RING * rows
    return pl.pallas_call(
        first_kernel,
        out_shape=[
            jax.ShapeDtypeStruct((2, RING, RING, HALF_ROWS, hidden), BF16),
            jax.ShapeDtypeStruct((2, HALF_ROWS, hidden), BF16),
            jax.ShapeDtypeStruct((2, SMALL, width), F32),
            jax.ShapeDtypeStruct((RING, rows, width), BF16),
            jax.ShapeDtypeStruct((rows, width), BF16),
            jax.ShapeDtypeStruct((rows, width), BF16),
            jax.ShapeDtypeStruct((8, group), jnp.int32),
            jax.ShapeDtypeStruct((RING, RING, group, 128), jnp.int32),
        ],
        in_specs=[vmem_spec()] * 7,
        out_specs=[any_spec()] + [vmem_spec()] * 7,
        scratch_shapes=[
            pltpu.VMEM((2, RING, RING) + small.shape, BF16),
            pltpu.VMEM((RING, RING * RING, 128), jnp.int32),
            pltpu.VMEM((RING * RING, group), jnp.int32),
        ]
        + gather_scratch()
        + gather_scratch()
        + [
            pltpu.SemaphoreType.DMA((6,)),
            pltpu.SemaphoreType.DMA((6,)),
            pltpu.SemaphoreType.DMA((6,)),
            pltpu.SemaphoreType.DMA((2, RING)),
            pltpu.SemaphoreType.DMA((2, RING)),
        ],
        compiler_params=comm_params(cid),
    )(tokens, cotangent, w_qkv, w_out, w_up, w_down, small)


class Scatter:
    ORDER = (FAR, PLUS, MINUS, 0)
    WAYS = {FAR: PLUS, 0: PLUS, PLUS: MINUS, MINUS: MINUS}

    def __init__(self, index, along_z, source, buffers, y, z, push):
        self.index, self.along_z, self.source = index, along_z, source
        self.passing, self.joined, self.summed, self.straight, self.middle = buffers[:5]
        self.far_two, self.joined_two, self.summed_two, self.straight_two = buffers[5:]
        self.y, self.z, self.push = y, z, push
        self.height, self.width = source.shape[-2:]
        self.via, self.direct, self.after = {}, {}, {}

    def at(self, along, across):
        ys, zs = (across, along) if self.along_z else (along, across)
        return step(self.y, ys), step(self.z, zs)

    def way(self, first, k):
        return dp_neighbour(self.y, self.z, self.along_z == first, k)

    def add(self, target, terms, top=0, height=None):
        height = self.height if height is None else height
        size = max(8, min(height, 65536 // self.width))
        while height % size:
            size -= 16

        def part(here):
            value = terms[0](here).astype(F32)
            for term in terms[1:]:
                value = value + term(here).astype(F32)
            target[here] = value.astype(target.dtype)

        if height <= size:
            part(pl.ds(top, height))
            return

        def each(number, carry):
            part(pl.ds(pl.multiple_of(top + number * size, size), size))
            return carry

        lax.fori_loop(0, height // size, each, 0)

    def send_via(self, j):
        self.via[j] = self.push(
            self.index, 0, j, self.source.at[self.at(FAR, j)], self.passing.at[j],
            self.way(True, self.WAYS[j]),
        )

    def send_direct(self, j):
        k = RING - self.WAYS[j]
        self.direct[j] = self.push(
            self.index, 1, j, self.source.at[self.at(k, j)], self.straight.at[j], self.way(True, k)
        )

    def begin(self):
        for j in self.ORDER:
            self.send_via(j)
        for j in self.ORDER:
            self.send_direct(j)

    def join_one(self, j):
        self.via[j].wait_recv()
        k = self.WAYS[j]
        at_y, at_z = self.at(k, j)
        self.add(
            self.joined.at[j],
            [lambda h: self.source[at_y, at_z, h], lambda h: self.passing[j, h]],
        )
        self.after[j] = self.push(
            self.index, 2, j, self.joined.at[j], self.summed.at[j], self.way(True, k)
        )

    def join(self):
        for j in self.ORDER:
            self.join_one(j)

    def turn(self):
        half = self.height // 2
        low, high = pl.ds(0, half), pl.ds(half, half)
        send = lambda kind, slot, source, target, k: self.push(
            self.index, kind, slot, source, target, self.way(False, k)
        )
        for j in self.ORDER:
            self.direct[j].wait_recv()
            self.after[j].wait_recv()
            at_y, at_z = self.at(0, j)
            self.add(
                self.middle.at[j],
                [
                    lambda h: self.source[at_y, at_z, h],
                    lambda h: self.summed[j, h],
                    lambda h: self.straight[j, h],
                ],
            )
            if j == FAR:
                self.via_two = [
                    send(3, 0, self.middle.at[j, low], self.far_two.at[low], PLUS),
                    send(3, 1, self.middle.at[j, high], self.far_two.at[high], MINUS),
                ]
            if j == PLUS:
                high_copy = send(4, 1, self.middle.at[j, high], self.straight_two.at[high], PLUS)
            if j == MINUS:
                low_copy = send(4, 0, self.middle.at[j, low], self.straight_two.at[low], MINUS)
        self.direct_two = [low_copy, high_copy]

    def join_two(self):
        half = self.height // 2
        self.after_two = []
        for number, (top, k) in enumerate(((0, PLUS), (half, MINUS))):
            self.via_two[number].wait_recv()
            self.add(
                self.joined_two,
                [lambda h: self.middle[k, h], lambda h: self.far_two[h]],
                top,
                half,
            )
            here = pl.ds(top, half)
            self.after_two.append(
                self.push(
                    self.index, 5, number, self.joined_two.at[here], self.summed_two.at[here],
                    self.way(False, k),
                )
            )

    def finish(self, out):
        for copy in self.direct_two + self.after_two:
            copy.wait_recv()
        self.add(
            out,
            [
                lambda h: self.middle[0, h],
                lambda h: self.summed_two[h],
                lambda h: self.straight_two[h],
            ],
        )

    @staticmethod
    def scratch(block, dtype):
        return [pltpu.VMEM((RING,) + block, dtype)] * 5 + [pltpu.VMEM(block, dtype)] * 4


SCATTER_BUFFERS = 9


def scatter_buffers(block, dtype):
    square = pltpu.VMEM((RING, RING) + block, dtype)
    return [square, square] + Scatter.scratch(block, dtype)


class LayerGradients:
    def __init__(self, grads, buffers, semaphores, y, z, section, push):
        self.grads, self.buffers, self.y, self.z = grads, buffers, y, z
        self.section, self.push = section, push
        self.keeps, self.swaps, self.parts = {}, {}, {}
        self.swap_send, self.swap_recv, self.keep_local = semaphores
        depth, width = grads[0].shape[2:]
        hidden = grads[5].shape[3]
        self.half = depth // 2
        self.places = [(0, 0, which * width, width) for which in range(4)]
        self.places += [(1, 0, 0, hidden), (1, self.half, 0, hidden)]

    def region(self, which, place):
        piece, row, column, columns = place
        return self.buffers[piece][which].at[:, :, pl.ds(row, self.half), pl.ds(column, columns)]

    def keep(self, piece):
        mine = half_of(self.section, self.half)
        for i, place in enumerate(self.places):
            if place[0] == piece:
                self.keeps[i] = pltpu.make_async_copy(
                    self.grads[i].at[:, :, mine], self.region(0, place), self.keep_local.at[i]
                )
                self.keeps[i].start()

    def swap(self, piece):
        others = half_of(1 - self.section, self.half)
        for i, place in enumerate(self.places):
            if place[0] == piece:
                self.swaps[i] = pltpu.make_async_remote_copy(
                    src_ref=self.grads[i].at[:, :, others],
                    dst_ref=self.region(1, place),
                    send_sem=self.swap_send.at[i],
                    recv_sem=self.swap_recv.at[i],
                    device_id={"section": 1 - self.section},
                    device_id_type=MESH,
                )
                self.swaps[i].start()

    def begin(self, piece):
        for i, place in enumerate(self.places):
            if place[0] == piece:
                self.keeps[i].wait()
                self.swaps[i].wait_recv()
        own, sibling = self.buffers[piece][:2]
        add_blocks(own, own, sibling)
        self.parts[piece] = Scatter(
            piece, piece == 0, own, self.buffers[piece][2:], self.y, self.z, self.push
        )
        self.parts[piece].begin()

    def join(self):
        for piece in (1, 0):
            self.parts[piece].join()

    def turn(self):
        for piece in (1, 0):
            self.parts[piece].turn()

    def join_two(self):
        for piece in (1, 0):
            self.parts[piece].join_two()

    def finish(self, out):
        self.parts[0].finish(out.at[pl.ds(0, self.half)])
        self.parts[1].finish(out.at[pl.ds(self.half, 2 * self.half)])

    def end(self):
        for copy in self.swaps.values():
            copy.wait_send()

    @staticmethod
    def scratch(half, hidden):
        return (
            scatter_buffers((half, hidden), BF16)
            + scatter_buffers((2 * half, hidden), BF16)
            + [pltpu.SemaphoreType.DMA((6,))] * 3
            + [pltpu.SemaphoreType.DMA((3, 7, RING))] * 2
        )


LAYER_SCRATCH = 2 * (2 + SCATTER_BUFFERS) + 5


def layer_gradients(grads, scratch, y, z, section, started):
    size = 2 + SCATTER_BUFFERS
    push = pusher(scratch[-2], scratch[-1], started)
    return LayerGradients(
        grads, [scratch[:size], scratch[size : 2 * size]], scratch[2 * size : 2 * size + 3],
        y, z, section, push,
    )


def add_blocks(out, former, latter):
    def add(number, carry):
        at_y, at_z = number // RING, lax.rem(number, RING)
        out[at_y, at_z] = (
            former[at_y, at_z].astype(F32) + latter[at_y, at_z].astype(F32)
        ).astype(out.dtype)
        return carry

    lax.fori_loop(0, RING * RING, add, 0)


def final_kernel(*refs):
    refs = list(refs)
    take = lambda count: [refs.pop(0) for _ in range(count)]
    sums = [take(5), take(5)]
    grad_qkv, *grads = take(4)
    grads = [grad_qkv.at[which] for which in range(3)] + grads
    summed_last = take(1)[0]
    extras = take(4)
    small_out, qkv_out, *matrix_outs = take(5)
    targets = [qkv_out.at[which] for which in range(3)] + matrix_outs
    extra_outs = take(2)
    small_in, small_rows, vector_own, vector_parts, summed = take(5)
    extra_sends = take(2)
    small_buffers = take(2 + SCATTER_BUFFERS)
    layer_scratch = take(LAYER_SCRATCH)
    vector_send, vector_recv, extra_send, extra_recv, result_send, result_recv, result_local, hand_local = take(8)
    rank = lax.axis_index("dp")
    y, z = rank // RING, lax.rem(rank, RING)
    section = lax.axis_index("section")
    me = lax.axis_index("tensor")
    other = {"section": 1 - section}
    barrier, count = tensor_barrier(me)
    count += dp_barrier(y, z, section)[1]

    started = []
    first_layer = layer_gradients(grads, layer_scratch, y, z, section, started)
    push = first_layer.push
    first_layer.keep(1)
    first_layer.keep(0)
    handed = pltpu.make_async_copy(summed_last, summed.at[1], hand_local)
    handed.start()
    depth = grads[0].shape[2]
    for i in range(2):
        last_value, first_value = extras[2 * i][...], extras[2 * i + 1][...]
        extra_outs[i][section] = jnp.where(section == 0, first_value, last_value)
        extra_sends[i][...] = jnp.where(section == 0, last_value, first_value)

    small_rows[...] = jnp.zeros_like(small_rows)
    model = small_rows.shape[1]
    for layer in range(2):
        first, middle, end, attend, up = sums[layer]
        top = SMALL * layer
        part = attend.shape[1]
        lanes = pl.ds(pl.multiple_of(me * part, part), part)
        small_rows[top : top + 2, :] = first[0:2, :]
        small_rows[top + 2 : top + 3, lanes] = attend[0:1, :]
        small_rows[top + 3 : top + 4, lanes] = attend[1:2, :]
        small_rows[top + 4 : top + 5, :] = middle[2:3, :]
        small_rows[top + 5 : top + 7, :] = middle[0:2, :]
        small_rows[top + 7 : top + 8, :] = end[1:2, :]
        small_rows[top + 8 : top + 9, :] = end[0:1, :]
        for rank_of in range(RING):
            small_rows[top + 9 + rank_of : top + 10 + rank_of, :] = jnp.where(
                me == rank_of, up[0:1, :], 0.0
            )
        small_rows[top + 13 : top + 14, :] = middle[3:4, :]
    small_in[...] = jnp.zeros_like(small_in)
    for number in range(RING * RING):
        small_in[number // RING, number % RING, :, 0:depth] = small_rows[
            :, number * depth : (number + 1) * depth
        ]
    pl.semaphore_wait(barrier, count)
    first_layer.swap(1)
    first_layer.swap(0)
    small_swap = push(2, 6, 0, small_in.at[:, :, half_of(1 - section, SMALL)], small_buffers[1], other)
    extra_copies = []
    for i in range(2):
        copy = pltpu.make_async_remote_copy(
            src_ref=extra_sends[i],
            dst_ref=extra_outs[i].at[section],
            send_sem=extra_send.at[i],
            recv_sem=extra_recv.at[i],
            device_id=other,
            device_id_type=MESH,
        )
        copy.start()
        extra_copies.append(copy)

    first_layer.begin(1)
    first_layer.begin(0)
    small_swap.wait_recv()
    add_blocks(small_buffers[0], small_in.at[:, :, half_of(section, SMALL)], small_buffers[1])
    small_part = Scatter(2, True, small_buffers[0], small_buffers[2:], y, z, push)
    small_part.begin()
    first_layer.join()
    small_part.join()
    first_layer.turn()
    small_part.turn()
    first_layer.join_two()
    small_part.join_two()
    small_part.finish(vector_own)
    vector_parts[me] = vector_own[...]
    vector_copies = []
    for k in range(1, RING):
        copy = pltpu.make_async_remote_copy(
            src_ref=vector_own,
            dst_ref=vector_parts.at[me],
            send_sem=vector_send.at[k],
            recv_sem=vector_recv.at[k],
            device_id={"tensor": step(me, k)},
            device_id_type=MESH,
        )
        copy.start()
        vector_copies.append(copy)
    first_layer.finish(summed.at[0])
    handed.wait()
    half = depth // 2
    mine = half_of(section, half)
    results = []
    for i, (row, column, columns) in enumerate(half_places(half, qkv_out.shape[2], summed.shape[2])):
        area = (pl.ds(row, half), pl.ds(column, columns))
        copy = pltpu.make_async_remote_copy(
            src_ref=summed.at[(1 - section,) + area],
            dst_ref=targets[i].at[mine],
            send_sem=result_send.at[i],
            recv_sem=result_recv.at[i],
            device_id=other,
            device_id_type=MESH,
        )
        copy.start()
        results.append(copy)
        copy = pltpu.make_async_copy(
            summed.at[(section,) + area], targets[i].at[mine], result_local.at[i]
        )
        copy.start()
        results.append(copy)
    for copy in results:
        copy.wait()
    for copy in vector_copies:
        copy.wait()
    total = vector_parts[0]
    for k in range(1, RING):
        total = total + vector_parts[k]
    small_out[...] = total
    for copy in extra_copies:
        copy.wait()
    first_layer.end()
    for copy in started:
        copy.wait_send()


def final_call(cid, sums, grads, summed_last, extras):
    extra = len(extras)
    width = sums[0].shape[1]
    hidden = grads[-1].shape[3]
    args = list(sums) + list(grads) + [summed_last] + list(extras)
    block = (HALF_ROWS, hidden)
    return pl.pallas_call(
        final_kernel,
        out_shape=[
            jax.ShapeDtypeStruct((SMALL, 128), F32),
            jax.ShapeDtypeStruct((3,) + grads[1].shape[2:], F32),
        ]
        + [jax.ShapeDtypeStruct(value.shape[2:], F32) for value in grads[1:]]
        + [jax.ShapeDtypeStruct((2,) + value.shape, value.dtype) for value in extras[::2]],
        in_specs=[vmem_spec()] * len(sums) + [any_spec()] * (len(grads) + 1) + [vmem_spec()] * extra,
        out_specs=[vmem_spec()] * 7,
        scratch_shapes=[
            pltpu.VMEM((RING, RING, 2 * SMALL, 128), F32),
            pltpu.VMEM((2 * SMALL, width), F32),
            pltpu.VMEM((SMALL, 128), F32),
            pltpu.VMEM((RING, SMALL, 128), F32),
            pltpu.VMEM((2,) + block, F32),
        ]
        + [pltpu.VMEM(value.shape, value.dtype) for value in extras[::2]]
        + scatter_buffers((SMALL, 128), F32)
        + LayerGradients.scratch(HALF_ROWS // 3, hidden)
        + [
            pltpu.SemaphoreType.DMA((RING,)),
            pltpu.SemaphoreType.DMA((RING,)),
            pltpu.SemaphoreType.DMA((extra,)),
            pltpu.SemaphoreType.DMA((extra,)),
            pltpu.SemaphoreType.DMA((6,)),
            pltpu.SemaphoreType.DMA((6,)),
            pltpu.SemaphoreType.DMA((6,)),
            pltpu.SemaphoreType.DMA,
        ],
        compiler_params=comm_params(cid),
    )(*args)


def flat_dot(former, latter):
    return lax.dot_general(former, latter, (((1,), (1,)), ((), ())), preferred_element_type=F32)


def rows_dot(former, latter):
    return lax.dot_general(former, latter, (((0,), (0,)), ((), ())), preferred_element_type=F32)


def head_stack(values, scale):
    column = lax.broadcasted_iota(jnp.int32, values.shape, 1) // HEAD_DIM
    heads_here = values.shape[1] // HEAD_DIM
    zero = jnp.zeros_like(values)
    scaled = values * jnp.asarray(scale, values.dtype)
    return jnp.concatenate(
        [jnp.where(column == head, scaled, zero) for head in range(heads_here)], axis=0
    )


def block_scores(key_block, stack, seg_column, seg_wide):
    scores = flat_dot(key_block, stack)
    return jnp.where(seg_column == seg_wide, scores, MASKED_SCORE)


def load_matrix(packed_any, target, number, half, semaphores):
    copies = []
    for which in range(2):
        copy = pltpu.make_async_copy(
            packed_any.at[which, :, :, pl.ds(number * half, half)],
            target.at[:, :, pl.ds(which * half, half)],
            semaphores.at[which],
        )
        copy.start()
        copies.append(copy)
    return copies


def attend_kernel(
    layer, normed_ref, packed_any, vec_ref, seg_q_ref, seg_k_ref,
    q_ref, k_ref, v_ref, mixed_ref, wide_ref, lse_ref, part_ref,
    pack_ref, stack, acc, top_ref, total_ref, send, recv, local,
):
    group, width = q_ref.shape
    heads_here = width // HEAD_DIM
    depth = group // RING
    loads = load_matrix(packed_any, pack_ref, 0, depth // 2, local)
    matrix = lambda which: pack_ref[:, :, :, which * width : (which + 1) * width].reshape(-1, width)
    rank = lax.axis_index("dp")
    y, z = rank // RING, lax.rem(rank, RING)
    barrier, count = dp_barrier(y, z, None)
    normed = normed_ref[...]
    start = pl.multiple_of(lax.axis_index("tensor") * width, width)
    query_bias = vec_ref[layer, 2:3, pl.ds(start, width)]
    value_bias = vec_ref[layer, 3:4, pl.ds(start, width)]
    for load in loads:
        load.wait()
    k_ref[y, z] = jnp.dot(normed, matrix(1), preferred_element_type=F32).astype(BF16)
    pl.semaphore_wait(barrier, count)
    started = []
    ring = Gather(((0, (), True), (1, (), False)), (k_ref, v_ref), y, z, (), pusher(send, recv, started))
    ring.begin(0, k_ref.at[y, z])
    v_ref[y, z] = (
        jnp.dot(normed, matrix(2), preferred_element_type=F32) + value_bias
    ).astype(BF16)
    ring.begin(1, v_ref.at[y, z])
    q_ref[...] = (
        jnp.dot(normed, matrix(0), preferred_element_type=F32) + query_bias
    ).astype(BF16)
    stack[...] = head_stack(q_ref[...], HEAD_DIM ** (-0.5))
    acc[...] = jnp.zeros_like(acc)
    top_ref[...] = jnp.full_like(top_ref, MASKED_SCORE)
    total_ref[...] = jnp.zeros_like(total_ref)
    seg_wide = jnp.concatenate([seg_q_ref[0:1, :]] * heads_here, axis=1)

    def attend(offset_y, offset_z):
        at_y, at_z = step(y, offset_y), step(z, offset_z)
        highest = top_ref[0:1, :]
        scores = block_scores(
            k_ref[at_y, at_z], stack[...], seg_k_ref[at_y, at_z, :, 0:1], seg_wide
        )
        above = jnp.maximum(highest, jnp.max(scores, axis=0, keepdims=True))
        weights = jnp.exp(scores - above)
        fade = jnp.exp(highest - above)
        total_ref[0:1, :] = total_ref[0:1, :] * fade + jnp.sum(weights, axis=0, keepdims=True)
        top_ref[0:1, :] = above
        low = weights.astype(BF16)
        turned = v_ref[at_y, at_z].T
        for head in range(heads_here):
            rows = pl.ds(head * HEAD_DIM, HEAD_DIM)
            lanes = slice(head * group, (head + 1) * group)
            term = jnp.dot(
                turned[head * HEAD_DIM : (head + 1) * HEAD_DIM], low[:, lanes],
                preferred_element_type=F32,
            )
            acc[rows, :] = acc[rows, :] * fade[:, lanes] + term

    def attend_all(count, offsets):
        def each(number, carry):
            attend(*offsets(number))
            return carry

        lax.fori_loop(0, count, each, 0)

    side = lambda t: 1 + 2 * lax.rem(t, 2)
    attend_all(1, lambda t: (t, t))
    ring.near()
    for i in ring.every:
        ring.relay(i, 0)
    for i in ring.every:
        ring.far(i)
        ring.other(i, 0)
    attend_all(4, lambda t: (side(t) * (t // 2), side(t) * (1 - t // 2)))
    for i in ring.every:
        ring.relay(i, MINUS)
        ring.relay(i, PLUS)
    for i in ring.every:
        ring.other(i, MINUS)
        ring.other(i, PLUS)
    attend_all(2, lambda t: (t * 0 + PLUS, side(t)))
    for i in ring.every:
        ring.relay(i, FAR)
        ring.relayed[i, 0].wait_recv()
    attend_all(2, lambda t: (t * 0 + MINUS, side(t)))
    attend_all(2, lambda t: (2 * t, 2 - 2 * t))
    for i in ring.every:
        ring.other(i, FAR)
        ring.relayed[i, MINUS].wait_recv()
        ring.relayed[i, PLUS].wait_recv()
    attend_all(
        4,
        lambda t: (
            2 * (t // 2) + side(t) * (1 - t // 2),
            2 * (1 - t // 2) + side(t) * (t // 2),
        ),
    )
    for i in ring.every:
        ring.relayed[i, FAR].wait_recv()
    attend_all(1, lambda t: (t + FAR, t + FAR))

    total = total_ref[0:1, :]
    inverse = 1.0 / total
    for head in range(heads_here):
        rows = pl.ds(head * HEAD_DIM, HEAD_DIM)
        wide_ref[rows, :] = acc[rows, :] * inverse[:, head * group : (head + 1) * group]
    mixed_ref[...] = wide_ref[...].T.astype(BF16)
    lse_ref[...] = jnp.broadcast_to(top_ref[0:1, :] + jnp.log(total), lse_ref.shape)
    part = flat_dot(mixed_ref[...], matrix(3)).astype(BF16)
    part_ref[...] = part.reshape(part_ref.shape)
    for copy in started:
        copy.wait_send()


def attend_call(cid, layer, normed, packed, vectors, seg_wide, seg_column):
    group, model = normed.shape
    width = model // RING
    heads_here = width // HEAD_DIM
    square = (RING, RING, group, width)
    return pl.pallas_call(
        functools.partial(attend_kernel, layer),
        out_shape=[
            jax.ShapeDtypeStruct((group, width), BF16),
            jax.ShapeDtypeStruct(square, BF16),
            jax.ShapeDtypeStruct(square, BF16),
            jax.ShapeDtypeStruct((group, width), BF16),
            jax.ShapeDtypeStruct((width, group), F32),
            jax.ShapeDtypeStruct((8, group * heads_here), F32),
            jax.ShapeDtypeStruct((RING, group // RING, model), BF16),
        ],
        in_specs=[vmem_spec(), any_spec()] + [vmem_spec()] * 3,
        out_specs=[vmem_spec()] * 7,
        scratch_shapes=[
            pltpu.VMEM((RING, RING, group // RING, model), BF16),
            pltpu.VMEM((group * heads_here, width), BF16),
            pltpu.VMEM((width, group), F32),
            pltpu.VMEM((8, group * heads_here), F32),
            pltpu.VMEM((8, group * heads_here), F32),
            pltpu.SemaphoreType.DMA((2, 5, RING)),
            pltpu.SemaphoreType.DMA((2, 5, RING)),
            pltpu.SemaphoreType.DMA((2,)),
        ],
        compiler_params=comm_params(cid),
    )(normed, packed, vectors, seg_wide, seg_column)


def attend_back_kernel(
    rows_ref, packed_any, q_ref, k_ref, v_ref, wide_ref, lse_ref, seg_q_ref, seg_k_ref,
    triple_ref, sums_ref, part_ref, *scratch,
):
    (
        pack_ref, grad_ref, stack, plain, grad_stack, grad_plain, acc, delta_ref,
        dk_ref, dv_ref, total_ref,
    ) = scratch[:11]
    buffers = scratch[11 : 11 + 2 * SCATTER_BUFFERS]
    send, recv, local = scratch[11 + 2 * SCATTER_BUFFERS :]
    group, width = q_ref.shape
    heads_here = width // HEAD_DIM
    scale = HEAD_DIM ** (-0.5)
    depth = group // RING
    loads = load_matrix(packed_any, pack_ref, 0, depth // 2, local)
    matrix = lambda which: pack_ref[:, :, :, which * width : (which + 1) * width].reshape(-1, width)
    rank = lax.axis_index("dp")
    y, z = rank // RING, lax.rem(rank, RING)
    barrier, count = dp_barrier(y, z, None)
    stack[...] = head_stack(q_ref[...], scale)
    plain[...] = head_stack(q_ref[...], 1.0)
    for load in loads:
        load.wait()
    grad_ref[...] = jnp.dot(rows_ref[...], matrix(3), preferred_element_type=F32).astype(BF16)
    grad_stack[...] = head_stack(grad_ref[...], scale)
    grad_plain[...] = head_stack(grad_ref[...], 1.0)
    acc[...] = jnp.zeros_like(acc)
    seg_wide = jnp.concatenate([seg_q_ref[0:1, :]] * heads_here, axis=1)
    product = grad_ref[...].astype(F32).T * wide_ref[...]
    for head in range(heads_here):
        delta_ref[0:1, pl.ds(head * group, group)] = scale * jnp.sum(
            product[head * HEAD_DIM : (head + 1) * HEAD_DIM], axis=0, keepdims=True
        )
    pl.semaphore_wait(barrier, count)
    started = []
    push = pusher(send, recv, started)
    keys = Scatter(0, True, dk_ref, buffers[:SCATTER_BUFFERS], y, z, push)
    values = Scatter(1, False, dv_ref, buffers[SCATTER_BUFFERS:], y, z, push)

    def attend(offset_y, offset_z):
        at_y, at_z = step(y, offset_y), step(z, offset_z)
        key_block = k_ref[at_y, at_z]
        scores = block_scores(key_block, stack[...], seg_k_ref[at_y, at_z, :, 0:1], seg_wide)
        weights = jnp.exp(scores - lse_ref[0:1, :])
        dv_ref[at_y, at_z] = jnp.dot(
            weights.astype(BF16), grad_plain[...], preferred_element_type=F32
        ).astype(BF16)
        prob_grad = flat_dot(v_ref[at_y, at_z], grad_stack[...])
        low = (weights * (prob_grad - delta_ref[0:1, :])).astype(BF16)
        dk_ref[at_y, at_z] = jnp.dot(low, plain[...], preferred_element_type=F32).astype(BF16)
        turned = key_block.T
        for head in range(heads_here):
            rows = pl.ds(head * HEAD_DIM, HEAD_DIM)
            acc[rows, :] += jnp.dot(
                turned[head * HEAD_DIM : (head + 1) * HEAD_DIM],
                low[:, head * group : (head + 1) * group],
                preferred_element_type=F32,
            )

    def attend_all(first, count, offsets):
        def each(number, carry):
            attend(*offsets(number))
            return carry

        lax.fori_loop(first, count, each, 0)

    attend_all(0, 4, lambda t: (t * 0 + FAR, step(t, FAR)))
    for j in Scatter.ORDER:
        values.send_via(j)
    keys.send_direct(FAR)
    attend_all(1, 4, lambda t: (step(t, FAR), t * 0 + FAR))
    for j in Scatter.ORDER:
        keys.send_via(j)
    values.send_direct(FAR)
    attend_all(1, 4, lambda t: (t * 0 + PLUS, step(t, FAR)))
    keys.send_direct(PLUS)
    values.send_direct(PLUS)
    values.send_direct(MINUS)
    attend_all(1, 4, lambda t: (t * 0 + MINUS, step(t, FAR)))
    keys.send_direct(MINUS)
    values.send_direct(0)
    values.join()
    for j in (FAR, PLUS, MINUS):
        keys.join_one(j)
    attend_all(0, 2, lambda t: (t * 0, 1 + 2 * t))
    keys.send_direct(0)
    keys.join_one(0)
    attend_all(0, 1, lambda t: (t, t))
    values.turn()
    keys.turn()
    values.join_two()
    keys.join_two()
    sums_ref[...] = jnp.zeros_like(sums_ref)
    query_grad = acc[...].T
    sums_ref[0:1, :] = jnp.sum(query_grad, axis=0, keepdims=True)
    triple_ref[0] = query_grad.astype(BF16)
    part = flat_dot(triple_ref[0], matrix(0))
    values.finish(total_ref)
    triple_ref[2] = total_ref[...].astype(BF16)
    sums_ref[1:2, :] = jnp.sum(total_ref[...], axis=0, keepdims=True)
    part = part + flat_dot(triple_ref[2], matrix(2))
    keys.finish(total_ref)
    triple_ref[1] = total_ref[...].astype(BF16)
    part = part + flat_dot(triple_ref[1], matrix(1))
    part_ref[...] = part.astype(BF16).reshape(part_ref.shape)
    for copy in started:
        copy.wait_send()


def attend_back_call(cid, attn_rows, packed, queries, keys, values, wide, lse, seg_wide, seg_column):
    group, model = attn_rows.shape
    width = queries.shape[1]
    heads_here = width // HEAD_DIM
    block = (group, width)
    stacked = pltpu.VMEM((group * heads_here, width), BF16)
    return pl.pallas_call(
        attend_back_kernel,
        out_shape=[
            jax.ShapeDtypeStruct((3, group, width), BF16),
            jax.ShapeDtypeStruct((8, width), F32),
            jax.ShapeDtypeStruct((RING, group // RING, model), BF16),
        ],
        in_specs=[vmem_spec(), any_spec()] + [vmem_spec()] * 7,
        out_specs=[vmem_spec()] * 3,
        scratch_shapes=[
            pltpu.VMEM((RING, RING, group // RING, model), BF16),
            pltpu.VMEM(block, BF16),
            stacked,
            stacked,
            stacked,
            stacked,
            pltpu.VMEM((width, group), F32),
            pltpu.VMEM((8, group * heads_here), F32),
            pltpu.VMEM((RING, RING) + block, BF16),
            pltpu.VMEM((RING, RING) + block, BF16),
            pltpu.VMEM(block, F32),
        ]
        + Scatter.scratch(block, BF16)
        + Scatter.scratch(block, BF16)
        + [
            pltpu.SemaphoreType.DMA((2, 6, RING)),
            pltpu.SemaphoreType.DMA((2, 6, RING)),
            pltpu.SemaphoreType.DMA((2,)),
        ],
        compiler_params=comm_params(cid),
    )(attn_rows, packed, queries, keys, values, wide, lse, seg_wide, seg_column)


class Exchange:
    def __init__(self, me, send, recv, landing, started):
        self.me, self.send, self.recv, self.landing, self.started = me, send, recv, landing, started
        self.reduces = {}

    def push(self, source, target, kind, index, k):
        copy = pltpu.make_async_remote_copy(
            src_ref=source,
            dst_ref=target,
            send_sem=self.send.at[kind, index, k - 1],
            recv_sem=self.recv.at[kind, index, k - 1],
            device_id={"tensor": step(self.me, k)},
            device_id_type=MESH,
        )
        copy.start()
        self.started.append(copy)
        return copy

    def reduce(self, part, peers=(1, 2, 3)):
        chunk = part.shape[-2] // CHUNKS
        for c in range(CHUNKS):
            here = pl.ds(c * chunk, chunk)
            for k in peers:
                self.reduces[c, k] = self.push(
                    part.at[step(self.me, k), here], self.landing.at[k - 1, here], 0, c, k
                )

    def run(self, part, function, rows_in, vecs, rows_out, sums_out, full, side=()):
        side = list(side)
        me = self.me
        chunk = part.shape[-2] // CHUNKS
        if side:
            side.pop(0)()
        sums, last = None, []
        for c in range(CHUNKS):
            here = pl.ds(c * chunk, chunk)
            for k in range(1, RING):
                self.reduces[c, k].wait_recv()
            total = part[me, here].astype(F32)
            for k in range(1, RING):
                total = total + self.landing[k - 1, here].astype(F32)
            spread, outs, parts = function(total, [ref[here].astype(F32) for ref in rows_in], vecs)
            if full is not None:
                full[me, here] = spread.astype(BF16)
                last += [
                    self.push(full.at[me, here], full.at[me, here], 1, c, k) for k in range(1, RING)
                ]
            for ref, value in zip(rows_out, outs):
                ref[here] = value.astype(ref.dtype)
            sums = parts if sums is None else [old + new for old, new in zip(sums, parts)]
        if sums_out is not None:
            sums_out[...] = jnp.concatenate(
                sums + [jnp.zeros((8 - len(sums), sums[0].shape[1]), F32)], axis=0
            )
        for work in side:
            work()
        for copy in last:
            copy.wait_recv()


TILES = ((2, 1), (3, 0))


def rows_of(ref, me, tile):
    return jnp.concatenate([ref[step(me, k)] for k in tile], axis=0)


def put_rows(ref, me, tile, value):
    rows = ref.shape[1]
    for i, k in enumerate(tile):
        ref[step(me, k)] = value[i * rows : (i + 1) * rows].astype(ref.dtype)


def wide_of(pack_ref):
    return pack_ref[...].reshape(-1, pack_ref.shape[-1])


def mlp_forward(me, full, up_ref, down_ref, bias, act_ref, slope_ref, part_ref, exchange):
    for tile in TILES:
        value = jnp.dot(rows_of(full, me, tile), wide_of(up_ref), preferred_element_type=F32)
        value = value + bias
        phi = 0.5 * (1.0 + lax.erf(value * (0.5**0.5)))
        act = (value * phi).astype(BF16)
        density = jnp.exp(-0.5 * value * value) * 0.3989422804014327
        put_rows(act_ref, me, tile, act)
        put_rows(slope_ref, me, tile, phi + value * density)
        put_rows(part_ref, me, tile, flat_dot(act, wide_of(down_ref)))
        exchange.reduce(part_ref, [k for k in tile if k])


def mlp_backward(me, full, up_ref, down_ref, slope_ref, pre_ref, bias_out, part_ref, exchange):
    total = None
    for tile in TILES:
        value = jnp.dot(rows_of(full, me, tile), wide_of(down_ref), preferred_element_type=F32)
        value = value * rows_of(slope_ref, me, tile)
        part = jnp.sum(value, axis=0, keepdims=True)
        total = part if total is None else total + part
        low = value.astype(BF16)
        put_rows(pre_ref, me, tile, low)
        put_rows(part_ref, me, tile, flat_dot(low, wide_of(up_ref)))
        exchange.reduce(part_ref, [k for k in tile if k])
    bias_out[...] = jnp.broadcast_to(total, bias_out.shape)


def product(former_ref, latter_ref, out_ref):
    def work():
        tokens = lambda ref: ref[...].reshape(-1, ref.shape[-1])
        size = 256

        def each(number, carry):
            columns = pl.ds(pl.multiple_of(number * size, size), size)
            left = former_ref[..., columns].reshape(-1, size)
            value = jnp.dot(left.T, tokens(latter_ref), preferred_element_type=F32)
            out_ref[number] = value.astype(BF16).reshape(out_ref.shape[1:])
            return carry

        lax.fori_loop(0, RING, each, 0)

    return work


def chain_call(cid, body, exchanges, packed_array, ins, outs, inside, any_names=(), extra=None):
    names = list(ins) + list(outs) + list(inside)
    rows, model = 64, 1024
    count = len(names)
    load_packed = packed_array is not None

    def kernel(*refs):
        refs = list(refs)
        packed = refs.pop(0) if load_packed else None
        env = SimpleNamespace(**dict(zip(names, refs[:count])))
        refs = refs[count:]
        me = lax.axis_index("tensor")
        barrier, peers = tensor_barrier(me)
        started = []
        loads = []
        if load_packed:
            env.up, env.down, local = refs[:3]
            refs = refs[3:]
            half = env.up.shape[2] // 2
            for i, matrix in enumerate((env.up, env.down)):
                loads += load_matrix(packed, matrix, i + 1, half, local.at[i])
        if extra is not None:
            env.extra = refs[3 * exchanges :]
            rank = lax.axis_index("dp")
            env.place = (rank // RING, lax.rem(rank, RING), lax.axis_index("section"))
            peers += dp_barrier(*env.place)[1]
        pl.semaphore_wait(barrier, peers)
        env.started = started
        rings = [
            Exchange(me, refs[3 * i + 1], refs[3 * i + 2], refs[3 * i], started)
            for i in range(exchanges)
        ]
        body(me, env, rings, loads)
        for copy in started:
            copy.wait_send()

    scratch = [pltpu.VMEM(shape, dtype) for shape, dtype in inside.values()]
    spec_of = lambda name: any_spec() if name in any_names else vmem_spec()
    args, in_specs = list(ins.values()), [spec_of(name) for name in ins]
    if load_packed:
        args, in_specs = [packed_array] + args, [any_spec()] + in_specs
        matrix = pltpu.VMEM((RING, RING, rows, model), BF16)
        scratch += [matrix, matrix, pltpu.SemaphoreType.DMA((2, 2))]
    for _ in range(exchanges):
        scratch += [
            pltpu.VMEM((RING - 1, rows, model), BF16),
            pltpu.SemaphoreType.DMA((2, CHUNKS, RING - 1)),
            pltpu.SemaphoreType.DMA((2, CHUNKS, RING - 1)),
        ]
    scratch += extra or []
    results = pl.pallas_call(
        kernel,
        out_shape=[jax.ShapeDtypeStruct(shape, dtype) for shape, dtype in outs.values()],
        in_specs=in_specs,
        out_specs=[spec_of(name) for name in outs],
        scratch_shapes=scratch,
        compiler_params=comm_params(cid),
    )(*args)
    return SimpleNamespace(**dict(zip(outs, results)))


def first_mlp_body(me, env, rings, loads):
    y, z, section = env.place
    send, recv, local = env.extra
    push = pusher(send, recv, env.started)
    halves = [pl.ds(0, HALF_ROWS // 2), pl.ds(HALF_ROWS // 2, HALF_ROWS // 2)]
    ring = Gather(
        ((0, (), True), (1, (), False)),
        [env.packed_next.at[section, :, :, half] for half in halves], y, z, (), push,
    )
    begin, near, middle, end, final = spread_stages(
        ring, [env.stage.at[1, half] for half in halves], local, section, push
    )
    rings[0].reduce(env.part)
    rings[0].run(
        env.part, middle_rows, [env.inputs], [env.vectors.at[0]],
        [env.attn_out, env.hidden], None, env.normed, [begin, near, middle],
    )
    for copy in loads:
        copy.wait()
    mlp_forward(
        me, env.normed, env.up, env.down, env.vectors[0, pl.ds(9 + me, 1), :], env.act, env.slope, env.sent, rings[1],
    )
    end()
    rings[1].run(
        env.sent, end_rows_first, [env.hidden], [env.vectors.at[0], env.vectors.at[1]],
        [env.mlp_out, env.outputs], None, env.next, [lambda: None, final],
    )


def last_mlp_body(me, env, rings, loads):
    rings[0].reduce(env.part)
    rings[0].run(
        env.part, middle_rows, [env.inputs], [env.vectors.at[1]],
        [env.attn_out, env.hidden], None, env.normed,
    )
    for copy in loads:
        copy.wait()
    mlp_forward(
        me, env.normed, env.up, env.down, env.vectors[1, pl.ds(9 + me, 1), :], env.act, env.slope,
        env.sent, rings[1],
    )
    rings[1].run(
        env.sent, end_rows_last, [env.hidden, env.upstream], [env.vectors.at[1]],
        [env.outputs], env.sums_end, env.mlp_rows,
    )
    mlp_backward(
        me, env.mlp_rows, env.up, env.down, env.slope, env.pre, env.bias_grad,
        env.sent_two, rings[2],
    )
    rings[2].run(
        env.sent_two, back_middle_rows, [env.upstream, env.hidden, env.attn_out],
        [env.vectors.at[1]], [env.hidden_grad], env.sums_middle, env.attn_rows,
        [
            product(env.mlp_rows, env.act, env.grad_down),
            product(env.normed, env.pre, env.grad_up),
        ],
    )


def attention_products(env):
    return [
        product(env.attn_rows_in, env.mixed, env.grad_out)
    ] + [
        product(env.normed_in, env.triple.at[which], env.grad_qkv.at[which])
        for which in range(3)
    ]


def between_body(me, env, rings, loads):
    y, z, section = env.place
    grads = [env.grad_qkv.at[which] for which in range(3)]
    grads += [env.grad_out, env.last_up, env.last_down]
    layer = layer_gradients(grads, env.extra, y, z, section, env.started)

    def swap():
        for work in attention_products(env):
            work()
        layer.keep(0)
        layer.swap(0)
        layer.begin(1)

    layer.swap(1)
    layer.keep(1)
    rings[0].reduce(env.part)
    rings[0].run(
        env.part, back_end_rows_last, [env.hidden_grad_in, env.inputs, env.mlp_out],
        [env.vectors.at[1], env.vectors.at[0]], [env.input_grad], env.sums_last, env.mlp_rows,
        [swap, lambda: layer.begin(0)],
    )
    for copy in loads:
        copy.wait()
    mlp_backward(
        me, env.mlp_rows, env.up, env.down, env.slope, env.pre, env.bias_grad, env.sent, rings[1],
    )
    layer.join()

    def products():
        product(env.mlp_rows, env.act, env.grad_down)()
        product(env.normed, env.pre, env.grad_up)()

    def rest():
        layer.turn()
        layer.join_two()
        layer.finish(env.summed)
        layer.end()

    rings[1].run(
        env.sent, back_middle_rows_low, [env.input_grad, env.hidden, env.attn_out],
        [env.vectors.at[0]], [env.hidden_grad], env.sums_middle, env.attn_rows, [products, rest],
    )


def back_middle_rows_low(total, rows, vecs):
    return back_middle_rows(total, [rows[0].astype(BF16).astype(F32)] + rows[1:], vecs)


def close_body(me, env, rings, loads):
    rings[0].reduce(env.part)
    rings[0].run(
        env.part, back_end_rows_first, [env.hidden_grad_in, env.inputs],
        [env.vectors.at[0]], [env.input_grad], env.sums_last, None, attention_products(env),
    )


def shards(tokens, segment_ids, w_qkv, w_out, w_up, w_down, vectors, out_bias, cotangent):
    section = lax.axis_index("section")
    tensor_rank = lax.axis_index("tensor")
    own = lambda pair: jnp.where(section == 0, pair[0], pair[1])
    rows = tokens.shape[1]
    width = tokens.shape[2]
    group = rows * RING
    square = (RING, RING)
    local_width = w_qkv.shape[3]
    local_hidden = w_up.shape[2]

    depth = w_out.shape[1]
    my_segments = own(segment_ids)
    wide_segments = jnp.pad(my_segments, (0, depth - rows)).astype(BF16)[None]
    small = jnp.pad(
        jnp.concatenate([vectors[0], out_bias, wide_segments], axis=0),
        ((0, 1), (0, 128 - depth)),
    )
    packed_first, stage, small_rows, normed, inputs, my_cotangent, seg_wide, seg_column = first_call(
        0, tokens, cotangent, w_qkv[0], w_out[0], w_up[0], w_down[0], small
    )

    whole = (RING, rows, width)
    blocks = lambda columns: square + (depth, columns)
    spread = (RING, rows, local_hidden)
    row_shape = (rows, width)
    def attend_layer(layer, normed, packed):
        return attend_call(
            2 + 12 * layer, layer, normed.reshape(group, width), packed, small_rows, seg_wide, seg_column
        )

    normed_first = normed
    *kept_first, part = attend_layer(0, normed_first, packed_first)
    first = chain_call(
        3, first_mlp_body, 2, packed_first,
        dict(
            part=part, inputs=inputs, vectors=small_rows, stage=stage,
        ),
        dict(
            attn_out=(row_shape, F32), hidden=(row_shape, F32), normed=(whole, BF16),
            act=(spread, BF16), slope=(spread, F32), mlp_out=(row_shape, F32),
            outputs=(row_shape, BF16), next=(whole, BF16),
            packed_next=((2,) + square + (HALF_ROWS, local_hidden), BF16),
        ),
        dict(sent=(whole, BF16)),
        ("packed_next",),
        gather_scratch(),
    )
    between = first.outputs
    packed_last = first.packed_next
    *kept_last, part = attend_layer(1, first.next, packed_last)
    last = chain_call(
        5, last_mlp_body, 3, packed_last,
        dict(
            part=part, inputs=between, vectors=small_rows, upstream=my_cotangent,
        ),
        dict(
            outputs=(row_shape, BF16), sums_end=((8, width), F32),
            hidden_grad=(row_shape, F32), sums_middle=((8, width), F32),
            attn_rows=(whole, BF16), bias_grad=((8, local_hidden), F32),
            grad_up=(blocks(local_hidden), BF16), grad_down=(blocks(local_hidden), BF16),
        ),
        dict(
            attn_out=(row_shape, F32), hidden=(row_shape, F32), normed=(whole, BF16),
            act=(spread, BF16), slope=(spread, F32), pre=(spread, BF16),
            mlp_rows=(whole, BF16), sent=(whole, BF16), sent_two=(whole, BF16),
        ),
    )
    outputs = last.outputs

    def attend_back_layer(layer, attn_rows, kept, packed):
        queries, keys_full, values_full, mixed, wide, lse = kept
        return attend_back_call(
            7 + 12 * layer, attn_rows.reshape(group, width), packed, queries, keys_full,
            values_full, wide, lse, seg_wide, seg_column,
        )

    attention_grads = dict(
        grad_out=(blocks(local_width), BF16), grad_qkv=((3,) + blocks(local_width), BF16),
    )
    triple, attend_last, part = attend_back_layer(1, last.attn_rows, kept_last, packed_last)
    middle = chain_call(
        8, between_body, 2, packed_first,
        dict(
            part=part, hidden_grad_in=last.hidden_grad, inputs=between,
            mlp_out=first.mlp_out, vectors=small_rows,
            slope=first.slope, act=first.act, normed=first.normed,
            hidden=first.hidden, attn_out=first.attn_out,
            attn_rows_in=last.attn_rows, mixed=kept_last[3], normed_in=first.next,
            triple=triple, last_up=last.grad_up, last_down=last.grad_down,
        ),
        dict(
            summed=((HALF_ROWS, local_hidden), F32),
            input_grad=(row_shape, F32), sums_last=((8, width), F32),
            hidden_grad=(row_shape, F32), sums_middle=((8, width), F32),
            attn_rows=(whole, BF16), bias_grad=((8, local_hidden), F32),
            grad_up=(blocks(local_hidden), BF16), grad_down=(blocks(local_hidden), BF16),
            **attention_grads,
        ),
        dict(pre=(spread, BF16), mlp_rows=(whole, BF16), sent=(whole, BF16)),
        ("last_up", "last_down"),
        LayerGradients.scratch(HALF_ROWS // 3, local_hidden),
    )
    last_grad = middle.input_grad
    triple, attend_first, part = attend_back_layer(0, middle.attn_rows, kept_first, packed_first)
    close = chain_call(
        9, close_body, 1, None,
        dict(
            part=part, hidden_grad_in=middle.hidden_grad, inputs=inputs,
            vectors=small_rows, attn_rows_in=middle.attn_rows, mixed=kept_first[3],
            normed_in=normed_first, triple=triple,
        ),
        dict(input_grad=(row_shape, F32), sums_last=((8, width), F32), **attention_grads),
        dict(),
    )
    input_grad = close.input_grad
    sums = [
        [close.sums_last, middle.sums_middle, middle.sums_last[2:], attend_first, middle.bias_grad],
        [middle.sums_last, last.sums_middle, last.sums_end, attend_last, last.bias_grad],
    ]
    grads = [close.grad_qkv, close.grad_out, middle.grad_up, middle.grad_down]
    first_grad = input_grad

    small_sum, sum_qkv, sum_out, sum_up, sum_down, out_pair, grad_pair = final_call(
        10, sums[0] + sums[1], grads, middle.summed, [outputs, between, last_grad, first_grad]
    )
    return (
        out_pair[None],
        grad_pair[None],
        sum_qkv[None],
        sum_out[None],
        sum_up[None],
        sum_down[None],
        small_sum[:13, :depth][None],
        small_sum[13:14, :depth],
    )


def solution(mesh):
    in_specs = (
        P(None, ("dp", "tensor"), None),
        P(None, ("dp", "tensor")),
        P("section", None, "dp", "tensor"),
        P("section", "dp", "tensor"),
        P("section", "dp", "tensor"),
        P("section", "dp", "tensor"),
        P("section", None, "dp"),
        P("section", "dp"),
        P(None, ("dp", "tensor"), None),
    )
    out_specs = (
        P("section", None, ("dp", "tensor"), None),
        P("section", None, ("dp", "tensor"), None),
        P("section", None, "dp", "tensor"),
        P("section", "dp", "tensor"),
        P("section", "dp", "tensor"),
        P("section", "dp", "tensor"),
        P("section", None, "dp"),
        P("section", "dp"),
    )
    return jax.shard_map(shards, mesh=mesh, in_specs=in_specs, out_specs=out_specs, check_vma=False)
```
